32 devices in a mesh: batch: 16 (over z, y, core), seq: 2 (over x).
Axes of the slice: x: 2, y: 2, z: 4, core: 2. Of those that a mesh axis runs over, the one named last changes fastest.
Arguments:
- source: bfloat16 [16, 1024, 512], P('batch', 'seq'), may hold values from -6 to 6
- target: bfloat16 [16, 1024, 512], P('batch', 'seq'), may hold values from -6 to 6
- source_ids: int32 [16, 1024], P('batch', 'seq'), may hold values from 0 to 2, as said below
- target_ids: int32 [16, 1024], P('batch', 'seq'), may hold values from 0 to 2, as said below
- out_grad: bfloat16 [16, 1024, 512], P('batch', 'seq'), may hold values from -6 to 6
- enc_qkv: bfloat16 [3, 512, 512], replicated, may hold values from -0.25 to 0.25
- enc_out: bfloat16 [512, 512], replicated, may hold values from -2 to 2
- enc_up: bfloat16 [512, 2048], replicated, may hold values from -0.25 to 0.25
- enc_up_bias: float32 [2048], replicated, may hold values from -3 to 3
- enc_down: bfloat16 [2048, 512], replicated, may hold values from -0.125 to 0.125
- enc_down_bias: float32 [512], replicated, may hold values from -3 to 3
- enc_gain: float32 [2, 512], replicated, may hold values from 0.1 to 1.9
- enc_shift: float32 [2, 512], replicated, may hold values from -3 to 3
- dec_qkv: bfloat16 [3, 512, 512], replicated, may hold values from -0.25 to 0.25
- dec_out: bfloat16 [512, 512], replicated, may hold values from -2 to 2
- cross_qkv: bfloat16 [3, 512, 512], replicated, may hold values from -0.25 to 0.25
- cross_out: bfloat16 [512, 512], replicated, may hold values from -2 to 2
- dec_up: bfloat16 [512, 2048], replicated, may hold values from -0.25 to 0.25
- dec_up_bias: float32 [2048], replicated, may hold values from -3 to 3
- dec_down: bfloat16 [2048, 512], replicated, may hold values from -0.125 to 0.125
- dec_down_bias: float32 [512], replicated, may hold values from -3 to 3
- dec_gain: float32 [3, 512], replicated, may hold values from 0.1 to 1.9
- dec_shift: float32 [3, 512], replicated, may hold values from -3 to 3
Outputs:
- decoded: bfloat16 [16, 1024, 512], P('batch', 'seq')
- source_grad: bfloat16 [16, 1024, 512], P('batch', 'seq')
- target_grad: bfloat16 [16, 1024, 512], P('batch', 'seq')
- enc_qkv_grad: float32 [3, 512, 512], P(None, 'seq', 'batch')
- enc_out_grad: float32 [512, 512], P('seq', 'batch')
- enc_up_grad: float32 [512, 2048], P('seq', 'batch')
- enc_up_bias_grad: float32 [2048], replicated
- enc_down_grad: float32 [2048, 512], P('seq', 'batch')
- enc_down_bias_grad: float32 [512], replicated
- enc_gain_grad: float32 [2, 512], replicated
- enc_shift_grad: float32 [2, 512], replicated
- dec_qkv_grad: float32 [3, 512, 512], P(None, 'seq', 'batch')
- dec_out_grad: float32 [512, 512], P('seq', 'batch')
- cross_qkv_grad: float32 [3, 512, 512], P(None, 'seq', 'batch')
- cross_out_grad: float32 [512, 512], P('seq', 'batch')
- dec_up_grad: float32 [512, 2048], P('seq', 'batch')
- dec_up_bias_grad: float32 [2048], replicated
- dec_down_grad: float32 [2048, 512], P('seq', 'batch')
- dec_down_bias_grad: float32 [512], replicated
- dec_gain_grad: float32 [3, 512], replicated
- dec_shift_grad: float32 [3, 512], replicated
The draws below stay inside these ranges and needn't reach their ends.
Inputs may be any that keep to these rules, and one draw needn't show every extreme that they name: `source_ids`: in every row the ids never fall and take each of the values 0, 1 and 2; id 1 begins at a position from 1 to 511 and id 2 at a position from 513 to 1023. `target_ids`: in every row the ids never fall and take each of the values 0, 1 and 2; id 1 begins at a position from 1 to 511 and id 2 at a position from 513 to 1023.
All inputs are finite; a program needn't handle non-finite values.
Results may differ from the reference program's by a relative error of at most 0.04.
Values may be sent and summed in bfloat16 or wider, within the bound.
A program may use at most 192 MiB of HBM per device.

```python
import math
import jax
import jax.numpy as jnp
from jax import lax

D = 512
HEADS = 8
HEAD_DIM = 64
FF = 2048
ROW_LEN = 1024
TOK_DEV = 512
ROWS = 16


def row_boundaries(key):
    first_key, last_key = jax.random.split(key)
    first = jax.random.randint(first_key, (ROWS, 1), 1, TOK_DEV)
    last = jax.random.randint(last_key, (ROWS, 1), ROW_LEN - TOK_DEV + 1, ROW_LEN)
    positions = jnp.arange(ROW_LEN, dtype=jnp.int32)[None, :]
    return (positions >= first).astype(jnp.int32) + (positions >= last).astype(jnp.int32)


def draw_source_ids(key, part):
    key = jax.random.fold_in(key, 11)
    return row_boundaries(key)


def draw_target_ids(key, part):
    key = jax.random.fold_in(key, 23)
    return row_boundaries(key)


def spiked(drawn, key, source, target, blocks, factor):
    def block_of(dim):
        return (jnp.arange(drawn.shape[dim]) // (drawn.shape[dim] // blocks)).reshape((-1,) + (1,) * (drawn.ndim - 1 - dim))

    first = jax.random.permutation(key, blocks)[block_of(target)]
    other_side = (block_of(target) + blocks // 2) % blocks
    return jnp.where((block_of(source) == first) | (block_of(source) == other_side), factor * drawn, drawn)


def steps_of(stream_key, shape, pieces, smallest, top_value):
    def one(dim, blocks):
        steps = jax.random.uniform(jax.random.fold_in(jax.random.fold_in(stream_key, 6), dim), (blocks,), jnp.float32, smallest / len(pieces), top_value / len(pieces))
        return jnp.repeat(jnp.exp(steps), shape[dim] // blocks).reshape((-1,) + (1,) * (len(shape) - dim - 1))

    level = one(*pieces[0])
    for cut in pieces[1:]:
        level = level * one(*cut)
    return level


def noise(stream_key, dims, scale, bound, shards=(), kind=jnp.bfloat16):
    entries = jax.random.normal(stream_key, dims, jnp.float32) * scale
    if len(shards) > 0:
        entries = steps_of(stream_key, dims, shards, -0.22, 0.18) * entries
    return jnp.clip(entries, min=-bound, max=bound).astype(kind)


def gaussian_with(own_key, dims, scale, reach, pieces, heavy, held_as=jnp.bfloat16):
    drawn = scale * jax.random.normal(own_key, dims, jnp.float32)
    if pieces:
        drawn = drawn * steps_of(own_key, dims, pieces, -0.22, 0.18)
    return jnp.clip(spiked(drawn, jax.random.fold_in(own_key, 3), *heavy), -reach, reach).astype(held_as)


def setup_inputs(seed: int = 0) -> dict:
    arg_keys = jax.random.split(jax.random.key(seed), 24)
    return {
        "source": noise(arg_keys[0], (ROWS, ROW_LEN, D), 1.0, 6.0, ((0, 16), (1, 2))),
        "target": noise(arg_keys[1], (ROWS, ROW_LEN, D), 1.0, 6.0, ((0, 16), (1, 2))),
        "source_ids": draw_source_ids(jax.random.fold_in(arg_keys[23], 71), 0),
        "target_ids": draw_target_ids(jax.random.fold_in(arg_keys[23], 71), 0),
        "out_grad": gaussian_with(arg_keys[4], (ROWS, ROW_LEN, D), 1.0, 6.0, ((0, 16), (1, 2)), (0, 2, 16, 2.0)),
        "enc_qkv": noise(arg_keys[5], (3, D, D), D ** -0.5, 0.25),
        "enc_out": noise(arg_keys[6], (D, D), (max(1, D * 16 // ROW_LEN)) ** -0.5, 2.0),
        "enc_up": noise(arg_keys[7], (D, FF), D ** -0.5, 0.25),
        "enc_up_bias": noise(arg_keys[8], (FF,), 0.5, 3.0, (), jnp.float32),
        "enc_down": noise(arg_keys[9], (FF, D), FF ** -0.5, 0.125),
        "enc_down_bias": noise(arg_keys[10], (D,), 0.5, 3.0, (), jnp.float32),
        "enc_gain": jnp.clip(1.0 + 0.18 * jax.random.normal(arg_keys[11], (2, D), jnp.float32), 0.1, 1.9),
        "enc_shift": noise(arg_keys[12], (2, D), 0.5, 3.0, (), jnp.float32),
        "dec_qkv": noise(arg_keys[13], (3, D, D), D ** -0.5, 0.25),
        "dec_out": noise(arg_keys[14], (D, D), (max(1, D * 16 // ROW_LEN)) ** -0.5, 2.0),
        "cross_qkv": noise(arg_keys[15], (3, D, D), D ** -0.5, 0.25),
        "cross_out": noise(arg_keys[16], (D, D), (max(1, D * 16 // ROW_LEN)) ** -0.5, 2.0),
        "dec_up": noise(arg_keys[17], (D, FF), D ** -0.5, 0.25),
        "dec_up_bias": noise(arg_keys[18], (FF,), 0.5, 3.0, (), jnp.float32),
        "dec_down": noise(arg_keys[19], (FF, D), FF ** -0.5, 0.125),
        "dec_down_bias": noise(arg_keys[20], (D,), 0.5, 3.0, (), jnp.float32),
        "dec_gain": jnp.clip(1.0 + 0.18 * jax.random.normal(arg_keys[21], (3, D), jnp.float32), 0.1, 1.9),
        "dec_shift": noise(arg_keys[22], (3, D), 0.5, 3.0, (), jnp.float32),
    }


@jax.custom_vjp
def low(v):
    return lax.optimization_barrier(v.astype(jnp.bfloat16)).astype(jnp.float32)

@jax.custom_vjp
def low_back(v):
    return v

def low_keep(v):
    return (low(v), None)

def low_pass(kept, grad):
    return (grad,)

def back_keep(v):
    return (v, None)

def back_low(kept, grad):
    return (low(grad),)
low.defvjp(low_keep, low_pass)
low_back.defvjp(back_keep, back_low)
NEGATIVE = -1e+30

def layer_norm(value, gain, shift):
    mean = lax.optimization_barrier(jnp.mean(value, axis=-1, keepdims=True))
    centred = value - mean
    spread = lax.optimization_barrier(jnp.mean(centred * centred, axis=-1, keepdims=True))
    return centred * lax.rsqrt(spread + 1e-06) * gain + shift

def project(value, weight):
    return jnp.dot(value, weight, precision=lax.Precision.HIGHEST, preferred_element_type=jnp.float32)

def split_heads(value):
    return value.reshape(value.shape[0], HEADS, HEAD_DIM)

def attention(queries, keys, values, query_ids, key_ids, causal):
    length = queries.shape[0]
    width = math.gcd(length, 512)
    count = length // width
    key_pos = jnp.arange(keys.shape[0], dtype=jnp.int32)
    heads_k = split_heads(keys)
    heads_v = split_heads(values)

    def one_block(inputs):
        block_q, block_ids, offset = inputs
        scores = jnp.einsum('qhe,khe->hqk', block_q, heads_k, precision=lax.Precision.HIGHEST) * 0.125
        scores = low_back(scores)
        allowed = block_ids[:, None] == key_ids[None, :]
        if causal:
            query_pos = offset + jnp.arange(width, dtype=jnp.int32)
            allowed = allowed & (query_pos[:, None] >= key_pos[None, :])
        scores = jnp.where(allowed[None], scores, NEGATIVE)
        largest = lax.optimization_barrier(jnp.max(scores, axis=-1, keepdims=True))
        total = largest + jnp.log(lax.optimization_barrier(jnp.sum(jnp.exp(scores - largest), axis=-1, keepdims=True)))
        chances = low(jnp.exp(scores - total))
        return jnp.einsum('hqk,khe->qhe', chances, heads_v, precision=lax.Precision.HIGHEST)
    offsets = jnp.arange(count, dtype=jnp.int32) * width
    blocks = lax.map(jax.checkpoint(one_block), (split_heads(queries).reshape(count, width, HEADS, HEAD_DIM), query_ids.reshape(count, width), offsets))
    return low_back(low(blocks.reshape(length, HEADS * HEAD_DIM)))

def row_forward(params, source_row, target_row, source_row_ids, target_row_ids):
    enc_qkv, enc_out, enc_up, enc_up_bias, enc_down, enc_down_bias, enc_gain, enc_shift, dec_qkv, dec_out, cross_qkv, cross_out, dec_up, dec_up_bias, dec_down, dec_down_bias, dec_gain, dec_shift = params

    def rounded(value, weight):
        return low_back(low(project(value, weight)))

    def feed_forward(value, up_weight, up_bias, down_weight, down_bias):
        inner = low_back(project(low(value), up_weight) + up_bias)
        return low_back(project(low(jax.nn.gelu(inner)), down_weight) + down_bias)
    attended = attention(rounded(source_row, enc_qkv[0]), rounded(source_row, enc_qkv[1]), rounded(source_row, enc_qkv[2]), source_row_ids, source_row_ids, False)
    hidden = layer_norm(source_row + low_back(project(attended, enc_out)), enc_gain[0], enc_shift[0])
    memory = layer_norm(hidden + feed_forward(hidden, enc_up, enc_up_bias, enc_down, enc_down_bias), enc_gain[1], enc_shift[1])
    memory_low = low(memory)
    attended = attention(rounded(target_row, dec_qkv[0]), rounded(target_row, dec_qkv[1]), rounded(target_row, dec_qkv[2]), target_row_ids, target_row_ids, True)
    first = layer_norm(target_row + low_back(project(attended, dec_out)), dec_gain[0], dec_shift[0])
    crossed = attention(rounded(low(first), cross_qkv[0]), rounded(memory_low, cross_qkv[1]), rounded(memory_low, cross_qkv[2]), target_row_ids, source_row_ids, False)
    second = layer_norm(first + low_back(project(crossed, cross_out)), dec_gain[1], dec_shift[1])
    return layer_norm(second + feed_forward(second, dec_up, dec_up_bias, dec_down, dec_down_bias), dec_gain[2], dec_shift[2])

def reference(source, target, source_ids, target_ids, out_grad, enc_qkv, enc_out, enc_up, enc_up_bias, enc_down, enc_down_bias, enc_gain, enc_shift, dec_qkv, dec_out, cross_qkv, cross_out, dec_up, dec_up_bias, dec_down, dec_down_bias, dec_gain, dec_shift):
    params = tuple((weight.astype(jnp.float32) for weight in (enc_qkv, enc_out, enc_up, enc_up_bias, enc_down, enc_down_bias, enc_gain, enc_shift, dec_qkv, dec_out, cross_qkv, cross_out, dec_up, dec_up_bias, dec_down, dec_down_bias, dec_gain, dec_shift)))

    def row_step(totals, row_data):
        source_row, target_row, source_row_ids, target_row_ids, upstream = row_data

        def forward(weights, first_input, second_input):
            return row_forward(weights, first_input, second_input, source_row_ids, target_row_ids)
        decoded_row, pull = jax.vjp(forward, params, source_row.astype(jnp.float32), target_row.astype(jnp.float32))
        weight_grads, source_row_grad, target_row_grad = pull(upstream.astype(jnp.float32))
        totals = jax.tree.map(lambda running, fresh: running + fresh, totals, weight_grads)
        return (totals, (decoded_row.astype(jnp.bfloat16), source_row_grad.astype(jnp.bfloat16), target_row_grad.astype(jnp.bfloat16)))
    start_totals = jax.tree.map(jnp.zeros_like, params)
    totals, outputs = lax.scan(row_step, start_totals, (source, target, source_ids, target_ids, out_grad))
    decoded, source_grad, target_grad = outputs
    return (decoded, source_grad, target_grad, totals[0], totals[1], totals[2], totals[3], totals[4], totals[5], totals[6], totals[7], totals[8], totals[9], totals[10], totals[11], totals[12], totals[13], totals[14], totals[15], totals[16], totals[17])
```

```python
import functools

import jax
import jax.numpy as jnp
from jax import lax
from jax.experimental import pallas as pl
from jax.experimental.pallas import tpu as pltpu
from jax.sharding import PartitionSpec as P

HEAD_DIM = 64
NEGATIVE = -1e30
BF = jnp.bfloat16
F32 = jnp.float32
BOTH = ("batch", "seq")


def layer_norm(value, gain, shift):
    mean = jnp.mean(value, axis=-1, keepdims=True)
    centred = value - mean
    spread = jnp.mean(centred * centred, axis=-1, keepdims=True)
    return centred * lax.rsqrt(spread + 1e-06) * gain + shift


def norm_back(value, gain, shift, grad):
    _, pull = jax.vjp(layer_norm, value, gain, shift)
    return pull(grad)


def gelu_back(inner, grad):
    _, pull = jax.vjp(jax.nn.gelu, inner)
    return pull(grad)[0]


def matmul(left, right):
    return jnp.dot(left, right, preferred_element_type=jnp.float32)


def weight_grad(inputs, grad):
    return lax.dot_general(
        inputs, grad, (((0,), (0,)), ((), ())), preferred_element_type=jnp.float32
    )


def input_grad(grad, weight):
    return lax.dot_general(
        grad, weight, (((1,), (1,)), ((), ())), preferred_element_type=jnp.float32
    )


def to_low(value):
    return value.astype(jnp.bfloat16)


def split_heads(value):
    return value.reshape(value.shape[0], -1, HEAD_DIM)


def block_live(query_ids, key_ids, offset, block, rows, causal):
    first_key = lax.dynamic_index_in_dim(key_ids, block * rows, 0, keepdims=False)
    last_key = lax.dynamic_index_in_dim(key_ids, block * rows + rows - 1, 0, keepdims=False)
    live = (first_key <= query_ids[rows - 1]) & (query_ids[0] <= last_key)
    if causal:
        live = live & (block * rows <= offset + rows - 1)
    return live


def block_scores(queries, keys_all, query_ids, key_ids, offset, block, causal):
    rows = queries.shape[0]
    key_block = lax.dynamic_slice_in_dim(keys_all, block * rows, rows, 0)
    id_block = lax.dynamic_slice_in_dim(key_ids, block * rows, rows, 0)
    scores = (
        jnp.einsum("qhe,khe->hqk", queries, key_block, preferred_element_type=jnp.float32) * 0.125
    )
    allowed = query_ids[:, None] == id_block[None, :]
    if causal:
        positions = jnp.arange(rows, dtype=jnp.int32)
        allowed = allowed & ((offset + positions)[:, None] >= (block * rows + positions)[None, :])
    allowed = allowed[None]
    return (jnp.where(allowed, scores, NEGATIVE), allowed, key_block)


def attend_forward(queries, keys_all, values_all, query_ids, key_ids, offset, causal):
    rows = queries.shape[0]
    heads_count = queries.shape[1]
    count = keys_all.shape[0] // rows

    def first_pass(block, carry):

        def first_compute(state):
            largest, total = state
            scores, allowed, _ = block_scores(
                queries, keys_all, query_ids, key_ids, offset, block, causal
            )
            newest = jnp.maximum(largest, jnp.max(scores, axis=-1))
            terms = jnp.where(allowed, jnp.exp(scores - newest[..., None]), 0.0)
            return (newest, total * jnp.exp(largest - newest) + jnp.sum(terms, axis=-1))

        live = block_live(query_ids, key_ids, offset, block, rows, causal)
        return lax.cond(live, first_compute, lambda state: state, carry)

    initial = (
        jnp.full((heads_count, rows), NEGATIVE, jnp.float32),
        jnp.zeros((heads_count, rows), jnp.float32),
    )
    largest, total = lax.fori_loop(0, count, first_pass, initial)
    log_total = largest + jnp.log(total)

    def second_pass(block, carry):

        def second_compute(output):
            scores, allowed, _ = block_scores(
                queries, keys_all, query_ids, key_ids, offset, block, causal
            )
            value_block = lax.dynamic_slice_in_dim(values_all, block * rows, rows, 0)
            chances = jnp.where(allowed, jnp.exp(scores - log_total[..., None]), 0.0)
            return output + jnp.einsum(
                "hqk,khe->qhe", to_low(chances), value_block, preferred_element_type=jnp.float32
            )

        live = block_live(query_ids, key_ids, offset, block, rows, causal)
        return lax.cond(live, second_compute, lambda output: output, carry)

    output = lax.fori_loop(0, count, second_pass, jnp.zeros(queries.shape, jnp.float32))
    return (output, log_total)


def attend_backward(
    queries, keys_all, values_all, query_ids, key_ids, offset, causal, grad_out, settle, log_total
):
    rows = queries.shape[0]
    count = keys_all.shape[0] // rows

    def step_block(block, carry):

        def step_compute(state):
            query_grad, key_grads, value_grads = state
            scores, allowed, key_block = block_scores(
                queries, keys_all, query_ids, key_ids, offset, block, causal
            )
            value_block = lax.dynamic_slice_in_dim(values_all, block * rows, rows, 0)
            chances = jnp.where(allowed, jnp.exp(scores - log_total[..., None]), 0.0)
            chance_grad = jnp.einsum(
                "qhe,khe->hqk", grad_out, value_block, preferred_element_type=jnp.float32
            )
            score_grad = to_low(chances * (chance_grad - settle[..., None]))
            query_grad = (
                query_grad
                + jnp.einsum(
                    "hqk,khe->qhe", score_grad, key_block, preferred_element_type=jnp.float32
                )
                * 0.125
            )
            key_part = (
                jnp.einsum("hqk,qhe->khe", score_grad, queries, preferred_element_type=jnp.float32)
                * 0.125
            )
            value_part = jnp.einsum(
                "hqk,qhe->khe", to_low(chances), grad_out, preferred_element_type=jnp.float32
            )
            key_grads = lax.dynamic_update_slice_in_dim(key_grads, key_part, block * rows, 0)
            value_grads = lax.dynamic_update_slice_in_dim(value_grads, value_part, block * rows, 0)
            return (query_grad, key_grads, value_grads)

        live = block_live(query_ids, key_ids, offset, block, rows, causal)
        return lax.cond(live, step_compute, lambda state: state, carry)

    initial = (
        jnp.zeros(queries.shape, jnp.float32),
        jnp.zeros(keys_all.shape, jnp.float32),
        jnp.zeros(values_all.shape, jnp.float32),
    )
    return lax.fori_loop(0, count, step_block, initial)


def attention_back(
    queries, keys_all, values_all, query_ids, key_ids_all, causal, grad_out, output, log_total
):
    rows = queries.shape[0]
    offset = lax.axis_index("seq") * rows
    settle = jnp.einsum("qhe,qhe->hq", grad_out.astype(jnp.float32), output)
    query_grad, key_terms, value_terms = attend_backward(
        queries,
        keys_all,
        values_all,
        query_ids,
        key_ids_all,
        offset,
        causal,
        grad_out,
        settle,
        log_total,
    )
    key_sum, value_sum = (
        lax.psum_scatter(
            key_terms.reshape(key_terms.shape[0], -1).astype(jnp.bfloat16),
            "seq",
            scatter_dimension=0,
            tiled=True,
        ).astype(jnp.float32),
        lax.psum_scatter(
            value_terms.reshape(value_terms.shape[0], -1).astype(jnp.bfloat16),
            "seq",
            scatter_dimension=0,
            tiled=True,
        ).astype(jnp.float32),
    )
    return (query_grad, key_sum, value_sum)


def general_shards(
    source,
    target,
    source_ids,
    target_ids,
    out_grad,
    enc_qkv,
    enc_out,
    enc_up,
    enc_up_bias,
    enc_down,
    enc_down_bias,
    enc_gain,
    enc_shift,
    dec_qkv,
    dec_out,
    cross_qkv,
    cross_out,
    dec_up,
    dec_up_bias,
    dec_down,
    dec_down_bias,
    dec_gain,
    dec_shift,
):
    src_rows = source[0]
    tgt_rows = target[0]
    src_ids = source_ids[0]
    tgt_ids = target_ids[0]
    rows = src_rows.shape[0]
    offset = lax.axis_index("seq") * rows
    enc_queries = to_low(matmul(src_rows, enc_qkv[0]))
    enc_keys = to_low(matmul(src_rows, enc_qkv[1]))
    enc_values = to_low(matmul(src_rows, enc_qkv[2]))
    enc_keys_all, enc_values_all, src_ids_all = (
        lax.all_gather(enc_keys, "seq", axis=0, tiled=True),
        lax.all_gather(enc_values, "seq", axis=0, tiled=True),
        lax.all_gather(src_ids, "seq", axis=0, tiled=True),
    )
    enc_att, enc_lse = attend_forward(
        split_heads(enc_queries),
        split_heads(enc_keys_all),
        split_heads(enc_values_all),
        src_ids,
        src_ids_all,
        offset,
        False,
    )
    enc_att_low = to_low(enc_att.reshape(rows, -1))
    enc_pre = src_rows.astype(jnp.float32) + matmul(enc_att_low, enc_out)
    hidden = layer_norm(enc_pre, enc_gain[0], enc_shift[0])
    hidden_low = to_low(hidden)
    enc_inner = matmul(hidden_low, enc_up) + enc_up_bias
    enc_act = to_low(jax.nn.gelu(enc_inner))
    enc_last = hidden + matmul(enc_act, enc_down) + enc_down_bias
    memory = layer_norm(enc_last, enc_gain[1], enc_shift[1])
    memory_low = to_low(memory)
    mem_keys = to_low(matmul(memory_low, cross_qkv[1]))
    mem_values = to_low(matmul(memory_low, cross_qkv[2]))
    mem_keys_all, mem_values_all = (
        lax.all_gather(mem_keys, "seq", axis=0, tiled=True),
        lax.all_gather(mem_values, "seq", axis=0, tiled=True),
    )
    dec_queries = to_low(matmul(tgt_rows, dec_qkv[0]))
    dec_keys = to_low(matmul(tgt_rows, dec_qkv[1]))
    dec_values = to_low(matmul(tgt_rows, dec_qkv[2]))
    dec_keys_all, dec_values_all, tgt_ids_all = (
        lax.all_gather(dec_keys, "seq", axis=0, tiled=True),
        lax.all_gather(dec_values, "seq", axis=0, tiled=True),
        lax.all_gather(tgt_ids, "seq", axis=0, tiled=True),
    )
    dec_att, dec_lse = attend_forward(
        split_heads(dec_queries),
        split_heads(dec_keys_all),
        split_heads(dec_values_all),
        tgt_ids,
        tgt_ids_all,
        offset,
        True,
    )
    dec_att_low = to_low(dec_att.reshape(rows, -1))
    dec_pre = tgt_rows.astype(jnp.float32) + matmul(dec_att_low, dec_out)
    first = layer_norm(dec_pre, dec_gain[0], dec_shift[0])
    first_low = to_low(first)
    cross_queries = to_low(matmul(first_low, cross_qkv[0]))
    cross_att, cross_lse = attend_forward(
        split_heads(cross_queries),
        split_heads(mem_keys_all),
        split_heads(mem_values_all),
        tgt_ids,
        src_ids_all,
        offset,
        False,
    )
    cross_att_low = to_low(cross_att.reshape(rows, -1))
    cross_pre = first + matmul(cross_att_low, cross_out)
    second = layer_norm(cross_pre, dec_gain[1], dec_shift[1])
    second_low = to_low(second)
    dec_inner = matmul(second_low, dec_up) + dec_up_bias
    dec_act = to_low(jax.nn.gelu(dec_inner))
    dec_last = second + matmul(dec_act, dec_down) + dec_down_bias
    decoded = layer_norm(dec_last, dec_gain[2], dec_shift[2])
    upstream = out_grad[0].astype(jnp.float32)
    grad_last, gain_two, shift_two = norm_back(dec_last, dec_gain[2], dec_shift[2], upstream)
    branch_low = to_low(grad_last)
    dec_down_g = weight_grad(dec_act, branch_low)
    dec_down_bias_g = jnp.sum(branch_low.astype(jnp.float32), axis=0)
    inner_low = to_low(gelu_back(dec_inner, input_grad(branch_low, dec_down)))
    dec_up_g = weight_grad(second_low, inner_low)
    dec_up_bias_g = jnp.sum(inner_low.astype(jnp.float32), axis=0)
    grad_second = grad_last + input_grad(inner_low, dec_up)
    grad_cross_pre, gain_one, shift_one = norm_back(
        cross_pre, dec_gain[1], dec_shift[1], grad_second
    )
    mixed_low = to_low(grad_cross_pre)
    cross_out_g = weight_grad(cross_att_low, mixed_low)
    cross_att_grad = to_low(input_grad(mixed_low, cross_out))
    cross_query_grad, mem_key_sum, mem_value_sum = attention_back(
        split_heads(cross_queries),
        split_heads(mem_keys_all),
        split_heads(mem_values_all),
        tgt_ids,
        src_ids_all,
        False,
        split_heads(cross_att_grad),
        cross_att,
        cross_lse,
    )
    mem_key_low = to_low(mem_key_sum)
    mem_value_low = to_low(mem_value_sum)
    cross_query_low = to_low(cross_query_grad.reshape(rows, -1))
    cross_qkv_g = jnp.stack(
        [
            weight_grad(first_low, cross_query_low),
            weight_grad(memory_low, mem_key_low),
            weight_grad(memory_low, mem_value_low),
        ]
    )
    grad_first = grad_cross_pre + input_grad(cross_query_low, cross_qkv[0])
    grad_dec_pre, gain_zero, shift_zero = norm_back(dec_pre, dec_gain[0], dec_shift[0], grad_first)
    self_low = to_low(grad_dec_pre)
    dec_out_g = weight_grad(dec_att_low, self_low)
    dec_att_grad = to_low(input_grad(self_low, dec_out))
    dec_query_grad, dec_key_sum, dec_value_sum = attention_back(
        split_heads(dec_queries),
        split_heads(dec_keys_all),
        split_heads(dec_values_all),
        tgt_ids,
        tgt_ids_all,
        True,
        split_heads(dec_att_grad),
        dec_att,
        dec_lse,
    )
    dec_query_low = to_low(dec_query_grad.reshape(rows, -1))
    dec_key_low = to_low(dec_key_sum)
    dec_value_low = to_low(dec_value_sum)
    dec_qkv_g = jnp.stack(
        [
            weight_grad(tgt_rows, dec_query_low),
            weight_grad(tgt_rows, dec_key_low),
            weight_grad(tgt_rows, dec_value_low),
        ]
    )
    tgt_grad = (
        grad_dec_pre
        + input_grad(dec_query_low, dec_qkv[0])
        + input_grad(dec_key_low, dec_qkv[1])
        + input_grad(dec_value_low, dec_qkv[2])
    )
    dec_gain_g = jnp.stack([gain_zero, gain_one, gain_two])
    dec_shift_g = jnp.stack([shift_zero, shift_one, shift_two])
    grad_memory = input_grad(mem_key_low, cross_qkv[1]) + input_grad(mem_value_low, cross_qkv[2])
    grad_enc_last, enc_gain_one, enc_shift_one = norm_back(
        enc_last, enc_gain[1], enc_shift[1], grad_memory
    )
    enc_branch_low = to_low(grad_enc_last)
    enc_down_g = weight_grad(enc_act, enc_branch_low)
    enc_down_bias_g = jnp.sum(enc_branch_low.astype(jnp.float32), axis=0)
    enc_inner_low = to_low(gelu_back(enc_inner, input_grad(enc_branch_low, enc_down)))
    enc_up_g = weight_grad(hidden_low, enc_inner_low)
    enc_up_bias_g = jnp.sum(enc_inner_low.astype(jnp.float32), axis=0)
    grad_hidden = grad_enc_last + input_grad(enc_inner_low, enc_up)
    grad_enc_pre, enc_gain_zero, enc_shift_zero = norm_back(
        enc_pre, enc_gain[0], enc_shift[0], grad_hidden
    )
    enc_mixed_low = to_low(grad_enc_pre)
    enc_out_g = weight_grad(enc_att_low, enc_mixed_low)
    enc_att_grad = to_low(input_grad(enc_mixed_low, enc_out))
    enc_query_grad, enc_key_sum, enc_value_sum = attention_back(
        split_heads(enc_queries),
        split_heads(enc_keys_all),
        split_heads(enc_values_all),
        src_ids,
        src_ids_all,
        False,
        split_heads(enc_att_grad),
        enc_att,
        enc_lse,
    )
    enc_query_low = to_low(enc_query_grad.reshape(rows, -1))
    enc_key_low = to_low(enc_key_sum)
    enc_value_low = to_low(enc_value_sum)
    enc_qkv_g = jnp.stack(
        [
            weight_grad(src_rows, enc_query_low),
            weight_grad(src_rows, enc_key_low),
            weight_grad(src_rows, enc_value_low),
        ]
    )
    src_grad = (
        grad_enc_pre
        + input_grad(enc_query_low, enc_qkv[0])
        + input_grad(enc_key_low, enc_qkv[1])
        + input_grad(enc_value_low, enc_qkv[2])
    )
    enc_gain_g = jnp.stack([enc_gain_zero, enc_gain_one])
    enc_shift_g = jnp.stack([enc_shift_zero, enc_shift_one])
    all_rows = (
        lax.psum_scatter(
            enc_qkv_g.astype(jnp.bfloat16), "seq", scatter_dimension=1, tiled=True
        ).astype(jnp.float32),
        lax.psum_scatter(
            enc_out_g.astype(jnp.bfloat16), "seq", scatter_dimension=0, tiled=True
        ).astype(jnp.float32),
        lax.psum_scatter(
            enc_up_g.astype(jnp.bfloat16), "seq", scatter_dimension=0, tiled=True
        ).astype(jnp.float32),
        lax.psum_scatter(
            enc_down_g.astype(jnp.bfloat16), "seq", scatter_dimension=0, tiled=True
        ).astype(jnp.float32),
        lax.psum_scatter(
            dec_qkv_g.astype(jnp.bfloat16), "seq", scatter_dimension=1, tiled=True
        ).astype(jnp.float32),
        lax.psum_scatter(
            dec_out_g.astype(jnp.bfloat16), "seq", scatter_dimension=0, tiled=True
        ).astype(jnp.float32),
        lax.psum_scatter(
            cross_qkv_g.astype(jnp.bfloat16), "seq", scatter_dimension=1, tiled=True
        ).astype(jnp.float32),
        lax.psum_scatter(
            cross_out_g.astype(jnp.bfloat16), "seq", scatter_dimension=0, tiled=True
        ).astype(jnp.float32),
        lax.psum_scatter(
            dec_up_g.astype(jnp.bfloat16), "seq", scatter_dimension=0, tiled=True
        ).astype(jnp.float32),
        lax.psum_scatter(
            dec_down_g.astype(jnp.bfloat16), "seq", scatter_dimension=0, tiled=True
        ).astype(jnp.float32),
    )
    reduced = (
        lax.psum_scatter(
            all_rows[0].astype(jnp.bfloat16), "batch", scatter_dimension=2, tiled=True
        ).astype(jnp.float32),
        lax.psum_scatter(
            all_rows[1].astype(jnp.bfloat16), "batch", scatter_dimension=1, tiled=True
        ).astype(jnp.float32),
        lax.psum_scatter(
            all_rows[2].astype(jnp.bfloat16), "batch", scatter_dimension=1, tiled=True
        ).astype(jnp.float32),
        lax.psum_scatter(
            all_rows[3].astype(jnp.bfloat16), "batch", scatter_dimension=1, tiled=True
        ).astype(jnp.float32),
        lax.psum_scatter(
            all_rows[4].astype(jnp.bfloat16), "batch", scatter_dimension=2, tiled=True
        ).astype(jnp.float32),
        lax.psum_scatter(
            all_rows[5].astype(jnp.bfloat16), "batch", scatter_dimension=1, tiled=True
        ).astype(jnp.float32),
        lax.psum_scatter(
            all_rows[6].astype(jnp.bfloat16), "batch", scatter_dimension=2, tiled=True
        ).astype(jnp.float32),
        lax.psum_scatter(
            all_rows[7].astype(jnp.bfloat16), "batch", scatter_dimension=1, tiled=True
        ).astype(jnp.float32),
        lax.psum_scatter(
            all_rows[8].astype(jnp.bfloat16), "batch", scatter_dimension=1, tiled=True
        ).astype(jnp.float32),
        lax.psum_scatter(
            all_rows[9].astype(jnp.bfloat16), "batch", scatter_dimension=1, tiled=True
        ).astype(jnp.float32),
    )
    vectors = lax.psum(
        (
            enc_up_bias_g,
            enc_down_bias_g,
            enc_gain_g,
            enc_shift_g,
            dec_up_bias_g,
            dec_down_bias_g,
            dec_gain_g,
            dec_shift_g,
        ),
        ("batch", "seq"),
    )
    return (
        to_low(decoded)[None],
        to_low(src_grad)[None],
        to_low(tgt_grad)[None],
        reduced[0],
        reduced[1],
        reduced[2],
        vectors[0],
        reduced[3],
        vectors[1],
        vectors[2],
        vectors[3],
        reduced[4],
        reduced[5],
        reduced[6],
        reduced[7],
        reduced[8],
        vectors[4],
        reduced[9],
        vectors[5],
        vectors[6],
        vectors[7],
    )


def general(mesh):
    placed = (
        P("batch", "seq", None),
        P("batch", "seq", None),
        P("batch", "seq"),
        P("batch", "seq"),
        P("batch", "seq", None),
        P(),
        P(),
        P(),
        P(),
        P(),
        P(),
        P(),
        P(),
        P(),
        P(),
        P(),
        P(),
        P(),
        P(),
        P(),
        P(),
        P(),
        P(),
    )
    return jax.shard_map(
        general_shards,
        mesh=mesh,
        in_specs=placed,
        out_specs=(
            P("batch", "seq", None),
            P("batch", "seq", None),
            P("batch", "seq", None),
            P(None, "seq", "batch"),
            P("seq", "batch"),
            P("seq", "batch"),
            P(),
            P("seq", "batch"),
            P(),
            P(),
            P(),
            P(None, "seq", "batch"),
            P("seq", "batch"),
            P(None, "seq", "batch"),
            P("seq", "batch"),
            P("seq", "batch"),
            P(),
            P("seq", "batch"),
            P(),
            P(),
            P(),
        ),
        check_vma=False,
    )


def dot(left, right, left_dim=1, right_dim=0):
    return lax.dot_general(
        left, right, (((left_dim,), (right_dim,)), ((), ())), preferred_element_type=F32
    )


def my_core():
    return lax.rem(lax.axis_index("batch"), 2)


def block(index, size):
    return pl.ds(pl.multiple_of(index * size, size), size)


def normed(value):
    centred = value - jnp.mean(value, axis=-1, keepdims=True)
    scale = lax.rsqrt(jnp.mean(centred * centred, axis=-1, keepdims=True) + 1e-06)
    return centred * scale, scale


def normed_back(grad, unit, scale, gain):
    scaled = grad * gain
    first = jnp.mean(scaled, axis=-1, keepdims=True)
    second = jnp.mean(scaled * unit, axis=-1, keepdims=True)
    return scale * (scaled - first - unit * second)


def gelu_and_slope(inner):
    square = inner * inner
    bent = jnp.tanh(0.7978845608028654 * inner * (1.0 + 0.044715 * square))
    half = 0.5 * (1.0 + bent)
    slope = half + 0.5 * inner * (1.0 - bent * bent) * (
        0.7978845608028654 * (1.0 + 0.134145 * square)
    )
    return inner * half, slope


def column_sum(value):
    return jnp.sum(value, axis=0, keepdims=True)


TILE = 256


def attend_kernel(causal, same, *refs):
    if same:
        own_q, other_q, weight, own_mq, other_mq, own_mk, other_mk = refs[:7]
        own_k, other_k = own_q, other_q
        refs = refs[7:]
    else:
        own_q, other_q, own_k, other_k, weight, own_mq, other_mq, own_mk, other_mk = refs[:9]
        refs = refs[9:]
    out_own, out_other, wide_out, queries, keys, values, chances, outs = refs
    step = pl.program_id(0)
    core = my_core()
    rows = own_q.shape[0]
    heads = queries.shape[0]
    length = queries.shape[1]
    width = heads * HEAD_DIM

    @pl.when(step == 0)
    def _():
        columns = block(core, width)
        lane = lax.broadcasted_iota(jnp.int32, (TILE, HEAD_DIM), 1)
        ones = (lane < 3).astype(BF)
        for q_ref, k_ref, mq_ref, mk_ref, half in (
            (own_q, own_k, own_mq, own_mk, core),
            (other_q, other_k, other_mq, other_mk, 1 - core),
        ):
            for tile in range(rows // TILE):
                here = slice(tile * TILE, (tile + 1) * TILE)
                there = pl.ds(pl.multiple_of(half * rows + tile * TILE, TILE), TILE)
                left_q = q_ref[here, :]
                left_k = k_ref[here, :]
                q_tile = dot(left_q, weight[0, :, columns]).astype(BF) * BF(0.125)
                k_tile = dot(left_k, weight[1, :, columns]).astype(BF)
                v_tile = dot(left_k, weight[2, :, columns]).astype(BF)
                for head in range(heads):
                    part = slice(head * HEAD_DIM, (head + 1) * HEAD_DIM)
                    queries[head, there, :] = jnp.concatenate([q_tile[:, part], mq_ref[here, :]], axis=1)
                    keys[head, there, :] = jnp.concatenate([k_tile[:, part], mk_ref[here, :]], axis=1)
                    values[head, there, :] = jnp.concatenate([v_tile[:, part], ones], axis=1)

    if causal:
        lower = lax.broadcasted_iota(jnp.int32, (TILE, TILE), 0) >= lax.broadcasted_iota(
            jnp.int32, (TILE, TILE), 1
        )
    for tile in range(length // TILE):
        here = slice(tile * TILE, (tile + 1) * TILE)
        seen = (tile + 1) * TILE if causal else length
        scores = dot(queries[step, here, :], keys[step, :seen, :], 1, 1)
        if causal:
            last = jnp.where(lower, scores[:, seen - TILE :], NEGATIVE)
            scores = last if tile == 0 else jnp.concatenate([scores[:, : seen - TILE], last], axis=1)
        largest = jnp.max(scores, axis=-1, keepdims=True)
        terms = jnp.exp(scores - largest)
        total = jnp.sum(terms, axis=-1, keepdims=True)
        low = (terms * (1.0 / total)).astype(BF)
        chances[0, here, :seen] = low
        outs[step, here, :] = dot(low, values[step, :seen, :])[:, :HEAD_DIM]

    @pl.when(step == heads - 1)
    def _():
        for half, ref in ((core, out_own), (1 - core, out_other)):
            for tile in range(rows // TILE):
                here = slice(tile * TILE, (tile + 1) * TILE)
                there = pl.ds(pl.multiple_of(half * rows + tile * TILE, TILE), TILE)
                joined = jnp.concatenate([outs[head, there, :] for head in range(heads)], axis=1)
                wide_out[there, :] = joined
                ref[here, :] = joined.astype(BF)


def attend_back_kernel(causal, same, *refs):
    if same:
        own_q, other_q = refs[:2]
        own_k, other_k = own_q, other_q
        refs = refs[2:]
    else:
        own_q, other_q, own_k, other_k = refs[:4]
        refs = refs[4:]
    queries, keys, values, chances, wide_out, grad_own, grad_other = refs[:7]
    d_own, d_other, sums, grads, score_grads, dq, dk, dv = refs[7:]
    step = pl.program_id(0)
    core = my_core()
    rows = own_q.shape[0]
    heads = queries.shape[0]
    length = queries.shape[1]

    @pl.when(step == 0)
    def _():
        lane = lax.broadcasted_iota(jnp.int32, (TILE, HEAD_DIM), 1)
        for ref, half in ((grad_own, core), (grad_other, 1 - core)):
            for tile in range(rows // TILE):
                here = slice(tile * TILE, (tile + 1) * TILE)
                there = pl.ds(pl.multiple_of(half * rows + tile * TILE, TILE), TILE)
                grad = ref[here, :]
                both = grad.astype(F32) * wide_out[there, :]
                for head in range(heads):
                    part = slice(head * HEAD_DIM, (head + 1) * HEAD_DIM)
                    settle = -jnp.sum(both[:, part], axis=-1, keepdims=True)
                    first = settle.astype(BF).astype(F32)
                    second = (settle - first).astype(BF).astype(F32)
                    third = settle - first - second
                    extra = jnp.where(
                        lane == 0,
                        first,
                        jnp.where(lane == 1, second, jnp.where(lane == 2, third, 0.0)),
                    )
                    grads[head, there, :] = jnp.concatenate([grad[:, part], extra.astype(BF)], axis=1)

    for tile in range(length // TILE):
        here = slice(tile * TILE, (tile + 1) * TILE)
        seen = (tile + 1) * TILE if causal else length
        change = dot(grads[step, here, :], values[step, :seen, :], 1, 1)
        low = (chances[0, here, :seen].astype(F32) * change).astype(BF)
        score_grads[here, :seen] = low
        dq[step, here, :] = dot(low, keys[step, :seen, :])[:, :HEAD_DIM] * 0.125
    for tile in range(length // TILE if causal else 1):
        here = slice(tile * TILE, (tile + 1) * TILE) if causal else slice(0, length)
        below = slice(tile * TILE, length)
        dk[block(step, HEAD_DIM), here] = dot(
            queries[step, below, :HEAD_DIM], score_grads[below, here], 0, 0
        )
        dv[block(step, HEAD_DIM), here] = dot(
            grads[step, below, :HEAD_DIM], chances[0, below, here], 0, 0
        )

    @pl.when(step == heads - 1)
    def _():
        for half, ref in ((core, d_own), (1 - core, d_other)):
            there = block(half, rows)
            ref[0, :, :] = jnp.concatenate(
                [dq[head, there, :] for head in range(heads)], axis=1
            ).astype(BF)
            ref[1, :, :] = dk[:, there].T.astype(BF)
            ref[2, :, :] = dv[:, there].T.astype(BF)
        for kind in range(3):
            x_own, x_other = (own_q, other_q) if kind == 0 else (own_k, other_k)
            total = dot(d_own[kind], x_own[...], 0, 0) + dot(d_other[kind], x_other[...], 0, 0)
            low = total.astype(BF)
            for part in range(low.shape[0] // 32):
                z_low, y, kept = part >> 2, (part >> 1) & 1, part & 1
                for s in range(2):
                    sums[kept ^ core, s, y, z_low, kind * 32 : (kind + 1) * 32, :] = low[
                        part * 32 : (part + 1) * 32, s * 256 : (s + 1) * 256
                    ]


def store_up(sums, value, index):
    core = my_core()
    z, y = index >> 1, index & 1
    low = value.astype(BF)
    for kept in range(2):
        for s in range(2):
            sums[kept ^ core, s, y, z & 1, (z >> 1) ^ kept, :, :] = low[
                kept * 128 : (kept + 1) * 128, s * 256 : (s + 1) * 256
            ]


def store_down(sums, value, index, column):
    core = my_core()
    low = value.astype(BF)
    for part in range(8):
        place = index * 8 + part
        z, y, kept = place >> 2, (place >> 1) & 1, place & 1
        for piece in range(2):
            s, slot = (column * 2 + piece) // 4, (column * 2 + piece) % 4
            sums[kept ^ core, s, y, z & 1, (z >> 1) ^ kept, slot * 32 : (slot + 1) * 32, :] = low[
                part * 32 : (part + 1) * 32, piece * 256 : (piece + 1) * 256
            ]


def store_out(sums, value, side):
    core = my_core()
    low = value.astype(BF)
    for place in range(16):
        z, y, kept = place >> 2, (place >> 1) & 1, place & 1
        sums[kept ^ core, side, y, z & 1, (z >> 1) ^ kept, :, :] = low[
            place * 32 : (place + 1) * 32, :
        ]


def projected(att_own, att_other, weight, here):
    core = my_core()
    width = att_own.shape[1]
    return dot(att_own[here, :], weight[block(core, width), :]) + dot(
        att_other[here, :], weight[block(1 - core, width), :]
    )


def projected_back(grad, weight, out_own, out_other, here):
    core = my_core()
    width = out_own.shape[1]
    out_own[here, :] = dot(grad, weight[block(core, width), :], 1, 1).astype(BF)
    out_other[here, :] = dot(grad, weight[block(1 - core, width), :], 1, 1).astype(BF)


def tiles_of(ref):
    return [slice(t * TILE, (t + 1) * TILE) for t in range(ref.shape[0] // TILE)]


def encode_kernel(
    x, att_own, att_other, out_w, up, up_bias, down, down_bias, gain, shift,
    memory, unit0, scale0, hidden_low, act, slope, unit1, scale1,
):
    for here in tiles_of(x):
        pre = x[here, :].astype(F32) + projected(att_own, att_other, out_w, here)
        unit, scale = normed(pre)
        unit0[here, :] = unit
        scale0[here, :] = scale
        hidden = unit * gain[0:1, :] + shift[0:1, :]
        low = hidden.astype(BF)
        hidden_low[here, :] = low
        value, bend = gelu_and_slope(dot(low, up[...]) + up_bias[...])
        slope[here, :] = bend
        value = value.astype(BF)
        act[here, :] = value
        unit, scale = normed(hidden + dot(value, down[...]) + down_bias[...])
        unit1[here, :] = unit
        scale1[here, :] = scale
        memory[here, :] = (unit * gain[1:2, :] + shift[1:2, :]).astype(BF)


def decode_first_kernel(y, att_own, att_other, out_w, gain, shift, first, first_low, unit0, scale0):
    for here in tiles_of(y):
        pre = y[here, :].astype(F32) + projected(att_own, att_other, out_w, here)
        unit, scale = normed(pre)
        unit0[here, :] = unit
        scale0[here, :] = scale
        value = unit * gain[0:1, :] + shift[0:1, :]
        first[here, :] = value
        first_low[here, :] = value.astype(BF)


def decode_last_kernel(
    first, att_own, att_other, out_w, up, up_bias, down, down_bias, gain, shift, upstream,
    decoded, grad_pre, grad_own, grad_other, up_sums, down_sums, out_sums, vectors,
    second_low, act, inner_low, branch_low, mixed_low,
):
    vectors[...] = jnp.zeros_like(vectors)
    for here in tiles_of(first):
        pre = first[here, :] + projected(att_own, att_other, out_w, here)
        unit1, scale1 = normed(pre)
        second = unit1 * gain[1:2, :] + shift[1:2, :]
        low = second.astype(BF)
        second_low[here, :] = low
        value, slope = gelu_and_slope(dot(low, up[...]) + up_bias[...])
        value = value.astype(BF)
        act[here, :] = value
        unit2, scale2 = normed(second + dot(value, down[...]) + down_bias[...])
        decoded[here, :] = (unit2 * gain[2:3, :] + shift[2:3, :]).astype(BF)
        grad = upstream[here, :].astype(F32)
        vectors[7:8, :] += column_sum(grad * unit2)
        vectors[8:9, :] += column_sum(grad)
        grad = normed_back(grad, unit2, scale2, gain[2:3, :])
        branch = grad.astype(BF)
        branch_low[here, :] = branch
        vectors[4:5, :] += column_sum(branch.astype(F32))
        inner = (dot(branch, down[...], 1, 1) * slope).astype(BF)
        inner_low[here, :] = inner
        bias = column_sum(inner.astype(F32))
        for part in range(4):
            vectors[part : part + 1, :] += bias[:, part * 512 : (part + 1) * 512]
        grad = grad + dot(inner, up[...], 1, 1)
        vectors[5:6, :] += column_sum(grad * unit1)
        vectors[6:7, :] += column_sum(grad)
        grad = normed_back(grad, unit1, scale1, gain[1:2, :])
        grad_pre[here, :] = grad
        mixed = grad.astype(BF)
        mixed_low[here, :] = mixed
        projected_back(mixed, out_w, grad_own, grad_other, here)
    layer_sums(
        second_low, act, inner_low, branch_low, mixed_low, att_own, att_other,
        up_sums, down_sums, out_sums,
    )


def layer_sums(
    entering, act, inner_low, branch_low, mixed_low, att_own, att_other, up_sums, down_sums, out_sums
):
    for index in range(inner_low.shape[1] // 256):
        store_up(up_sums, dot(inner_low[:, index * 256 : (index + 1) * 256], entering[...], 0, 0), index)
    for index in range(2):
        for column in range(act.shape[1] // 512):
            store_down(
                down_sums,
                dot(
                    branch_low[:, index * 256 : (index + 1) * 256],
                    act[:, column * 512 : (column + 1) * 512],
                    0,
                    0,
                ),
                index,
                column,
            )
    core = my_core()
    store_out(out_sums, dot(mixed_low[...], att_own[...], 0, 0), core)
    store_out(out_sums, dot(mixed_low[...], att_other[...], 0, 0), 1 - core)


def encode_back_kernel(
    d_own, d_other, cross_w, up, down, gain, out_w, unit0, scale0, hidden_low, act, slope, unit1, scale1,
    att_own, att_other,
    grad_pre, grad_own, grad_other, up_sums, down_sums, out_sums, vectors,
    inner_low, branch_low, mixed_low,
):
    core = my_core()
    width = d_own.shape[2]
    vectors[...] = jnp.zeros_like(vectors)
    for here in tiles_of(unit0):
        grad = jnp.zeros(unit0[here, :].shape, F32)
        for kind in (1, 2):
            grad = grad + dot(d_own[kind, here, :], cross_w[kind, :, block(core, width)], 1, 1)
            grad = grad + dot(d_other[kind, here, :], cross_w[kind, :, block(1 - core, width)], 1, 1)
        unit = unit1[here, :]
        vectors[7:8, :] += column_sum(grad * unit)
        vectors[8:9, :] += column_sum(grad)
        grad = normed_back(grad, unit, scale1[here, :], gain[1:2, :])
        branch = grad.astype(BF)
        branch_low[here, :] = branch
        vectors[4:5, :] += column_sum(branch.astype(F32))
        inner = (dot(branch, down[...], 1, 1) * slope[here, :]).astype(BF)
        inner_low[here, :] = inner
        bias = column_sum(inner.astype(F32))
        for part in range(4):
            vectors[part : part + 1, :] += bias[:, part * 512 : (part + 1) * 512]
        grad = grad + dot(inner, up[...], 1, 1)
        unit = unit0[here, :]
        vectors[5:6, :] += column_sum(grad * unit)
        vectors[6:7, :] += column_sum(grad)
        grad = normed_back(grad, unit, scale0[here, :], gain[0:1, :])
        grad_pre[here, :] = grad
        mixed = grad.astype(BF)
        mixed_low[here, :] = mixed
        projected_back(mixed, out_w, grad_own, grad_other, here)
    layer_sums(
        hidden_low, act, inner_low, branch_low, mixed_low, att_own, att_other,
        up_sums, down_sums, out_sums,
    )


def decode_first_back_kernel(
    grad_in, d_own, d_other, cross_w, unit0, scale0, gain, out_w, att_own, att_other,
    grad_pre, grad_own, grad_other, out_sums, vectors, mixed_low,
):
    core = my_core()
    width = d_own.shape[2]
    vectors[...] = jnp.zeros_like(vectors)
    for here in tiles_of(unit0):
        grad = grad_in[here, :]
        grad = grad + dot(d_own[0, here, :], cross_w[0, :, block(core, width)], 1, 1)
        grad = grad + dot(d_other[0, here, :], cross_w[0, :, block(1 - core, width)], 1, 1)
        unit = unit0[here, :]
        vectors[0:1, :] += column_sum(grad * unit)
        vectors[1:2, :] += column_sum(grad)
        grad = normed_back(grad, unit, scale0[here, :], gain[0:1, :])
        grad_pre[here, :] = grad
        mixed = grad.astype(BF)
        mixed_low[here, :] = mixed
        projected_back(mixed, out_w, grad_own, grad_other, here)
    store_out(out_sums, dot(mixed_low[...], att_own[...], 0, 0), core)
    store_out(out_sums, dot(mixed_low[...], att_other[...], 0, 0), 1 - core)


def input_kernel(grad_pre, d_own, d_other, weight, grad):
    core = my_core()
    width = d_own.shape[2]
    for here in tiles_of(grad_pre):
        total = grad_pre[here, :]
        for kind in range(3):
            total = total + dot(d_own[kind, here, :], weight[kind, :, block(core, width)], 1, 1)
            total = total + dot(d_other[kind, here, :], weight[kind, :, block(1 - core, width)], 1, 1)
        grad[here, :] = total.astype(BF)


VMEM = pl.BlockSpec(memory_space=pltpu.VMEM)


def call(kernel, name, micros, operands, outs, scratch=(), grid=None, in_specs=None, out_specs=None):
    shapes = tuple(jax.ShapeDtypeStruct(shape, kind) for shape, kind in outs)
    extra = {} if grid is None else {"grid": grid}
    return pl.pallas_call(
        kernel,
        out_shape=shapes,
        in_specs=in_specs or [VMEM] * len(operands),
        out_specs=out_specs or tuple([VMEM] * len(outs)),
        scratch_shapes=list(scratch),
        compiler_params=pltpu.CompilerParams(vmem_limit_bytes=56 * 2**20),
        cost_estimate=pl.CostEstimate(
            flops=int(micros * 1e9), bytes_accessed=0, transcendentals=0
        ),
        name=name,
        **extra,
    )(*operands)


def whole(array):
    rank = len(array.shape)
    return pl.BlockSpec(array.shape, lambda step: (0,) * rank)


def attend(name, causal, same, sides, weight, masks):
    rows = sides[0].shape[0]
    width = weight.shape[2] // 2
    heads = width // HEAD_DIM
    length = 2 * rows
    wide = 2 * HEAD_DIM
    operands = (*sides, weight, *masks)
    outs = (
        ((rows, width), BF),
        ((rows, width), BF),
        ((length, width), F32),
        ((heads, length, wide), BF),
        ((heads, length, wide), BF),
        ((heads, length, wide), BF),
        ((heads, length, length), BF),
    )
    shapes = [jax.ShapeDtypeStruct(shape, kind) for shape, kind in outs]
    return call(
        functools.partial(attend_kernel, causal, same),
        name,
        10,
        operands,
        outs,
        scratch=[pltpu.VMEM((heads, length, HEAD_DIM), F32)],
        grid=(heads,),
        in_specs=[whole(one) for one in operands],
        out_specs=tuple(whole(one) for one in shapes[:-1])
        + (pl.BlockSpec((1, length, length), lambda step: (step, 0, 0)),),
    )


def attend_back(name, causal, same, sides, saved, grads):
    wide_out, queries, keys, values, chances = saved
    rows = sides[0].shape[0]
    heads, length, wide = queries.shape
    width = heads * HEAD_DIM
    operands = (*sides, queries, keys, values, chances, wide_out, *grads)
    outs = (
        ((3, rows, width), BF),
        ((3, rows, width), BF),
        ((2, 2, 2, 2, 96, 256), BF),
    )
    in_specs = [whole(one) for one in operands]
    in_specs[len(sides) + 3] = pl.BlockSpec((1, length, length), lambda step: (step, 0, 0))
    shapes = [jax.ShapeDtypeStruct(shape, kind) for shape, kind in outs]
    return call(
        functools.partial(attend_back_kernel, causal, same),
        name,
        15,
        operands,
        outs,
        scratch=[
            pltpu.VMEM((heads, length, wide), BF),
            pltpu.VMEM((length, length), BF),
            pltpu.VMEM((heads, length, HEAD_DIM), F32),
            pltpu.VMEM((width, length), F32),
            pltpu.VMEM((width, length), F32),
        ],
        grid=(heads,),
        in_specs=in_specs,
        out_specs=tuple(whole(one) for one in shapes),
    )


def pairs(count, move):
    found = []
    for index in range(count):
        z, y, core, s = index >> 3, (index >> 2) & 1, (index >> 1) & 1, index & 1
        z, y, core, s = move(z, y, core, s)
        found.append((index, (((z * 2 + y) * 2 + core) * 2) + s))
    return found


def fast_shards(count, source, target, source_ids, target_ids, out_grad, *params):
    (
        enc_qkv, enc_out, enc_up, enc_up_bias, enc_down, enc_down_bias, enc_gain, enc_shift, dec_qkv, dec_out,
        cross_qkv, cross_out, dec_up, dec_up_bias, dec_down, dec_down_bias, dec_gain, dec_shift,
    ) = params
    moves = {
        "swap": pairs(count, lambda z, y, c, s: (z, y, s, c)),
        "core": pairs(count, lambda z, y, c, s: (z, y, 1 - c, s)),
        "x": pairs(count, lambda z, y, c, s: (z, y, c, 1 - s)),
        "y": pairs(count, lambda z, y, c, s: (z, 1 - y, c, s)),
        "z1": pairs(count, lambda z, y, c, s: (z ^ 1, y, c, s)),
        "z2": pairs(count, lambda z, y, c, s: (z ^ 2, y, c, s)),
    }
    row = lax.axis_index("batch")
    core = row % 2
    place = {"x": lax.axis_index("seq"), "y": (row // 2) % 2, "z1": (row // 4) % 2, "z2": (row // 8) ^ core}

    def move(value, way):
        return lax.ppermute(value, BOTH, moves[way])

    ids = move(jnp.stack([source_ids[0], target_ids[0]]), "swap")
    src = move(source[0], "swap")
    tgt = move(target[0], "swap")
    upstream = move(out_grad[0], "swap")
    ids_other = move(ids, "core")
    src_other = move(src, "core")
    tgt_other = move(tgt, "core")
    lane = jnp.arange(HEAD_DIM, dtype=jnp.int32)[None, :]

    def masks(which):
        marks = [side[which][:, None] == lane for side in (ids, ids_other)]
        asks = [mark.astype(BF) for mark in marks]
        bars = [jnp.where(~mark & (lane < 3), NEGATIVE, 0.0).astype(BF) for mark in marks]
        return asks, bars

    src_ask, src_bar = masks(0)
    tgt_ask, tgt_bar = masks(1)
    rows, wide = src.shape
    inner = enc_up.shape[1]
    width = wide // 2
    full, thin = ((rows, wide), F32), ((rows, 1), F32)
    low_full, low_half = ((rows, wide), BF), ((rows, width), BF)
    low_inner = ((rows, inner), BF)
    keep, keep_out = ((2, 2, 2, 2, 2, 128, 256), BF), ((2, 2, 2, 2, 2, 32, 256), BF)
    biases = [one[None, :] for one in (enc_up_bias, enc_down_bias, dec_up_bias, dec_down_bias)]
    enc_up_b, enc_down_b, dec_up_b, dec_down_b = biases

    def scratch(shape):
        return pltpu.VMEM(*shape)

    att, att_send, *enc_saved = attend(
        "enc_attend", False, True, (src, src_other), enc_qkv, (*src_ask, *src_bar)
    )
    enc_att = (att, move(att_send, "core"))
    att, att_send, *dec_saved = attend(
        "dec_attend", True, True, (tgt, tgt_other), dec_qkv, (*tgt_ask, *tgt_bar)
    )
    dec_att = (att, move(att_send, "core"))
    memory, *enc_kept = call(
        encode_kernel,
        "encode",
        8,
        (src, *enc_att, enc_out, enc_up, enc_up_b, enc_down, enc_down_b, enc_gain, enc_shift),
        (low_full, full, thin, low_full, low_inner, ((rows, inner), F32), full, thin),
    )
    first, first_low, first_unit, first_scale = call(
        decode_first_kernel,
        "decode_first",
        2,
        (tgt, *dec_att, dec_out, dec_gain, dec_shift),
        (full, low_full, full, thin),
    )
    first_sides = (first_low, move(first_low, "core"))
    memory_sides = (memory, move(memory, "core"))
    cross_sides = (*first_sides, *memory_sides)
    att, att_send, *cross_saved = attend(
        "cross_attend", False, False, cross_sides, cross_qkv, (*tgt_ask, *src_bar)
    )
    cross_att = (att, move(att_send, "core"))
    decoded, grad_second, grad_att, grad_send, dec_up_s, dec_down_s, cross_out_s, dec_vectors = call(
        decode_last_kernel,
        "decode_last",
        20,
        (first, *cross_att, cross_out, dec_up, dec_up_b, dec_down, dec_down_b, dec_gain, dec_shift, upstream),
        (low_full, full, low_half, low_half, keep, keep, keep_out, ((16, wide), F32)),
        scratch=[scratch(low_full), scratch(low_inner), scratch(low_inner), scratch(low_full), scratch(low_full)],
    )
    decoded = move(decoded, "swap")
    d_cross, d_send, cross_qkv_s = attend_back(
        "cross_attend_back", False, False, cross_sides, cross_saved, (grad_att, move(grad_send, "core"))
    )
    d_cross = (d_cross, move(d_send, "core"))
    grad_dec_pre, grad_att, grad_send, dec_out_s, first_vectors = call(
        decode_first_back_kernel,
        "decode_first_back",
        3,
        (grad_second, *d_cross, cross_qkv, first_unit, first_scale, dec_gain, dec_out, *dec_att),
        (full, low_half, low_half, keep_out, ((8, wide), F32)),
        scratch=[scratch(low_full)],
    )
    dec_grads = (grad_att, move(grad_send, "core"))
    unit0, scale0, hidden_low, act, slope, unit1, scale1 = enc_kept
    grad_enc_pre, grad_att, grad_send, enc_up_s, enc_down_s, enc_out_s, enc_vectors = call(
        encode_back_kernel,
        "encode_back",
        12,
        (
            *d_cross, cross_qkv, enc_up, enc_down, enc_gain, enc_out, unit0, scale0, hidden_low, act, slope,
            unit1, scale1, *enc_att,
        ),
        (full, low_half, low_half, keep, keep, keep_out, ((16, wide), F32)),
        scratch=[scratch(low_inner), scratch(low_full), scratch(low_full)],
    )
    enc_grads = (grad_att, move(grad_send, "core"))
    d_dec, d_send, dec_qkv_s = attend_back(
        "dec_attend_back", True, True, (tgt, tgt_other), dec_saved, dec_grads
    )
    (tgt_grad,) = call(
        input_kernel, "target_grad", 2, (grad_dec_pre, d_dec, move(d_send, "core"), dec_qkv), (low_full,)
    )
    tgt_grad = move(tgt_grad, "swap")
    d_enc, d_send, enc_qkv_s = attend_back(
        "enc_attend_back", False, True, (src, src_other), enc_saved, enc_grads
    )
    (src_grad,) = call(
        input_kernel, "source_grad", 2, (grad_enc_pre, d_enc, move(d_send, "core"), enc_qkv), (low_full,)
    )
    src_grad = move(src_grad, "swap")

    def added(kept, got):
        return kept.astype(F32) + got.astype(F32)

    def meet(pair):
        return added(pair[0], move(pair[1], "core")).astype(BF)

    def joined(pair):
        return jnp.stack([pair[0], move(pair[1], "core")], axis=3)

    def reduced(value, order):
        left = ["x", "y", "z1", "z2"]
        for way in order:
            axis = left.index(way)
            left.remove(way)
            kept = lax.dynamic_index_in_dim(value, place[way], axis, keepdims=False)
            sent = lax.dynamic_index_in_dim(value, 1 - place[way], axis, keepdims=False)
            total = added(kept, move(sent, way))
            value = total.astype(BF)
        return total

    xyz, yxz = ("x", "y", "z1", "z2"), ("y", "x", "z1", "z2")
    dec_down_r = reduced(meet(dec_down_s), xyz)
    dec_up_r = reduced(meet(dec_up_s), yxz)
    mixed = jnp.concatenate([meet(cross_out_s), meet(dec_out_s)], axis=4)
    rest = jnp.concatenate([joined(cross_qkv_s), joined(dec_qkv_s)], axis=4)
    enc_down_r = reduced(meet(enc_down_s), xyz)
    enc_up_r = reduced(meet(enc_up_s), yxz)
    rest_r = reduced(jnp.concatenate([mixed, rest], axis=4), xyz)
    tail_r = reduced(jnp.concatenate([meet(enc_out_s), joined(enc_qkv_s)], axis=4), yxz)
    vectors = jnp.concatenate([dec_vectors, first_vectors, enc_vectors])
    for way in ("core", "x", "y", "z1", "z2"):
        vectors = vectors + move(vectors, way)

    def up_shape(value):
        return value.T

    def down_shape(value):
        return jnp.swapaxes(value.reshape(4, 32, 256), 1, 2).reshape(1024, 32)

    def out_shape(value):
        return value.T

    def qkv_shape(value):
        return jnp.swapaxes(value.reshape(3, 32, 256), 1, 2)

    dec_v, first_v, enc_v = vectors[:16], vectors[16:24], vectors[24:]
    return (
        decoded[None],
        src_grad[None],
        tgt_grad[None],
        qkv_shape(tail_r[32:]),
        out_shape(tail_r[:32]),
        up_shape(enc_up_r),
        enc_v[:4].reshape(-1),
        down_shape(enc_down_r),
        enc_v[4],
        jnp.stack([enc_v[5], enc_v[7]]),
        jnp.stack([enc_v[6], enc_v[8]]),
        qkv_shape(rest_r[160:]),
        out_shape(rest_r[32:64]),
        qkv_shape(rest_r[64:160]),
        out_shape(rest_r[:32]),
        up_shape(dec_up_r),
        dec_v[:4].reshape(-1),
        down_shape(dec_down_r),
        dec_v[4],
        jnp.stack([first_v[0], dec_v[5], dec_v[7]]),
        jnp.stack([first_v[1], dec_v[6], dec_v[8]]),
    )


def solution(mesh):
    if mesh.shape["seq"] != 2 or mesh.shape["batch"] != 16:
        return general(mesh)
    tokens = P("batch", "seq", None)
    ids = P("batch", "seq")
    cut, cut3 = P("seq", "batch"), P(None, "seq", "batch")
    return jax.shard_map(
        functools.partial(fast_shards, mesh.size),
        mesh=mesh,
        in_specs=(tokens, tokens, ids, ids, tokens) + (P(),) * 18,
        out_specs=(
            tokens, tokens, tokens, cut3, cut, cut, P(), cut, P(), P(), P(), cut3, cut, cut3, cut, cut, P(), cut,
            P(), P(), P(),
        ),
        check_vma=False,
    )
```

```python
import functools

import jax
import jax.numpy as jnp
from jax import lax
from jax.experimental import pallas as pl
from jax.experimental.pallas import tpu as pltpu
from jax.sharding import PartitionSpec as P

HEAD_DIM = 64
NEGATIVE = -1e30
BF = jnp.bfloat16
F32 = jnp.float32
BOTH = ("batch", "seq")


def layer_norm(value, gain, shift):
    mean = jnp.mean(value, axis=-1, keepdims=True)
    centred = value - mean
    spread = jnp.mean(centred * centred, axis=-1, keepdims=True)
    return centred * lax.rsqrt(spread + 1e-06) * gain + shift


def norm_back(value, gain, shift, grad):
    _, pull = jax.vjp(layer_norm, value, gain, shift)
    return pull(grad)


def gelu_back(inner, grad):
    _, pull = jax.vjp(jax.nn.gelu, inner)
    return pull(grad)[0]


def matmul(left, right):
    return jnp.dot(left, right, preferred_element_type=jnp.float32)


def weight_grad(inputs, grad):
    return lax.dot_general(
        inputs, grad, (((0,), (0,)), ((), ())), preferred_element_type=jnp.float32
    )


def input_grad(grad, weight):
    return lax.dot_general(
        grad, weight, (((1,), (1,)), ((), ())), preferred_element_type=jnp.float32
    )


def to_low(value):
    return value.astype(jnp.bfloat16)


def split_heads(value):
    return value.reshape(value.shape[0], -1, HEAD_DIM)


def block_live(query_ids, key_ids, offset, block, rows, causal):
    first_key = lax.dynamic_index_in_dim(key_ids, block * rows, 0, keepdims=False)
    last_key = lax.dynamic_index_in_dim(key_ids, block * rows + rows - 1, 0, keepdims=False)
    live = (first_key <= query_ids[rows - 1]) & (query_ids[0] <= last_key)
    if causal:
        live = live & (block * rows <= offset + rows - 1)
    return live


def block_scores(queries, keys_all, query_ids, key_ids, offset, block, causal):
    rows = queries.shape[0]
    key_block = lax.dynamic_slice_in_dim(keys_all, block * rows, rows, 0)
    id_block = lax.dynamic_slice_in_dim(key_ids, block * rows, rows, 0)
    scores = (
        jnp.einsum("qhe,khe->hqk", queries, key_block, preferred_element_type=jnp.float32) * 0.125
    )
    allowed = query_ids[:, None] == id_block[None, :]
    if causal:
        positions = jnp.arange(rows, dtype=jnp.int32)
        allowed = allowed & ((offset + positions)[:, None] >= (block * rows + positions)[None, :])
    allowed = allowed[None]
    return (jnp.where(allowed, scores, NEGATIVE), allowed, key_block)


def attend_forward(queries, keys_all, values_all, query_ids, key_ids, offset, causal):
    rows = queries.shape[0]
    heads_count = queries.shape[1]
    count = keys_all.shape[0] // rows

    def first_pass(block, carry):

        def first_compute(state):
            largest, total = state
            scores, allowed, _ = block_scores(
                queries, keys_all, query_ids, key_ids, offset, block, causal
            )
            newest = jnp.maximum(largest, jnp.max(scores, axis=-1))
            terms = jnp.where(allowed, jnp.exp(scores - newest[..., None]), 0.0)
            return (newest, total * jnp.exp(largest - newest) + jnp.sum(terms, axis=-1))

        live = block_live(query_ids, key_ids, offset, block, rows, causal)
        return lax.cond(live, first_compute, lambda state: state, carry)

    initial = (
        jnp.full((heads_count, rows), NEGATIVE, jnp.float32),
        jnp.zeros((heads_count, rows), jnp.float32),
    )
    largest, total = lax.fori_loop(0, count, first_pass, initial)
    log_total = largest + jnp.log(total)

    def second_pass(block, carry):

        def second_compute(output):
            scores, allowed, _ = block_scores(
                queries, keys_all, query_ids, key_ids, offset, block, causal
            )
            value_block = lax.dynamic_slice_in_dim(values_all, block * rows, rows, 0)
            chances = jnp.where(allowed, jnp.exp(scores - log_total[..., None]), 0.0)
            return output + jnp.einsum(
                "hqk,khe->qhe", to_low(chances), value_block, preferred_element_type=jnp.float32
            )

        live = block_live(query_ids, key_ids, offset, block, rows, causal)
        return lax.cond(live, second_compute, lambda output: output, carry)

    output = lax.fori_loop(0, count, second_pass, jnp.zeros(queries.shape, jnp.float32))
    return (output, log_total)


def attend_backward(
    queries, keys_all, values_all, query_ids, key_ids, offset, causal, grad_out, settle, log_total
):
    rows = queries.shape[0]
    count = keys_all.shape[0] // rows

    def step_block(block, carry):

        def step_compute(state):
            query_grad, key_grads, value_grads = state
            scores, allowed, key_block = block_scores(
                queries, keys_all, query_ids, key_ids, offset, block, causal
            )
            value_block = lax.dynamic_slice_in_dim(values_all, block * rows, rows, 0)
            chances = jnp.where(allowed, jnp.exp(scores - log_total[..., None]), 0.0)
            chance_grad = jnp.einsum(
                "qhe,khe->hqk", grad_out, value_block, preferred_element_type=jnp.float32
            )
            score_grad = to_low(chances * (chance_grad - settle[..., None]))
            query_grad = (
                query_grad
                + jnp.einsum(
                    "hqk,khe->qhe", score_grad, key_block, preferred_element_type=jnp.float32
                )
                * 0.125
            )
            key_part = (
                jnp.einsum("hqk,qhe->khe", score_grad, queries, preferred_element_type=jnp.float32)
                * 0.125
            )
            value_part = jnp.einsum(
                "hqk,qhe->khe", to_low(chances), grad_out, preferred_element_type=jnp.float32
            )
            key_grads = lax.dynamic_update_slice_in_dim(key_grads, key_part, block * rows, 0)
            value_grads = lax.dynamic_update_slice_in_dim(value_grads, value_part, block * rows, 0)
            return (query_grad, key_grads, value_grads)

        live = block_live(query_ids, key_ids, offset, block, rows, causal)
        return lax.cond(live, step_compute, lambda state: state, carry)

    initial = (
        jnp.zeros(queries.shape, jnp.float32),
        jnp.zeros(keys_all.shape, jnp.float32),
        jnp.zeros(values_all.shape, jnp.float32),
    )
    return lax.fori_loop(0, count, step_block, initial)


def attention_back(
    queries, keys_all, values_all, query_ids, key_ids_all, causal, grad_out, output, log_total
):
    rows = queries.shape[0]
    offset = lax.axis_index("seq") * rows
    settle = jnp.einsum("qhe,qhe->hq", grad_out.astype(jnp.float32), output)
    query_grad, key_terms, value_terms = attend_backward(
        queries,
        keys_all,
        values_all,
        query_ids,
        key_ids_all,
        offset,
        causal,
        grad_out,
        settle,
        log_total,
    )
    key_sum, value_sum = (
        lax.psum_scatter(
            key_terms.reshape(key_terms.shape[0], -1).astype(jnp.bfloat16),
            "seq",
            scatter_dimension=0,
            tiled=True,
        ).astype(jnp.float32),
        lax.psum_scatter(
            value_terms.reshape(value_terms.shape[0], -1).astype(jnp.bfloat16),
            "seq",
            scatter_dimension=0,
            tiled=True,
        ).astype(jnp.float32),
    )
    return (query_grad, key_sum, value_sum)


def general_shards(
    source,
    target,
    source_ids,
    target_ids,
    out_grad,
    enc_qkv,
    enc_out,
    enc_up,
    enc_up_bias,
    enc_down,
    enc_down_bias,
    enc_gain,
    enc_shift,
    dec_qkv,
    dec_out,
    cross_qkv,
    cross_out,
    dec_up,
    dec_up_bias,
    dec_down,
    dec_down_bias,
    dec_gain,
    dec_shift,
):
    src_rows = source[0]
    tgt_rows = target[0]
    src_ids = source_ids[0]
    tgt_ids = target_ids[0]
    rows = src_rows.shape[0]
    offset = lax.axis_index("seq") * rows
    enc_queries = to_low(matmul(src_rows, enc_qkv[0]))
    enc_keys = to_low(matmul(src_rows, enc_qkv[1]))
    enc_values = to_low(matmul(src_rows, enc_qkv[2]))
    enc_keys_all, enc_values_all, src_ids_all = (
        lax.all_gather(enc_keys, "seq", axis=0, tiled=True),
        lax.all_gather(enc_values, "seq", axis=0, tiled=True),
        lax.all_gather(src_ids, "seq", axis=0, tiled=True),
    )
    enc_att, enc_lse = attend_forward(
        split_heads(enc_queries),
        split_heads(enc_keys_all),
        split_heads(enc_values_all),
        src_ids,
        src_ids_all,
        offset,
        False,
    )
    enc_att_low = to_low(enc_att.reshape(rows, -1))
    enc_pre = src_rows.astype(jnp.float32) + matmul(enc_att_low, enc_out)
    hidden = layer_norm(enc_pre, enc_gain[0], enc_shift[0])
    hidden_low = to_low(hidden)
    enc_inner = matmul(hidden_low, enc_up) + enc_up_bias
    enc_act = to_low(jax.nn.gelu(enc_inner))
    enc_last = hidden + matmul(enc_act, enc_down) + enc_down_bias
    memory = layer_norm(enc_last, enc_gain[1], enc_shift[1])
    memory_low = to_low(memory)
    mem_keys = to_low(matmul(memory_low, cross_qkv[1]))
    mem_values = to_low(matmul(memory_low, cross_qkv[2]))
    mem_keys_all, mem_values_all = (
        lax.all_gather(mem_keys, "seq", axis=0, tiled=True),
        lax.all_gather(mem_values, "seq", axis=0, tiled=True),
    )
    dec_queries = to_low(matmul(tgt_rows, dec_qkv[0]))
    dec_keys = to_low(matmul(tgt_rows, dec_qkv[1]))
    dec_values = to_low(matmul(tgt_rows, dec_qkv[2]))
    dec_keys_all, dec_values_all, tgt_ids_all = (
        lax.all_gather(dec_keys, "seq", axis=0, tiled=True),
        lax.all_gather(dec_values, "seq", axis=0, tiled=True),
        lax.all_gather(tgt_ids, "seq", axis=0, tiled=True),
    )
    dec_att, dec_lse = attend_forward(
        split_heads(dec_queries),
        split_heads(dec_keys_all),
        split_heads(dec_values_all),
        tgt_ids,
        tgt_ids_all,
        offset,
        True,
    )
    dec_att_low = to_low(dec_att.reshape(rows, -1))
    dec_pre = tgt_rows.astype(jnp.float32) + matmul(dec_att_low, dec_out)
    first = layer_norm(dec_pre, dec_gain[0], dec_shift[0])
    first_low = to_low(first)
    cross_queries = to_low(matmul(first_low, cross_qkv[0]))
    cross_att, cross_lse = attend_forward(
        split_heads(cross_queries),
        split_heads(mem_keys_all),
        split_heads(mem_values_all),
        tgt_ids,
        src_ids_all,
        offset,
        False,
    )
    cross_att_low = to_low(cross_att.reshape(rows, -1))
    cross_pre = first + matmul(cross_att_low, cross_out)
    second = layer_norm(cross_pre, dec_gain[1], dec_shift[1])
    second_low = to_low(second)
    dec_inner = matmul(second_low, dec_up) + dec_up_bias
    dec_act = to_low(jax.nn.gelu(dec_inner))
    dec_last = second + matmul(dec_act, dec_down) + dec_down_bias
    decoded = layer_norm(dec_last, dec_gain[2], dec_shift[2])
    upstream = out_grad[0].astype(jnp.float32)
    grad_last, gain_two, shift_two = norm_back(dec_last, dec_gain[2], dec_shift[2], upstream)
    branch_low = to_low(grad_last)
    dec_down_g = weight_grad(dec_act, branch_low)
    dec_down_bias_g = jnp.sum(branch_low.astype(jnp.float32), axis=0)
    inner_low = to_low(gelu_back(dec_inner, input_grad(branch_low, dec_down)))
    dec_up_g = weight_grad(second_low, inner_low)
    dec_up_bias_g = jnp.sum(inner_low.astype(jnp.float32), axis=0)
    grad_second = grad_last + input_grad(inner_low, dec_up)
    grad_cross_pre, gain_one, shift_one = norm_back(
        cross_pre, dec_gain[1], dec_shift[1], grad_second
    )
    mixed_low = to_low(grad_cross_pre)
    cross_out_g = weight_grad(cross_att_low, mixed_low)
    cross_att_grad = to_low(input_grad(mixed_low, cross_out))
    cross_query_grad, mem_key_sum, mem_value_sum = attention_back(
        split_heads(cross_queries),
        split_heads(mem_keys_all),
        split_heads(mem_values_all),
        tgt_ids,
        src_ids_all,
        False,
        split_heads(cross_att_grad),
        cross_att,
        cross_lse,
    )
    mem_key_low = to_low(mem_key_sum)
    mem_value_low = to_low(mem_value_sum)
    cross_query_low = to_low(cross_query_grad.reshape(rows, -1))
    cross_qkv_g = jnp.stack(
        [
            weight_grad(first_low, cross_query_low),
            weight_grad(memory_low, mem_key_low),
            weight_grad(memory_low, mem_value_low),
        ]
    )
    grad_first = grad_cross_pre + input_grad(cross_query_low, cross_qkv[0])
    grad_dec_pre, gain_zero, shift_zero = norm_back(dec_pre, dec_gain[0], dec_shift[0], grad_first)
    self_low = to_low(grad_dec_pre)
    dec_out_g = weight_grad(dec_att_low, self_low)
    dec_att_grad = to_low(input_grad(self_low, dec_out))
    dec_query_grad, dec_key_sum, dec_value_sum = attention_back(
        split_heads(dec_queries),
        split_heads(dec_keys_all),
        split_heads(dec_values_all),
        tgt_ids,
        tgt_ids_all,
        True,
        split_heads(dec_att_grad),
        dec_att,
        dec_lse,
    )
    dec_query_low = to_low(dec_query_grad.reshape(rows, -1))
    dec_key_low = to_low(dec_key_sum)
    dec_value_low = to_low(dec_value_sum)
    dec_qkv_g = jnp.stack(
        [
            weight_grad(tgt_rows, dec_query_low),
            weight_grad(tgt_rows, dec_key_low),
            weight_grad(tgt_rows, dec_value_low),
        ]
    )
    tgt_grad = (
        grad_dec_pre
        + input_grad(dec_query_low, dec_qkv[0])
        + input_grad(dec_key_low, dec_qkv[1])
        + input_grad(dec_value_low, dec_qkv[2])
    )
    dec_gain_g = jnp.stack([gain_zero, gain_one, gain_two])
    dec_shift_g = jnp.stack([shift_zero, shift_one, shift_two])
    grad_memory = input_grad(mem_key_low, cross_qkv[1]) + input_grad(mem_value_low, cross_qkv[2])
    grad_enc_last, enc_gain_one, enc_shift_one = norm_back(
        enc_last, enc_gain[1], enc_shift[1], grad_memory
    )
    enc_branch_low = to_low(grad_enc_last)
    enc_down_g = weight_grad(enc_act, enc_branch_low)
    enc_down_bias_g = jnp.sum(enc_branch_low.astype(jnp.float32), axis=0)
    enc_inner_low = to_low(gelu_back(enc_inner, input_grad(enc_branch_low, enc_down)))
    enc_up_g = weight_grad(hidden_low, enc_inner_low)
    enc_up_bias_g = jnp.sum(enc_inner_low.astype(jnp.float32), axis=0)
    grad_hidden = grad_enc_last + input_grad(enc_inner_low, enc_up)
    grad_enc_pre, enc_gain_zero, enc_shift_zero = norm_back(
        enc_pre, enc_gain[0], enc_shift[0], grad_hidden
    )
    enc_mixed_low = to_low(grad_enc_pre)
    enc_out_g = weight_grad(enc_att_low, enc_mixed_low)
    enc_att_grad = to_low(input_grad(enc_mixed_low, enc_out))
    enc_query_grad, enc_key_sum, enc_value_sum = attention_back(
        split_heads(enc_queries),
        split_heads(enc_keys_all),
        split_heads(enc_values_all),
        src_ids,
        src_ids_all,
        False,
        split_heads(enc_att_grad),
        enc_att,
        enc_lse,
    )
    enc_query_low = to_low(enc_query_grad.reshape(rows, -1))
    enc_key_low = to_low(enc_key_sum)
    enc_value_low = to_low(enc_value_sum)
    enc_qkv_g = jnp.stack(
        [
            weight_grad(src_rows, enc_query_low),
            weight_grad(src_rows, enc_key_low),
            weight_grad(src_rows, enc_value_low),
        ]
    )
    src_grad = (
        grad_enc_pre
        + input_grad(enc_query_low, enc_qkv[0])
        + input_grad(enc_key_low, enc_qkv[1])
        + input_grad(enc_value_low, enc_qkv[2])
    )
    enc_gain_g = jnp.stack([enc_gain_zero, enc_gain_one])
    enc_shift_g = jnp.stack([enc_shift_zero, enc_shift_one])
    all_rows = (
        lax.psum_scatter(
            enc_qkv_g.astype(jnp.bfloat16), "seq", scatter_dimension=1, tiled=True
        ).astype(jnp.float32),
        lax.psum_scatter(
            enc_out_g.astype(jnp.bfloat16), "seq", scatter_dimension=0, tiled=True
        ).astype(jnp.float32),
        lax.psum_scatter(
            enc_up_g.astype(jnp.bfloat16), "seq", scatter_dimension=0, tiled=True
        ).astype(jnp.float32),
        lax.psum_scatter(
            enc_down_g.astype(jnp.bfloat16), "seq", scatter_dimension=0, tiled=True
        ).astype(jnp.float32),
        lax.psum_scatter(
            dec_qkv_g.astype(jnp.bfloat16), "seq", scatter_dimension=1, tiled=True
        ).astype(jnp.float32),
        lax.psum_scatter(
            dec_out_g.astype(jnp.bfloat16), "seq", scatter_dimension=0, tiled=True
        ).astype(jnp.float32),
        lax.psum_scatter(
            cross_qkv_g.astype(jnp.bfloat16), "seq", scatter_dimension=1, tiled=True
        ).astype(jnp.float32),
        lax.psum_scatter(
            cross_out_g.astype(jnp.bfloat16), "seq", scatter_dimension=0, tiled=True
        ).astype(jnp.float32),
        lax.psum_scatter(
            dec_up_g.astype(jnp.bfloat16), "seq", scatter_dimension=0, tiled=True
        ).astype(jnp.float32),
        lax.psum_scatter(
            dec_down_g.astype(jnp.bfloat16), "seq", scatter_dimension=0, tiled=True
        ).astype(jnp.float32),
    )
    reduced = (
        lax.psum_scatter(
            all_rows[0].astype(jnp.bfloat16), "batch", scatter_dimension=2, tiled=True
        ).astype(jnp.float32),
        lax.psum_scatter(
            all_rows[1].astype(jnp.bfloat16), "batch", scatter_dimension=1, tiled=True
        ).astype(jnp.float32),
        lax.psum_scatter(
            all_rows[2].astype(jnp.bfloat16), "batch", scatter_dimension=1, tiled=True
        ).astype(jnp.float32),
        lax.psum_scatter(
            all_rows[3].astype(jnp.bfloat16), "batch", scatter_dimension=1, tiled=True
        ).astype(jnp.float32),
        lax.psum_scatter(
            all_rows[4].astype(jnp.bfloat16), "batch", scatter_dimension=2, tiled=True
        ).astype(jnp.float32),
        lax.psum_scatter(
            all_rows[5].astype(jnp.bfloat16), "batch", scatter_dimension=1, tiled=True
        ).astype(jnp.float32),
        lax.psum_scatter(
            all_rows[6].astype(jnp.bfloat16), "batch", scatter_dimension=2, tiled=True
        ).astype(jnp.float32),
        lax.psum_scatter(
            all_rows[7].astype(jnp.bfloat16), "batch", scatter_dimension=1, tiled=True
        ).astype(jnp.float32),
        lax.psum_scatter(
            all_rows[8].astype(jnp.bfloat16), "batch", scatter_dimension=1, tiled=True
        ).astype(jnp.float32),
        lax.psum_scatter(
            all_rows[9].astype(jnp.bfloat16), "batch", scatter_dimension=1, tiled=True
        ).astype(jnp.float32),
    )
    vectors = lax.psum(
        (
            enc_up_bias_g,
            enc_down_bias_g,
            enc_gain_g,
            enc_shift_g,
            dec_up_bias_g,
            dec_down_bias_g,
            dec_gain_g,
            dec_shift_g,
        ),
        ("batch", "seq"),
    )
    return (
        to_low(decoded)[None],
        to_low(src_grad)[None],
        to_low(tgt_grad)[None],
        reduced[0],
        reduced[1],
        reduced[2],
        vectors[0],
        reduced[3],
        vectors[1],
        vectors[2],
        vectors[3],
        reduced[4],
        reduced[5],
        reduced[6],
        reduced[7],
        reduced[8],
        vectors[4],
        reduced[9],
        vectors[5],
        vectors[6],
        vectors[7],
    )


def general(mesh):
    placed = (
        P("batch", "seq", None),
        P("batch", "seq", None),
        P("batch", "seq"),
        P("batch", "seq"),
        P("batch", "seq", None),
        P(),
        P(),
        P(),
        P(),
        P(),
        P(),
        P(),
        P(),
        P(),
        P(),
        P(),
        P(),
        P(),
        P(),
        P(),
        P(),
        P(),
        P(),
    )
    return jax.shard_map(
        general_shards,
        mesh=mesh,
        in_specs=placed,
        out_specs=(
            P("batch", "seq", None),
            P("batch", "seq", None),
            P("batch", "seq", None),
            P(None, "seq", "batch"),
            P("seq", "batch"),
            P("seq", "batch"),
            P(),
            P("seq", "batch"),
            P(),
            P(),
            P(),
            P(None, "seq", "batch"),
            P("seq", "batch"),
            P(None, "seq", "batch"),
            P("seq", "batch"),
            P("seq", "batch"),
            P(),
            P("seq", "batch"),
            P(),
            P(),
            P(),
        ),
        check_vma=False,
    )


def dot(left, right, left_dim=1, right_dim=0):
    return lax.dot_general(
        left, right, (((left_dim,), (right_dim,)), ((), ())), preferred_element_type=F32
    )


def my_core():
    return lax.rem(lax.axis_index("batch"), 2)


def block(index, size):
    return pl.ds(pl.multiple_of(index * size, size), size)


def normed(value):
    centred = value - jnp.mean(value, axis=-1, keepdims=True)
    scale = lax.rsqrt(jnp.mean(centred * centred, axis=-1, keepdims=True) + 1e-06)
    return centred * scale, scale


def normed_back(grad, unit, scale, gain):
    scaled = grad * gain
    first = jnp.mean(scaled, axis=-1, keepdims=True)
    second = jnp.mean(scaled * unit, axis=-1, keepdims=True)
    return scale * (scaled - first - unit * second)


def gelu_and_slope(inner):
    square = inner * inner
    bent = jnp.tanh(0.7978845608028654 * inner * (1.0 + 0.044715 * square))
    half = 0.5 * (1.0 + bent)
    slope = half + 0.5 * inner * (1.0 - bent * bent) * (
        0.7978845608028654 * (1.0 + 0.134145 * square)
    )
    return inner * half, slope


def column_sum(value):
    return jnp.sum(value, axis=0, keepdims=True)


TILE = 256
MESH = pl.DeviceIdType.MESH


def places():
    row, s = lax.axis_index("batch"), lax.axis_index("seq")
    core = lax.rem(row, 2)
    y = lax.rem(row // 2, 2)
    low = lax.rem(row // 4, 2)
    high = row // 8
    mine = {"core": core, "x": s, "y": y, "z1": low, "z2": high + core - 2 * high * core}
    partner = {
        "core": {"batch": row + 1 - 2 * core},
        "x": {"seq": 1 - s},
        "y": {"batch": row + 2 - 4 * y},
        "z1": {"batch": row + 4 - 8 * low},
        "z2": {"batch": row + 8 - 16 * high},
        "swap": {"batch": row - core + s, "seq": core},
    }
    return mine, partner


def greet(ways, swapping=False):
    mine, partner = places()
    barrier = pltpu.get_barrier_semaphore()
    for way in ways:
        pl.semaphore_signal(barrier, inc=1, device_id=partner[way], device_id_type=MESH)
    if swapping:
        away = mine["core"] + mine["x"] - 2 * mine["core"] * mine["x"]

        @pl.when(away == 1)
        def _():
            pl.semaphore_signal(barrier, inc=1, device_id=partner["swap"], device_id_type=MESH)

        pl.semaphore_wait(barrier, len(ways) + away)
    else:
        pl.semaphore_wait(barrier, len(ways))


def sending(source, target, sems, slot, way):
    _, partner = places()
    return pltpu.make_async_remote_copy(
        src_ref=source,
        dst_ref=target,
        send_sem=sems.at[0, slot],
        recv_sem=sems.at[1, slot],
        device_id=partner[way],
        device_id_type=MESH,
    )


def start_swap(source, target, sems, slot):
    mine, _ = places()

    @pl.when(mine["core"] != mine["x"])
    def _():
        sending(source, target, sems, slot, "swap").start()

    @pl.when(mine["core"] == mine["x"])
    def _():
        pltpu.make_async_copy(source, target, sems.at[0, slot]).start()


def wait_swap(source, target, sems, slot):
    mine, _ = places()

    @pl.when(mine["core"] != mine["x"])
    def _():
        sending(source, target, sems, slot, "swap").wait()

    @pl.when(mine["core"] == mine["x"])
    def _():
        pltpu.make_async_copy(source, target, sems.at[0, slot]).wait()


def part_of(ref, axis, index):
    return ref.at[(slice(None),) * axis + (index,)]


class Halving:
    def __init__(self, source, axis, way, got, sems, slot):
        mine, _ = places()
        self.kept = part_of(source, axis, mine[way])
        self.got = got
        self.copy = lambda: sending(part_of(source, axis, 1 - mine[way]), got, sems, slot, way)

    def start(self):
        self.copy().start()

    def finish(self, total):
        self.copy().wait()
        if total.dtype == F32:
            total[...] = self.kept[...].astype(F32) + self.got[...].astype(F32)
        else:
            total[...] = self.kept[...] + self.got[...]


def attend_kernel(causal, same, *refs):
    if same:
        own_q, other_q, weight, own_mq, other_mq, own_mk, other_mk = refs[:7]
        own_k, other_k = own_q, other_q
        refs = refs[7:]
    else:
        own_q, other_q, own_k, other_k, weight, own_mq, other_mq, own_mk, other_mk = refs[:9]
        refs = refs[9:]
    out_own, out_other, wide_out, queries, keys, values, chances, outs = refs
    step = pl.program_id(0)
    core = my_core()
    rows = own_q.shape[0]
    heads = queries.shape[0]
    length = queries.shape[1]
    width = heads * HEAD_DIM

    @pl.when(step == 0)
    def _():
        columns = block(core, width)
        lane = lax.broadcasted_iota(jnp.int32, (TILE, HEAD_DIM), 1)
        ones = (lane < 3).astype(BF)
        for q_ref, k_ref, mq_ref, mk_ref, half in (
            (own_q, own_k, own_mq, own_mk, core),
            (other_q, other_k, other_mq, other_mk, 1 - core),
        ):
            for tile in range(rows // TILE):
                here = slice(tile * TILE, (tile + 1) * TILE)
                there = pl.ds(pl.multiple_of(half * rows + tile * TILE, TILE), TILE)
                left_q = q_ref[here, :]
                left_k = k_ref[here, :]
                q_tile = dot(left_q, weight[0, :, columns]).astype(BF) * BF(0.125)
                k_tile = dot(left_k, weight[1, :, columns]).astype(BF)
                v_tile = dot(left_k, weight[2, :, columns]).astype(BF)
                for head in range(heads):
                    part = slice(head * HEAD_DIM, (head + 1) * HEAD_DIM)
                    queries[head, there, :] = jnp.concatenate([q_tile[:, part], mq_ref[here, :]], axis=1)
                    keys[head, there, :] = jnp.concatenate([k_tile[:, part], mk_ref[here, :]], axis=1)
                    values[head, there, :] = jnp.concatenate([v_tile[:, part], ones], axis=1)

    if causal:
        lower = lax.broadcasted_iota(jnp.int32, (TILE, TILE), 0) >= lax.broadcasted_iota(
            jnp.int32, (TILE, TILE), 1
        )
    for tile in range(length // TILE):
        here = slice(tile * TILE, (tile + 1) * TILE)
        seen = (tile + 1) * TILE if causal else length
        scores = dot(queries[step, here, :], keys[step, :seen, :], 1, 1)
        if causal:
            last = jnp.where(lower, scores[:, seen - TILE :], NEGATIVE)
            scores = last if tile == 0 else jnp.concatenate([scores[:, : seen - TILE], last], axis=1)
        largest = jnp.max(scores, axis=-1, keepdims=True)
        terms = jnp.exp(scores - largest)
        total = jnp.sum(terms, axis=-1, keepdims=True)
        low = (terms * (1.0 / total)).astype(BF)
        chances[0, here, :seen] = low
        outs[step, here, :] = dot(low, values[step, :seen, :])[:, :HEAD_DIM]

    @pl.when(step == heads - 1)
    def _():
        for half, ref in ((core, out_own), (1 - core, out_other)):
            for tile in range(rows // TILE):
                here = slice(tile * TILE, (tile + 1) * TILE)
                there = pl.ds(pl.multiple_of(half * rows + tile * TILE, TILE), TILE)
                joined = jnp.concatenate([outs[head, there, :] for head in range(heads)], axis=1)
                wide_out[there, :] = joined
                ref[here, :] = joined.astype(BF)


def attend_back_kernel(causal, same, work, *refs):
    if same:
        own_q, other_q = refs[:2]
        own_k, other_k = own_q, other_q
        refs = refs[2:]
    else:
        own_q, other_q, own_k, other_k = refs[:4]
        refs = refs[4:]
    queries, keys, values, chances, wide_out, grad_own, grad_other, out_part = refs[:8]
    given, refs = refs[8 : 8 + work.given], refs[8 + work.given :]
    d_own, d_other, unit = refs[:3]
    results, refs = refs[3 : 3 + work.results], refs[3 + work.results :]
    d_send, sums, sems, grads, score_grads, dq, dk, dv = refs[:8]
    scratch = refs[8:]
    step = pl.program_id(0)
    mine, partner = places()
    core = mine["core"]
    rows = own_q.shape[0]
    heads = queries.shape[0]
    length = queries.shape[1]

    @pl.when(step == 0)
    def _():
        greet(work.ways, work.swapping)
        pltpu.make_async_copy(out_part, unit.at[:, :, :, :, pl.ds(0, 32)], sems.at[0, 2]).start()

    work.before(step, given, results, scratch)

    @pl.when(step == 0)
    def _():
        lane = lax.broadcasted_iota(jnp.int32, (TILE, HEAD_DIM), 1)
        for ref, half in ((grad_own, core), (grad_other, 1 - core)):
            for tile in range(rows // TILE):
                here = slice(tile * TILE, (tile + 1) * TILE)
                there = pl.ds(pl.multiple_of(half * rows + tile * TILE, TILE), TILE)
                grad = ref[here, :]
                both = grad.astype(F32) * wide_out[there, :]
                for head in range(heads):
                    part = slice(head * HEAD_DIM, (head + 1) * HEAD_DIM)
                    settle = -jnp.sum(both[:, part], axis=-1, keepdims=True)
                    first = settle.astype(BF).astype(F32)
                    second = (settle - first).astype(BF).astype(F32)
                    third = settle - first - second
                    extra = jnp.where(
                        lane == 0,
                        first,
                        jnp.where(lane == 1, second, jnp.where(lane == 2, third, 0.0)),
                    )
                    grads[head, there, :] = jnp.concatenate([grad[:, part], extra.astype(BF)], axis=1)

    for tile in range(length // TILE):
        here = slice(tile * TILE, (tile + 1) * TILE)
        seen = (tile + 1) * TILE if causal else length
        change = dot(grads[step, here, :], values[step, :seen, :], 1, 1)
        low = (chances[0, here, :seen].astype(F32) * change).astype(BF)
        score_grads[here, :seen] = low
        dq[step, here, :] = dot(low, keys[step, :seen, :])[:, :HEAD_DIM] * 0.125
    for tile in range(length // TILE if causal else 1):
        here = slice(tile * TILE, (tile + 1) * TILE) if causal else slice(0, length)
        below = slice(tile * TILE, length)
        dk[block(step, HEAD_DIM), here] = dot(
            queries[step, below, :HEAD_DIM], score_grads[below, here], 0, 0
        )
        dv[block(step, HEAD_DIM), here] = dot(
            grads[step, below, :HEAD_DIM], chances[0, below, here], 0, 0
        )

    @pl.when(step == heads - 1)
    def _():
        to_other = sending(d_send, d_other, sems, 0, "core")
        for half, ref in ((1 - core, d_send), (core, d_own)):
            there = block(half, rows)
            ref[0, :, :] = jnp.concatenate(
                [dq[head, there, :] for head in range(heads)], axis=1
            ).astype(BF)
            ref[1, :, :] = dk[:, there].T.astype(BF)
            ref[2, :, :] = dv[:, there].T.astype(BF)
            if ref is d_send:
                to_other.start()
        for kind in range(3):
            x_own, x_other = (own_q, other_q) if kind == 0 else (own_k, other_k)
            total = dot(d_own[kind], x_own[...], 0, 0) + dot(d_send[kind], x_other[...], 0, 0)
            low = total.astype(BF)
            for part in range(low.shape[0] // 32):
                z_low, y, kept = part >> 2, (part >> 1) & 1, part & 1
                for s in range(2):
                    sums[core if kept == 0 else 1 - core, s, y, z_low, kind * 32 : (kind + 1) * 32, :] = low[
                        part * 32 : (part + 1) * 32, s * 256 : (s + 1) * 256
                    ]
        mine_there = unit.at[:, :, :, 0, pl.ds(32, 96)]
        other_there = unit.at[:, :, :, 1, pl.ds(32, 96)]
        across = sending(sums.at[1], other_there, sems, 1, "core")
        across.start()
        along = pltpu.make_async_copy(sums.at[0], mine_there, sems.at[0, 3])
        along.start()
        work.after(given, results, scratch)
        along.wait()
        pltpu.make_async_copy(out_part, unit.at[:, :, :, :, pl.ds(0, 32)], sems.at[0, 2]).wait()
        across.wait()
        to_other.wait()


BIG = (2, 2, 2, 2, 128, 256)
MID = BIG[1:]
LESS = BIG[2:]
LEAST = BIG[3:]


def scratch_of(*shapes):
    return [pltpu.VMEM(shape, kind) for shape, kind in shapes]


class CrossBackWork:
    given, results = 2, 1
    ways, swapping, far = ("core", "x", "y"), False, ()
    outs = (((2, *LESS), BF),)
    scratch = [pltpu.SemaphoreType.DMA((2, 4)), *scratch_of((MID, BF), (MID, BF), (MID, BF), (MID, BF), (LESS, BF), (LESS, BF))]

    def steps(self, given, scratch):
        down, up = given
        sems, got_a, got_b, mid_a, mid_b, got_c, got_d = scratch
        return (
            (Halving(down, 0, "x", got_a, sems, 0), mid_a),
            (Halving(up, 1, "y", got_b, sems, 1), mid_b),
            Halving(mid_a, 0, "y", got_c, sems, 2),
            Halving(mid_b, 0, "x", got_d, sems, 3),
        )

    def before(self, step, given, results, scratch):
        @pl.when(step == 0)
        def _():
            (one, _), (two, _), _, _ = self.steps(given, scratch)
            one.start()
            two.start()

        @pl.when(step == 3)
        def _():
            (one, mid_a), (two, mid_b), three, four = self.steps(given, scratch)
            one.finish(mid_a)
            three.start()
            two.finish(mid_b)
            four.start()

    def after(self, given, results, scratch):
        _, _, three, four = self.steps(given, scratch)
        three.finish(results[0].at[0])
        four.finish(results[0].at[1])


class EncodeBackWork(CrossBackWork):
    given, results = 4, 3
    ways, swapping, far = ("core", "x", "y", "z1", "z2"), False, ()
    outs = (((2, *LESS), BF), ((128, 256), F32), ((40, 512), F32))
    scratch = [
        pltpu.SemaphoreType.DMA((2, 10)),
        *scratch_of((MID, BF), (MID, BF), (MID, BF), (MID, BF), (LESS, BF), (LESS, BF)),
        *scratch_of((LEAST, BF), (LEAST, BF), ((128, 256), BF), ((4, 40, 512), F32), ((4, 40, 512), F32)),
    ]

    def before(self, step, given, results, scratch):
        down, up, cross, vectors = given
        more = scratch[7:]
        super().before(step, (down, up), results, scratch[:7])
        sems = scratch[0]
        got, mid, last, got_v, sum_v = more
        one = Halving(cross, 0, "z1", got, sems, 4)
        two = Halving(mid, 0, "z2", last, sems, 5)

        def vector(index, way):
            source = vectors if index == 0 else sum_v.at[index - 1]
            return sending(source, got_v.at[index], sems, 6 + index, way), source

        def vector_done(index, way):
            copy, source = vector(index, way)
            copy.wait()
            sum_v[index] = source[...] + got_v[index]

        @pl.when(step == 0)
        def _():
            one.start()
            vector(0, "core")[0].start()

        @pl.when(step == 1)
        def _():
            one.finish(mid)
            two.start()
            vector_done(0, "core")
            vector(1, "x")[0].start()

        @pl.when(step == 2)
        def _():
            two.finish(results[1])
            vector_done(1, "x")
            vector(2, "y")[0].start()

        @pl.when(step == 3)
        def _():
            vector_done(2, "y")
            vector(3, "z1")[0].start()

    def after(self, given, results, scratch):
        super().after(given[:2], results, scratch[:7])
        got_v, sum_v = scratch[10:]
        sending(sum_v.at[2], got_v.at[3], scratch[0], 9, "z1").wait()
        results[2][...] = sum_v[2] + got_v[3]


class DecodeBackWork:
    given, results = 7, 4
    ways, swapping, far = ("core", "x", "y", "z1", "z2"), True, (3,)
    outs = (((2, 128, 256), F32), (LESS, BF), ((40, 512), F32), ((512, 512), BF))
    scratch = [
        pltpu.SemaphoreType.DMA((2, 6)),
        *scratch_of(((2, *LEAST), BF), ((2, *LEAST), BF), ((2, 128, 256), BF)),
        *scratch_of((MID, BF), (MID, BF), (LESS, BF), ((40, 512), F32), ((512, 512), BF)),
    ]

    def before(self, step, given, results, scratch):
        both, attention, vectors, grad_pre, d_own, d_other, weight = given
        sems, got, mid, last, got_x, mid_x, got_y, got_v, grad = scratch
        one = Halving(both, 1, "z1", got, sems, 0)
        two = Halving(mid, 1, "z2", last, sems, 1)
        three = Halving(attention, 0, "x", got_x, sems, 2)
        four = Halving(mid_x, 0, "y", got_y, sems, 3)
        vector = sending(vectors, got_v, sems, 4, "z2")

        @pl.when(step == 0)
        def _():
            one.start()
            three.start()
            vector.start()
            input_kernel(grad_pre, d_own, d_other, weight, grad)
            start_swap(grad, results[3], sems, 5)

        @pl.when(step == 1)
        def _():
            one.finish(mid)
            two.start()
            vector.wait()
            results[2][...] = vectors[...] + got_v[...]

        @pl.when(step == 2)
        def _():
            two.finish(results[0])

        @pl.when(step == 3)
        def _():
            three.finish(mid_x)
            four.start()

    def after(self, given, results, scratch):
        sems, got, mid, last, got_x, mid_x, got_y, got_v, grad = scratch
        Halving(mid_x, 0, "y", got_y, sems, 3).finish(results[1])
        wait_swap(grad, results[3], sems, 5)


def tail_kernel(
    grad_pre, d_own, d_other, weight, attention, decode,
    grad_there, enc_sum, dec_sum,
    sems, grad, got_1, mid_1, got_2, half_a, half_b, got_a, got_b, mid_a, mid_b, got_c, got_d, mid_c, mid_d, got_e,
    mid_e, got_f,
):
    greet(("x", "y", "z1", "z2"), True)
    a = Halving(half_a, 0, "x", got_a, sems, 2)
    b = Halving(half_b, 1, "y", got_b, sems, 3)
    half_a[...] = decode[:, :, :, :, :64, :]
    a.start()
    half_b[...] = decode[:, :, :, :, 64:, :]
    b.start()
    one = Halving(attention, 0, "z1", got_1, sems, 0)
    one.start()
    input_kernel(grad_pre, d_own, d_other, weight, grad)
    start_swap(grad, grad_there, sems, 1)
    one.finish(mid_1)
    two = Halving(mid_1, 0, "z2", got_2, sems, 4)
    two.start()
    b.finish(mid_b)
    d = Halving(mid_b, 0, "x", got_d, sems, 6)
    d.start()
    a.finish(mid_a)
    c = Halving(mid_a, 0, "y", got_c, sems, 5)
    c.start()
    two.finish(enc_sum)
    c.finish(mid_c.at[0])
    d.finish(mid_c.at[1])
    e = Halving(mid_c, 1, "z1", got_e, sems, 7)
    e.start()
    e.finish(mid_e)
    f = Halving(mid_e, 1, "z2", got_f, sems, 8)
    f.start()
    f.finish(dec_sum)
    wait_swap(grad, grad_there, sems, 1)


def finish_kernel(
    decoded, src_grad, tgt_grad, dec_sums, enc_sums, cross_sum, enc_att_sum, dec_att_sum, vectors,
    decoded_o, src_o, tgt_o, enc_qkv, enc_out, enc_up, enc_up_bias, enc_down, enc_down_bias, enc_gain, enc_shift,
    dec_qkv, dec_out, cross_qkv, cross_out, dec_up, dec_up_bias, dec_down, dec_down_bias, dec_gain, dec_shift,
):
    decoded_o[...] = decoded[...]
    src_o[...] = src_grad[...]
    tgt_o[...] = tgt_grad[...]
    for sums, down, up in ((dec_sums, dec_down, dec_up), (enc_sums, enc_down, enc_up)):
        for slot in range(4):
            down[slot * 256 : (slot + 1) * 256, :] = sums[0, slot * 32 : (slot + 1) * 32, :].T
        up[...] = sums[1].T
    dec_att = jnp.concatenate([dec_att_sum[0], dec_att_sum[1]], axis=0)
    for sums, out, qkv in ((cross_sum[...], cross_out, cross_qkv), (enc_att_sum[...], enc_out, enc_qkv), (dec_att, dec_out, dec_qkv)):
        out[...] = sums[:32].T
        for kind in range(3):
            qkv[kind] = sums[32 + kind * 32 : 64 + kind * 32].T
    for part in range(4):
        dec_up_bias[:, part * 512 : (part + 1) * 512] = vectors[part : part + 1, :]
        enc_up_bias[:, part * 512 : (part + 1) * 512] = vectors[24 + part : 25 + part, :]
    dec_down_bias[...] = vectors[4:5, :]
    enc_down_bias[...] = vectors[28:29, :]
    for ref, places_of in (
        (dec_gain, (16, 5, 7)),
        (dec_shift, (17, 6, 8)),
        (enc_gain, (29, 31)),
        (enc_shift, (30, 32)),
    ):
        for index, place in enumerate(places_of):
            ref[index : index + 1, :] = vectors[place : place + 1, :]


def store_up(sums, value, index):
    core = my_core()
    z, y = index >> 1, index & 1
    low = value.astype(BF)
    for kept in range(2):
        for s in range(2):
            sums[core if kept == 0 else 1 - core, s, y, z & 1, (z >> 1) ^ kept, :, :] = low[
                kept * 128 : (kept + 1) * 128, s * 256 : (s + 1) * 256
            ]


def store_down(sums, value, index, column):
    core = my_core()
    low = value.astype(BF)
    for part in range(8):
        place = index * 8 + part
        z, y, kept = place >> 2, (place >> 1) & 1, place & 1
        for piece in range(2):
            s, slot = (column * 2 + piece) // 4, (column * 2 + piece) % 4
            sums[core if kept == 0 else 1 - core, s, y, z & 1, (z >> 1) ^ kept, slot * 32 : (slot + 1) * 32, :] = low[
                part * 32 : (part + 1) * 32, piece * 256 : (piece + 1) * 256
            ]


def store_out(sums, value, side):
    core = my_core()
    low = value.astype(BF)
    for place in range(16):
        z, y, kept = place >> 2, (place >> 1) & 1, place & 1
        sums[core if kept == 0 else 1 - core, side, y, z & 1, (z >> 1) ^ kept, :, :] = low[
            place * 32 : (place + 1) * 32, :
        ]


def projected(att_own, att_other, weight, here):
    core = my_core()
    width = att_own.shape[1]
    return dot(att_own[here, :], weight[block(core, width), :]) + dot(
        att_other[here, :], weight[block(1 - core, width), :]
    )


def projected_back(grad, weight, out_own, out_other, here):
    core = my_core()
    width = out_own.shape[1]
    out_own[here, :] = dot(grad, weight[block(core, width), :], 1, 1).astype(BF)
    out_other[here, :] = dot(grad, weight[block(1 - core, width), :], 1, 1).astype(BF)


def tiles_of(ref):
    return [slice(t * TILE, (t + 1) * TILE) for t in range(ref.shape[0] // TILE)]


def encode_kernel(
    x, att_own, att_other, out_w, up, up_bias, down, down_bias, gain, shift,
    memory, unit0, scale0, hidden_low, act, slope, unit1, scale1,
):
    for here in tiles_of(x):
        pre = x[here, :].astype(F32) + projected(att_own, att_other, out_w, here)
        unit, scale = normed(pre)
        unit0[here, :] = unit
        scale0[here, :] = scale
        hidden = unit * gain[0:1, :] + shift[0:1, :]
        low = hidden.astype(BF)
        hidden_low[here, :] = low
        value, bend = gelu_and_slope(dot(low, up[...]) + up_bias[...])
        slope[here, :] = bend
        value = value.astype(BF)
        act[here, :] = value
        unit, scale = normed(hidden + dot(value, down[...]) + down_bias[...])
        unit1[here, :] = unit
        scale1[here, :] = scale
        memory[here, :] = (unit * gain[1:2, :] + shift[1:2, :]).astype(BF)


def decode_first_kernel(y, att_own, att_other, out_w, gain, shift, first, first_low, unit0, scale0):
    for here in tiles_of(y):
        pre = y[here, :].astype(F32) + projected(att_own, att_other, out_w, here)
        unit, scale = normed(pre)
        unit0[here, :] = unit
        scale0[here, :] = scale
        value = unit * gain[0:1, :] + shift[0:1, :]
        first[here, :] = value
        first_low[here, :] = value.astype(BF)


def decode_last_kernel(
    first, att_own, att_other, out_w, up, up_bias, down, down_bias, gain, shift, upstream,
    decoded, grad_pre, grad_own, grad_other, down_unit, up_unit, out_unit, vectors,
    sems, grad_send, sums, gots, second_low, act, inner_low, branch_low, mixed_low,
):
    greet(("core",))
    vectors[...] = jnp.zeros_like(vectors)
    for here in tiles_of(first):
        pre = first[here, :] + projected(att_own, att_other, out_w, here)
        unit1, scale1 = normed(pre)
        second = unit1 * gain[1:2, :] + shift[1:2, :]
        low = second.astype(BF)
        second_low[here, :] = low
        value, slope = gelu_and_slope(dot(low, up[...]) + up_bias[...])
        value = value.astype(BF)
        act[here, :] = value
        unit2, scale2 = normed(second + dot(value, down[...]) + down_bias[...])
        decoded[here, :] = (unit2 * gain[2:3, :] + shift[2:3, :]).astype(BF)
        grad = upstream[here, :].astype(F32)
        vectors[7:8, :] += column_sum(grad * unit2)
        vectors[8:9, :] += column_sum(grad)
        grad = normed_back(grad, unit2, scale2, gain[2:3, :])
        branch = grad.astype(BF)
        branch_low[here, :] = branch
        vectors[4:5, :] += column_sum(branch.astype(F32))
        inner = (dot(branch, down[...], 1, 1) * slope).astype(BF)
        inner_low[here, :] = inner
        bias = column_sum(inner.astype(F32))
        for part in range(4):
            vectors[part : part + 1, :] += bias[:, part * 512 : (part + 1) * 512]
        grad = grad + dot(inner, up[...], 1, 1)
        vectors[5:6, :] += column_sum(grad * unit1)
        vectors[6:7, :] += column_sum(grad)
        grad = normed_back(grad, unit1, scale1, gain[1:2, :])
        grad_pre[here, :] = grad
        mixed = grad.astype(BF)
        mixed_low[here, :] = mixed
        projected_back(mixed, out_w, grad_own, grad_send, here)
    across = sending(grad_send, grad_other, sems, 0, "core")
    across.start()
    down_sums, up_sums, out_sums = sums
    copies = [sending(one.at[1], got, sems, 1 + i, "core") for i, (one, got) in enumerate(zip(sums, gots))]
    sum_down(down_sums, branch_low, act)
    copies[0].start()
    sum_up(up_sums, inner_low, second_low)
    copies[1].start()
    sum_out(out_sums, mixed_low, att_own, att_other)
    copies[2].start()
    across.wait()
    for one, got, copy, unit in zip(sums, gots, copies, (down_unit, up_unit, out_unit)):
        copy.wait()
        unit[...] = one[0] + got[...]


def sum_down(down_sums, branch_low, act):
    for index in range(2):
        for column in range(act.shape[1] // 512):
            part = dot(
                branch_low[:, index * 256 : (index + 1) * 256],
                act[:, column * 512 : (column + 1) * 512],
                0,
                0,
            )
            store_down(down_sums, part, index, column)


def sum_up(up_sums, inner_low, entering):
    for index in range(inner_low.shape[1] // 256):
        store_up(up_sums, dot(inner_low[:, index * 256 : (index + 1) * 256], entering[...], 0, 0), index)


def sum_out(out_sums, mixed_low, att_own, att_other):
    core = my_core()
    store_out(out_sums, dot(mixed_low[...], att_own[...], 0, 0), core)
    store_out(out_sums, dot(mixed_low[...], att_other[...], 0, 0), 1 - core)


def middle_back_kernel(
    d_own, d_other, cross_w, up, down, enc_gain, enc_w, unit0, scale0, hidden_low, act, slope, unit1, scale1,
    enc_att_own, enc_att_other, grad_second, first_unit, first_scale, dec_gain, dec_w, dec_att_own, dec_att_other,
    dec_both, cross_unit, decoded, dec_vectors,
    enc_pre, enc_own, enc_other, dec_pre, dec_own, dec_other, down_unit, up_unit, enc_out_unit, dec_out_unit,
    vectors, dec_sums, cross_half, decoded_there,
    sems, enc_send, dec_send, sums, gots, inner_low, branch_low, mixed_low, got_1, mid_1, got_2, got_x, mid_x, got_y,
):
    mine, _ = places()
    core = mine["core"]
    greet(("core", "x", "y", "z1", "z2"), True)
    one = Halving(dec_both, 1, "z1", got_1, sems, 0)
    two = Halving(mid_1, 1, "z2", got_2, sems, 1)
    three = Halving(cross_unit, 0, "x", got_x, sems, 2)
    four = Halving(mid_x, 0, "y", got_y, sems, 3)
    one.start()
    three.start()
    start_swap(decoded, decoded_there, sems, 4)
    enc_across = sending(enc_send, enc_other, sems, 5, "core")
    dec_across = sending(dec_send, dec_other, sems, 6, "core")
    copies = [sending(a.at[1], got, sems, 7 + i, "core") for i, (a, got) in enumerate(zip(sums, gots))]
    down_sums, up_sums, enc_out_sums, dec_out_sums = sums
    width = d_own.shape[2]
    vectors[...] = jnp.zeros_like(vectors)
    vectors[0:16, :] = dec_vectors[...]
    for here in tiles_of(unit0):
        grad = jnp.zeros(unit0[here, :].shape, F32)
        for kind in (1, 2):
            grad = grad + dot(d_own[kind, here, :], cross_w[kind, :, block(core, width)], 1, 1)
            grad = grad + dot(d_other[kind, here, :], cross_w[kind, :, block(1 - core, width)], 1, 1)
        unit = unit1[here, :]
        vectors[31:32, :] += column_sum(grad * unit)
        vectors[32:33, :] += column_sum(grad)
        grad = normed_back(grad, unit, scale1[here, :], enc_gain[1:2, :])
        branch = grad.astype(BF)
        branch_low[here, :] = branch
        vectors[28:29, :] += column_sum(branch.astype(F32))
        inner = (dot(branch, down[...], 1, 1) * slope[here, :]).astype(BF)
        inner_low[here, :] = inner
        bias = column_sum(inner.astype(F32))
        for part in range(4):
            vectors[24 + part : 25 + part, :] += bias[:, part * 512 : (part + 1) * 512]
        grad = grad + dot(inner, up[...], 1, 1)
        unit = unit0[here, :]
        vectors[29:30, :] += column_sum(grad * unit)
        vectors[30:31, :] += column_sum(grad)
        grad = normed_back(grad, unit, scale0[here, :], enc_gain[0:1, :])
        enc_pre[here, :] = grad
        mixed = grad.astype(BF)
        mixed_low[here, :] = mixed
        projected_back(mixed, enc_w, enc_own, enc_send, here)
    enc_across.start()
    one.finish(mid_1)
    two.start()
    sum_down(down_sums, branch_low, act)
    copies[0].start()
    two.finish(dec_sums)
    three.finish(mid_x)
    four.start()
    sum_up(up_sums, inner_low, hidden_low)
    copies[1].start()
    sum_out(enc_out_sums, mixed_low, enc_att_own, enc_att_other)
    copies[2].start()
    for here in tiles_of(first_unit):
        grad = grad_second[here, :]
        grad = grad + dot(d_own[0, here, :], cross_w[0, :, block(core, width)], 1, 1)
        grad = grad + dot(d_other[0, here, :], cross_w[0, :, block(1 - core, width)], 1, 1)
        unit = first_unit[here, :]
        vectors[16:17, :] += column_sum(grad * unit)
        vectors[17:18, :] += column_sum(grad)
        grad = normed_back(grad, unit, first_scale[here, :], dec_gain[0:1, :])
        dec_pre[here, :] = grad
        mixed = grad.astype(BF)
        mixed_low[here, :] = mixed
        projected_back(mixed, dec_w, dec_own, dec_send, here)
    dec_across.start()
    sum_out(dec_out_sums, mixed_low, dec_att_own, dec_att_other)
    copies[3].start()
    four.finish(cross_half)
    enc_across.wait()
    for a, got, copy, unit in zip(sums, gots, copies, (down_unit, up_unit, enc_out_unit, dec_out_unit)):
        copy.wait()
        unit[...] = a[0] + got[...]
    dec_across.wait()
    wait_swap(decoded, decoded_there, sems, 4)


def input_kernel(grad_pre, d_own, d_other, weight, grad):
    core = my_core()
    width = d_own.shape[2]
    for here in tiles_of(grad_pre):
        total = grad_pre[here, :]
        for kind in range(3):
            total = total + dot(d_own[kind, here, :], weight[kind, :, block(core, width)], 1, 1)
            total = total + dot(d_other[kind, here, :], weight[kind, :, block(1 - core, width)], 1, 1)
        grad[here, :] = total.astype(BF)


VMEM = pl.BlockSpec(memory_space=pltpu.VMEM)
ANY = pl.BlockSpec(memory_space=pl.ANY)


def call(
    kernel, name, micros, operands, outs, scratch=(), grid=None, in_specs=None, out_specs=None, meeting=None
):
    shapes = tuple(jax.ShapeDtypeStruct(shape, kind) for shape, kind in outs)
    extra = {} if grid is None else {"grid": grid}
    return pl.pallas_call(
        kernel,
        out_shape=shapes,
        in_specs=in_specs or [VMEM] * len(operands),
        out_specs=out_specs or tuple([VMEM] * len(outs)),
        scratch_shapes=list(scratch),
        compiler_params=pltpu.CompilerParams(
            vmem_limit_bytes=56 * 2**20, collective_id=meeting, has_side_effects=meeting is not None
        ),
        cost_estimate=pl.CostEstimate(
            flops=int(micros * 1e9), bytes_accessed=0, transcendentals=0
        ),
        name=name,
        **extra,
    )(*operands)


def whole(array):
    rank = len(array.shape)
    return pl.BlockSpec(array.shape, lambda step: (0,) * rank)


def attend(name, causal, same, sides, weight, masks):
    rows = sides[0].shape[0]
    width = weight.shape[2] // 2
    heads = width // HEAD_DIM
    length = 2 * rows
    wide = 2 * HEAD_DIM
    operands = (*sides, weight, *masks)
    outs = (
        ((rows, width), BF),
        ((rows, width), BF),
        ((length, width), F32),
        ((heads, length, wide), BF),
        ((heads, length, wide), BF),
        ((heads, length, wide), BF),
        ((heads, length, length), BF),
    )
    shapes = [jax.ShapeDtypeStruct(shape, kind) for shape, kind in outs]
    return call(
        functools.partial(attend_kernel, causal, same),
        name,
        10,
        operands,
        outs,
        scratch=[pltpu.VMEM((heads, length, HEAD_DIM), F32)],
        grid=(heads,),
        in_specs=[whole(one) for one in operands],
        out_specs=tuple(whole(one) for one in shapes[:-1])
        + (pl.BlockSpec((1, length, length), lambda step: (step, 0, 0)),),
    )


def attend_back(name, causal, same, work, meeting, sides, saved, grads, out_part, given):
    wide_out, queries, keys, values, chances = saved
    rows = sides[0].shape[0]
    heads, length, wide = queries.shape
    width = heads * HEAD_DIM
    operands = (*sides, queries, keys, values, chances, wide_out, *grads, out_part, *given)
    outs = (((3, rows, width), BF), ((3, rows, width), BF), (BIG, BF), *work.outs)
    in_specs = [whole(one) for one in operands]
    in_specs[len(sides) + 3] = pl.BlockSpec((1, length, length), lambda step: (step, 0, 0))
    shapes = [jax.ShapeDtypeStruct(shape, kind) for shape, kind in outs]
    return call(
        functools.partial(attend_back_kernel, causal, same, work),
        name,
        15,
        operands,
        outs,
        scratch=[
            pltpu.VMEM((3, rows, width), BF),
            pltpu.VMEM((2, 2, 2, 2, 96, 256), BF),
            pltpu.SemaphoreType.DMA((2, 4)),
            pltpu.VMEM((heads, length, wide), BF),
            pltpu.VMEM((length, length), BF),
            pltpu.VMEM((heads, length, HEAD_DIM), F32),
            pltpu.VMEM((width, length), F32),
            pltpu.VMEM((width, length), F32),
            *work.scratch,
        ],
        grid=(heads,),
        in_specs=in_specs,
        out_specs=(whole(shapes[0]), ANY, ANY)
        + tuple(ANY if place in work.far else whole(one) for place, one in enumerate(shapes[3:])),
        meeting=meeting,
    )


def pairs(count, move):
    found = []
    for index in range(count):
        z, y, core, s = index >> 3, (index >> 2) & 1, (index >> 1) & 1, index & 1
        z, y, core, s = move(z, y, core, s)
        found.append((index, (((z * 2 + y) * 2 + core) * 2) + s))
    return found


def fast_shards(count, source, target, source_ids, target_ids, out_grad, *params):
    (
        enc_qkv, enc_out, enc_up, enc_up_bias, enc_down, enc_down_bias, enc_gain, enc_shift, dec_qkv, dec_out,
        cross_qkv, cross_out, dec_up, dec_up_bias, dec_down, dec_down_bias, dec_gain, dec_shift,
    ) = params
    moves = {
        "swap": pairs(count, lambda z, y, c, s: (z, y, s, c)),
        "core": pairs(count, lambda z, y, c, s: (z, y, 1 - c, s)),
        "x": pairs(count, lambda z, y, c, s: (z, y, c, 1 - s)),
        "y": pairs(count, lambda z, y, c, s: (z, 1 - y, c, s)),
        "z1": pairs(count, lambda z, y, c, s: (z ^ 1, y, c, s)),
        "z2": pairs(count, lambda z, y, c, s: (z ^ 2, y, c, s)),
    }
    row = lax.axis_index("batch")
    core = row % 2
    place = {"x": lax.axis_index("seq"), "y": (row // 2) % 2, "z1": (row // 4) % 2, "z2": (row // 8) ^ core}

    def move(value, way):
        return lax.ppermute(value, BOTH, moves[way])

    ids = move(jnp.stack([source_ids[0], target_ids[0]]), "swap")
    src = move(source[0], "swap")
    tgt = move(target[0], "swap")
    upstream = move(out_grad[0], "swap")
    ids_other = move(ids, "core")
    src_other = move(src, "core")
    tgt_other = move(tgt, "core")
    lane = jnp.arange(HEAD_DIM, dtype=jnp.int32)[None, :]

    def masks(which):
        marks = [side[which][:, None] == lane for side in (ids, ids_other)]
        asks = [mark.astype(BF) for mark in marks]
        bars = [jnp.where(~mark & (lane < 3), NEGATIVE, 0.0).astype(BF) for mark in marks]
        return asks, bars

    src_ask, src_bar = masks(0)
    tgt_ask, tgt_bar = masks(1)
    rows, wide = src.shape
    inner = enc_up.shape[1]
    width = wide // 2
    full, thin = ((rows, wide), F32), ((rows, 1), F32)
    low_full, low_half = ((rows, wide), BF), ((rows, width), BF)
    low_inner = ((rows, inner), BF)
    biases = [one[None, :] for one in (enc_up_bias, enc_down_bias, dec_up_bias, dec_down_bias)]
    enc_up_b, enc_down_b, dec_up_b, dec_down_b = biases

    def scratch(shape):
        return pltpu.VMEM(*shape)

    att, att_send, *enc_saved = attend(
        "enc_attend", False, True, (src, src_other), enc_qkv, (*src_ask, *src_bar)
    )
    enc_att = (att, move(att_send, "core"))
    att, att_send, *dec_saved = attend(
        "dec_attend", True, True, (tgt, tgt_other), dec_qkv, (*tgt_ask, *tgt_bar)
    )
    dec_att = (att, move(att_send, "core"))
    memory, *enc_kept = call(
        encode_kernel,
        "encode",
        8,
        (src, *enc_att, enc_out, enc_up, enc_up_b, enc_down, enc_down_b, enc_gain, enc_shift),
        (low_full, full, thin, low_full, low_inner, ((rows, inner), F32), full, thin),
    )
    first, first_low, first_unit, first_scale = call(
        decode_first_kernel,
        "decode_first",
        2,
        (tgt, *dec_att, dec_out, dec_gain, dec_shift),
        (full, low_full, full, thin),
    )
    first_sides = (first_low, move(first_low, "core"))
    memory_sides = (memory, move(memory, "core"))
    cross_sides = (*first_sides, *memory_sides)
    att, att_send, *cross_saved = attend(
        "cross_attend", False, False, cross_sides, cross_qkv, (*tgt_ask, *src_bar)
    )
    cross_att = (att, move(att_send, "core"))
    sem = pltpu.SemaphoreType.DMA
    big, out_unit = (BIG, BF), ((2, 2, 2, 2, 32, 256), BF)
    big_pair, out_pair = scratch(((2, *BIG), BF)), scratch(((2, 2, 2, 2, 2, 32, 256), BF))
    big_got, out_got = scratch(big), scratch(out_unit)
    back_scratch = [scratch(low_inner), scratch(low_full), scratch(low_full)]
    decoded, grad_second, *cross_grads, dec_down_u, dec_up_u, cross_out_u, dec_vectors = call(
        decode_last_kernel,
        "decode_last",
        20,
        (first, *cross_att, cross_out, dec_up, dec_up_b, dec_down, dec_down_b, dec_gain, dec_shift, upstream),
        (low_full, full, low_half, low_half, big, big, out_unit, ((16, wide), F32)),
        scratch=[
            sem((2, 4)), scratch(low_half), [big_pair, big_pair, out_pair], [big_got, big_got, out_got],
            scratch(low_full), scratch(low_inner), *back_scratch,
        ],
        out_specs=(VMEM, VMEM, VMEM, ANY, VMEM, VMEM, VMEM, VMEM),
        meeting=0,
    )
    *d_cross, cross_u, dec_both = attend_back(
        "cross_attend_back", False, False, CrossBackWork(), 1, cross_sides, cross_saved, cross_grads, cross_out_u,
        (dec_down_u, dec_up_u),
    )
    operands = (
        *d_cross, cross_qkv, enc_up, enc_down, enc_gain, enc_out, *enc_kept, *enc_att,
        grad_second, first_unit, first_scale, dec_gain, dec_out, *dec_att, dec_both, cross_u, decoded, dec_vectors,
    )
    (
        grad_enc_pre, enc_own, enc_other, grad_dec_pre, dec_own, dec_other, enc_down_u, enc_up_u, enc_out_u, dec_out_u,
        vectors, dec_sums, cross_half, decoded,
    ) = call(
        middle_back_kernel,
        "middle_back",
        18,
        operands,
        (
            full, low_half, low_half, full, low_half, low_half, big, big, out_unit, out_unit, ((40, wide), F32),
            ((2, 128, 256), F32), (LESS, BF), low_full,
        ),
        scratch=[
            sem((2, 11)), scratch(low_half), scratch(low_half), [big_pair, big_pair, out_pair, out_pair],
            [big_got, big_got, out_got, out_got], *back_scratch,
            *scratch_of(((2, *LEAST), BF), ((2, *LEAST), BF), ((2, 128, 256), BF), (MID, BF), (MID, BF), (LESS, BF)),
        ],
        out_specs=(VMEM, VMEM, ANY, VMEM, VMEM, ANY, VMEM, VMEM, VMEM, VMEM, VMEM, VMEM, VMEM, ANY),
        meeting=2,
    )
    *d_enc, enc_u, enc_both, cross_sum, vectors = attend_back(
        "enc_attend_back", False, True, EncodeBackWork(), 3, (src, src_other), enc_saved, (enc_own, enc_other), enc_out_u,
        (enc_down_u, enc_up_u, cross_half, vectors),
    )
    *d_dec, dec_u, enc_sums, enc_att_half, vectors, src_grad = attend_back(
        "dec_attend_back", True, True, DecodeBackWork(), 4, (tgt, tgt_other), dec_saved, (dec_own, dec_other), dec_out_u,
        (enc_both, enc_u, vectors, grad_enc_pre, *d_enc, enc_qkv),
    )
    half, half_mid, half_less = (2, 2, 2, 2, 64, 256), (2, 2, 2, 64, 256), (2, 2, 64, 256)
    tgt_grad, enc_att_sum, dec_att_sum = call(
        tail_kernel,
        "tail",
        20,
        (grad_dec_pre, *d_dec, dec_qkv, enc_att_half, dec_u),
        (low_full, ((128, 256), F32), ((2, 64, 256), F32)),
        scratch=[
            sem((2, 9)),
            *scratch_of(
                low_full, (LEAST, BF), (LEAST, BF), ((128, 256), BF), (half, BF), (half, BF), (half_mid, BF),
                (half_mid, BF), (half_mid, BF), (half_mid, BF), (half_less, BF), (half_less, BF),
                ((2, *half_less), BF), ((2, 64, 256), BF), ((2, 2, 64, 256), BF), ((2, 2, 64, 256), BF), ((2, 64, 256), BF),
            ),
        ],
        out_specs=(ANY, VMEM, VMEM),
        meeting=5,
    )
    cut3, cut, pair, triple = ((3, 256, 32), F32), ((256, 32), F32), ((2, wide), F32), ((3, wide), F32)
    up_cut, down_cut, up_b, down_b = ((256, 128), F32), ((1024, 32), F32), ((1, inner), F32), ((1, wide), F32)
    outs = call(
        finish_kernel,
        "finish",
        2,
        (decoded, src_grad, tgt_grad, dec_sums, enc_sums, cross_sum, enc_att_sum, dec_att_sum, vectors),
        (
            low_full, low_full, low_full, cut3, cut, up_cut, up_b, down_cut, down_b, pair, pair,
            cut3, cut, cut3, cut, up_cut, up_b, down_cut, down_b, triple, triple,
        ),
    )
    return tuple(
        one[None] if place < 3 else one[0] if place in (6, 8, 16, 18) else one for place, one in enumerate(outs)
    )


def solution(mesh):
    if mesh.shape["seq"] != 2 or mesh.shape["batch"] != 16:
        return general(mesh)
    tokens = P("batch", "seq", None)
    ids = P("batch", "seq")
    cut, cut3 = P("seq", "batch"), P(None, "seq", "batch")
    return jax.shard_map(
        functools.partial(fast_shards, mesh.size),
        mesh=mesh,
        in_specs=(tokens, tokens, ids, ids, tokens) + (P(),) * 18,
        out_specs=(
            tokens, tokens, tokens, cut3, cut, cut, P(), cut, P(), P(), P(), cut3, cut, cut3, cut, cut, P(), cut,
            P(), P(), P(),
        ),
        check_vma=False,
    )
```

```python
import functools
import types

import jax
import jax.numpy as jnp
from jax import lax
from jax.experimental import pallas as pl
from jax.experimental.pallas import tpu as pltpu
from jax.sharding import PartitionSpec as P

HEAD_DIM = 64
NEGATIVE = -1e30
BF = jnp.bfloat16
F32 = jnp.float32
BOTH = ("batch", "seq")


def layer_norm(value, gain, shift):
    mean = jnp.mean(value, axis=-1, keepdims=True)
    centred = value - mean
    spread = jnp.mean(centred * centred, axis=-1, keepdims=True)
    return centred * lax.rsqrt(spread + 1e-06) * gain + shift


def norm_back(value, gain, shift, grad):
    _, pull = jax.vjp(layer_norm, value, gain, shift)
    return pull(grad)


def gelu_back(inner, grad):
    _, pull = jax.vjp(jax.nn.gelu, inner)
    return pull(grad)[0]


def matmul(left, right):
    return jnp.dot(left, right, preferred_element_type=jnp.float32)


def weight_grad(inputs, grad):
    return lax.dot_general(
        inputs, grad, (((0,), (0,)), ((), ())), preferred_element_type=jnp.float32
    )


def input_grad(grad, weight):
    return lax.dot_general(
        grad, weight, (((1,), (1,)), ((), ())), preferred_element_type=jnp.float32
    )


def to_low(value):
    return value.astype(jnp.bfloat16)


def split_heads(value):
    return value.reshape(value.shape[0], -1, HEAD_DIM)


def block_live(query_ids, key_ids, offset, block, rows, causal):
    first_key = lax.dynamic_index_in_dim(key_ids, block * rows, 0, keepdims=False)
    last_key = lax.dynamic_index_in_dim(key_ids, block * rows + rows - 1, 0, keepdims=False)
    live = (first_key <= query_ids[rows - 1]) & (query_ids[0] <= last_key)
    if causal:
        live = live & (block * rows <= offset + rows - 1)
    return live


def block_scores(queries, keys_all, query_ids, key_ids, offset, block, causal):
    rows = queries.shape[0]
    key_block = lax.dynamic_slice_in_dim(keys_all, block * rows, rows, 0)
    id_block = lax.dynamic_slice_in_dim(key_ids, block * rows, rows, 0)
    scores = (
        jnp.einsum("qhe,khe->hqk", queries, key_block, preferred_element_type=jnp.float32) * 0.125
    )
    allowed = query_ids[:, None] == id_block[None, :]
    if causal:
        positions = jnp.arange(rows, dtype=jnp.int32)
        allowed = allowed & ((offset + positions)[:, None] >= (block * rows + positions)[None, :])
    allowed = allowed[None]
    return (jnp.where(allowed, scores, NEGATIVE), allowed, key_block)


def attend_forward(queries, keys_all, values_all, query_ids, key_ids, offset, causal):
    rows = queries.shape[0]
    heads_count = queries.shape[1]
    count = keys_all.shape[0] // rows

    def first_pass(block, carry):

        def first_compute(state):
            largest, total = state
            scores, allowed, _ = block_scores(
                queries, keys_all, query_ids, key_ids, offset, block, causal
            )
            newest = jnp.maximum(largest, jnp.max(scores, axis=-1))
            terms = jnp.where(allowed, jnp.exp(scores - newest[..., None]), 0.0)
            return (newest, total * jnp.exp(largest - newest) + jnp.sum(terms, axis=-1))

        live = block_live(query_ids, key_ids, offset, block, rows, causal)
        return lax.cond(live, first_compute, lambda state: state, carry)

    initial = (
        jnp.full((heads_count, rows), NEGATIVE, jnp.float32),
        jnp.zeros((heads_count, rows), jnp.float32),
    )
    largest, total = lax.fori_loop(0, count, first_pass, initial)
    log_total = largest + jnp.log(total)

    def second_pass(block, carry):

        def second_compute(output):
            scores, allowed, _ = block_scores(
                queries, keys_all, query_ids, key_ids, offset, block, causal
            )
            value_block = lax.dynamic_slice_in_dim(values_all, block * rows, rows, 0)
            chances = jnp.where(allowed, jnp.exp(scores - log_total[..., None]), 0.0)
            return output + jnp.einsum(
                "hqk,khe->qhe", to_low(chances), value_block, preferred_element_type=jnp.float32
            )

        live = block_live(query_ids, key_ids, offset, block, rows, causal)
        return lax.cond(live, second_compute, lambda output: output, carry)

    output = lax.fori_loop(0, count, second_pass, jnp.zeros(queries.shape, jnp.float32))
    return (output, log_total)


def attend_backward(
    queries, keys_all, values_all, query_ids, key_ids, offset, causal, grad_out, settle, log_total
):
    rows = queries.shape[0]
    count = keys_all.shape[0] // rows

    def step_block(block, carry):

        def step_compute(state):
            query_grad, key_grads, value_grads = state
            scores, allowed, key_block = block_scores(
                queries, keys_all, query_ids, key_ids, offset, block, causal
            )
            value_block = lax.dynamic_slice_in_dim(values_all, block * rows, rows, 0)
            chances = jnp.where(allowed, jnp.exp(scores - log_total[..., None]), 0.0)
            chance_grad = jnp.einsum(
                "qhe,khe->hqk", grad_out, value_block, preferred_element_type=jnp.float32
            )
            score_grad = to_low(chances * (chance_grad - settle[..., None]))
            query_grad = (
                query_grad
                + jnp.einsum(
                    "hqk,khe->qhe", score_grad, key_block, preferred_element_type=jnp.float32
                )
                * 0.125
            )
            key_part = (
                jnp.einsum("hqk,qhe->khe", score_grad, queries, preferred_element_type=jnp.float32)
                * 0.125
            )
            value_part = jnp.einsum(
                "hqk,qhe->khe", to_low(chances), grad_out, preferred_element_type=jnp.float32
            )
            key_grads = lax.dynamic_update_slice_in_dim(key_grads, key_part, block * rows, 0)
            value_grads = lax.dynamic_update_slice_in_dim(value_grads, value_part, block * rows, 0)
            return (query_grad, key_grads, value_grads)

        live = block_live(query_ids, key_ids, offset, block, rows, causal)
        return lax.cond(live, step_compute, lambda state: state, carry)

    initial = (
        jnp.zeros(queries.shape, jnp.float32),
        jnp.zeros(keys_all.shape, jnp.float32),
        jnp.zeros(values_all.shape, jnp.float32),
    )
    return lax.fori_loop(0, count, step_block, initial)


def attention_back(
    queries, keys_all, values_all, query_ids, key_ids_all, causal, grad_out, output, log_total
):
    rows = queries.shape[0]
    offset = lax.axis_index("seq") * rows
    settle = jnp.einsum("qhe,qhe->hq", grad_out.astype(jnp.float32), output)
    query_grad, key_terms, value_terms = attend_backward(
        queries,
        keys_all,
        values_all,
        query_ids,
        key_ids_all,
        offset,
        causal,
        grad_out,
        settle,
        log_total,
    )
    key_sum, value_sum = (
        lax.psum_scatter(
            key_terms.reshape(key_terms.shape[0], -1).astype(jnp.bfloat16),
            "seq",
            scatter_dimension=0,
            tiled=True,
        ).astype(jnp.float32),
        lax.psum_scatter(
            value_terms.reshape(value_terms.shape[0], -1).astype(jnp.bfloat16),
            "seq",
            scatter_dimension=0,
            tiled=True,
        ).astype(jnp.float32),
    )
    return (query_grad, key_sum, value_sum)


def general_shards(
    source,
    target,
    source_ids,
    target_ids,
    out_grad,
    enc_qkv,
    enc_out,
    enc_up,
    enc_up_bias,
    enc_down,
    enc_down_bias,
    enc_gain,
    enc_shift,
    dec_qkv,
    dec_out,
    cross_qkv,
    cross_out,
    dec_up,
    dec_up_bias,
    dec_down,
    dec_down_bias,
    dec_gain,
    dec_shift,
):
    src_rows = source[0]
    tgt_rows = target[0]
    src_ids = source_ids[0]
    tgt_ids = target_ids[0]
    rows = src_rows.shape[0]
    offset = lax.axis_index("seq") * rows
    enc_queries = to_low(matmul(src_rows, enc_qkv[0]))
    enc_keys = to_low(matmul(src_rows, enc_qkv[1]))
    enc_values = to_low(matmul(src_rows, enc_qkv[2]))
    enc_keys_all, enc_values_all, src_ids_all = (
        lax.all_gather(enc_keys, "seq", axis=0, tiled=True),
        lax.all_gather(enc_values, "seq", axis=0, tiled=True),
        lax.all_gather(src_ids, "seq", axis=0, tiled=True),
    )
    enc_att, enc_lse = attend_forward(
        split_heads(enc_queries),
        split_heads(enc_keys_all),
        split_heads(enc_values_all),
        src_ids,
        src_ids_all,
        offset,
        False,
    )
    enc_att_low = to_low(enc_att.reshape(rows, -1))
    enc_pre = src_rows.astype(jnp.float32) + matmul(enc_att_low, enc_out)
    hidden = layer_norm(enc_pre, enc_gain[0], enc_shift[0])
    hidden_low = to_low(hidden)
    enc_inner = matmul(hidden_low, enc_up) + enc_up_bias
    enc_act = to_low(jax.nn.gelu(enc_inner))
    enc_last = hidden + matmul(enc_act, enc_down) + enc_down_bias
    memory = layer_norm(enc_last, enc_gain[1], enc_shift[1])
    memory_low = to_low(memory)
    mem_keys = to_low(matmul(memory_low, cross_qkv[1]))
    mem_values = to_low(matmul(memory_low, cross_qkv[2]))
    mem_keys_all, mem_values_all = (
        lax.all_gather(mem_keys, "seq", axis=0, tiled=True),
        lax.all_gather(mem_values, "seq", axis=0, tiled=True),
    )
    dec_queries = to_low(matmul(tgt_rows, dec_qkv[0]))
    dec_keys = to_low(matmul(tgt_rows, dec_qkv[1]))
    dec_values = to_low(matmul(tgt_rows, dec_qkv[2]))
    dec_keys_all, dec_values_all, tgt_ids_all = (
        lax.all_gather(dec_keys, "seq", axis=0, tiled=True),
        lax.all_gather(dec_values, "seq", axis=0, tiled=True),
        lax.all_gather(tgt_ids, "seq", axis=0, tiled=True),
    )
    dec_att, dec_lse = attend_forward(
        split_heads(dec_queries),
        split_heads(dec_keys_all),
        split_heads(dec_values_all),
        tgt_ids,
        tgt_ids_all,
        offset,
        True,
    )
    dec_att_low = to_low(dec_att.reshape(rows, -1))
    dec_pre = tgt_rows.astype(jnp.float32) + matmul(dec_att_low, dec_out)
    first = layer_norm(dec_pre, dec_gain[0], dec_shift[0])
    first_low = to_low(first)
    cross_queries = to_low(matmul(first_low, cross_qkv[0]))
    cross_att, cross_lse = attend_forward(
        split_heads(cross_queries),
        split_heads(mem_keys_all),
        split_heads(mem_values_all),
        tgt_ids,
        src_ids_all,
        offset,
        False,
    )
    cross_att_low = to_low(cross_att.reshape(rows, -1))
    cross_pre = first + matmul(cross_att_low, cross_out)
    second = layer_norm(cross_pre, dec_gain[1], dec_shift[1])
    second_low = to_low(second)
    dec_inner = matmul(second_low, dec_up) + dec_up_bias
    dec_act = to_low(jax.nn.gelu(dec_inner))
    dec_last = second + matmul(dec_act, dec_down) + dec_down_bias
    decoded = layer_norm(dec_last, dec_gain[2], dec_shift[2])
    upstream = out_grad[0].astype(jnp.float32)
    grad_last, gain_two, shift_two = norm_back(dec_last, dec_gain[2], dec_shift[2], upstream)
    branch_low = to_low(grad_last)
    dec_down_g = weight_grad(dec_act, branch_low)
    dec_down_bias_g = jnp.sum(branch_low.astype(jnp.float32), axis=0)
    inner_low = to_low(gelu_back(dec_inner, input_grad(branch_low, dec_down)))
    dec_up_g = weight_grad(second_low, inner_low)
    dec_up_bias_g = jnp.sum(inner_low.astype(jnp.float32), axis=0)
    grad_second = grad_last + input_grad(inner_low, dec_up)
    grad_cross_pre, gain_one, shift_one = norm_back(
        cross_pre, dec_gain[1], dec_shift[1], grad_second
    )
    mixed_low = to_low(grad_cross_pre)
    cross_out_g = weight_grad(cross_att_low, mixed_low)
    cross_att_grad = to_low(input_grad(mixed_low, cross_out))
    cross_query_grad, mem_key_sum, mem_value_sum = attention_back(
        split_heads(cross_queries),
        split_heads(mem_keys_all),
        split_heads(mem_values_all),
        tgt_ids,
        src_ids_all,
        False,
        split_heads(cross_att_grad),
        cross_att,
        cross_lse,
    )
    mem_key_low = to_low(mem_key_sum)
    mem_value_low = to_low(mem_value_sum)
    cross_query_low = to_low(cross_query_grad.reshape(rows, -1))
    cross_qkv_g = jnp.stack(
        [
            weight_grad(first_low, cross_query_low),
            weight_grad(memory_low, mem_key_low),
            weight_grad(memory_low, mem_value_low),
        ]
    )
    grad_first = grad_cross_pre + input_grad(cross_query_low, cross_qkv[0])
    grad_dec_pre, gain_zero, shift_zero = norm_back(dec_pre, dec_gain[0], dec_shift[0], grad_first)
    self_low = to_low(grad_dec_pre)
    dec_out_g = weight_grad(dec_att_low, self_low)
    dec_att_grad = to_low(input_grad(self_low, dec_out))
    dec_query_grad, dec_key_sum, dec_value_sum = attention_back(
        split_heads(dec_queries),
        split_heads(dec_keys_all),
        split_heads(dec_values_all),
        tgt_ids,
        tgt_ids_all,
        True,
        split_heads(dec_att_grad),
        dec_att,
        dec_lse,
    )
    dec_query_low = to_low(dec_query_grad.reshape(rows, -1))
    dec_key_low = to_low(dec_key_sum)
    dec_value_low = to_low(dec_value_sum)
    dec_qkv_g = jnp.stack(
        [
            weight_grad(tgt_rows, dec_query_low),
            weight_grad(tgt_rows, dec_key_low),
            weight_grad(tgt_rows, dec_value_low),
        ]
    )
    tgt_grad = (
        grad_dec_pre
        + input_grad(dec_query_low, dec_qkv[0])
        + input_grad(dec_key_low, dec_qkv[1])
        + input_grad(dec_value_low, dec_qkv[2])
    )
    dec_gain_g = jnp.stack([gain_zero, gain_one, gain_two])
    dec_shift_g = jnp.stack([shift_zero, shift_one, shift_two])
    grad_memory = input_grad(mem_key_low, cross_qkv[1]) + input_grad(mem_value_low, cross_qkv[2])
    grad_enc_last, enc_gain_one, enc_shift_one = norm_back(
        enc_last, enc_gain[1], enc_shift[1], grad_memory
    )
    enc_branch_low = to_low(grad_enc_last)
    enc_down_g = weight_grad(enc_act, enc_branch_low)
    enc_down_bias_g = jnp.sum(enc_branch_low.astype(jnp.float32), axis=0)
    enc_inner_low = to_low(gelu_back(enc_inner, input_grad(enc_branch_low, enc_down)))
    enc_up_g = weight_grad(hidden_low, enc_inner_low)
    enc_up_bias_g = jnp.sum(enc_inner_low.astype(jnp.float32), axis=0)
    grad_hidden = grad_enc_last + input_grad(enc_inner_low, enc_up)
    grad_enc_pre, enc_gain_zero, enc_shift_zero = norm_back(
        enc_pre, enc_gain[0], enc_shift[0], grad_hidden
    )
    enc_mixed_low = to_low(grad_enc_pre)
    enc_out_g = weight_grad(enc_att_low, enc_mixed_low)
    enc_att_grad = to_low(input_grad(enc_mixed_low, enc_out))
    enc_query_grad, enc_key_sum, enc_value_sum = attention_back(
        split_heads(enc_queries),
        split_heads(enc_keys_all),
        split_heads(enc_values_all),
        src_ids,
        src_ids_all,
        False,
        split_heads(enc_att_grad),
        enc_att,
        enc_lse,
    )
    enc_query_low = to_low(enc_query_grad.reshape(rows, -1))
    enc_key_low = to_low(enc_key_sum)
    enc_value_low = to_low(enc_value_sum)
    enc_qkv_g = jnp.stack(
        [
            weight_grad(src_rows, enc_query_low),
            weight_grad(src_rows, enc_key_low),
            weight_grad(src_rows, enc_value_low),
        ]
    )
    src_grad = (
        grad_enc_pre
        + input_grad(enc_query_low, enc_qkv[0])
        + input_grad(enc_key_low, enc_qkv[1])
        + input_grad(enc_value_low, enc_qkv[2])
    )
    enc_gain_g = jnp.stack([enc_gain_zero, enc_gain_one])
    enc_shift_g = jnp.stack([enc_shift_zero, enc_shift_one])
    all_rows = (
        lax.psum_scatter(
            enc_qkv_g.astype(jnp.bfloat16), "seq", scatter_dimension=1, tiled=True
        ).astype(jnp.float32),
        lax.psum_scatter(
            enc_out_g.astype(jnp.bfloat16), "seq", scatter_dimension=0, tiled=True
        ).astype(jnp.float32),
        lax.psum_scatter(
            enc_up_g.astype(jnp.bfloat16), "seq", scatter_dimension=0, tiled=True
        ).astype(jnp.float32),
        lax.psum_scatter(
            enc_down_g.astype(jnp.bfloat16), "seq", scatter_dimension=0, tiled=True
        ).astype(jnp.float32),
        lax.psum_scatter(
            dec_qkv_g.astype(jnp.bfloat16), "seq", scatter_dimension=1, tiled=True
        ).astype(jnp.float32),
        lax.psum_scatter(
            dec_out_g.astype(jnp.bfloat16), "seq", scatter_dimension=0, tiled=True
        ).astype(jnp.float32),
        lax.psum_scatter(
            cross_qkv_g.astype(jnp.bfloat16), "seq", scatter_dimension=1, tiled=True
        ).astype(jnp.float32),
        lax.psum_scatter(
            cross_out_g.astype(jnp.bfloat16), "seq", scatter_dimension=0, tiled=True
        ).astype(jnp.float32),
        lax.psum_scatter(
            dec_up_g.astype(jnp.bfloat16), "seq", scatter_dimension=0, tiled=True
        ).astype(jnp.float32),
        lax.psum_scatter(
            dec_down_g.astype(jnp.bfloat16), "seq", scatter_dimension=0, tiled=True
        ).astype(jnp.float32),
    )
    reduced = (
        lax.psum_scatter(
            all_rows[0].astype(jnp.bfloat16), "batch", scatter_dimension=2, tiled=True
        ).astype(jnp.float32),
        lax.psum_scatter(
            all_rows[1].astype(jnp.bfloat16), "batch", scatter_dimension=1, tiled=True
        ).astype(jnp.float32),
        lax.psum_scatter(
            all_rows[2].astype(jnp.bfloat16), "batch", scatter_dimension=1, tiled=True
        ).astype(jnp.float32),
        lax.psum_scatter(
            all_rows[3].astype(jnp.bfloat16), "batch", scatter_dimension=1, tiled=True
        ).astype(jnp.float32),
        lax.psum_scatter(
            all_rows[4].astype(jnp.bfloat16), "batch", scatter_dimension=2, tiled=True
        ).astype(jnp.float32),
        lax.psum_scatter(
            all_rows[5].astype(jnp.bfloat16), "batch", scatter_dimension=1, tiled=True
        ).astype(jnp.float32),
        lax.psum_scatter(
            all_rows[6].astype(jnp.bfloat16), "batch", scatter_dimension=2, tiled=True
        ).astype(jnp.float32),
        lax.psum_scatter(
            all_rows[7].astype(jnp.bfloat16), "batch", scatter_dimension=1, tiled=True
        ).astype(jnp.float32),
        lax.psum_scatter(
            all_rows[8].astype(jnp.bfloat16), "batch", scatter_dimension=1, tiled=True
        ).astype(jnp.float32),
        lax.psum_scatter(
            all_rows[9].astype(jnp.bfloat16), "batch", scatter_dimension=1, tiled=True
        ).astype(jnp.float32),
    )
    vectors = lax.psum(
        (
            enc_up_bias_g,
            enc_down_bias_g,
            enc_gain_g,
            enc_shift_g,
            dec_up_bias_g,
            dec_down_bias_g,
            dec_gain_g,
            dec_shift_g,
        ),
        ("batch", "seq"),
    )
    return (
        to_low(decoded)[None],
        to_low(src_grad)[None],
        to_low(tgt_grad)[None],
        reduced[0],
        reduced[1],
        reduced[2],
        vectors[0],
        reduced[3],
        vectors[1],
        vectors[2],
        vectors[3],
        reduced[4],
        reduced[5],
        reduced[6],
        reduced[7],
        reduced[8],
        vectors[4],
        reduced[9],
        vectors[5],
        vectors[6],
        vectors[7],
    )


def general(mesh):
    placed = (
        P("batch", "seq", None),
        P("batch", "seq", None),
        P("batch", "seq"),
        P("batch", "seq"),
        P("batch", "seq", None),
        P(),
        P(),
        P(),
        P(),
        P(),
        P(),
        P(),
        P(),
        P(),
        P(),
        P(),
        P(),
        P(),
        P(),
        P(),
        P(),
        P(),
        P(),
    )
    return jax.shard_map(
        general_shards,
        mesh=mesh,
        in_specs=placed,
        out_specs=(
            P("batch", "seq", None),
            P("batch", "seq", None),
            P("batch", "seq", None),
            P(None, "seq", "batch"),
            P("seq", "batch"),
            P("seq", "batch"),
            P(),
            P("seq", "batch"),
            P(),
            P(),
            P(),
            P(None, "seq", "batch"),
            P("seq", "batch"),
            P(None, "seq", "batch"),
            P("seq", "batch"),
            P("seq", "batch"),
            P(),
            P("seq", "batch"),
            P(),
            P(),
            P(),
        ),
        check_vma=False,
    )


def dot(left, right, left_dim=1, right_dim=0):
    return lax.dot_general(
        left, right, (((left_dim,), (right_dim,)), ((), ())), preferred_element_type=F32
    )


def my_core():
    return lax.rem(lax.axis_index("batch"), 2)


def block(index, size):
    return pl.ds(pl.multiple_of(index * size, size), size)


def normed(value):
    centred = value - jnp.mean(value, axis=-1, keepdims=True)
    scale = lax.rsqrt(jnp.mean(centred * centred, axis=-1, keepdims=True) + 1e-06)
    return centred * scale, scale


def normed_back(grad, unit, scale, gain):
    scaled = grad * gain
    first = jnp.mean(scaled, axis=-1, keepdims=True)
    second = jnp.mean(scaled * unit, axis=-1, keepdims=True)
    return scale * (scaled - first - unit * second)


def gelu_and_slope(inner):
    square = inner * inner
    bent = jnp.tanh(0.7978845608028654 * inner * (1.0 + 0.044715 * square))
    half = 0.5 * (1.0 + bent)
    slope = half + 0.5 * inner * (1.0 - bent * bent) * (
        0.7978845608028654 * (1.0 + 0.134145 * square)
    )
    return inner * half, slope


def column_sum(value):
    return jnp.sum(value, axis=0, keepdims=True)


TILE = 256
MESH = pl.DeviceIdType.MESH


def places():
    row, s = lax.axis_index("batch"), lax.axis_index("seq")
    core = lax.rem(row, 2)
    y = lax.rem(row // 2, 2)
    low = lax.rem(row // 4, 2)
    high = row // 8
    mine = {"core": core, "x": s, "y": y, "z1": low, "z2": high + core - 2 * high * core}
    partner = {
        "core": {"batch": row + 1 - 2 * core},
        "x": {"seq": 1 - s},
        "y": {"batch": row + 2 - 4 * y},
        "z1": {"batch": row + 4 - 8 * low},
        "z2": {"batch": row + 8 - 16 * high},
        "swap": {"batch": row - core + s, "seq": core},
    }
    return mine, partner


def call_out(ways, swapping=False):
    mine, partner = places()
    barrier = pltpu.get_barrier_semaphore()
    for way in ways:
        pl.semaphore_signal(barrier, inc=1, device_id=partner[way], device_id_type=MESH)
    if swapping:

        @pl.when(mine["core"] != mine["x"])
        def _():
            pl.semaphore_signal(barrier, inc=1, device_id=partner["swap"], device_id_type=MESH)


def hear(ways, swapping=False):
    mine, _ = places()
    away = mine["core"] + mine["x"] - 2 * mine["core"] * mine["x"]
    pl.semaphore_wait(pltpu.get_barrier_semaphore(), len(ways) + away if swapping else len(ways))


def greet(ways, swapping=False):
    call_out(ways, swapping)
    hear(ways, swapping)


def sending(source, target, sems, slot, way):
    _, partner = places()
    return pltpu.make_async_remote_copy(
        src_ref=source,
        dst_ref=target,
        send_sem=sems.at[0, slot],
        recv_sem=sems.at[1, slot],
        device_id=partner[way],
        device_id_type=MESH,
    )


def start_swap(source, target, sems, slot):
    mine, _ = places()

    @pl.when(mine["core"] != mine["x"])
    def _():
        sending(source, target, sems, slot, "swap").start()

    @pl.when(mine["core"] == mine["x"])
    def _():
        pltpu.make_async_copy(source, target, sems.at[0, slot]).start()


def wait_swap(source, target, sems, slot):
    mine, _ = places()

    @pl.when(mine["core"] != mine["x"])
    def _():
        sending(source, target, sems, slot, "swap").wait()

    @pl.when(mine["core"] == mine["x"])
    def _():
        pltpu.make_async_copy(source, target, sems.at[0, slot]).wait()


def part_of(ref, axis, index):
    return ref.at[(slice(None),) * axis + (index,)]


class Halving:
    def __init__(self, source, axis, way, got, total, sems, slot, far=False):
        mine, _ = places()
        kept = part_of(source, axis, mine[way])
        self.kept, self.got, self.total = (total if far else kept), got, total
        self.sent = lambda: sending(part_of(source, axis, 1 - mine[way]), got, sems, slot, way)
        self.near = (lambda: pltpu.make_async_copy(kept, total, sems.at[2, slot])) if far else None

    def start(self):
        self.sent().start()
        if self.near is not None:
            self.near().start()

    def finish(self):
        if self.near is not None:
            self.near().wait()
        self.sent().wait()
        if self.total.dtype == F32:
            self.total[...] = self.kept[...].astype(F32) + self.got[...].astype(F32)
        else:
            self.total[...] = self.kept[...] + self.got[...]


class Across:
    def __init__(self, sums, got, far, sems, slot):
        self.sums, self.got = sums, got
        self.sent = lambda: sending(sums.at[1], got, sems, slot, "core")
        self.out = lambda: pltpu.make_async_copy(sums.at[0], far, sems.at[2, slot])

    def start(self):
        self.sent().start()

    def finish(self):
        self.sent().wait()
        self.sums[0] = self.sums[0] + self.got[...]

    def copy_out(self):
        self.out().start()

    def end(self):
        self.out().wait()


def start_loads(pairs_of, sems):
    for place, (far, near) in enumerate(pairs_of):
        pltpu.make_async_copy(far, near, sems.at[place]).start()


def wait_loads(pairs_of, sems):
    for place, (far, near) in enumerate(pairs_of):
        pltpu.make_async_copy(far, near, sems.at[place]).wait()


def attend_kernel(causal, same, *refs):
    if same:
        own_q, other_q, weight, own_mq, other_mq, own_mk, other_mk = refs[:7]
        own_k, other_k = own_q, other_q
        refs = refs[7:]
    else:
        own_q, other_q, own_k, other_k, weight, own_mq, other_mq, own_mk, other_mk = refs[:9]
        refs = refs[9:]
    out_own, out_other, wide_out, queries, keys, values, chances, outs = refs
    step = pl.program_id(0)
    core = my_core()
    rows = own_q.shape[0]
    heads = queries.shape[0]
    length = queries.shape[1]
    width = heads * HEAD_DIM

    @pl.when(step == 0)
    def _():
        columns = block(core, width)
        lane = lax.broadcasted_iota(jnp.int32, (TILE, HEAD_DIM), 1)
        ones = (lane < 3).astype(BF)
        for q_ref, k_ref, mq_ref, mk_ref, half in (
            (own_q, own_k, own_mq, own_mk, core),
            (other_q, other_k, other_mq, other_mk, 1 - core),
        ):
            for tile in range(rows // TILE):
                here = slice(tile * TILE, (tile + 1) * TILE)
                there = pl.ds(pl.multiple_of(half * rows + tile * TILE, TILE), TILE)
                left_q = q_ref[here, :]
                left_k = k_ref[here, :]
                q_tile = dot(left_q, weight[0, :, columns]).astype(BF) * BF(0.125)
                k_tile = dot(left_k, weight[1, :, columns]).astype(BF)
                v_tile = dot(left_k, weight[2, :, columns]).astype(BF)
                for head in range(heads):
                    part = slice(head * HEAD_DIM, (head + 1) * HEAD_DIM)
                    queries[head, there, :] = jnp.concatenate([q_tile[:, part], mq_ref[here, :]], axis=1)
                    keys[head, there, :] = jnp.concatenate([k_tile[:, part], mk_ref[here, :]], axis=1)
                    values[head, there, :] = jnp.concatenate([v_tile[:, part], ones], axis=1)

    if causal:
        lower = lax.broadcasted_iota(jnp.int32, (TILE, TILE), 0) >= lax.broadcasted_iota(
            jnp.int32, (TILE, TILE), 1
        )
    for tile in range(length // TILE):
        here = slice(tile * TILE, (tile + 1) * TILE)
        seen = (tile + 1) * TILE if causal else length
        scores = dot(queries[step, here, :], keys[step, :seen, :], 1, 1)
        if causal:
            last = jnp.where(lower, scores[:, seen - TILE :], NEGATIVE)
            scores = last if tile == 0 else jnp.concatenate([scores[:, : seen - TILE], last], axis=1)
        largest = jnp.max(scores, axis=-1, keepdims=True)
        terms = jnp.exp(scores - largest)
        total = jnp.sum(terms, axis=-1, keepdims=True)
        low = (terms * (1.0 / total)).astype(BF)
        chances[0, here, :seen] = low
        outs[step, here, :] = dot(low, values[step, :seen, :])[:, :HEAD_DIM]

    @pl.when(step == heads - 1)
    def _():
        for half, ref in ((core, out_own), (1 - core, out_other)):
            for tile in range(rows // TILE):
                here = slice(tile * TILE, (tile + 1) * TILE)
                there = pl.ds(pl.multiple_of(half * rows + tile * TILE, TILE), TILE)
                joined = jnp.concatenate([outs[head, there, :] for head in range(heads)], axis=1)
                wide_out[there, :] = joined
                ref[here, :] = joined.astype(BF)


def back_begin(a, work):
    mine, _ = places()
    heads, rows = a.queries.shape[0], a.grad_own.shape[0]
    lane = lax.broadcasted_iota(jnp.int32, (TILE, HEAD_DIM), 1)
    for ref, half in ((a.grad_own, mine["core"]), (a.grad_other, 1 - mine["core"])):
        for tile in range(rows // TILE):
            here = slice(tile * TILE, (tile + 1) * TILE)
            there = pl.ds(pl.multiple_of(half * rows + tile * TILE, TILE), TILE)
            grad = ref[here, :]
            both = grad.astype(F32) * a.wide_out[there, :]
            for head in range(heads):
                part = slice(head * HEAD_DIM, (head + 1) * HEAD_DIM)
                settle = -jnp.sum(both[:, part], axis=-1, keepdims=True)
                first = settle.astype(BF).astype(F32)
                second = (settle - first).astype(BF).astype(F32)
                third = settle - first - second
                extra = jnp.where(
                    lane == 0, first, jnp.where(lane == 1, second, jnp.where(lane == 2, third, 0.0))
                )
                work.grads[head, there, :] = jnp.concatenate([grad[:, part], extra.astype(BF)], axis=1)


def back_head(a, work, chances, head, causal):
    length = a.queries.shape[1]
    for tile in range(length // TILE):
        here = slice(tile * TILE, (tile + 1) * TILE)
        seen = (tile + 1) * TILE if causal else length
        change = dot(work.grads[head, here, :], a.values[head, :seen, :], 1, 1)
        low = (chances[0, here, :seen].astype(F32) * change).astype(BF)
        work.score_grads[here, :seen] = low
        work.dq[head, here, :] = (dot(low, a.keys[head, :seen, :])[:, :HEAD_DIM] * 0.125).astype(BF)
    for tile in range(length // TILE if causal else 1):
        here = slice(tile * TILE, (tile + 1) * TILE) if causal else slice(0, length)
        below = slice(tile * TILE, length)
        work.dk[block(head, HEAD_DIM), here] = dot(
            a.queries[head, below, :HEAD_DIM], work.score_grads[below, here], 0, 0
        )
        work.dv[block(head, HEAD_DIM), here] = dot(
            work.grads[head, below, :HEAD_DIM], chances[0, below, here], 0, 0
        )


class BackEnd:
    def __init__(self, a, sems):
        self.a = a
        out_part = a.out_part
        self.other = lambda: sending(a.d_send, a.d_other, sems, 0, "core")
        self.across = lambda: sending(a.sums.at[1], a.unit.at[:, :, :, 1, pl.ds(32, 96)], sems, 1, "core")
        self.along = lambda: pltpu.make_async_copy(a.sums.at[0], a.unit.at[:, :, :, 0, pl.ds(32, 96)], sems.at[2, 0])
        self.beside = lambda: pltpu.make_async_copy(out_part, a.unit.at[:, :, :, :, pl.ds(0, 32)], sems.at[2, 1])

    def start(self, work):
        a = self.a
        core = my_core()
        rows, heads = a.grad_own.shape[0], a.queries.shape[0]
        self.beside().start()
        for half, ref in ((1 - core, a.d_send), (core, a.d_own)):
            there = block(half, rows)
            ref[0, :, :] = jnp.concatenate([work.dq[head, there, :] for head in range(heads)], axis=1)
            ref[1, :, :] = work.dk[:, there].T.astype(BF)
            ref[2, :, :] = work.dv[:, there].T.astype(BF)
            if ref is a.d_send:
                self.other().start()
        for kind in range(3):
            x_own, x_other = (a.own_q, a.other_q) if kind == 0 else (a.own_k, a.other_k)
            total = dot(a.d_own[kind], x_own[...], 0, 0) + dot(a.d_send[kind], x_other[...], 0, 0)
            low = total.astype(BF)
            for part in range(low.shape[0] // 32):
                z_low, y, kept = part >> 2, (part >> 1) & 1, part & 1
                for s in range(2):
                    a.sums[core if kept == 0 else 1 - core, s, y, z_low, kind * 32 : (kind + 1) * 32, :] = low[
                        part * 32 : (part + 1) * 32, s * 256 : (s + 1) * 256
                    ]
        self.across().start()
        self.along().start()

    def wait_grads(self):
        self.other().wait()

    def wait_sums(self):
        self.along().wait()
        self.beside().wait()
        self.across().wait()


BIG = (2, 2, 2, 2, 128, 256)
MID = BIG[1:]
LESS = BIG[2:]
LEAST = BIG[3:]


def low_scratch(*shapes):
    return [pltpu.VMEM(shape, BF) for shape in shapes]


def middle_layers(r, events):
    core = my_core()
    width = r.d_own.shape[2]
    vectors = r.vectors
    @over_tiles(r.unit0)
    def _(here):
        grad = jnp.zeros(r.unit0[here, :].shape, F32)
        for kind in (1, 2):
            grad = grad + dot(r.d_own[kind, here, :], r.cross_w[kind, :, block(core, width)], 1, 1)
            grad = grad + dot(r.d_other[kind, here, :], r.cross_w[kind, :, block(1 - core, width)], 1, 1)
        unit = r.unit1[here, :]
        vectors[31:32, :] += column_sum(grad * unit)
        vectors[32:33, :] += column_sum(grad)
        grad = normed_back(grad, unit, r.scale1[here, :], r.enc_gain[1:2, :])
        branch = grad.astype(BF)
        r.branch_low[here, :] = branch
        vectors[28:29, :] += column_sum(branch.astype(F32))
        for place, part in enumerate(parts_of(r.up)):
            inner = (dot(branch, r.down[part, :], 1, 1) * r.slope[here, part].astype(F32)).astype(BF)
            r.inner_low[here, part] = inner
            vectors[24 + place : 25 + place, :] += column_sum(inner.astype(F32))
        grad = grad + dot(r.inner_low[here, :], r.up[...], 1, 1)
        unit = r.unit0[here, :]
        vectors[29:30, :] += column_sum(grad * unit)
        vectors[30:31, :] += column_sum(grad)
        grad = normed_back(grad, unit, r.scale0[here, :], r.enc_gain[0:1, :])
        r.enc_pre[here, :] = grad
        mixed = grad.astype(BF)
        r.mixed_low[here, :] = mixed
        projected_back(mixed, r.enc_w, r.enc_own, r.enc_send, here)
    events("encoder")
    sum_down(r.down_sums, r.branch_low, r.act)
    events("down")
    sum_up(r.up_sums, r.inner_low, r.hidden_low)
    events("up")
    sum_out(r.enc_out_sums, r.mixed_low, r.enc_att_own, r.enc_att_other)
    events("enc_out")
    @over_tiles(r.first_unit)
    def _(here):
        grad = r.grad_second[here, :]
        grad = grad + dot(r.d_own[0, here, :], r.cross_w[0, :, block(core, width)], 1, 1)
        grad = grad + dot(r.d_other[0, here, :], r.cross_w[0, :, block(1 - core, width)], 1, 1)
        unit = r.first_unit[here, :]
        vectors[16:17, :] += column_sum(grad * unit)
        vectors[17:18, :] += column_sum(grad)
        grad = normed_back(grad, unit, r.first_scale[here, :], r.dec_gain[0:1, :])
        r.dec_pre[here, :] = grad
        mixed = grad.astype(BF)
        r.mixed_low[here, :] = mixed
        projected_back(mixed, r.dec_w, r.dec_own, r.dec_send, here)
    events("decoder")
    sum_out(r.dec_out_sums, r.mixed_low, r.dec_att_own, r.dec_att_other)
    events("dec_out")


NEAR_FIRST = ("first", "att_own", "att_other", "cross_out", "upstream")
NEAR_CROSS = ("queries", "keys", "values", "wide_out", "own_q", "other_q", "own_k", "other_k")
NEAR_MIDDLE = (
    "cross_w", "enc_w", "dec_w", "unit0", "scale0", "hidden_low", "slope", "unit1", "scale1",
    "enc_att_own", "enc_att_other", "first_unit", "first_scale", "dec_att_own", "dec_att_other",
)


def split_halvings(unit, bufs, totals, sems, slot):
    upper, lower = unit.at[:, :, :, :, pl.ds(0, 64)], unit.at[:, :, :, :, pl.ds(64, 64)]
    return (
        Halving(upper, 0, "x", bufs.at[0], totals.at[0], sems, slot),
        Halving(lower, 1, "y", bufs.at[1], totals.at[1], sems, slot + 1),
    )


def join_halvings(source, less, both, last, final, total, sems, slot):
    return (
        Halving(source.at[0], 0, "y", less.at[0], both.at[0], sems, slot),
        Halving(source.at[1], 0, "x", less.at[1], both.at[1], sems, slot + 1),
        Halving(both, 1, "z1", last.at[0], last.at[1], sems, slot + 2),
        Halving(last.at[1], 1, "z2", final, total, sems, slot + 3),
    )


def decode_middle_body(r):
    step = pl.program_id(0)
    ways = ("core", "x", "y", "z1", "z2")
    far = {name: (getattr(r, "far_" + name), getattr(r, name)) for name in (*NEAR_FIRST, *NEAR_CROSS, *NEAR_MIDDLE)}
    order = list(far)

    def load(names, wait=False):
        for name in names:
            copy = pltpu.make_async_copy(*far[name], r.load_sems.at[order.index(name)])
            copy.wait() if wait else copy.start()

    def layer(side, wait=False):
        first = len(order) + (2 if side == "enc" else 0)
        for place, name in enumerate(("up", "down")):
            copy = pltpu.make_async_copy(getattr(r, side + "_" + name), getattr(r, name), r.load_sems.at[first + place])
            copy.wait() if wait else copy.start()

    enc_act = lambda: pltpu.make_async_copy(r.far_act, r.act, r.load_sems.at[len(order) + 4])
    sems = r.sems
    down_x = Halving(r.down_sums.at[0], 0, "x", r.got_a, r.mid_a, sems, 0)
    up_y = Halving(r.up_sums.at[0], 1, "y", r.got_b, r.mid_b, sems, 1)
    down_y = Halving(r.mid_a, 0, "y", r.got_c, r.pair.at[0], sems, 2)
    up_x = Halving(r.mid_b, 0, "x", r.got_d, r.pair.at[1], sems, 3)
    both_z1 = Halving(r.pair, 1, "z1", r.got_e, r.mid_e, sems, 4)
    both_z2 = Halving(r.mid_e, 1, "z2", r.got_f, r.dec_sums, sems, 5)
    cross_x, cross_y = split_halvings(r.unit, r.got_g, r.cross_half, sems, 6)
    r.out_part = r.cross_out_sums.at[0]
    end = BackEnd(r, r.end_sems)
    cross_across = sending(r.grad_send, r.grad_other, sems, 16, "core")
    enc_across = sending(r.enc_send, r.enc_other, sems, 8, "core")
    dec_across = sending(r.dec_send, r.dec_other, sems, 9, "core")
    shared = [
        Across(r.down_sums, r.down_got, r.down_unit, sems, 10),
        Across(r.up_sums, r.up_got, r.up_unit, sems, 11),
        Across(r.enc_out_sums, r.enc_out_got, r.enc_out_unit, sems, 12),
        Across(r.dec_out_sums, r.dec_out_got, r.dec_out_unit, sems, 13),
    ]
    first_shared = [
        Across(r.down_sums, r.down_got, None, sems, 17),
        Across(r.up_sums, r.up_got, None, sems, 18),
        Across(r.cross_out_sums, r.cross_out_got, None, sems, 15),
    ]

    @pl.when(step == 0)
    def _():
        call_out(ways, True)
        load(NEAR_FIRST)
        layer("dec")
        load(NEAR_CROSS)
        load(NEAR_FIRST, wait=True)
        decode_last_layers(r, lambda: layer("dec", wait=True))
        layer("enc")
        load(NEAR_MIDDLE)
        hear(ways, True)
        cross_across.start()
        sum_down(r.down_sums, r.branch_low, r.act)
        first_shared[0].start()
        enc_act().start()
        sum_up(r.up_sums, r.inner_low, r.second_low)
        first_shared[1].start()
        first_shared[0].finish()
        down_x.start()
        sum_out(r.cross_out_sums, r.mixed_low, r.att_own, r.att_other)
        first_shared[2].start()
        load(NEAR_CROSS, wait=True)
        cross_across.wait()
        start_swap(r.decoded, r.decoded_there, sems, 14)
        back_begin(r, r)
        first_shared[1].finish()
        up_y.start()
        first_shared[2].finish()

    @pl.when((step >= 1) & (step < 5))
    def _():
        back_head(r, r, r.chances, step - 1, False)

    @pl.when(step == 4)
    def _():
        end.start(r)
        down_x.finish()
        up_y.finish()
        down_y.start()
        up_x.start()

    @pl.when(step == 5)
    def _():
        load(NEAR_MIDDLE, wait=True)
        layer("enc", wait=True)
        enc_act().wait()
        end.wait_sums()
        cross_y.start()
        cross_x.start()
        end.wait_grads()

        def events(place):
            if place == "encoder":
                enc_across.start()
                down_y.finish()
                up_x.finish()
                both_z1.start()
            elif place == "down":
                shared[0].start()
            elif place == "up":
                shared[1].start()
                shared[0].finish()
                shared[0].copy_out()
            elif place == "enc_out":
                shared[2].start()
                both_z1.finish()
                both_z2.start()
            elif place == "decoder":
                dec_across.start()
                shared[1].finish()
                shared[1].copy_out()
                shared[2].finish()
                shared[2].copy_out()
            else:
                shared[3].start()

        middle_layers(r, events)
        enc_across.wait()
        dec_across.wait()
        shared[3].finish()
        shared[3].copy_out()
        both_z2.finish()
        cross_y.finish()
        cross_x.finish()
        for one in shared:
            one.end()
        wait_swap(r.decoded, r.decoded_there, sems, 14)


NEAR_DECODE = ("queries", "keys", "values", "wide_out", "grad_own", "grad_other", "own_q", "other_q")


def last_back_body(r):
    step = pl.program_id(0)
    ways = ("core", "x", "y", "z1", "z2")
    names = (*NEAR_DECODE, "d_own", "d_other", "d_send", "sums_", "unit", "out_part")
    enc = types.SimpleNamespace(**{name: getattr(r, "enc_" + name) for name in names})
    dec = types.SimpleNamespace(**{name: getattr(r, "dec_" + name) for name in names})
    for one in (enc, dec):
        one.own_k, one.other_k, one.sums = one.own_q, one.other_q, one.sums_
    loads = [(getattr(r, "far_" + name), getattr(dec, name)) for name in NEAR_DECODE]
    loads += [(r.far_enc_pre, r.enc_pre), (r.far_dec_pre, r.dec_pre), (r.far_enc_w, r.enc_w), (r.far_dec_w, r.dec_w)]
    sems = r.sems

    def layer_steps(unit, bufs, total, slot):
        got, mid, less, least = bufs
        return (
            Halving(unit, 1, "y", got, mid, sems, slot, far=True),
            Halving(mid, 1, "z1", less.at[0], less.at[1], sems, slot + 1),
            Halving(less.at[1], 1, "z2", least.at[0], least.at[1], sems, slot + 2),
            Halving(least.at[1], 0, "x", r.layer_got.at[slot // 4], total, sems, slot + 3),
        )

    down = layer_steps(r.enc_down, r.down_bufs, r.enc_sums.at[0], 0)
    up = layer_steps(r.enc_up, r.up_bufs, r.enc_sums.at[1], 4)
    cross = join_halvings(r.cross_half, r.cross_less, r.cross_both, r.cross_last, r.cross_final, r.cross_sum, sems, 8)
    vector_ways = ("z1", "z2", "core", "x", "y")
    enc_att = (
        Halving(enc.unit, 0, "x", r.enc_got, r.enc_mid, sems, 17),
        Halving(r.enc_mid, 0, "y", r.enc_less.at[0], r.enc_less.at[1], sems, 18),
        Halving(r.enc_less.at[1], 0, "z1", r.enc_least.at[0], r.enc_least.at[1], sems, 19),
        Halving(r.enc_least.at[1], 0, "z2", r.enc_final, r.enc_att_sum, sems, 20),
    )
    dec_x, dec_y = split_halvings(dec.unit, r.dec_got, r.dec_mid, sems, 21)
    dec_att = join_halvings(r.dec_mid, r.dec_less, r.dec_both, r.dec_last, r.dec_final, r.dec_att_sum, sems, 23)

    def vector_parts(place):
        source = r.vectors if place == 0 else r.vector_mid.at[place - 1]
        total = r.vector_sum if place == len(ways) - 1 else r.vector_mid.at[place]
        copy = sending(source, r.vector_got.at[place], sems, 12 + place, vector_ways[place])
        return source, r.vector_got.at[place], total, copy

    def vector_start(place):
        vector_parts(place)[3].start()

    def vector_finish(place):
        source, got, total, copy = vector_parts(place)
        copy.wait()
        total[...] = source[...] + got[...]

    enc_end, dec_end = BackEnd(enc, r.enc_sems), BackEnd(dec, r.dec_sems)

    @pl.when(step == 0)
    def _():
        call_out(ways, True)
        start_loads(loads, r.load_sems)
        back_begin(enc, r)
        hear(ways, True)
        cross[0].start()
        cross[1].start()
        down[0].start()
        up[0].start()
        vector_start(0)

    @pl.when(step == 1)
    def _():
        vector_finish(0)
        vector_start(1)

    @pl.when(step == 2)
    def _():
        vector_finish(1)
        vector_start(2)
        cross[0].finish()
        cross[1].finish()
        cross[2].start()

    @pl.when(step == 3)
    def _():
        vector_finish(2)
        vector_start(3)
        cross[2].finish()
        cross[3].start()

    @pl.when(step < 4)
    def _():
        back_head(enc, r, r.enc_chances, step, False)

    @pl.when(step == 3)
    def _():
        enc_end.start(r)
        down[0].finish()
        down[1].start()

    @pl.when(step == 4)
    def _():
        wait_loads(loads, r.load_sems)
        enc_end.wait_sums()
        enc_att[0].start()
        vector_finish(3)
        vector_start(4)
        cross[3].finish()
        enc_end.wait_grads()
        input_kernel(r.enc_pre, enc.d_own, enc.d_other, r.enc_w, r.src_grad)
        start_swap(r.src_grad, r.src_there, sems, 27)
        back_begin(dec, r)

    @pl.when(step == 5)
    def _():
        down[1].finish()
        down[2].start()

    @pl.when(step == 7)
    def _():
        up[0].finish()
        up[1].start()

    @pl.when(step >= 4)
    def _():
        back_head(dec, r, r.dec_chances, step - 4, True)

    @pl.when(step == 7)
    def _():
        dec_end.start(r)
        down[2].finish()
        down[3].start()
        enc_att[0].finish()
        enc_att[1].start()
        dec_end.wait_sums()
        dec_x.start()
        dec_y.start()
        dec_end.wait_grads()
        input_kernel(r.dec_pre, dec.d_own, dec.d_other, r.dec_w, r.tgt_grad)
        start_swap(r.tgt_grad, r.tgt_there, sems, 28)
        up[1].finish()
        up[2].start()
        vector_finish(4)
        enc_att[1].finish()
        enc_att[2].start()
        dec_x.finish()
        dec_att[0].start()
        dec_y.finish()
        dec_att[1].start()
        down[3].finish()
        up[2].finish()
        up[3].start()
        enc_att[2].finish()
        enc_att[3].start()
        dec_att[0].finish()
        dec_att[1].finish()
        dec_att[2].start()
        enc_att[3].finish()
        up[3].finish()
        dec_att[2].finish()
        dec_att[3].start()
        dec_att[3].finish()
        wait_swap(r.src_grad, r.src_there, sems, 27)
        wait_swap(r.tgt_grad, r.tgt_there, sems, 28)


def finish_kernel(
    decoded, src_grad, tgt_grad, dec_sums, enc_sums, cross_sum, enc_att_sum, dec_att_sum, vectors,
    decoded_o, src_o, tgt_o, enc_qkv, enc_out, enc_up, enc_up_bias, enc_down, enc_down_bias, enc_gain, enc_shift,
    dec_qkv, dec_out, cross_qkv, cross_out, dec_up, dec_up_bias, dec_down, dec_down_bias, dec_gain, dec_shift,
):
    decoded_o[...] = decoded[...]
    src_o[...] = src_grad[...]
    tgt_o[...] = tgt_grad[...]
    for sums, down, up in ((dec_sums, dec_down, dec_up), (enc_sums, enc_down, enc_up)):
        for slot in range(4):
            down[:, slot * 256 : (slot + 1) * 256] = sums[0, slot * 32 : (slot + 1) * 32, :]
        up[...] = sums[1].T
    cross, dec_att = [jnp.concatenate([one[0], one[1]], axis=0) for one in (cross_sum, dec_att_sum)]
    for sums, out, qkv in ((cross, cross_out, cross_qkv), (enc_att_sum[...], enc_out, enc_qkv), (dec_att, dec_out, dec_qkv)):
        out[...] = sums[:32]
        for kind in range(3):
            qkv[kind] = sums[32 + kind * 32 : 64 + kind * 32]
    for part in range(4):
        dec_up_bias[:, part * 512 : (part + 1) * 512] = vectors[part : part + 1, :]
        enc_up_bias[:, part * 512 : (part + 1) * 512] = vectors[24 + part : 25 + part, :]
    dec_down_bias[...] = vectors[4:5, :]
    enc_down_bias[...] = vectors[28:29, :]
    for ref, places_of in (
        (dec_gain, (16, 5, 7)),
        (dec_shift, (17, 6, 8)),
        (enc_gain, (29, 31)),
        (enc_shift, (30, 32)),
    ):
        for index, place in enumerate(places_of):
            ref[index : index + 1, :] = vectors[place : place + 1, :]


def store_up(sums, value, index):
    core = my_core()
    z, y = index >> 1, index & 1
    low = value.astype(BF)
    for kept in range(2):
        for s in range(2):
            sums[core if kept == 0 else 1 - core, s, y, z & 1, (z >> 1) ^ kept, :, :] = low[
                kept * 128 : (kept + 1) * 128, s * 256 : (s + 1) * 256
            ]


def store_down(sums, value, index, column):
    core = my_core()
    low = value.astype(BF)
    for part in range(8):
        place = index * 8 + part
        z, y, kept = place >> 2, (place >> 1) & 1, place & 1
        for piece in range(2):
            s, slot = (column * 2 + piece) // 4, (column * 2 + piece) % 4
            sums[core if kept == 0 else 1 - core, s, y, z & 1, (z >> 1) ^ kept, slot * 32 : (slot + 1) * 32, :] = low[
                part * 32 : (part + 1) * 32, piece * 256 : (piece + 1) * 256
            ]


def store_out(sums, value, side):
    core = my_core()
    low = value.astype(BF)
    for place in range(16):
        z, y, kept = place >> 2, (place >> 1) & 1, place & 1
        sums[core if kept == 0 else 1 - core, side, y, z & 1, (z >> 1) ^ kept, :, :] = low[
            place * 32 : (place + 1) * 32, :
        ]


def projected(att_own, att_other, weight, here):
    core = my_core()
    width = att_own.shape[1]
    return dot(att_own[here, :], weight[block(core, width), :]) + dot(
        att_other[here, :], weight[block(1 - core, width), :]
    )


def projected_back(grad, weight, out_own, out_other, here):
    core = my_core()
    width = out_own.shape[1]
    out_own[here, :] = dot(grad, weight[block(core, width), :], 1, 1).astype(BF)
    out_other[here, :] = dot(grad, weight[block(1 - core, width), :], 1, 1).astype(BF)


def over_tiles(ref):
    def run(body):
        @pl.loop(0, ref.shape[0] // TILE)
        def _(tile):
            body(pl.ds(pl.multiple_of(tile * TILE, TILE), TILE))

    return run


def parts_of(up):
    return [slice(p * 512, (p + 1) * 512) for p in range(up.shape[1] // 512)]


def encode_kernel(
    x, att_own, att_other, out_w, up, up_bias, down, down_bias, gain, shift,
    memory, unit0, scale0, hidden_low, act, slope, unit1, scale1,
):
    @over_tiles(x)
    def _(here):
        pre = x[here, :].astype(F32) + projected(att_own, att_other, out_w, here)
        unit, scale = normed(pre)
        unit0[here, :] = unit
        scale0[here, :] = scale
        hidden = unit * gain[0:1, :] + shift[0:1, :]
        low = hidden.astype(BF)
        hidden_low[here, :] = low
        for part in parts_of(up):
            value, bend = gelu_and_slope(dot(low, up[:, part]) + up_bias[:, part])
            slope[here, part] = bend.astype(BF)
            act[here, part] = value.astype(BF)
        unit, scale = normed(hidden + dot(act[here, :], down[...]) + down_bias[...])
        unit1[here, :] = unit
        scale1[here, :] = scale
        memory[here, :] = (unit * gain[1:2, :] + shift[1:2, :]).astype(BF)


def decode_first_kernel(y, att_own, att_other, out_w, gain, shift, first, first_low, unit0, scale0):
    @over_tiles(y)
    def _(here):
        pre = y[here, :].astype(F32) + projected(att_own, att_other, out_w, here)
        unit, scale = normed(pre)
        unit0[here, :] = unit
        scale0[here, :] = scale
        value = unit * gain[0:1, :] + shift[0:1, :]
        first[here, :] = value
        first_low[here, :] = value.astype(BF)


def decode_last_layers(r, wait_layer):
    vectors = r.vectors
    vectors[...] = jnp.zeros_like(vectors)
    wait_layer()
    @over_tiles(r.first)
    def _(here):
        pre = r.first[here, :] + projected(r.att_own, r.att_other, r.cross_out, here)
        unit1, scale1 = normed(pre)
        second = unit1 * r.dec_gain[1:2, :] + r.dec_shift[1:2, :]
        low = second.astype(BF)
        r.second_low[here, :] = low
        for part in parts_of(r.up):
            value, slope = gelu_and_slope(dot(low, r.up[:, part]) + r.up_bias[:, part])
            r.act[here, part] = value.astype(BF)
            r.inner_low[here, part] = slope.astype(BF)
        unit2, scale2 = normed(second + dot(r.act[here, :], r.down[...]) + r.down_bias[...])
        r.decoded[here, :] = (unit2 * r.dec_gain[2:3, :] + r.dec_shift[2:3, :]).astype(BF)
        grad = r.upstream[here, :].astype(F32)
        vectors[7:8, :] += column_sum(grad * unit2)
        vectors[8:9, :] += column_sum(grad)
        grad = normed_back(grad, unit2, scale2, r.dec_gain[2:3, :])
        branch = grad.astype(BF)
        r.branch_low[here, :] = branch
        vectors[4:5, :] += column_sum(branch.astype(F32))
        for place, part in enumerate(parts_of(r.up)):
            inner = (dot(branch, r.down[part, :], 1, 1) * r.inner_low[here, part].astype(F32)).astype(BF)
            r.inner_low[here, part] = inner
            vectors[place : place + 1, :] += column_sum(inner.astype(F32))
        grad = grad + dot(r.inner_low[here, :], r.up[...], 1, 1)
        vectors[5:6, :] += column_sum(grad * unit1)
        vectors[6:7, :] += column_sum(grad)
        grad = normed_back(grad, unit1, scale1, r.dec_gain[1:2, :])
        r.grad_second[here, :] = grad
        mixed = grad.astype(BF)
        r.mixed_low[here, :] = mixed
        projected_back(mixed, r.cross_out, r.grad_own, r.grad_send, here)


def sum_down(down_sums, branch_low, act):
    for index in range(2):
        for column in range(act.shape[1] // 512):
            part = dot(
                branch_low[:, index * 256 : (index + 1) * 256],
                act[:, column * 512 : (column + 1) * 512],
                0,
                0,
            )
            store_down(down_sums, part, index, column)


def sum_up(up_sums, inner_low, entering):
    for index in range(inner_low.shape[1] // 256):
        store_up(up_sums, dot(inner_low[:, index * 256 : (index + 1) * 256], entering[...], 0, 0), index)


def sum_out(out_sums, mixed_low, att_own, att_other):
    core = my_core()
    store_out(out_sums, dot(mixed_low[...], att_own[...], 0, 0), core)
    store_out(out_sums, dot(mixed_low[...], att_other[...], 0, 0), 1 - core)


def input_kernel(grad_pre, d_own, d_other, weight, grad):
    core = my_core()
    width = d_own.shape[2]
    @over_tiles(grad_pre)
    def _(here):
        total = grad_pre[here, :]
        for kind in range(3):
            total = total + dot(d_own[kind, here, :], weight[kind, :, block(core, width)], 1, 1)
            total = total + dot(d_other[kind, here, :], weight[kind, :, block(1 - core, width)], 1, 1)
        grad[here, :] = total.astype(BF)


VMEM = pl.BlockSpec(memory_space=pltpu.VMEM)
ANY = pl.BlockSpec(memory_space=pl.ANY)


def call(
    kernel, name, micros, operands, outs, scratch=(), grid=None, in_specs=None, out_specs=None, meeting=None
):
    shapes = tuple(jax.ShapeDtypeStruct(shape, kind) for shape, kind in outs)
    extra = {} if grid is None else {"grid": grid}
    return pl.pallas_call(
        kernel,
        out_shape=shapes,
        in_specs=in_specs or [VMEM] * len(operands),
        out_specs=out_specs or tuple([VMEM] * len(outs)),
        scratch_shapes=list(scratch),
        compiler_params=pltpu.CompilerParams(
            vmem_limit_bytes=62 * 2**20, collective_id=meeting, has_side_effects=meeting is not None
        ),
        cost_estimate=pl.CostEstimate(
            flops=int(micros * 1e9), bytes_accessed=0, transcendentals=0
        ),
        name=name,
        **extra,
    )(*operands)


def whole(array):
    rank = len(array.shape)
    return pl.BlockSpec(array.shape, lambda step: (0,) * rank)


def attend(name, causal, same, sides, weight, masks):
    rows = sides[0].shape[0]
    width = weight.shape[2] // 2
    heads = width // HEAD_DIM
    length = 2 * rows
    wide = 2 * HEAD_DIM
    operands = (*sides, weight, *masks)
    outs = (
        ((rows, width), BF),
        ((rows, width), BF),
        ((length, width), F32),
        ((heads, length, wide), BF),
        ((heads, length, wide), BF),
        ((heads, length, wide), BF),
        ((heads, length, length), BF),
    )
    shapes = [jax.ShapeDtypeStruct(shape, kind) for shape, kind in outs]
    return call(
        functools.partial(attend_kernel, causal, same),
        name,
        10,
        operands,
        outs,
        scratch=[pltpu.VMEM((heads, length, HEAD_DIM), F32)],
        grid=(heads,),
        in_specs=[whole(one) for one in operands],
        out_specs=tuple(whole(one) for one in shapes[:-1])
        + (pl.BlockSpec((1, length, length), lambda step: (step, 0, 0)),),
    )


def launch(name, body, micros, grid, meeting, operands, outs, scratch):
    names = (*operands, *outs, *scratch)

    def once(array):
        rank = len(array.shape)
        return pl.BlockSpec(array.shape, lambda step: (0,) * rank, pipeline_mode=pl.Buffered(1))

    arrays, in_specs, shapes, out_specs = [], [], [], []
    for one in operands.values():
        array, spec = one if isinstance(one, tuple) else (one, None)
        arrays.append(array)
        in_specs.append(spec or once(array))
    for shape, kind, spec in outs.values():
        shapes.append((shape, kind))
        out_specs.append(spec or once(jax.ShapeDtypeStruct(shape, kind)))

    def kernel(*refs):
        body(types.SimpleNamespace(**dict(zip(names, refs))))

    results = call(
        kernel, name, micros, arrays, shapes, scratch=list(scratch.values()), grid=(grid,), in_specs=in_specs,
        out_specs=tuple(out_specs), meeting=meeting,
    )
    return types.SimpleNamespace(**dict(zip(outs, results)))


def pairs(count, move):
    found = []
    for index in range(count):
        z, y, core, s = index >> 3, (index >> 2) & 1, (index >> 1) & 1, index & 1
        z, y, core, s = move(z, y, core, s)
        found.append((index, (((z * 2 + y) * 2 + core) * 2) + s))
    return found


def fast_shards(count, source, target, source_ids, target_ids, out_grad, *params):
    (
        enc_qkv, enc_out, enc_up, enc_up_bias, enc_down, enc_down_bias, enc_gain, enc_shift, dec_qkv, dec_out,
        cross_qkv, cross_out, dec_up, dec_up_bias, dec_down, dec_down_bias, dec_gain, dec_shift,
    ) = params
    moves = {
        "swap": pairs(count, lambda z, y, c, s: (z, y, s, c)),
        "core": pairs(count, lambda z, y, c, s: (z, y, 1 - c, s)),
        "x": pairs(count, lambda z, y, c, s: (z, y, c, 1 - s)),
        "y": pairs(count, lambda z, y, c, s: (z, 1 - y, c, s)),
        "z1": pairs(count, lambda z, y, c, s: (z ^ 1, y, c, s)),
        "z2": pairs(count, lambda z, y, c, s: (z ^ 2, y, c, s)),
    }
    row = lax.axis_index("batch")
    core = row % 2
    place = {"x": lax.axis_index("seq"), "y": (row // 2) % 2, "z1": (row // 4) % 2, "z2": (row // 8) ^ core}

    def move(value, way):
        return lax.ppermute(value, BOTH, moves[way])

    ids = move(jnp.stack([source_ids[0], target_ids[0]]), "swap")
    src = move(source[0], "swap")
    tgt = move(target[0], "swap")
    upstream = move(out_grad[0], "swap")
    ids_other = move(ids, "core")
    src_other = move(src, "core")
    tgt_other = move(tgt, "core")
    lane = jnp.arange(HEAD_DIM, dtype=jnp.int32)[None, :]

    def masks(which):
        marks = [side[which][:, None] == lane for side in (ids, ids_other)]
        asks = [mark.astype(BF) for mark in marks]
        bars = [jnp.where(~mark & (lane < 3), NEGATIVE, 0.0).astype(BF) for mark in marks]
        return asks, bars

    src_ask, src_bar = masks(0)
    tgt_ask, tgt_bar = masks(1)
    rows, wide = src.shape
    inner = enc_up.shape[1]
    width = wide // 2
    full, thin = ((rows, wide), F32), ((rows, 1), F32)
    low_full, low_half = ((rows, wide), BF), ((rows, width), BF)
    low_inner = ((rows, inner), BF)
    biases = [one[None, :] for one in (enc_up_bias, enc_down_bias, dec_up_bias, dec_down_bias)]
    enc_up_b, enc_down_b, dec_up_b, dec_down_b = biases

    def scratch(shape):
        return pltpu.VMEM(*shape)

    att, att_send, *enc_saved = attend(
        "enc_attend", False, True, (src, src_other), enc_qkv, (*src_ask, *src_bar)
    )
    enc_att = (att, move(att_send, "core"))
    att, att_send, *dec_saved = attend(
        "dec_attend", True, True, (tgt, tgt_other), dec_qkv, (*tgt_ask, *tgt_bar)
    )
    dec_att = (att, move(att_send, "core"))
    memory, *enc_kept = call(
        encode_kernel,
        "encode",
        8,
        (src, *enc_att, enc_out, enc_up, enc_up_b, enc_down, enc_down_b, enc_gain, enc_shift),
        (low_full, full, thin, low_full, low_inner, low_inner, full, thin),
    )
    first, first_low, first_unit, first_scale = call(
        decode_first_kernel,
        "decode_first",
        2,
        (tgt, *dec_att, dec_out, dec_gain, dec_shift),
        (full, low_full, full, thin),
    )
    first_sides = (first_low, move(first_low, "core"))
    memory_sides = (memory, move(memory, "core"))
    cross_sides = (*first_sides, *memory_sides)
    att, att_send, *cross_saved = attend(
        "cross_attend", False, False, cross_sides, cross_qkv, (*tgt_ask, *src_bar)
    )
    cross_att = (att, move(att_send, "core"))
    sem = pltpu.SemaphoreType.DMA
    big, out_unit = (BIG, BF), ((2, 2, 2, 2, 32, 256), BF)
    big_pair, out_pair = scratch(((2, *BIG), BF)), scratch(((2, 2, 2, 2, 2, 32, 256), BF))
    big_got, out_got = scratch(big), scratch(out_unit)
    def shaped(array):
        return pltpu.VMEM(array.shape, array.dtype)

    heads, length = cross_saved[1].shape[:2]
    head_block = (1, length, length)
    work = {
        "grads": scratch(((heads, length, 2 * HEAD_DIM), BF)),
        "score_grads": scratch(((length, length), BF)),
        "dq": scratch(((heads, length, HEAD_DIM), BF)),
        "dk": scratch(((width, length), F32)),
        "dv": scratch(((width, length), F32)),
    }
    thirds, shares = ((3, rows, width), BF), ((2, 2, 2, 2, 96, 256), BF)
    sum_bufs = {
        "got_a": scratch((MID, BF)), "mid_a": scratch((MID, BF)), "got_b": scratch((MID, BF)),
        "mid_b": scratch((MID, BF)), "got_c": scratch((LESS, BF)), "got_d": scratch((LESS, BF)),
        "pair": scratch(((2, *LESS), BF)), "got_e": scratch(((2, *LEAST), BF)), "mid_e": scratch(((2, *LEAST), BF)),
        "got_f": scratch(((2, 128, 256), BF)),
    }
    unit0, scale0, hidden_low, act, slope, unit1, scale1 = enc_kept
    wide_out, queries, keys, values, chances = cross_saved
    near = {
        **dict(zip(NEAR_FIRST, (first, *cross_att, cross_out, upstream))),
        **dict(zip(NEAR_CROSS, (queries, keys, values, wide_out, *cross_sides))),
        **dict(zip(NEAR_MIDDLE, (
            cross_qkv, enc_out, dec_out, unit0, scale0, hidden_low, slope, unit1, scale1, *enc_att, first_unit,
            first_scale, *dec_att,
        ))),
    }
    found = launch(
        "decode_middle",
        decode_middle_body,
        60,
        6,
        0,
        {
            "chances": (chances, pl.BlockSpec(head_block, lambda step: (jnp.clip(step - 1, 0, 3), 0, 0))),
            "dec_gain": dec_gain, "dec_shift": dec_shift, "enc_gain": enc_gain,
            "up_bias": dec_up_b, "down_bias": dec_down_b,
            "dec_up": (dec_up, ANY), "dec_down": (dec_down, ANY), "enc_up": (enc_up, ANY), "enc_down": (enc_down, ANY),
            "far_act": (act, ANY),
            **{"far_" + name: (array, ANY) for name, array in near.items()},
        },
        {
            "enc_pre": (*full, None), "enc_own": (*low_half, None), "enc_other": (*low_half, ANY),
            "dec_pre": (*full, None), "dec_own": (*low_half, None), "dec_other": (*low_half, ANY),
            "down_unit": (*big, ANY), "up_unit": (*big, ANY), "enc_out_unit": (*out_unit, ANY),
            "dec_out_unit": (*out_unit, ANY), "vectors": ((40, wide), F32, None),
            "dec_sums": ((2, 128, 256), F32, None), "cross_half": ((2, 2, 2, 2, 64, 256), BF, None),
            "decoded_there": (*low_full, ANY),
        },
        {
            **work, **sum_bufs, **{name: shaped(array) for name, array in near.items()},
            "sems": sem((3, 19)), "end_sems": sem((3, 2)), "load_sems": sem((len(near) + 5,)),
            "up": shaped(enc_up), "down": shaped(enc_down), "act": shaped(act),
            "d_own": scratch(thirds), "d_other": scratch(thirds), "d_send": scratch(thirds), "sums": scratch(shares),
            "unit": scratch(big), "got_g": scratch(((2, 2, 2, 2, 64, 256), BF)),
            "grad_own": scratch(low_half), "grad_other": scratch(low_half), "grad_send": scratch(low_half),
            "enc_send": scratch(low_half), "dec_send": scratch(low_half), "decoded": scratch(low_full),
            "second_low": scratch(low_full), "grad_second": scratch(full),
            "inner_low": scratch(low_inner), "branch_low": scratch(low_full), "mixed_low": scratch(low_full),
            "down_sums": big_pair, "up_sums": big_pair, "enc_out_sums": out_pair, "dec_out_sums": out_pair,
            "cross_out_sums": out_pair, "cross_out_got": out_got,
            "down_got": big_got, "up_got": big_got, "enc_out_got": out_got, "dec_out_got": out_got,
        },
    )
    encs, decs = [
        dict(zip(NEAR_DECODE, (*saved[1:4], saved[0], *grads, *sides)))
        for saved, grads, sides in (
            (enc_saved, (found.enc_own, found.enc_other), (src, src_other)),
            (dec_saved, (found.dec_own, found.dec_other), (tgt, tgt_other)),
        )
    ]
    layer_bufs = [scratch((MID, BF)), scratch((MID, BF)), scratch(((2, *LESS), BF)), scratch(((2, *LEAST), BF))]
    pair_64, less_64, both_64 = (((2, 64, 256), BF), ((2, 2, 2, 64, 256), BF), ((2, 2, 2, 64, 256), BF))
    last = launch(
        "last_back",
        last_back_body,
        60,
        8,
        1,
        {
            **{"enc_" + name: array for name, array in encs.items()},
            "enc_chances": (enc_saved[4], pl.BlockSpec(head_block, lambda step: (jnp.minimum(step, 3), 0, 0))),
            "dec_chances": (dec_saved[4], pl.BlockSpec(head_block, lambda step: (jnp.maximum(step - 4, 0), 0, 0))),
            **{"far_" + name: (array, ANY) for name, array in decs.items()},
            "far_enc_pre": (found.enc_pre, ANY), "far_dec_pre": (found.dec_pre, ANY),
            "far_enc_w": (enc_qkv, ANY), "far_dec_w": (dec_qkv, ANY),
            "enc_out_part": (found.enc_out_unit, ANY), "dec_out_part": (found.dec_out_unit, ANY),
            "enc_down": (found.down_unit, ANY), "enc_up": (found.up_unit, ANY), "cross_half": found.cross_half,
            "vectors": found.vectors,
        },
        {
            "enc_sums": ((2, 128, 256), F32, None), "cross_sum": ((2, 64, 256), F32, None),
            "enc_att_sum": ((128, 256), F32, None), "dec_att_sum": ((2, 64, 256), F32, None),
            "vector_sum": ((40, wide), F32, None), "src_there": (*low_full, ANY), "tgt_there": (*low_full, ANY),
        },
        {
            **work, **{"dec_" + name: shaped(array) for name, array in decs.items()},
            "sems": sem((3, 29)), "enc_sems": sem((3, 2)), "dec_sems": sem((3, 2)), "load_sems": sem((12,)),
            "down_bufs": layer_bufs, "up_bufs": layer_bufs, "layer_got": scratch(((2, 128, 256), BF)),
            "cross_less": scratch(less_64), "cross_both": scratch(both_64), "cross_last": scratch(both_64),
            "cross_final": scratch(pair_64),
            "enc_got": scratch((MID, BF)), "enc_mid": scratch((MID, BF)), "enc_less": scratch(((2, *LESS), BF)),
            "enc_least": scratch(((2, *LEAST), BF)), "enc_final": scratch(((128, 256), BF)),
            "dec_got": scratch(((2, 2, 2, 2, 64, 256), BF)), "dec_mid": scratch(((2, 2, 2, 2, 64, 256), BF)),
            "dec_less": scratch(less_64), "dec_both": scratch(both_64), "dec_last": scratch(both_64),
            "dec_final": scratch(pair_64),
            "vector_got": scratch(((5, 40, wide), F32)), "vector_mid": scratch(((4, 40, wide), F32)),
            "enc_pre": scratch(full), "dec_pre": scratch(full), "enc_w": shaped(enc_qkv), "dec_w": shaped(dec_qkv),
            "src_grad": scratch(low_full), "tgt_grad": scratch(low_full),
            **{side + name: scratch(thirds) for side in ("enc_", "dec_") for name in ("d_own", "d_other", "d_send")},
            "enc_sums_": scratch(shares), "dec_sums_": scratch(shares), "enc_unit": scratch(big), "dec_unit": scratch(big),
        },
    )
    cut3, cut, pair, triple = ((3, 32, 256), F32), ((32, 256), F32), ((2, wide), F32), ((3, wide), F32)
    up_cut, down_cut, up_b, down_b = ((256, 128), F32), ((32, 1024), F32), ((1, inner), F32), ((1, wide), F32)
    outs = call(
        finish_kernel,
        "finish",
        2,
        (
            found.decoded_there, last.src_there, last.tgt_there, found.dec_sums, last.enc_sums, last.cross_sum,
            last.enc_att_sum, last.dec_att_sum, last.vector_sum,
        ),
        (
            low_full, low_full, low_full, cut3, cut, up_cut, up_b, down_cut, down_b, pair, pair,
            cut3, cut, cut3, cut, up_cut, up_b, down_cut, down_b, triple, triple,
        ),
    )
    return tuple(
        one[None]
        if place < 3
        else one[0]
        if place in (6, 8, 16, 18)
        else jnp.swapaxes(one, -1, -2)
        if place in (3, 4, 7, 11, 12, 13, 14, 17)
        else one
        for place, one in enumerate(outs)
    )


def solution(mesh):
    if mesh.shape["seq"] != 2 or mesh.shape["batch"] != 16:
        return general(mesh)
    tokens = P("batch", "seq", None)
    ids = P("batch", "seq")
    cut, cut3 = P("seq", "batch"), P(None, "seq", "batch")
    return jax.shard_map(
        functools.partial(fast_shards, mesh.size),
        mesh=mesh,
        in_specs=(tokens, tokens, ids, ids, tokens) + (P(),) * 18,
        out_specs=(
            tokens, tokens, tokens, cut3, cut, cut, P(), cut, P(), P(), P(), cut3, cut, cut3, cut, cut, P(), cut,
            P(), P(), P(),
        ),
        check_vma=False,
    )
```

```python
import types

import jax
import jax.numpy as jnp
from jax import lax
from jax.experimental import pallas as pl
from jax.experimental.pallas import tpu as pltpu
from jax.sharding import PartitionSpec as P

HEAD_DIM = 64
NEGATIVE = -1e30
BF = jnp.bfloat16
F32 = jnp.float32


def layer_norm(value, gain, shift):
    mean = jnp.mean(value, axis=-1, keepdims=True)
    centred = value - mean
    spread = jnp.mean(centred * centred, axis=-1, keepdims=True)
    return centred * lax.rsqrt(spread + 1e-06) * gain + shift


def norm_back(value, gain, shift, grad):
    _, pull = jax.vjp(layer_norm, value, gain, shift)
    return pull(grad)


def gelu_back(inner, grad):
    _, pull = jax.vjp(jax.nn.gelu, inner)
    return pull(grad)[0]


def matmul(left, right):
    return jnp.dot(left, right, preferred_element_type=jnp.float32)


def weight_grad(inputs, grad):
    return lax.dot_general(
        inputs, grad, (((0,), (0,)), ((), ())), preferred_element_type=jnp.float32
    )


def input_grad(grad, weight):
    return lax.dot_general(
        grad, weight, (((1,), (1,)), ((), ())), preferred_element_type=jnp.float32
    )


def to_low(value):
    return value.astype(jnp.bfloat16)


def split_heads(value):
    return value.reshape(value.shape[0], -1, HEAD_DIM)


def block_live(query_ids, key_ids, offset, block, rows, causal):
    first_key = lax.dynamic_index_in_dim(key_ids, block * rows, 0, keepdims=False)
    last_key = lax.dynamic_index_in_dim(key_ids, block * rows + rows - 1, 0, keepdims=False)
    live = (first_key <= query_ids[rows - 1]) & (query_ids[0] <= last_key)
    if causal:
        live = live & (block * rows <= offset + rows - 1)
    return live


def block_scores(queries, keys_all, query_ids, key_ids, offset, block, causal):
    rows = queries.shape[0]
    key_block = lax.dynamic_slice_in_dim(keys_all, block * rows, rows, 0)
    id_block = lax.dynamic_slice_in_dim(key_ids, block * rows, rows, 0)
    scores = (
        jnp.einsum("qhe,khe->hqk", queries, key_block, preferred_element_type=jnp.float32) * 0.125
    )
    allowed = query_ids[:, None] == id_block[None, :]
    if causal:
        positions = jnp.arange(rows, dtype=jnp.int32)
        allowed = allowed & ((offset + positions)[:, None] >= (block * rows + positions)[None, :])
    allowed = allowed[None]
    return (jnp.where(allowed, scores, NEGATIVE), allowed, key_block)


def attend_forward(queries, keys_all, values_all, query_ids, key_ids, offset, causal):
    rows = queries.shape[0]
    heads_count = queries.shape[1]
    count = keys_all.shape[0] // rows

    def first_pass(block, carry):

        def first_compute(state):
            largest, total = state
            scores, allowed, _ = block_scores(
                queries, keys_all, query_ids, key_ids, offset, block, causal
            )
            newest = jnp.maximum(largest, jnp.max(scores, axis=-1))
            terms = jnp.where(allowed, jnp.exp(scores - newest[..., None]), 0.0)
            return (newest, total * jnp.exp(largest - newest) + jnp.sum(terms, axis=-1))

        live = block_live(query_ids, key_ids, offset, block, rows, causal)
        return lax.cond(live, first_compute, lambda state: state, carry)

    initial = (
        jnp.full((heads_count, rows), NEGATIVE, jnp.float32),
        jnp.zeros((heads_count, rows), jnp.float32),
    )
    largest, total = lax.fori_loop(0, count, first_pass, initial)
    log_total = largest + jnp.log(total)

    def second_pass(block, carry):

        def second_compute(output):
            scores, allowed, _ = block_scores(
                queries, keys_all, query_ids, key_ids, offset, block, causal
            )
            value_block = lax.dynamic_slice_in_dim(values_all, block * rows, rows, 0)
            chances = jnp.where(allowed, jnp.exp(scores - log_total[..., None]), 0.0)
            return output + jnp.einsum(
                "hqk,khe->qhe", to_low(chances), value_block, preferred_element_type=jnp.float32
            )

        live = block_live(query_ids, key_ids, offset, block, rows, causal)
        return lax.cond(live, second_compute, lambda output: output, carry)

    output = lax.fori_loop(0, count, second_pass, jnp.zeros(queries.shape, jnp.float32))
    return (output, log_total)


def attend_backward(
    queries, keys_all, values_all, query_ids, key_ids, offset, causal, grad_out, settle, log_total
):
    rows = queries.shape[0]
    count = keys_all.shape[0] // rows

    def step_block(block, carry):

        def step_compute(state):
            query_grad, key_grads, value_grads = state
            scores, allowed, key_block = block_scores(
                queries, keys_all, query_ids, key_ids, offset, block, causal
            )
            value_block = lax.dynamic_slice_in_dim(values_all, block * rows, rows, 0)
            chances = jnp.where(allowed, jnp.exp(scores - log_total[..., None]), 0.0)
            chance_grad = jnp.einsum(
                "qhe,khe->hqk", grad_out, value_block, preferred_element_type=jnp.float32
            )
            score_grad = to_low(chances * (chance_grad - settle[..., None]))
            query_grad = (
                query_grad
                + jnp.einsum(
                    "hqk,khe->qhe", score_grad, key_block, preferred_element_type=jnp.float32
                )
                * 0.125
            )
            key_part = (
                jnp.einsum("hqk,qhe->khe", score_grad, queries, preferred_element_type=jnp.float32)
                * 0.125
            )
            value_part = jnp.einsum(
                "hqk,qhe->khe", to_low(chances), grad_out, preferred_element_type=jnp.float32
            )
            key_grads = lax.dynamic_update_slice_in_dim(key_grads, key_part, block * rows, 0)
            value_grads = lax.dynamic_update_slice_in_dim(value_grads, value_part, block * rows, 0)
            return (query_grad, key_grads, value_grads)

        live = block_live(query_ids, key_ids, offset, block, rows, causal)
        return lax.cond(live, step_compute, lambda state: state, carry)

    initial = (
        jnp.zeros(queries.shape, jnp.float32),
        jnp.zeros(keys_all.shape, jnp.float32),
        jnp.zeros(values_all.shape, jnp.float32),
    )
    return lax.fori_loop(0, count, step_block, initial)


def attention_back(
    queries, keys_all, values_all, query_ids, key_ids_all, causal, grad_out, output, log_total
):
    rows = queries.shape[0]
    offset = lax.axis_index("seq") * rows
    settle = jnp.einsum("qhe,qhe->hq", grad_out.astype(jnp.float32), output)
    query_grad, key_terms, value_terms = attend_backward(
        queries,
        keys_all,
        values_all,
        query_ids,
        key_ids_all,
        offset,
        causal,
        grad_out,
        settle,
        log_total,
    )
    key_sum, value_sum = (
        lax.psum_scatter(
            key_terms.reshape(key_terms.shape[0], -1).astype(jnp.bfloat16),
            "seq",
            scatter_dimension=0,
            tiled=True,
        ).astype(jnp.float32),
        lax.psum_scatter(
            value_terms.reshape(value_terms.shape[0], -1).astype(jnp.bfloat16),
            "seq",
            scatter_dimension=0,
            tiled=True,
        ).astype(jnp.float32),
    )
    return (query_grad, key_sum, value_sum)


def general_shards(
    source,
    target,
    source_ids,
    target_ids,
    out_grad,
    enc_qkv,
    enc_out,
    enc_up,
    enc_up_bias,
    enc_down,
    enc_down_bias,
    enc_gain,
    enc_shift,
    dec_qkv,
    dec_out,
    cross_qkv,
    cross_out,
    dec_up,
    dec_up_bias,
    dec_down,
    dec_down_bias,
    dec_gain,
    dec_shift,
):
    src_rows = source[0]
    tgt_rows = target[0]
    src_ids = source_ids[0]
    tgt_ids = target_ids[0]
    rows = src_rows.shape[0]
    offset = lax.axis_index("seq") * rows
    enc_queries = to_low(matmul(src_rows, enc_qkv[0]))
    enc_keys = to_low(matmul(src_rows, enc_qkv[1]))
    enc_values = to_low(matmul(src_rows, enc_qkv[2]))
    enc_keys_all, enc_values_all, src_ids_all = (
        lax.all_gather(enc_keys, "seq", axis=0, tiled=True),
        lax.all_gather(enc_values, "seq", axis=0, tiled=True),
        lax.all_gather(src_ids, "seq", axis=0, tiled=True),
    )
    enc_att, enc_lse = attend_forward(
        split_heads(enc_queries),
        split_heads(enc_keys_all),
        split_heads(enc_values_all),
        src_ids,
        src_ids_all,
        offset,
        False,
    )
    enc_att_low = to_low(enc_att.reshape(rows, -1))
    enc_pre = src_rows.astype(jnp.float32) + matmul(enc_att_low, enc_out)
    hidden = layer_norm(enc_pre, enc_gain[0], enc_shift[0])
    hidden_low = to_low(hidden)
    enc_inner = matmul(hidden_low, enc_up) + enc_up_bias
    enc_act = to_low(jax.nn.gelu(enc_inner))
    enc_last = hidden + matmul(enc_act, enc_down) + enc_down_bias
    memory = layer_norm(enc_last, enc_gain[1], enc_shift[1])
    memory_low = to_low(memory)
    mem_keys = to_low(matmul(memory_low, cross_qkv[1]))
    mem_values = to_low(matmul(memory_low, cross_qkv[2]))
    mem_keys_all, mem_values_all = (
        lax.all_gather(mem_keys, "seq", axis=0, tiled=True),
        lax.all_gather(mem_values, "seq", axis=0, tiled=True),
    )
    dec_queries = to_low(matmul(tgt_rows, dec_qkv[0]))
    dec_keys = to_low(matmul(tgt_rows, dec_qkv[1]))
    dec_values = to_low(matmul(tgt_rows, dec_qkv[2]))
    dec_keys_all, dec_values_all, tgt_ids_all = (
        lax.all_gather(dec_keys, "seq", axis=0, tiled=True),
        lax.all_gather(dec_values, "seq", axis=0, tiled=True),
        lax.all_gather(tgt_ids, "seq", axis=0, tiled=True),
    )
    dec_att, dec_lse = attend_forward(
        split_heads(dec_queries),
        split_heads(dec_keys_all),
        split_heads(dec_values_all),
        tgt_ids,
        tgt_ids_all,
        offset,
        True,
    )
    dec_att_low = to_low(dec_att.reshape(rows, -1))
    dec_pre = tgt_rows.astype(jnp.float32) + matmul(dec_att_low, dec_out)
    first = layer_norm(dec_pre, dec_gain[0], dec_shift[0])
    first_low = to_low(first)
    cross_queries = to_low(matmul(first_low, cross_qkv[0]))
    cross_att, cross_lse = attend_forward(
        split_heads(cross_queries),
        split_heads(mem_keys_all),
        split_heads(mem_values_all),
        tgt_ids,
        src_ids_all,
        offset,
        False,
    )
    cross_att_low = to_low(cross_att.reshape(rows, -1))
    cross_pre = first + matmul(cross_att_low, cross_out)
    second = layer_norm(cross_pre, dec_gain[1], dec_shift[1])
    second_low = to_low(second)
    dec_inner = matmul(second_low, dec_up) + dec_up_bias
    dec_act = to_low(jax.nn.gelu(dec_inner))
    dec_last = second + matmul(dec_act, dec_down) + dec_down_bias
    decoded = layer_norm(dec_last, dec_gain[2], dec_shift[2])
    upstream = out_grad[0].astype(jnp.float32)
    grad_last, gain_two, shift_two = norm_back(dec_last, dec_gain[2], dec_shift[2], upstream)
    branch_low = to_low(grad_last)
    dec_down_g = weight_grad(dec_act, branch_low)
    dec_down_bias_g = jnp.sum(branch_low.astype(jnp.float32), axis=0)
    inner_low = to_low(gelu_back(dec_inner, input_grad(branch_low, dec_down)))
    dec_up_g = weight_grad(second_low, inner_low)
    dec_up_bias_g = jnp.sum(inner_low.astype(jnp.float32), axis=0)
    grad_second = grad_last + input_grad(inner_low, dec_up)
    grad_cross_pre, gain_one, shift_one = norm_back(
        cross_pre, dec_gain[1], dec_shift[1], grad_second
    )
    mixed_low = to_low(grad_cross_pre)
    cross_out_g = weight_grad(cross_att_low, mixed_low)
    cross_att_grad = to_low(input_grad(mixed_low, cross_out))
    cross_query_grad, mem_key_sum, mem_value_sum = attention_back(
        split_heads(cross_queries),
        split_heads(mem_keys_all),
        split_heads(mem_values_all),
        tgt_ids,
        src_ids_all,
        False,
        split_heads(cross_att_grad),
        cross_att,
        cross_lse,
    )
    mem_key_low = to_low(mem_key_sum)
    mem_value_low = to_low(mem_value_sum)
    cross_query_low = to_low(cross_query_grad.reshape(rows, -1))
    cross_qkv_g = jnp.stack(
        [
            weight_grad(first_low, cross_query_low),
            weight_grad(memory_low, mem_key_low),
            weight_grad(memory_low, mem_value_low),
        ]
    )
    grad_first = grad_cross_pre + input_grad(cross_query_low, cross_qkv[0])
    grad_dec_pre, gain_zero, shift_zero = norm_back(dec_pre, dec_gain[0], dec_shift[0], grad_first)
    self_low = to_low(grad_dec_pre)
    dec_out_g = weight_grad(dec_att_low, self_low)
    dec_att_grad = to_low(input_grad(self_low, dec_out))
    dec_query_grad, dec_key_sum, dec_value_sum = attention_back(
        split_heads(dec_queries),
        split_heads(dec_keys_all),
        split_heads(dec_values_all),
        tgt_ids,
        tgt_ids_all,
        True,
        split_heads(dec_att_grad),
        dec_att,
        dec_lse,
    )
    dec_query_low = to_low(dec_query_grad.reshape(rows, -1))
    dec_key_low = to_low(dec_key_sum)
    dec_value_low = to_low(dec_value_sum)
    dec_qkv_g = jnp.stack(
        [
            weight_grad(tgt_rows, dec_query_low),
            weight_grad(tgt_rows, dec_key_low),
            weight_grad(tgt_rows, dec_value_low),
        ]
    )
    tgt_grad = (
        grad_dec_pre
        + input_grad(dec_query_low, dec_qkv[0])
        + input_grad(dec_key_low, dec_qkv[1])
        + input_grad(dec_value_low, dec_qkv[2])
    )
    dec_gain_g = jnp.stack([gain_zero, gain_one, gain_two])
    dec_shift_g = jnp.stack([shift_zero, shift_one, shift_two])
    grad_memory = input_grad(mem_key_low, cross_qkv[1]) + input_grad(mem_value_low, cross_qkv[2])
    grad_enc_last, enc_gain_one, enc_shift_one = norm_back(
        enc_last, enc_gain[1], enc_shift[1], grad_memory
    )
    enc_branch_low = to_low(grad_enc_last)
    enc_down_g = weight_grad(enc_act, enc_branch_low)
    enc_down_bias_g = jnp.sum(enc_branch_low.astype(jnp.float32), axis=0)
    enc_inner_low = to_low(gelu_back(enc_inner, input_grad(enc_branch_low, enc_down)))
    enc_up_g = weight_grad(hidden_low, enc_inner_low)
    enc_up_bias_g = jnp.sum(enc_inner_low.astype(jnp.float32), axis=0)
    grad_hidden = grad_enc_last + input_grad(enc_inner_low, enc_up)
    grad_enc_pre, enc_gain_zero, enc_shift_zero = norm_back(
        enc_pre, enc_gain[0], enc_shift[0], grad_hidden
    )
    enc_mixed_low = to_low(grad_enc_pre)
    enc_out_g = weight_grad(enc_att_low, enc_mixed_low)
    enc_att_grad = to_low(input_grad(enc_mixed_low, enc_out))
    enc_query_grad, enc_key_sum, enc_value_sum = attention_back(
        split_heads(enc_queries),
        split_heads(enc_keys_all),
        split_heads(enc_values_all),
        src_ids,
        src_ids_all,
        False,
        split_heads(enc_att_grad),
        enc_att,
        enc_lse,
    )
    enc_query_low = to_low(enc_query_grad.reshape(rows, -1))
    enc_key_low = to_low(enc_key_sum)
    enc_value_low = to_low(enc_value_sum)
    enc_qkv_g = jnp.stack(
        [
            weight_grad(src_rows, enc_query_low),
            weight_grad(src_rows, enc_key_low),
            weight_grad(src_rows, enc_value_low),
        ]
    )
    src_grad = (
        grad_enc_pre
        + input_grad(enc_query_low, enc_qkv[0])
        + input_grad(enc_key_low, enc_qkv[1])
        + input_grad(enc_value_low, enc_qkv[2])
    )
    enc_gain_g = jnp.stack([enc_gain_zero, enc_gain_one])
    enc_shift_g = jnp.stack([enc_shift_zero, enc_shift_one])
    all_rows = (
        lax.psum_scatter(
            enc_qkv_g.astype(jnp.bfloat16), "seq", scatter_dimension=1, tiled=True
        ).astype(jnp.float32),
        lax.psum_scatter(
            enc_out_g.astype(jnp.bfloat16), "seq", scatter_dimension=0, tiled=True
        ).astype(jnp.float32),
        lax.psum_scatter(
            enc_up_g.astype(jnp.bfloat16), "seq", scatter_dimension=0, tiled=True
        ).astype(jnp.float32),
        lax.psum_scatter(
            enc_down_g.astype(jnp.bfloat16), "seq", scatter_dimension=0, tiled=True
        ).astype(jnp.float32),
        lax.psum_scatter(
            dec_qkv_g.astype(jnp.bfloat16), "seq", scatter_dimension=1, tiled=True
        ).astype(jnp.float32),
        lax.psum_scatter(
            dec_out_g.astype(jnp.bfloat16), "seq", scatter_dimension=0, tiled=True
        ).astype(jnp.float32),
        lax.psum_scatter(
            cross_qkv_g.astype(jnp.bfloat16), "seq", scatter_dimension=1, tiled=True
        ).astype(jnp.float32),
        lax.psum_scatter(
            cross_out_g.astype(jnp.bfloat16), "seq", scatter_dimension=0, tiled=True
        ).astype(jnp.float32),
        lax.psum_scatter(
            dec_up_g.astype(jnp.bfloat16), "seq", scatter_dimension=0, tiled=True
        ).astype(jnp.float32),
        lax.psum_scatter(
            dec_down_g.astype(jnp.bfloat16), "seq", scatter_dimension=0, tiled=True
        ).astype(jnp.float32),
    )
    reduced = (
        lax.psum_scatter(
            all_rows[0].astype(jnp.bfloat16), "batch", scatter_dimension=2, tiled=True
        ).astype(jnp.float32),
        lax.psum_scatter(
            all_rows[1].astype(jnp.bfloat16), "batch", scatter_dimension=1, tiled=True
        ).astype(jnp.float32),
        lax.psum_scatter(
            all_rows[2].astype(jnp.bfloat16), "batch", scatter_dimension=1, tiled=True
        ).astype(jnp.float32),
        lax.psum_scatter(
            all_rows[3].astype(jnp.bfloat16), "batch", scatter_dimension=1, tiled=True
        ).astype(jnp.float32),
        lax.psum_scatter(
            all_rows[4].astype(jnp.bfloat16), "batch", scatter_dimension=2, tiled=True
        ).astype(jnp.float32),
        lax.psum_scatter(
            all_rows[5].astype(jnp.bfloat16), "batch", scatter_dimension=1, tiled=True
        ).astype(jnp.float32),
        lax.psum_scatter(
            all_rows[6].astype(jnp.bfloat16), "batch", scatter_dimension=2, tiled=True
        ).astype(jnp.float32),
        lax.psum_scatter(
            all_rows[7].astype(jnp.bfloat16), "batch", scatter_dimension=1, tiled=True
        ).astype(jnp.float32),
        lax.psum_scatter(
            all_rows[8].astype(jnp.bfloat16), "batch", scatter_dimension=1, tiled=True
        ).astype(jnp.float32),
        lax.psum_scatter(
            all_rows[9].astype(jnp.bfloat16), "batch", scatter_dimension=1, tiled=True
        ).astype(jnp.float32),
    )
    vectors = lax.psum(
        (
            enc_up_bias_g,
            enc_down_bias_g,
            enc_gain_g,
            enc_shift_g,
            dec_up_bias_g,
            dec_down_bias_g,
            dec_gain_g,
            dec_shift_g,
        ),
        ("batch", "seq"),
    )
    return (
        to_low(decoded)[None],
        to_low(src_grad)[None],
        to_low(tgt_grad)[None],
        reduced[0],
        reduced[1],
        reduced[2],
        vectors[0],
        reduced[3],
        vectors[1],
        vectors[2],
        vectors[3],
        reduced[4],
        reduced[5],
        reduced[6],
        reduced[7],
        reduced[8],
        vectors[4],
        reduced[9],
        vectors[5],
        vectors[6],
        vectors[7],
    )


def general(mesh):
    placed = (
        P("batch", "seq", None),
        P("batch", "seq", None),
        P("batch", "seq"),
        P("batch", "seq"),
        P("batch", "seq", None),
        P(),
        P(),
        P(),
        P(),
        P(),
        P(),
        P(),
        P(),
        P(),
        P(),
        P(),
        P(),
        P(),
        P(),
        P(),
        P(),
        P(),
        P(),
    )
    return jax.shard_map(
        general_shards,
        mesh=mesh,
        in_specs=placed,
        out_specs=(
            P("batch", "seq", None),
            P("batch", "seq", None),
            P("batch", "seq", None),
            P(None, "seq", "batch"),
            P("seq", "batch"),
            P("seq", "batch"),
            P(),
            P("seq", "batch"),
            P(),
            P(),
            P(),
            P(None, "seq", "batch"),
            P("seq", "batch"),
            P(None, "seq", "batch"),
            P("seq", "batch"),
            P("seq", "batch"),
            P(),
            P("seq", "batch"),
            P(),
            P(),
            P(),
        ),
        check_vma=False,
    )


BATCH, SEQ = "batch", "seq"
CORE, X, Y, LOW, HIGH, SWAP = range(6)
ALL = (CORE, X, Y, LOW, HIGH)
TILE = 256
MESH = pl.DeviceIdType.MESH
VMEM = pl.BlockSpec(memory_space=pltpu.VMEM)
ANY = pl.BlockSpec(memory_space=pl.ANY)


def dot(left, right, left_dim=1, right_dim=0):
    return lax.dot_general(
        left, right, (((left_dim,), (right_dim,)), ((), ())), preferred_element_type=F32
    )


def block(index, size):
    return pl.ds(pl.multiple_of(index * size, size), size)


def normed(value):
    centred = value - jnp.mean(value, axis=-1, keepdims=True)
    scale = lax.rsqrt(jnp.mean(centred * centred, axis=-1, keepdims=True) + 1e-06)
    return centred * scale, scale


def normed_back(grad, unit, scale, gain):
    scaled = grad * gain
    first = jnp.mean(scaled, axis=-1, keepdims=True)
    second = jnp.mean(scaled * unit, axis=-1, keepdims=True)
    return scale * (scaled - first - unit * second)


def gelu_and_slope(inner):
    square = inner * inner
    bent = jnp.tanh(0.7978845608028654 * inner * (1.0 + 0.044715 * square))
    half = 0.5 * (1.0 + bent)
    slope = half + 0.5 * inner * (1.0 - bent * bent) * (
        0.7978845608028654 * (1.0 + 0.134145 * square)
    )
    return inner * half, slope


def column_sum(value):
    return jnp.sum(value, axis=0, keepdims=True)


def parts_of(up):
    return [slice(p * 512, (p + 1) * 512) for p in range(up.shape[1] // 512)]


def over_tiles(rows):
    def run(body):
        @pl.loop(0, rows // TILE)
        def _(tile):
            body(block(tile, TILE))

    return run


def places():
    row, s = lax.axis_index(BATCH), lax.axis_index(SEQ)
    core = lax.rem(row, 2)
    y = lax.rem(row // 2, 2)
    low = lax.rem(row // 4, 2)
    high = row // 8
    mine = (core, s, y, low, high + core - 2 * high * core)
    partner = (
        {BATCH: row + 1 - 2 * core},
        {SEQ: 1 - s},
        {BATCH: row + 2 - 4 * y},
        {BATCH: row + 4 - 8 * low},
        {BATCH: row + 8 - 16 * high},
        {BATCH: row - core + s, SEQ: core},
    )
    return mine, partner


def my_core():
    return places()[0][CORE]


def call_out(ways):
    mine, partner = places()
    barrier = pltpu.get_barrier_semaphore()
    for way in ways:
        pl.semaphore_signal(barrier, inc=1, device_id=partner[way], device_id_type=MESH)

    @pl.when(mine[CORE] != mine[X])
    def _():
        pl.semaphore_signal(barrier, inc=1, device_id=partner[SWAP], device_id_type=MESH)


def hear(ways):
    mine, _ = places()
    away = mine[CORE] + mine[X] - 2 * mine[CORE] * mine[X]
    pl.semaphore_wait(pltpu.get_barrier_semaphore(), len(ways) + away)


def sending(source, target, sems, slot, way):
    return pltpu.make_async_remote_copy(
        src_ref=source,
        dst_ref=target,
        send_sem=sems.at[0, slot],
        recv_sem=sems.at[1, slot],
        device_id=places()[1][way],
        device_id_type=MESH,
    )


def start_swap(source, target, sems, slot):
    mine, _ = places()

    @pl.when(mine[CORE] != mine[X])
    def _():
        sending(source, target, sems, slot, SWAP).start()

    @pl.when(mine[CORE] == mine[X])
    def _():
        pltpu.make_async_copy(source, target, sems.at[0, slot]).start()


def wait_swap(source, target, sems, slot):
    mine, _ = places()

    @pl.when(mine[CORE] != mine[X])
    def _():
        sending(source, target, sems, slot, SWAP).wait()

    @pl.when(mine[CORE] == mine[X])
    def _():
        pltpu.make_async_copy(source, target, sems.at[0, slot]).wait()


class RowSwap:
    def __init__(self, source, target, pieces, sems, slot, near_sem):
        mine, _ = places()
        self.here = mine[CORE] == mine[X]
        self.pieces = range(len(pieces))
        whole = target(mine[X], None)
        self.near = lambda: pltpu.make_async_copy(source, whole, near_sem)
        self.early = lambda: sending(source, whole, sems, slot, CORE)
        self.across = lambda k: sending(source.at[pieces[k]], target(mine[X], pieces[k]), sems, slot + 1 + k, SWAP)

        def onward(k):
            ref = target(mine[CORE], pieces[k])
            return sending(ref, ref, sems, slot + 1 + len(pieces) + k, CORE)

        self.onward = onward

    def start(self):
        @pl.when(self.here)
        def _():
            self.near().start()
            self.early().start()

        @pl.when(jnp.logical_not(self.here))
        def _():
            for k in self.pieces:
                self.across(k).start()

    def pass_on(self):
        @pl.when(jnp.logical_not(self.here))
        def _():
            for k in self.pieces:
                self.across(k).wait()
                self.onward(k).start()

    def finish(self):
        @pl.when(self.here)
        def _():
            self.near().wait()
            self.early().wait_send()
            for k in self.pieces:
                self.onward(k).wait_recv()

        @pl.when(jnp.logical_not(self.here))
        def _():
            self.early().wait_recv()
            for k in self.pieces:
                self.onward(k).wait_send()


def part_of(ref, axis, index):
    return ref.at[(slice(None),) * axis + (index,)]


class Halving:
    def __init__(self, source, axis, way, got, total, sems, slot, far=False):
        mine, _ = places()
        kept = part_of(source, axis, mine[way])
        self.kept, self.got, self.total = (total if far else kept), got, total
        self.sent = lambda: sending(part_of(source, axis, 1 - mine[way]), got, sems, slot, way)
        self.near = (lambda: pltpu.make_async_copy(kept, total, sems.at[2, slot])) if far else None

    def start(self):
        self.sent().start()
        if self.near is not None:
            self.near().start()

    def finish(self):
        if self.near is not None:
            self.near().wait()
        self.sent().wait()
        if self.total.dtype == F32:
            self.total[...] = self.kept[...].astype(F32) + self.got[...].astype(F32)
        else:
            self.total[...] = self.kept[...] + self.got[...]


class Across:
    def __init__(self, sums, got, sems, slot):
        self.sums, self.got = sums, got
        self.sent = lambda: sending(sums.at[1], got, sems, slot, CORE)

    def start(self):
        self.sent().start()

    def finish(self):
        self.sent().wait()
        self.sums[0] = self.sums[0] + self.got[...]


class Copies:
    def __init__(self, pairs, sems, first=0):
        self.copies = [
            (lambda source=source, target=target, place=place: pltpu.make_async_copy(source, target, sems.at[first + place]))
            for place, (source, target) in enumerate(pairs)
        ]

    def start(self):
        for copy in self.copies:
            copy().start()

    def wait(self):
        for copy in self.copies:
            copy().wait()


def attend_begin(r, att):
    heads = r.queries.shape[1]
    width = heads * HEAD_DIM
    columns = block(my_core(), width)
    q_from, k_from = att, att + att // 2
    q_side, k_side = jnp.minimum(att, 1), att * (2 - att)
    which = lax.rem(att, 2)
    place = lax.broadcasted_iota(jnp.int32, (HEAD_DIM, TILE), 0)
    ones = (lax.broadcasted_iota(jnp.int32, (TILE, HEAD_DIM), 1) < 3).astype(BF)
    half_tiles = r.ids.shape[3] // TILE

    @pl.loop(0, r.x_all.shape[1] // TILE)
    def _(tile):
        here = block(tile, TILE)
        lanes = block(lax.rem(tile, half_tiles), TILE)
        q_ids = r.ids[q_side, tile // half_tiles, :, lanes]
        k_ids = r.ids[k_side, tile // half_tiles, :, lanes]
        asks = jnp.where(place == q_ids, 1.0, 0.0).T.astype(BF)
        bars = jnp.where((place != k_ids) & (place < 3), NEGATIVE, 0.0).T.astype(BF)
        left_q, left_k = r.x_all[q_from, here, :], r.x_all[k_from, here, :]
        q_tile = dot(left_q, r.weights[att, 0, :, columns]).astype(BF) * BF(0.125)
        k_tile = dot(left_k, r.weights[att, 1, :, columns]).astype(BF)
        v_tile = dot(left_k, r.weights[att, 2, :, columns]).astype(BF)
        for head in range(heads):
            part = slice(head * HEAD_DIM, (head + 1) * HEAD_DIM)
            r.queries[which, head, here, :] = jnp.concatenate([q_tile[:, part], asks], axis=1)
            r.keys[which, head, here, :] = jnp.concatenate([k_tile[:, part], bars], axis=1)
            r.values[which, head, here, :] = jnp.concatenate([v_tile[:, part], ones], axis=1)


def attend_head(r, which, head, causal):
    length = r.queries.shape[2]
    if causal:
        lower = lax.broadcasted_iota(jnp.int32, (TILE, TILE), 0) >= lax.broadcasted_iota(
            jnp.int32, (TILE, TILE), 1
        )
    for tile in range(length // TILE):
        here = slice(tile * TILE, (tile + 1) * TILE)
        seen = (tile + 1) * TILE if causal else length
        scores = dot(r.queries[which, head, here, :], r.keys[which, head, :seen, :], 1, 1)
        if causal:
            last = jnp.where(lower, scores[:, seen - TILE :], NEGATIVE)
            scores = last if tile == 0 else jnp.concatenate([scores[:, : seen - TILE], last], axis=1)
        largest = jnp.max(scores, axis=-1, keepdims=True)
        terms = jnp.exp(scores - largest)
        total = jnp.sum(terms, axis=-1, keepdims=True)
        low = (terms * (1.0 / total)).astype(BF)
        r.chances[0, here, :seen] = low
        r.outs[head, here, :] = dot(low, r.values[which, head, :seen, :])[:, :HEAD_DIM]


def forward_body(r):
    step = pl.program_id(0)
    core = my_core()
    att = jnp.minimum(step // 4, 2)
    rows = r.source.shape[0]
    width = r.outs.shape[0] * HEAD_DIM
    sems = r.sems

    def rows_of(side):
        def target(half, piece):
            first = half * rows if piece is None else half * rows + piece.start
            count = rows if piece is None else piece.size
            return r.x_all.at[side, pl.ds(pl.multiple_of(first, count), count)]

        return target

    def ids_of(side):
        return lambda half, piece: r.ids.at[side, half]

    quarters = [pl.ds(k * rows // 4, rows // 4) for k in range(4)]
    source = RowSwap(r.source, rows_of(0), quarters, sems, 0, r.near_sems.at[0])
    target = RowSwap(r.target, rows_of(1), quarters, sems, 9, r.near_sems.at[1])
    one = [pl.ds(0, 1)]
    ids = (
        RowSwap(r.source_ids, ids_of(0), one, sems, 18, r.near_sems.at[2]),
        RowSwap(r.target_ids, ids_of(1), one, sems, 21, r.near_sems.at[3]),
    )
    first_across = sending(r.x_all.at[2, block(core, rows)], r.x_all.at[2, block(core, rows)], sems, 24, CORE)

    def att_across(index):
        return sending(r.att_send.at[index], r.att_all.at[index, :, block(core, width)], sems, 25 + index, CORE)

    def memory_across(tile):
        ref = r.x_all.at[3, pl.ds(pl.multiple_of(core * rows + tile * TILE, TILE), TILE)]
        return sending(ref, ref, sems, 28 + tile, CORE)

    loads = Copies(
        [
            (r.enc_qkv, r.weights.at[0]), (r.dec_qkv, r.weights.at[1]), (r.cross_qkv, r.weights.at[2]),
            (r.enc_out_far, r.enc_out), (r.dec_out_far, r.dec_out), (r.up_far, r.up), (r.down_far, r.down),
        ],
        r.load_sems,
    )

    def saved(index):
        which = index % 2
        return Copies(
            [
                (r.queries.at[which], r.queries_far.at[index]), (r.keys.at[which], r.keys_far.at[index]),
                (r.values.at[which], r.values_far.at[index]), (r.wide.at[index], r.wide_far.at[index]),
            ],
            r.save_sems,
            index * 4,
        )

    kept = Copies(
        [
            (r.unit0, r.unit0_far), (r.scale0, r.scale0_far), (r.unit1, r.unit1_far), (r.scale1, r.scale1_far),
            (r.hidden_low, r.hidden_far), (r.act, r.act_far), (r.slope, r.slope_far), (r.first, r.first_far),
            (r.first_unit, r.first_unit_far), (r.first_scale, r.first_scale_far), (r.x_all, r.x_far),
        ],
        r.save_sems,
        12,
    )
    att_kept = Copies([(r.att_all, r.att_far)], r.save_sems, 23)

    @pl.when(step == 0)
    def _():
        call_out((CORE,))
        loads.start()
        hear((CORE,))
        for one_side in ids:
            one_side.start()
        source.start()
        target.start()
        start_swap(r.upstream, r.upstream_there, sems, 30)
        for one_side in ids:
            one_side.pass_on()
        source.pass_on()
        for one_side in ids:
            one_side.finish()
        source.finish()
        loads.wait()

    @pl.when(step == 4)
    def _():
        target.pass_on()
        target.finish()

    @pl.when(step == 9)
    def _():
        saved(0).wait()
        first_across.wait()

        @pl.loop(0, rows // TILE)
        def _(tile):
            memory_across(tile).wait()

        kept.start()

    @pl.when((step == 0) | (step == 4) | (step == 9))
    def _():
        attend_begin(r, att)

    @pl.when((step < 4) | (step > 8))
    def _():
        attend_head(r, 0, lax.rem(step - att // 2, 4), False)

    @pl.when((step >= 4) & (step < 8))
    def _():
        attend_head(r, 1, step - 4, True)

    @pl.when((step == 3) | (step == 7) | (step == 12))
    def _():
        for half in (1 - core, core):
            there = block(half, rows)
            joined = jnp.concatenate([r.outs[head, there, :] for head in range(r.outs.shape[0])], axis=1)
            r.wide[att, there, :] = joined
            if half is core:
                r.att_all[att, :, block(core, width)] = joined.astype(BF)
            else:
                r.att_send[att] = joined.astype(BF)
                att_across(att).start()

    for index, last in enumerate((3, 7, 12)):

        @pl.when(step == last)
        def _(index=index):
            saved(index).start()

    @pl.when(step == 8)
    def _():
        att_across(0).wait()
        att_across(1).wait()

        @over_tiles(rows)
        def _(here):
            own = pl.ds(pl.multiple_of(core * rows + here.start, TILE), TILE)
            unit, scale = normed(r.x_all[1, own, :].astype(F32) + dot(r.att_all[1, here, :], r.dec_out[...]))
            r.first_unit[here, :] = unit
            r.first_scale[here, :] = scale
            value = unit * r.dec_gain[0:1, :] + r.dec_shift[0:1, :]
            r.first[here, :] = value
            r.x_all[2, own, :] = value.astype(BF)

        first_across.start()

        @pl.loop(0, rows // TILE)
        def _(tile):
            here = block(tile, TILE)
            own = pl.ds(pl.multiple_of(core * rows + tile * TILE, TILE), TILE)
            unit, scale = normed(r.x_all[0, own, :].astype(F32) + dot(r.att_all[0, here, :], r.enc_out[...]))
            r.unit0[here, :] = unit
            r.scale0[here, :] = scale
            hidden = unit * r.enc_gain[0:1, :] + r.enc_shift[0:1, :]
            low = hidden.astype(BF)
            r.hidden_low[here, :] = low
            for part in parts_of(r.up):
                value, bend = gelu_and_slope(dot(low, r.up[:, part]) + r.up_bias[:, part])
                r.slope[here, part] = bend.astype(BF)
                r.act[here, part] = value.astype(BF)
            unit, scale = normed(hidden + dot(r.act[here, :], r.down[...]) + r.down_bias[...])
            r.unit1[here, :] = unit
            r.scale1[here, :] = scale
            r.x_all[3, own, :] = (unit * r.enc_gain[1:2, :] + r.enc_shift[1:2, :]).astype(BF)
            memory_across(tile).start()

    @pl.when(step == 12)
    def _():
        kept.wait()
        saved(1).wait()
        wait_swap(r.upstream, r.upstream_there, sems, 30)
        att_across(2).wait()
        att_kept.start()
        saved(2).wait()
        att_kept.wait()


def back_begin(r, which):
    heads = r.queries.shape[1]
    lane = lax.broadcasted_iota(jnp.int32, (TILE, HEAD_DIM), 1)

    @over_tiles(r.queries.shape[2])
    def _(here):
        grad = r.grad_all[which, here, :]
        both = grad.astype(F32) * r.wide[which, here, :]
        for head in range(heads):
            part = slice(head * HEAD_DIM, (head + 1) * HEAD_DIM)
            settle = -jnp.sum(both[:, part], axis=-1, keepdims=True)
            first = settle.astype(BF).astype(F32)
            second = (settle - first).astype(BF).astype(F32)
            third = settle - first - second
            extra = jnp.where(
                lane == 0, first, jnp.where(lane == 1, second, jnp.where(lane == 2, third, 0.0))
            )
            r.grads[head, here, :] = jnp.concatenate([grad[:, part], extra.astype(BF)], axis=1)


def back_head(r, which, head, causal):
    length = r.queries.shape[2]
    for tile in range(length // TILE):
        here = slice(tile * TILE, (tile + 1) * TILE)
        seen = (tile + 1) * TILE if causal else length
        change = dot(r.grads[head, here, :], r.values[which, head, :seen, :], 1, 1)
        low = (r.chances[0, here, :seen].astype(F32) * change).astype(BF)
        r.score_grads[here, :seen] = low
        r.dq[head, here, :] = (dot(low, r.keys[which, head, :seen, :])[:, :HEAD_DIM] * 0.125).astype(BF)
    for tile in range(length // TILE if causal else 1):
        here = slice(tile * TILE, (tile + 1) * TILE) if causal else slice(0, length)
        below = slice(tile * TILE, length)
        r.dk[block(head, HEAD_DIM), here] = dot(
            r.queries[which, head, below, :HEAD_DIM], r.score_grads[below, here], 0, 0
        )
        r.dv[block(head, HEAD_DIM), here] = dot(
            r.grads[head, below, :HEAD_DIM], r.chances[0, below, here], 0, 0
        )


class BackEnd:
    def __init__(self, r, which, unit, q_from, k_from, sems):
        self.r, self.q_from, self.k_from = r, q_from, k_from
        core = my_core()
        rows = r.d_full.shape[2]
        width = r.d_all.shape[2]
        lanes = block(core, width)
        self.other = lambda: sending(
            r.d_all.at[:, block(1 - core, rows)], r.d_full.at[which, :, :, lanes], sems, 2 * which, CORE
        )
        self.own = lambda: pltpu.make_async_copy(
            r.d_all.at[:, block(core, rows)], r.d_full.at[which, :, :, lanes], sems.at[2, 2 * which]
        )
        below = pl.ds(32, 96)
        self.across = lambda: sending(r.shares.at[1], unit.at[:, :, :, 1, below], sems, 2 * which + 1, CORE)
        self.along = lambda: pltpu.make_async_copy(r.shares.at[0], unit.at[:, :, :, 0, below], sems.at[2, 2 * which + 1])

    def start(self):
        r = self.r
        core = my_core()
        rows, heads = r.d_full.shape[2], r.dq.shape[0]

        @pl.loop(0, 2)
        def _(half):
            there = block(half, rows)
            r.d_all[0, there, :] = jnp.concatenate([r.dq[head, there, :] for head in range(heads)], axis=1)
            r.d_all[1, there, :] = r.dk[:, there].T.astype(BF)
            r.d_all[2, there, :] = r.dv[:, there].T.astype(BF)

        self.other().start()
        self.own().start()

        @pl.loop(0, 3)
        def _(kind):
            x_from = jnp.where(kind == 0, self.q_from, self.k_from)
            low = dot(r.d_all[kind], r.x_all[x_from], 0, 0).astype(BF)
            for part in range(low.shape[0] // 32):
                z_low, y, kept = part >> 2, (part >> 1) & 1, part & 1
                for s in range(2):
                    r.shares[core if kept == 0 else 1 - core, s, y, z_low, block(kind, 32), :] = low[
                        part * 32 : (part + 1) * 32, s * 256 : (s + 1) * 256
                    ]

        self.across().start()
        self.along().start()

    def wait_grads(self):
        self.own().wait()
        self.other().wait()

    def wait_sums(self):
        self.along().wait()
        self.across().wait()


BIG = (2, 2, 2, 2, 128, 256)
MID = BIG[1:]
LESS = BIG[2:]
LEAST = BIG[3:]
OUT = (2, 2, 2, 2, 32, 256)
HALF = (2, 2, 2, 2, 64, 256)


def sum_up(sums, inner_low, entering):
    core = my_core()

    @pl.loop(0, 4)
    def _(z):
        for y in range(2):
            low = dot(inner_low[:, block(z * 2 + y, 256)], entering[...], 0, 0).astype(BF)
            high = z // 2
            for kept in range(2):
                for s in range(2):
                    sums[
                        core if kept == 0 else 1 - core, s, y, lax.rem(z, 2), 1 - high if kept else high, :, :
                    ] = low[kept * 128 : (kept + 1) * 128, s * 256 : (s + 1) * 256]


def sum_down(sums, branch_low, act):
    core = my_core()

    @pl.loop(0, act.shape[1] // 512)
    def _(column):
        for index in range(2):
            low = dot(branch_low[:, index * 256 : (index + 1) * 256], act[:, block(column, 512)], 0, 0).astype(BF)
            for part in range(8):
                place = index * 8 + part
                z, y, kept = place >> 2, (place >> 1) & 1, place & 1
                for piece in range(2):
                    slot = lax.rem(column, 2) * 2 + piece
                    sums[
                        core if kept == 0 else 1 - core, column // 2, y, z & 1, (z >> 1) ^ kept, block(slot, 32), :
                    ] = low[part * 32 : (part + 1) * 32, piece * 256 : (piece + 1) * 256]


def sum_out(sums, mixed_low, att):
    core = my_core()

    @pl.loop(0, 2)
    def _(s):
        low = dot(mixed_low[...], att[:, block(s, 256)], 0, 0).astype(BF)
        for place in range(16):
            z, y, kept = place >> 2, (place >> 1) & 1, place & 1
            sums[core if kept == 0 else 1 - core, s, y, z & 1, (z >> 1) ^ kept, :, :] = low[
                place * 32 : (place + 1) * 32, :
            ]


def split_halvings(unit, bufs, totals, sems, slot):
    upper, lower = unit.at[:, :, :, :, pl.ds(0, 64)], unit.at[:, :, :, :, pl.ds(64, 64)]
    return (
        Halving(upper, 0, X, bufs.at[0], totals.at[0], sems, slot),
        Halving(lower, 1, Y, bufs.at[1], totals.at[1], sems, slot + 1),
    )


def join_halvings(source, less, both, last, final, total, sems, slot):
    return (
        Halving(source.at[0], 0, Y, less.at[0], both.at[0], sems, slot),
        Halving(source.at[1], 0, X, less.at[1], both.at[1], sems, slot + 1),
        Halving(both, 1, LOW, last.at[0], last.at[1], sems, slot + 2),
        Halving(last.at[1], 1, HIGH, final, total, sems, slot + 3),
    )


def decode_last_layers(r):
    @over_tiles(r.first.shape[0])
    def _(here):
        unit, scale = normed(r.first[here, :] + dot(r.att[here, :], r.out_w[...]))
        r.unit0[here, :] = unit
        r.scale0[here, :] = scale
        second = unit * r.dec_gain[1:2, :] + r.dec_shift[1:2, :]
        low = second.astype(BF)
        r.entering[here, :] = low
        for part in parts_of(r.up):
            value, slope = gelu_and_slope(dot(low, r.up[:, part]) + r.up_bias[:, part])
            r.act[here, part] = value.astype(BF)
            r.inner_low[here, part] = slope.astype(BF)
        unit, scale = normed(second + dot(r.act[here, :], r.down[...]) + r.down_bias[...])
        r.unit1[here, :] = unit
        r.scale1[here, :] = scale
        r.decoded[here, :] = (unit * r.dec_gain[2:3, :] + r.dec_shift[2:3, :]).astype(BF)
        r.grad[here, :] = r.upstream[here, :].astype(F32)


def layers_back(r, which):
    vectors = r.vectors

    def add(place, value):
        vectors[which, place : place + 1, :] += value

    @over_tiles(r.grad.shape[0])
    def _(here):
        grad, unit = r.grad[here, :], r.unit1[here, :]
        add(7, column_sum(grad * unit))
        add(8, column_sum(grad))
        grad = normed_back(grad, unit, r.scale1[here, :], r.gains[which, 1:2, :])
        branch = grad.astype(BF)
        r.branch_low[here, :] = branch
        add(4, column_sum(branch.astype(F32)))
        for place, part in enumerate(parts_of(r.up)):
            inner = (dot(branch, r.down[part, :], 1, 1) * r.inner_low[here, part].astype(F32)).astype(BF)
            r.inner_low[here, part] = inner
            add(place, column_sum(inner.astype(F32)))
        grad = grad + dot(r.inner_low[here, :], r.up[...], 1, 1)
        unit = r.unit0[here, :]
        add(5, column_sum(grad * unit))
        add(6, column_sum(grad))
        grad = normed_back(grad, unit, r.scale0[here, :], r.gains[which, 0:1, :])
        r.pre[which, here, :] = grad
        mixed = grad.astype(BF)
        r.mixed_low[here, :] = mixed
        r.att_grad[here, :] = dot(mixed, r.out_w[...], 1, 1).astype(BF)


def middle_body(r):
    step = pl.program_id(0)
    mine, _ = places()
    core = mine[CORE]
    sems = r.sems
    rows, width = r.first.shape[0], r.d_all.shape[2]
    cross = 2
    before = Copies(
        [(r.first_far, r.first), (r.att_far.at[2], r.att), (r.upstream_far, r.upstream), (r.cross_out, r.out_w)], r.load_sems
    )
    dec_layer = Copies([(r.dec_up, r.up), (r.dec_down, r.down)], r.load_sems, 4)
    around = Copies(
        [
            (r.queries_far.at[pl.ds(2, 1)], r.queries), (r.keys_far.at[pl.ds(2, 1)], r.keys),
            (r.values_far.at[pl.ds(2, 1)], r.values), (r.wide_far.at[pl.ds(2, 1)], r.wide), (r.x_far.at[pl.ds(2, 2)], r.x_all),
        ],
        r.load_sems,
        6,
    )
    first_layer = Copies(
        [
            (r.cross_qkv, r.cross_w), (r.dec_out, r.dec_w), (r.first_unit_far, r.first_unit),
            (r.first_scale_far, r.first_scale), (r.att_far.at[1], r.dec_att),
        ],
        r.load_sems,
        11,
    )
    enc_layer = Copies(
        [
            (r.enc_up, r.up), (r.enc_down, r.down), (r.enc_out, r.out_w), (r.unit0_far, r.unit0), (r.scale0_far, r.scale0),
            (r.unit1_far, r.unit1), (r.scale1_far, r.scale1), (r.hidden_far, r.entering), (r.act_far, r.act),
            (r.slope_far, r.inner_low), (r.att_far.at[0], r.att),
        ],
        r.load_sems,
        16,
    )
    down_x = Halving(r.down_sums.at[0], 0, X, r.got_a, r.mid_a, sems, 0)
    up_y = Halving(r.up_sums.at[0], 1, Y, r.got_b, r.mid_b, sems, 1)
    down_y = Halving(r.mid_a, 0, Y, r.got_c, r.pair.at[0], sems, 2)
    up_x = Halving(r.mid_b, 0, X, r.got_d, r.pair.at[1], sems, 3)
    both_low = Halving(r.pair, 1, LOW, r.got_e, r.mid_e, sems, 4)
    both_high = Halving(r.mid_e, 1, HIGH, r.got_f, r.dec_sums, sems, 5)
    cross_x, cross_y = split_halvings(r.unit, r.got_g, r.cross_half, sems, 6)
    end = BackEnd(r, 0, r.unit, 0, 1, r.end_sems)
    shared = [
        Across(r.down_sums, r.down_got, sems, 8),
        Across(r.up_sums, r.up_got, sems, 9),
        Across(r.out_sums, r.out_got, sems, 10),
    ]
    dec_shared = Across(r.dec_out_sums, r.dec_out_got, sems, 11)
    lanes, other_lanes = block(core, width), block(1 - core, width)
    there = block(core, rows)

    def grads_of(source, target, slot):
        across = sending(source.at[:, other_lanes], target.at[there], sems, slot, CORE)
        stay = pltpu.make_async_copy(source.at[:, lanes], target.at[there], sems.at[2, slot])
        return across, stay

    cross_grads = grads_of(r.att_grad, r.grad_all.at[0], 12)
    dec_grads = grads_of(r.dec_att_grad, r.grads_far.at[1], 13)
    enc_grads = grads_of(r.att_grad, r.grads_far.at[0], 14)
    beside = pltpu.make_async_copy(r.out_sums.at[0], r.unit.at[:, :, :, :, pl.ds(0, 32)], sems.at[2, 15])
    results = Copies(
        [
            (r.down_sums.at[0], r.down_unit), (r.up_sums.at[0], r.up_unit), (r.out_sums.at[0], r.out_units.at[0]),
            (r.dec_out_sums.at[0], r.out_units.at[1]), (r.pre, r.pre_far),
        ],
        r.load_sems,
        27,
    )

    @pl.when(step == 0)
    def _():
        call_out(ALL)
        before.start()
        dec_layer.start()
        around.start()
        r.vectors[...] = jnp.zeros_like(r.vectors)
        for place, (ref, row) in enumerate(((r.dec_gain, 1), (r.dec_gain, 2), (r.enc_gain, 0), (r.enc_gain, 1))):
            r.gains[place // 2, place % 2 : place % 2 + 1, :] = ref[row : row + 1, :]
        before.wait()
        dec_layer.wait()
        decode_last_layers(r)
        hear(ALL)
        start_swap(r.decoded, r.decoded_there, sems, 16)

    @pl.when(step == 6)
    def _():
        beside.wait()
        end.wait_sums()
        cross_y.start()
        cross_x.start()
        end.wait_grads()

        @over_tiles(rows)
        def _(here):
            r.grad[here, :] = dot(r.d_full[0, 1, here, :], r.cross_w[1], 1, 1) + dot(
                r.d_full[0, 2, here, :], r.cross_w[2], 1, 1
            )
            grad = r.pre[0, here, :] + dot(r.d_full[0, 0, here, :], r.cross_w[0], 1, 1)
            unit = r.first_unit[here, :]
            r.vectors[2, 0:1, :] += column_sum(grad * unit)
            r.vectors[2, 1:2, :] += column_sum(grad)
            grad = normed_back(grad, unit, r.first_scale[here, :], r.dec_gain[0:1, :])
            r.pre[0, here, :] = grad
            mixed = grad.astype(BF)
            r.dec_mixed[here, :] = mixed
            r.dec_att_grad[here, :] = dot(mixed, r.dec_w[...], 1, 1).astype(BF)

        for copy in dec_grads:
            copy.start()
        sum_out(r.dec_out_sums, r.dec_mixed, r.dec_att)
        dec_shared.start()

    @pl.when(step == 7)
    def _():
        enc_layer.wait()

    @pl.when((step == 1) | (step == 7))
    def _():
        layers_back(r, step // 7)

    @pl.when(step == 1)
    def _():
        for copy in cross_grads:
            copy.start()

    @pl.when(step == 7)
    def _():
        for copy in enc_grads:
            copy.start()
        down_y.finish()
        up_x.finish()
        both_low.start()

    @pl.when((step == 1) | (step == 7))
    def _():
        sum_down(r.down_sums, r.branch_low, r.act)
        shared[0].start()
        sum_up(r.up_sums, r.inner_low, r.entering)
        shared[1].start()
        shared[0].finish()

        @pl.when(step == 1)
        def _():
            down_x.start()

        sum_out(r.out_sums, r.mixed_low, r.att)
        shared[2].start()
        shared[1].finish()

        @pl.when(step == 1)
        def _():
            up_y.start()

        shared[2].finish()

    @pl.when(step == 1)
    def _():
        beside.start()
        for copy in cross_grads:
            copy.wait()
        around.wait()
        enc_layer.start()
        first_layer.start()
        back_begin(r, 0)

    @pl.when((step >= 2) & (step < 6))
    def _():
        back_head(r, 0, step - 2, False)

    @pl.when(step == 5)
    def _():
        first_layer.wait()
        end.start()
        down_x.finish()
        up_y.finish()
        down_y.start()
        up_x.start()

    @pl.when(step == 7)
    def _():
        dec_shared.finish()
        results.start()
        both_low.finish()
        both_high.start()
        for copy in (*dec_grads, *enc_grads):
            copy.wait()
        both_high.finish()
        cross_y.finish()
        cross_x.finish()
        results.wait()
        wait_swap(r.decoded, r.decoded_there, sems, 16)


def last_body(r):
    step = pl.program_id(0)
    which = step // 4
    mine, _ = places()
    sems = r.sems
    rows = r.pre.shape[1]

    def side(att):
        return Copies(
            [
                (r.queries_far.at[att], r.queries.at[att]), (r.keys_far.at[att], r.keys.at[att]),
                (r.values_far.at[att], r.values.at[att]), (r.wide_far.at[att], r.wide.at[att]),
                (r.grads_far.at[att], r.grad_all.at[att]), (r.x_far.at[att], r.x_all.at[att]),
                ((r.enc_qkv, r.dec_qkv)[att], r.weights.at[att]), (r.pre_far.at[1 - att], r.pre.at[att]),
                (r.out_units.at[att], r.units.at[att, :, :, :, :, pl.ds(0, 32)]),
            ],
            r.load_sems,
            att * 9,
        )

    def layer_steps(unit, bufs, total, slot):
        got, mid, less, least, last = bufs
        return (
            Halving(unit, 1, Y, got, mid, sems, slot, far=True),
            Halving(mid, 1, LOW, less.at[0], less.at[1], sems, slot + 1),
            Halving(less.at[1], 1, HIGH, least.at[0], least.at[1], sems, slot + 2),
            Halving(least.at[1], 0, X, last, total, sems, slot + 3),
        )

    down = layer_steps(r.down_unit, r.down_bufs, r.enc_sums.at[0], 0)
    up = layer_steps(r.up_unit, r.up_bufs, r.enc_sums.at[1], 4)
    cross = join_halvings(r.cross_half, *r.cross_bufs, r.cross_sum, sems, 8)
    enc_got, enc_mid, enc_less, enc_least, enc_final = r.enc_bufs
    enc_att = (
        Halving(r.units.at[0], 0, X, enc_got, enc_mid, sems, 17),
        Halving(enc_mid, 0, Y, enc_less.at[0], enc_less.at[1], sems, 18),
        Halving(enc_less.at[1], 0, LOW, enc_least.at[0], enc_least.at[1], sems, 19),
        Halving(enc_least.at[1], 0, HIGH, enc_final, r.enc_att_sum, sems, 20),
    )
    dec_got, dec_mid, *dec_bufs = r.dec_bufs
    dec_x, dec_y = split_halvings(r.units.at[1], dec_got, dec_mid, sems, 21)
    dec_att = join_halvings(dec_mid, *dec_bufs, r.dec_att_sum, sems, 23)
    vector_ways = (LOW, HIGH, CORE, X, Y)

    def vector_parts(place):
        source = r.vectors if place == 0 else r.vector_mid.at[place - 1]
        total = r.vector_sum if place == 4 else r.vector_mid.at[place]
        copy = sending(source, r.vector_got.at[place], sems, 12 + place, vector_ways[place])
        return source, r.vector_got.at[place], total, copy

    def vector_start(place):
        vector_parts(place)[3].start()

    def vector_finish(place):
        source, got, total, copy = vector_parts(place)
        copy.wait()
        total[...] = source[...] + got[...]

    end = BackEnd(r, which, r.units.at[which], which, which, r.end_sems)

    def row_grads(index, target):
        @over_tiles(rows)
        def _(here):
            total = r.pre[index, here, :]
            for kind in range(3):
                total = total + dot(r.d_full[index, kind, here, :], r.weights[index, kind], 1, 1)
            r.row_grad[index, here, :] = total.astype(BF)

        start_swap(r.row_grad.at[index], target, sems, 27 + index)

    @pl.when(step == 0)
    def _():
        call_out(ALL)
        side(0).start()
        side(1).start()
        side(0).wait()

    @pl.when(step == 4)
    def _():
        side(1).wait()

    @pl.when((step == 0) | (step == 4))
    def _():
        back_begin(r, which)

    @pl.when(step == 0)
    def _():
        hear(ALL)
        cross[0].start()
        cross[1].start()
        down[0].start()
        up[0].start()
        vector_start(0)

    @pl.when(step == 4)
    def _():
        end_of_enc = BackEnd(r, 0, r.units.at[0], 0, 0, r.end_sems)
        end_of_enc.wait_sums()
        enc_att[0].start()
        vector_finish(3)
        vector_start(4)
        cross[3].finish()
        end_of_enc.wait_grads()
        row_grads(0, r.src_there)

    @pl.when(step == 1)
    def _():
        vector_finish(0)
        vector_start(1)

    @pl.when(step == 2)
    def _():
        vector_finish(1)
        vector_start(2)
        cross[0].finish()
        cross[1].finish()
        cross[2].start()

    @pl.when(step == 3)
    def _():
        vector_finish(2)
        vector_start(3)
        cross[2].finish()
        cross[3].start()

    @pl.when(step == 5)
    def _():
        down[1].finish()
        down[2].start()

    @pl.when(step == 7)
    def _():
        up[0].finish()
        up[1].start()

    @pl.when(step < 4)
    def _():
        back_head(r, 0, step, False)

    @pl.when(step >= 4)
    def _():
        back_head(r, 1, step - 4, True)

    @pl.when((step == 3) | (step == 7))
    def _():
        end.start()

    @pl.when(step == 3)
    def _():
        down[0].finish()
        down[1].start()

    @pl.when(step == 7)
    def _():
        down[2].finish()
        down[3].start()
        enc_att[0].finish()
        enc_att[1].start()
        end_of_dec = BackEnd(r, 1, r.units.at[1], 1, 1, r.end_sems)
        end_of_dec.wait_sums()
        dec_x.start()
        dec_y.start()
        end_of_dec.wait_grads()
        row_grads(1, r.tgt_there)
        up[1].finish()
        up[2].start()
        vector_finish(4)
        enc_att[1].finish()
        enc_att[2].start()
        dec_x.finish()
        dec_att[0].start()
        dec_y.finish()
        dec_att[1].start()
        down[3].finish()
        up[2].finish()
        up[3].start()
        enc_att[2].finish()
        enc_att[3].start()
        dec_att[0].finish()
        dec_att[1].finish()
        dec_att[2].start()
        enc_att[3].finish()
        up[3].finish()
        dec_att[2].finish()
        dec_att[3].start()
        dec_att[3].finish()
        wait_swap(r.row_grad.at[0], r.src_there, sems, 27)
        wait_swap(r.row_grad.at[1], r.tgt_there, sems, 28)


def finish_body(r):
    r.decoded_out[...] = r.decoded[...]
    r.src_out[...] = r.src[...]
    r.tgt_out[...] = r.tgt[...]
    for sums, down, up in ((r.dec_sums, r.dec_down, r.dec_up), (r.enc_sums, r.enc_down, r.enc_up)):
        for slot in range(4):
            down[:, slot * 256 : (slot + 1) * 256] = sums[0, slot * 32 : (slot + 1) * 32, :]
        up[...] = sums[1].T
    cross, dec_att = [jnp.concatenate([one[0], one[1]], axis=0) for one in (r.cross_sum, r.dec_att_sum)]
    for sums, out, qkv in (
        (cross, r.cross_out, r.cross_qkv),
        (r.enc_att_sum[...], r.enc_out, r.enc_qkv),
        (dec_att, r.dec_out, r.dec_qkv),
    ):
        out[...] = sums[:32]
        for kind in range(3):
            qkv[kind] = sums[32 + kind * 32 : 64 + kind * 32]
    vectors = r.vectors
    for which, up_bias, down_bias in ((0, r.dec_up_bias, r.dec_down_bias), (1, r.enc_up_bias, r.enc_down_bias)):
        for part in range(4):
            up_bias[:, part * 512 : (part + 1) * 512] = vectors[which, part : part + 1, :]
        down_bias[...] = vectors[which, 4:5, :]
    for ref, found in (
        (r.dec_gain, ((2, 0), (0, 5), (0, 7))),
        (r.dec_shift, ((2, 1), (0, 6), (0, 8))),
        (r.enc_gain, ((1, 5), (1, 7))),
        (r.enc_shift, ((1, 6), (1, 8))),
    ):
        for index, (which, place) in enumerate(found):
            ref[index : index + 1, :] = vectors[which, place : place + 1, :]


def launch(body, micros, grid, meeting, ins, far, blocks, outs, far_outs, scratch):
    def once(shape):
        rank = len(shape)
        return pl.BlockSpec(shape, lambda step: (0,) * rank, pipeline_mode=pl.Buffered(1))

    names, arrays, in_specs, out_names, shapes, out_specs = [], [], [], [], [], []
    for name, array in {**ins, **far}.items():
        names.append(name)
        arrays.append(array)
        in_specs.append(once(array.shape) if name in ins else ANY)
    for name, (shape, kind) in {**outs, **far_outs}.items():
        out_names.append(name)
        shapes.append(jax.ShapeDtypeStruct(shape, kind))
        out_specs.append(once(shape) if name in outs else ANY)
    for name, (array, part, index, is_out) in blocks.items():
        spec = pl.BlockSpec(part, index)
        if is_out:
            out_names.append(name)
            shapes.append(jax.ShapeDtypeStruct(*array))
            out_specs.append(spec)
        else:
            names.append(name)
            arrays.append(array)
            in_specs.append(spec)
    every = (*names, *out_names, *scratch)

    def kernel(*refs):
        body(types.SimpleNamespace(**dict(zip(every, refs))))

    results = pl.pallas_call(
        kernel,
        grid=(grid,),
        out_shape=shapes,
        in_specs=in_specs,
        out_specs=out_specs,
        scratch_shapes=list(scratch.values()),
        compiler_params=pltpu.CompilerParams(
            vmem_limit_bytes=60 * 2**20, collective_id=meeting, has_side_effects=meeting is not None
        ),
        cost_estimate=pl.CostEstimate(flops=int(micros * 1e9), bytes_accessed=0, transcendentals=0),
        name=body.__name__,
    )(*arrays)
    return types.SimpleNamespace(**dict(zip(out_names, results)))


def low(*shape):
    return pltpu.VMEM(shape, BF)


def wide(*shape):
    return pltpu.VMEM(shape, F32)


def fast_shards(source, target, source_ids, target_ids, out_grad, *params):
    (
        enc_qkv, enc_out, enc_up, enc_up_bias, enc_down, enc_down_bias, enc_gain, enc_shift, dec_qkv, dec_out,
        cross_qkv, cross_out, dec_up, dec_up_bias, dec_down, dec_down_bias, dec_gain, dec_shift,
    ) = params
    source, target, upstream = source[0], target[0], out_grad[0]
    rows, size = source.shape
    length, inner, width = 2 * rows, enc_up.shape[1], size // 2
    heads = width // HEAD_DIM
    sem = pltpu.SemaphoreType.DMA
    full, thin, low_full, low_inner = ((rows, size), F32), ((rows, 1), F32), ((rows, size), BF), ((rows, inner), BF)
    biases = [one[None, :] for one in (enc_up_bias, enc_down_bias, dec_up_bias, dec_down_bias)]
    enc_up_b, enc_down_b, dec_up_b, dec_down_b = biases
    head_block = (1, length, length)
    per_head = (heads, length, 2 * HEAD_DIM)

    f = launch(
        forward_body,
        60,
        13,
        0,
        dict(up_bias=enc_up_b, down_bias=enc_down_b, enc_gain=enc_gain, enc_shift=enc_shift, dec_gain=dec_gain, dec_shift=dec_shift),
        dict(
            source=source, target=target, source_ids=source_ids, target_ids=target_ids, upstream=upstream,
            enc_qkv=enc_qkv, dec_qkv=dec_qkv, cross_qkv=cross_qkv, enc_out_far=enc_out, dec_out_far=dec_out,
            up_far=enc_up, down_far=enc_down,
        ),
        dict(
            chances=(
                ((3 * heads, length, length), BF),
                head_block,
                lambda step: (jnp.where(step < 8, step, jnp.maximum(step - 1, 8)), 0, 0),
                True,
            )
        ),
        {},
        dict(
            x_far=((4, length, size), BF), upstream_there=low_full, queries_far=((3, *per_head), BF),
            keys_far=((3, *per_head), BF), values_far=((3, *per_head), BF), wide_far=((3, length, width), F32),
            att_far=((3, rows, size), BF), unit0_far=full, scale0_far=thin, unit1_far=full, scale1_far=thin,
            hidden_far=low_full, act_far=low_inner, slope_far=low_inner, first_far=full, first_unit_far=full,
            first_scale_far=thin,
        ),
        dict(
            sems=sem((2, 31)), near_sems=sem((4,)), load_sems=sem((7,)), save_sems=sem((24,)),
            x_all=low(4, length, size), ids=pltpu.VMEM((2, 2, 1, rows), jnp.int32), weights=low(3, 3, size, size),
            queries=low(2, *per_head), keys=low(2, *per_head), values=low(2, *per_head),
            outs=wide(heads, length, HEAD_DIM), wide=wide(3, length, width), att_all=low(3, rows, size),
            att_send=low(3, rows, width), enc_out=low(size, size), dec_out=low(size, size), up=low(size, inner),
            down=low(inner, size), unit0=wide(rows, size), scale0=wide(rows, 1), unit1=wide(rows, size),
            scale1=wide(rows, 1), hidden_low=low(rows, size), act=low(rows, inner), slope=low(rows, inner),
            first=wide(rows, size), first_unit=wide(rows, size), first_scale=wide(rows, 1),
        ),
    )
    work = dict(
        grads=low(*per_head), score_grads=low(length, length), dq=low(heads, length, HEAD_DIM), dk=wide(width, length),
        dv=wide(width, length), d_all=low(3, length, width), shares=low(2, 2, 2, 2, 96, 256), end_sems=sem((3, 4)),
    )
    sums_out = ((2, 128, 256), F32)
    halves = ((2, 64, 256), F32)
    m = launch(
        middle_body,
        50,
        8,
        1,
        dict(dec_gain=dec_gain, dec_shift=dec_shift, enc_gain=enc_gain, up_bias=dec_up_b, down_bias=dec_down_b),
        dict(
            first_far=f.first_far, att_far=f.att_far, upstream_far=f.upstream_there, cross_out=cross_out, dec_up=dec_up,
            dec_down=dec_down, queries_far=f.queries_far, keys_far=f.keys_far, values_far=f.values_far,
            wide_far=f.wide_far, x_far=f.x_far, cross_qkv=cross_qkv, dec_out=dec_out, first_unit_far=f.first_unit_far,
            first_scale_far=f.first_scale_far, enc_up=enc_up, enc_down=enc_down, enc_out=enc_out,
            unit0_far=f.unit0_far, scale0_far=f.scale0_far, unit1_far=f.unit1_far, scale1_far=f.scale1_far,
            hidden_far=f.hidden_far, act_far=f.act_far, slope_far=f.slope_far,
        ),
        dict(chances=(f.chances, head_block, lambda step: (8 + jnp.clip(step - 2, 0, 3), 0, 0), False)),
        dict(dec_sums=sums_out, cross_half=(HALF, BF), vectors=((3, 16, size), F32)),
        dict(
            decoded_there=low_full, grads_far=((2, length, width), BF), down_unit=(BIG, BF), up_unit=(BIG, BF),
            out_units=((2, *OUT), BF), pre_far=((2, rows, size), F32),
        ),
        dict(
            sems=sem((3, 17)), load_sems=sem((32,)), **work,
            first=wide(rows, size), att=low(rows, size), upstream=low(rows, size), out_w=low(size, size),
            up=low(size, inner), down=low(inner, size), queries=low(1, *per_head), keys=low(1, *per_head),
            values=low(1, *per_head), wide=wide(1, length, width), x_all=low(2, length, size), cross_w=low(3, size, size),
            dec_w=low(size, size), first_unit=wide(rows, size), first_scale=wide(rows, 1), dec_att=low(rows, size),
            unit0=wide(rows, size), scale0=wide(rows, 1), unit1=wide(rows, size), scale1=wide(rows, 1),
            entering=low(rows, size), act=low(rows, inner), inner_low=low(rows, inner), branch_low=low(rows, size),
            mixed_low=low(rows, size), att_grad=low(rows, size), dec_att_grad=low(rows, size), dec_mixed=low(rows, size),
            grad=wide(rows, size), pre=wide(2, rows, size), gains=wide(2, 2, size), decoded=low(rows, size),
            grad_all=low(1, length, width), d_full=low(1, 3, rows, size), unit=low(*BIG),
            down_sums=low(2, *BIG), up_sums=low(2, *BIG), out_sums=low(2, *OUT), dec_out_sums=low(2, *OUT),
            down_got=low(*BIG), up_got=low(*BIG), out_got=low(*OUT), dec_out_got=low(*OUT),
            got_a=low(*MID), mid_a=low(*MID), got_b=low(*MID), mid_b=low(*MID), got_c=low(*LESS), got_d=low(*LESS),
            pair=low(2, *LESS), got_e=low(2, *LEAST), mid_e=low(2, *LEAST), got_f=low(2, 128, 256), got_g=low(*HALF),
        ),
    )
    less, least = (2, 2, 2, 64, 256), (2, 64, 256)
    layer_bufs = [low(*MID), low(*MID), low(2, *LESS), low(2, *LEAST), low(128, 256)]
    join_bufs = [low(*less), low(*less), low(*less), low(*least)]
    b = launch(
        last_body,
        60,
        8,
        2,
        dict(cross_half=m.cross_half, vectors=m.vectors),
        dict(
            queries_far=f.queries_far, keys_far=f.keys_far, values_far=f.values_far, wide_far=f.wide_far, x_far=f.x_far,
            grads_far=m.grads_far, enc_qkv=enc_qkv, dec_qkv=dec_qkv, pre_far=m.pre_far, out_units=m.out_units,
            down_unit=m.down_unit, up_unit=m.up_unit,
        ),
        dict(chances=(f.chances, head_block, lambda step: (step, 0, 0), False)),
        dict(
            enc_sums=sums_out, cross_sum=halves, enc_att_sum=((128, 256), F32), dec_att_sum=halves,
            vector_sum=((3, 16, size), F32),
        ),
        dict(src_there=low_full, tgt_there=low_full),
        dict(
            sems=sem((3, 29)), load_sems=sem((18,)), **work,
            queries=low(2, *per_head), keys=low(2, *per_head), values=low(2, *per_head), wide=wide(2, length, width),
            grad_all=low(2, length, width), x_all=low(2, length, size), weights=low(2, 3, size, size),
            pre=wide(2, rows, size), d_full=low(2, 3, rows, size), units=low(2, *BIG), row_grad=low(2, rows, size),
            vector_got=wide(5, 3, 16, size), vector_mid=wide(4, 3, 16, size), down_bufs=layer_bufs, up_bufs=layer_bufs,
            enc_bufs=layer_bufs, cross_bufs=join_bufs, dec_bufs=[low(*HALF), low(*HALF), *join_bufs],
        ),
    )
    cut3, cut, pair, triple = ((3, 32, 256), F32), ((32, 256), F32), ((2, size), F32), ((3, size), F32)
    up_cut, down_cut, up_b, down_b = ((256, 128), F32), ((32, 1024), F32), ((1, inner), F32), ((1, size), F32)
    o = launch(
        finish_body,
        2,
        1,
        None,
        dict(
            decoded=m.decoded_there, src=b.src_there, tgt=b.tgt_there, dec_sums=m.dec_sums, enc_sums=b.enc_sums,
            cross_sum=b.cross_sum, enc_att_sum=b.enc_att_sum, dec_att_sum=b.dec_att_sum, vectors=b.vector_sum,
        ),
        {},
        {},
        dict(
            decoded_out=low_full, src_out=low_full, tgt_out=low_full, enc_qkv=cut3, enc_out=cut, enc_up=up_cut,
            enc_up_bias=up_b, enc_down=down_cut, enc_down_bias=down_b, enc_gain=pair, enc_shift=pair, dec_qkv=cut3,
            dec_out=cut, cross_qkv=cut3, cross_out=cut, dec_up=up_cut, dec_up_bias=up_b, dec_down=down_cut,
            dec_down_bias=down_b, dec_gain=triple, dec_shift=triple,
        ),
        {},
        {},
    )

    def turned(value):
        return jnp.swapaxes(value, -1, -2)

    return (
        o.decoded_out[None], o.src_out[None], o.tgt_out[None], turned(o.enc_qkv), turned(o.enc_out), o.enc_up,
        o.enc_up_bias[0], turned(o.enc_down), o.enc_down_bias[0], o.enc_gain, o.enc_shift, turned(o.dec_qkv),
        turned(o.dec_out), turned(o.cross_qkv), turned(o.cross_out), o.dec_up, o.dec_up_bias[0], turned(o.dec_down),
        o.dec_down_bias[0], o.dec_gain, o.dec_shift,
    )


def solution(mesh):
    if mesh.shape[SEQ] != 2 or mesh.shape[BATCH] != 16:
        return general(mesh)
    tokens = P(BATCH, SEQ, None)
    ids = P(BATCH, SEQ)
    cut, cut3 = P(SEQ, BATCH), P(None, SEQ, BATCH)
    return jax.shard_map(
        fast_shards,
        mesh=mesh,
        in_specs=(tokens, tokens, ids, ids, tokens) + (P(),) * 18,
        out_specs=(
            tokens, tokens, tokens, cut3, cut, cut, P(), cut, P(), P(), P(), cut3, cut, cut3, cut, cut, P(), cut,
            P(), P(), P(),
        ),
        check_vma=False,
    )
```

```python
import types

import jax
import jax.numpy as jnp
from jax import lax
from jax.experimental import pallas as pl
from jax.experimental.pallas import tpu as pltpu
from jax.sharding import PartitionSpec as P

HEAD_DIM = 64
NEGATIVE = -1e30
BF = jnp.bfloat16
F32 = jnp.float32


def layer_norm(value, gain, shift):
    mean = jnp.mean(value, axis=-1, keepdims=True)
    centred = value - mean
    spread = jnp.mean(centred * centred, axis=-1, keepdims=True)
    return centred * lax.rsqrt(spread + 1e-06) * gain + shift


def norm_back(value, gain, shift, grad):
    _, pull = jax.vjp(layer_norm, value, gain, shift)
    return pull(grad)


def gelu_back(inner, grad):
    _, pull = jax.vjp(jax.nn.gelu, inner)
    return pull(grad)[0]


def matmul(left, right):
    return jnp.dot(left, right, preferred_element_type=jnp.float32)


def weight_grad(inputs, grad):
    return lax.dot_general(
        inputs, grad, (((0,), (0,)), ((), ())), preferred_element_type=jnp.float32
    )


def input_grad(grad, weight):
    return lax.dot_general(
        grad, weight, (((1,), (1,)), ((), ())), preferred_element_type=jnp.float32
    )


def to_low(value):
    return value.astype(jnp.bfloat16)


def split_heads(value):
    return value.reshape(value.shape[0], -1, HEAD_DIM)


def block_live(query_ids, key_ids, offset, block, rows, causal):
    first_key = lax.dynamic_index_in_dim(key_ids, block * rows, 0, keepdims=False)
    last_key = lax.dynamic_index_in_dim(key_ids, block * rows + rows - 1, 0, keepdims=False)
    live = (first_key <= query_ids[rows - 1]) & (query_ids[0] <= last_key)
    if causal:
        live = live & (block * rows <= offset + rows - 1)
    return live


def block_scores(queries, keys_all, query_ids, key_ids, offset, block, causal):
    rows = queries.shape[0]
    key_block = lax.dynamic_slice_in_dim(keys_all, block * rows, rows, 0)
    id_block = lax.dynamic_slice_in_dim(key_ids, block * rows, rows, 0)
    scores = (
        jnp.einsum("qhe,khe->hqk", queries, key_block, preferred_element_type=jnp.float32) * 0.125
    )
    allowed = query_ids[:, None] == id_block[None, :]
    if causal:
        positions = jnp.arange(rows, dtype=jnp.int32)
        allowed = allowed & ((offset + positions)[:, None] >= (block * rows + positions)[None, :])
    allowed = allowed[None]
    return (jnp.where(allowed, scores, NEGATIVE), allowed, key_block)


def attend_forward(queries, keys_all, values_all, query_ids, key_ids, offset, causal):
    rows = queries.shape[0]
    heads_count = queries.shape[1]
    count = keys_all.shape[0] // rows

    def first_pass(block, carry):

        def first_compute(state):
            largest, total = state
            scores, allowed, _ = block_scores(
                queries, keys_all, query_ids, key_ids, offset, block, causal
            )
            newest = jnp.maximum(largest, jnp.max(scores, axis=-1))
            terms = jnp.where(allowed, jnp.exp(scores - newest[..., None]), 0.0)
            return (newest, total * jnp.exp(largest - newest) + jnp.sum(terms, axis=-1))

        live = block_live(query_ids, key_ids, offset, block, rows, causal)
        return lax.cond(live, first_compute, lambda state: state, carry)

    initial = (
        jnp.full((heads_count, rows), NEGATIVE, jnp.float32),
        jnp.zeros((heads_count, rows), jnp.float32),
    )
    largest, total = lax.fori_loop(0, count, first_pass, initial)
    log_total = largest + jnp.log(total)

    def second_pass(block, carry):

        def second_compute(output):
            scores, allowed, _ = block_scores(
                queries, keys_all, query_ids, key_ids, offset, block, causal
            )
            value_block = lax.dynamic_slice_in_dim(values_all, block * rows, rows, 0)
            chances = jnp.where(allowed, jnp.exp(scores - log_total[..., None]), 0.0)
            return output + jnp.einsum(
                "hqk,khe->qhe", to_low(chances), value_block, preferred_element_type=jnp.float32
            )

        live = block_live(query_ids, key_ids, offset, block, rows, causal)
        return lax.cond(live, second_compute, lambda output: output, carry)

    output = lax.fori_loop(0, count, second_pass, jnp.zeros(queries.shape, jnp.float32))
    return (output, log_total)


def attend_backward(
    queries, keys_all, values_all, query_ids, key_ids, offset, causal, grad_out, settle, log_total
):
    rows = queries.shape[0]
    count = keys_all.shape[0] // rows

    def step_block(block, carry):

        def step_compute(state):
            query_grad, key_grads, value_grads = state
            scores, allowed, key_block = block_scores(
                queries, keys_all, query_ids, key_ids, offset, block, causal
            )
            value_block = lax.dynamic_slice_in_dim(values_all, block * rows, rows, 0)
            chances = jnp.where(allowed, jnp.exp(scores - log_total[..., None]), 0.0)
            chance_grad = jnp.einsum(
                "qhe,khe->hqk", grad_out, value_block, preferred_element_type=jnp.float32
            )
            score_grad = to_low(chances * (chance_grad - settle[..., None]))
            query_grad = (
                query_grad
                + jnp.einsum(
                    "hqk,khe->qhe", score_grad, key_block, preferred_element_type=jnp.float32
                )
                * 0.125
            )
            key_part = (
                jnp.einsum("hqk,qhe->khe", score_grad, queries, preferred_element_type=jnp.float32)
                * 0.125
            )
            value_part = jnp.einsum(
                "hqk,qhe->khe", to_low(chances), grad_out, preferred_element_type=jnp.float32
            )
            key_grads = lax.dynamic_update_slice_in_dim(key_grads, key_part, block * rows, 0)
            value_grads = lax.dynamic_update_slice_in_dim(value_grads, value_part, block * rows, 0)
            return (query_grad, key_grads, value_grads)

        live = block_live(query_ids, key_ids, offset, block, rows, causal)
        return lax.cond(live, step_compute, lambda state: state, carry)

    initial = (
        jnp.zeros(queries.shape, jnp.float32),
        jnp.zeros(keys_all.shape, jnp.float32),
        jnp.zeros(values_all.shape, jnp.float32),
    )
    return lax.fori_loop(0, count, step_block, initial)


def attention_back(
    queries, keys_all, values_all, query_ids, key_ids_all, causal, grad_out, output, log_total
):
    rows = queries.shape[0]
    offset = lax.axis_index("seq") * rows
    settle = jnp.einsum("qhe,qhe->hq", grad_out.astype(jnp.float32), output)
    query_grad, key_terms, value_terms = attend_backward(
        queries,
        keys_all,
        values_all,
        query_ids,
        key_ids_all,
        offset,
        causal,
        grad_out,
        settle,
        log_total,
    )
    key_sum, value_sum = (
        lax.psum_scatter(
            key_terms.reshape(key_terms.shape[0], -1).astype(jnp.bfloat16),
            "seq",
            scatter_dimension=0,
            tiled=True,
        ).astype(jnp.float32),
        lax.psum_scatter(
            value_terms.reshape(value_terms.shape[0], -1).astype(jnp.bfloat16),
            "seq",
            scatter_dimension=0,
            tiled=True,
        ).astype(jnp.float32),
    )
    return (query_grad, key_sum, value_sum)


def general_shards(
    source,
    target,
    source_ids,
    target_ids,
    out_grad,
    enc_qkv,
    enc_out,
    enc_up,
    enc_up_bias,
    enc_down,
    enc_down_bias,
    enc_gain,
    enc_shift,
    dec_qkv,
    dec_out,
    cross_qkv,
    cross_out,
    dec_up,
    dec_up_bias,
    dec_down,
    dec_down_bias,
    dec_gain,
    dec_shift,
):
    src_rows = source[0]
    tgt_rows = target[0]
    src_ids = source_ids[0]
    tgt_ids = target_ids[0]
    rows = src_rows.shape[0]
    offset = lax.axis_index("seq") * rows
    enc_queries = to_low(matmul(src_rows, enc_qkv[0]))
    enc_keys = to_low(matmul(src_rows, enc_qkv[1]))
    enc_values = to_low(matmul(src_rows, enc_qkv[2]))
    enc_keys_all, enc_values_all, src_ids_all = (
        lax.all_gather(enc_keys, "seq", axis=0, tiled=True),
        lax.all_gather(enc_values, "seq", axis=0, tiled=True),
        lax.all_gather(src_ids, "seq", axis=0, tiled=True),
    )
    enc_att, enc_lse = attend_forward(
        split_heads(enc_queries),
        split_heads(enc_keys_all),
        split_heads(enc_values_all),
        src_ids,
        src_ids_all,
        offset,
        False,
    )
    enc_att_low = to_low(enc_att.reshape(rows, -1))
    enc_pre = src_rows.astype(jnp.float32) + matmul(enc_att_low, enc_out)
    hidden = layer_norm(enc_pre, enc_gain[0], enc_shift[0])
    hidden_low = to_low(hidden)
    enc_inner = matmul(hidden_low, enc_up) + enc_up_bias
    enc_act = to_low(jax.nn.gelu(enc_inner))
    enc_last = hidden + matmul(enc_act, enc_down) + enc_down_bias
    memory = layer_norm(enc_last, enc_gain[1], enc_shift[1])
    memory_low = to_low(memory)
    mem_keys = to_low(matmul(memory_low, cross_qkv[1]))
    mem_values = to_low(matmul(memory_low, cross_qkv[2]))
    mem_keys_all, mem_values_all = (
        lax.all_gather(mem_keys, "seq", axis=0, tiled=True),
        lax.all_gather(mem_values, "seq", axis=0, tiled=True),
    )
    dec_queries = to_low(matmul(tgt_rows, dec_qkv[0]))
    dec_keys = to_low(matmul(tgt_rows, dec_qkv[1]))
    dec_values = to_low(matmul(tgt_rows, dec_qkv[2]))
    dec_keys_all, dec_values_all, tgt_ids_all = (
        lax.all_gather(dec_keys, "seq", axis=0, tiled=True),
        lax.all_gather(dec_values, "seq", axis=0, tiled=True),
        lax.all_gather(tgt_ids, "seq", axis=0, tiled=True),
    )
    dec_att, dec_lse = attend_forward(
        split_heads(dec_queries),
        split_heads(dec_keys_all),
        split_heads(dec_values_all),
        tgt_ids,
        tgt_ids_all,
        offset,
        True,
    )
    dec_att_low = to_low(dec_att.reshape(rows, -1))
    dec_pre = tgt_rows.astype(jnp.float32) + matmul(dec_att_low, dec_out)
    first = layer_norm(dec_pre, dec_gain[0], dec_shift[0])
    first_low = to_low(first)
    cross_queries = to_low(matmul(first_low, cross_qkv[0]))
    cross_att, cross_lse = attend_forward(
        split_heads(cross_queries),
        split_heads(mem_keys_all),
        split_heads(mem_values_all),
        tgt_ids,
        src_ids_all,
        offset,
        False,
    )
    cross_att_low = to_low(cross_att.reshape(rows, -1))
    cross_pre = first + matmul(cross_att_low, cross_out)
    second = layer_norm(cross_pre, dec_gain[1], dec_shift[1])
    second_low = to_low(second)
    dec_inner = matmul(second_low, dec_up) + dec_up_bias
    dec_act = to_low(jax.nn.gelu(dec_inner))
    dec_last = second + matmul(dec_act, dec_down) + dec_down_bias
    decoded = layer_norm(dec_last, dec_gain[2], dec_shift[2])
    upstream = out_grad[0].astype(jnp.float32)
    grad_last, gain_two, shift_two = norm_back(dec_last, dec_gain[2], dec_shift[2], upstream)
    branch_low = to_low(grad_last)
    dec_down_g = weight_grad(dec_act, branch_low)
    dec_down_bias_g = jnp.sum(branch_low.astype(jnp.float32), axis=0)
    inner_low = to_low(gelu_back(dec_inner, input_grad(branch_low, dec_down)))
    dec_up_g = weight_grad(second_low, inner_low)
    dec_up_bias_g = jnp.sum(inner_low.astype(jnp.float32), axis=0)
    grad_second = grad_last + input_grad(inner_low, dec_up)
    grad_cross_pre, gain_one, shift_one = norm_back(
        cross_pre, dec_gain[1], dec_shift[1], grad_second
    )
    mixed_low = to_low(grad_cross_pre)
    cross_out_g = weight_grad(cross_att_low, mixed_low)
    cross_att_grad = to_low(input_grad(mixed_low, cross_out))
    cross_query_grad, mem_key_sum, mem_value_sum = attention_back(
        split_heads(cross_queries),
        split_heads(mem_keys_all),
        split_heads(mem_values_all),
        tgt_ids,
        src_ids_all,
        False,
        split_heads(cross_att_grad),
        cross_att,
        cross_lse,
    )
    mem_key_low = to_low(mem_key_sum)
    mem_value_low = to_low(mem_value_sum)
    cross_query_low = to_low(cross_query_grad.reshape(rows, -1))
    cross_qkv_g = jnp.stack(
        [
            weight_grad(first_low, cross_query_low),
            weight_grad(memory_low, mem_key_low),
            weight_grad(memory_low, mem_value_low),
        ]
    )
    grad_first = grad_cross_pre + input_grad(cross_query_low, cross_qkv[0])
    grad_dec_pre, gain_zero, shift_zero = norm_back(dec_pre, dec_gain[0], dec_shift[0], grad_first)
    self_low = to_low(grad_dec_pre)
    dec_out_g = weight_grad(dec_att_low, self_low)
    dec_att_grad = to_low(input_grad(self_low, dec_out))
    dec_query_grad, dec_key_sum, dec_value_sum = attention_back(
        split_heads(dec_queries),
        split_heads(dec_keys_all),
        split_heads(dec_values_all),
        tgt_ids,
        tgt_ids_all,
        True,
        split_heads(dec_att_grad),
        dec_att,
        dec_lse,
    )
    dec_query_low = to_low(dec_query_grad.reshape(rows, -1))
    dec_key_low = to_low(dec_key_sum)
    dec_value_low = to_low(dec_value_sum)
    dec_qkv_g = jnp.stack(
        [
            weight_grad(tgt_rows, dec_query_low),
            weight_grad(tgt_rows, dec_key_low),
            weight_grad(tgt_rows, dec_value_low),
        ]
    )
    tgt_grad = (
        grad_dec_pre
        + input_grad(dec_query_low, dec_qkv[0])
        + input_grad(dec_key_low, dec_qkv[1])
        + input_grad(dec_value_low, dec_qkv[2])
    )
    dec_gain_g = jnp.stack([gain_zero, gain_one, gain_two])
    dec_shift_g = jnp.stack([shift_zero, shift_one, shift_two])
    grad_memory = input_grad(mem_key_low, cross_qkv[1]) + input_grad(mem_value_low, cross_qkv[2])
    grad_enc_last, enc_gain_one, enc_shift_one = norm_back(
        enc_last, enc_gain[1], enc_shift[1], grad_memory
    )
    enc_branch_low = to_low(grad_enc_last)
    enc_down_g = weight_grad(enc_act, enc_branch_low)
    enc_down_bias_g = jnp.sum(enc_branch_low.astype(jnp.float32), axis=0)
    enc_inner_low = to_low(gelu_back(enc_inner, input_grad(enc_branch_low, enc_down)))
    enc_up_g = weight_grad(hidden_low, enc_inner_low)
    enc_up_bias_g = jnp.sum(enc_inner_low.astype(jnp.float32), axis=0)
    grad_hidden = grad_enc_last + input_grad(enc_inner_low, enc_up)
    grad_enc_pre, enc_gain_zero, enc_shift_zero = norm_back(
        enc_pre, enc_gain[0], enc_shift[0], grad_hidden
    )
    enc_mixed_low = to_low(grad_enc_pre)
    enc_out_g = weight_grad(enc_att_low, enc_mixed_low)
    enc_att_grad = to_low(input_grad(enc_mixed_low, enc_out))
    enc_query_grad, enc_key_sum, enc_value_sum = attention_back(
        split_heads(enc_queries),
        split_heads(enc_keys_all),
        split_heads(enc_values_all),
        src_ids,
        src_ids_all,
        False,
        split_heads(enc_att_grad),
        enc_att,
        enc_lse,
    )
    enc_query_low = to_low(enc_query_grad.reshape(rows, -1))
    enc_key_low = to_low(enc_key_sum)
    enc_value_low = to_low(enc_value_sum)
    enc_qkv_g = jnp.stack(
        [
            weight_grad(src_rows, enc_query_low),
            weight_grad(src_rows, enc_key_low),
            weight_grad(src_rows, enc_value_low),
        ]
    )
    src_grad = (
        grad_enc_pre
        + input_grad(enc_query_low, enc_qkv[0])
        + input_grad(enc_key_low, enc_qkv[1])
        + input_grad(enc_value_low, enc_qkv[2])
    )
    enc_gain_g = jnp.stack([enc_gain_zero, enc_gain_one])
    enc_shift_g = jnp.stack([enc_shift_zero, enc_shift_one])
    all_rows = (
        lax.psum_scatter(
            enc_qkv_g.astype(jnp.bfloat16), "seq", scatter_dimension=1, tiled=True
        ).astype(jnp.float32),
        lax.psum_scatter(
            enc_out_g.astype(jnp.bfloat16), "seq", scatter_dimension=0, tiled=True
        ).astype(jnp.float32),
        lax.psum_scatter(
            enc_up_g.astype(jnp.bfloat16), "seq", scatter_dimension=0, tiled=True
        ).astype(jnp.float32),
        lax.psum_scatter(
            enc_down_g.astype(jnp.bfloat16), "seq", scatter_dimension=0, tiled=True
        ).astype(jnp.float32),
        lax.psum_scatter(
            dec_qkv_g.astype(jnp.bfloat16), "seq", scatter_dimension=1, tiled=True
        ).astype(jnp.float32),
        lax.psum_scatter(
            dec_out_g.astype(jnp.bfloat16), "seq", scatter_dimension=0, tiled=True
        ).astype(jnp.float32),
        lax.psum_scatter(
            cross_qkv_g.astype(jnp.bfloat16), "seq", scatter_dimension=1, tiled=True
        ).astype(jnp.float32),
        lax.psum_scatter(
            cross_out_g.astype(jnp.bfloat16), "seq", scatter_dimension=0, tiled=True
        ).astype(jnp.float32),
        lax.psum_scatter(
            dec_up_g.astype(jnp.bfloat16), "seq", scatter_dimension=0, tiled=True
        ).astype(jnp.float32),
        lax.psum_scatter(
            dec_down_g.astype(jnp.bfloat16), "seq", scatter_dimension=0, tiled=True
        ).astype(jnp.float32),
    )
    reduced = (
        lax.psum_scatter(
            all_rows[0].astype(jnp.bfloat16), "batch", scatter_dimension=2, tiled=True
        ).astype(jnp.float32),
        lax.psum_scatter(
            all_rows[1].astype(jnp.bfloat16), "batch", scatter_dimension=1, tiled=True
        ).astype(jnp.float32),
        lax.psum_scatter(
            all_rows[2].astype(jnp.bfloat16), "batch", scatter_dimension=1, tiled=True
        ).astype(jnp.float32),
        lax.psum_scatter(
            all_rows[3].astype(jnp.bfloat16), "batch", scatter_dimension=1, tiled=True
        ).astype(jnp.float32),
        lax.psum_scatter(
            all_rows[4].astype(jnp.bfloat16), "batch", scatter_dimension=2, tiled=True
        ).astype(jnp.float32),
        lax.psum_scatter(
            all_rows[5].astype(jnp.bfloat16), "batch", scatter_dimension=1, tiled=True
        ).astype(jnp.float32),
        lax.psum_scatter(
            all_rows[6].astype(jnp.bfloat16), "batch", scatter_dimension=2, tiled=True
        ).astype(jnp.float32),
        lax.psum_scatter(
            all_rows[7].astype(jnp.bfloat16), "batch", scatter_dimension=1, tiled=True
        ).astype(jnp.float32),
        lax.psum_scatter(
            all_rows[8].astype(jnp.bfloat16), "batch", scatter_dimension=1, tiled=True
        ).astype(jnp.float32),
        lax.psum_scatter(
            all_rows[9].astype(jnp.bfloat16), "batch", scatter_dimension=1, tiled=True
        ).astype(jnp.float32),
    )
    vectors = lax.psum(
        (
            enc_up_bias_g,
            enc_down_bias_g,
            enc_gain_g,
            enc_shift_g,
            dec_up_bias_g,
            dec_down_bias_g,
            dec_gain_g,
            dec_shift_g,
        ),
        ("batch", "seq"),
    )
    return (
        to_low(decoded)[None],
        to_low(src_grad)[None],
        to_low(tgt_grad)[None],
        reduced[0],
        reduced[1],
        reduced[2],
        vectors[0],
        reduced[3],
        vectors[1],
        vectors[2],
        vectors[3],
        reduced[4],
        reduced[5],
        reduced[6],
        reduced[7],
        reduced[8],
        vectors[4],
        reduced[9],
        vectors[5],
        vectors[6],
        vectors[7],
    )


def general(mesh):
    placed = (
        P("batch", "seq", None),
        P("batch", "seq", None),
        P("batch", "seq"),
        P("batch", "seq"),
        P("batch", "seq", None),
        P(),
        P(),
        P(),
        P(),
        P(),
        P(),
        P(),
        P(),
        P(),
        P(),
        P(),
        P(),
        P(),
        P(),
        P(),
        P(),
        P(),
        P(),
    )
    return jax.shard_map(
        general_shards,
        mesh=mesh,
        in_specs=placed,
        out_specs=(
            P("batch", "seq", None),
            P("batch", "seq", None),
            P("batch", "seq", None),
            P(None, "seq", "batch"),
            P("seq", "batch"),
            P("seq", "batch"),
            P(),
            P("seq", "batch"),
            P(),
            P(),
            P(),
            P(None, "seq", "batch"),
            P("seq", "batch"),
            P(None, "seq", "batch"),
            P("seq", "batch"),
            P("seq", "batch"),
            P(),
            P("seq", "batch"),
            P(),
            P(),
            P(),
        ),
        check_vma=False,
    )


BATCH, SEQ = "batch", "seq"
CORE, X, Y, LOW, HIGH, SWAP = range(6)
ALL = (CORE, X, Y, LOW, HIGH)
TILE = 256
MESH = pl.DeviceIdType.MESH
VMEM = pl.BlockSpec(memory_space=pltpu.VMEM)
ANY = pl.BlockSpec(memory_space=pl.ANY)


def dot(left, right, left_dim=1, right_dim=0):
    return lax.dot_general(
        left, right, (((left_dim,), (right_dim,)), ((), ())), preferred_element_type=F32
    )


def block(index, size):
    return pl.ds(pl.multiple_of(index * size, size), size)


def normed(value):
    centred = value - jnp.mean(value, axis=-1, keepdims=True)
    scale = lax.rsqrt(jnp.mean(centred * centred, axis=-1, keepdims=True) + 1e-06)
    return centred * scale, scale


def normed_back(grad, unit, scale, gain):
    scaled = grad * gain
    first = jnp.mean(scaled, axis=-1, keepdims=True)
    second = jnp.mean(scaled * unit, axis=-1, keepdims=True)
    return scale * (scaled - first - unit * second)


def gelu_and_slope(inner):
    square = inner * inner
    bent = jnp.tanh(0.7978845608028654 * inner * (1.0 + 0.044715 * square))
    half = 0.5 * (1.0 + bent)
    slope = half + 0.5 * inner * (1.0 - bent * bent) * (
        0.7978845608028654 * (1.0 + 0.134145 * square)
    )
    return inner * half, slope


def column_sum(value):
    return jnp.sum(value, axis=0, keepdims=True)


def parts_of(up):
    return [slice(p * 512, (p + 1) * 512) for p in range(up.shape[1] // 512)]


def over_tiles(rows):
    def run(body):
        @pl.loop(0, rows // TILE)
        def _(tile):
            body(block(tile, TILE))

    return run


def places():
    row, s = lax.axis_index(BATCH), lax.axis_index(SEQ)
    core = lax.rem(row, 2)
    y = lax.rem(row // 2, 2)
    low = lax.rem(row // 4, 2)
    high = row // 8
    mine = (core, s, y, low, high + core - 2 * high * core)
    partner = (
        {BATCH: row + 1 - 2 * core},
        {SEQ: 1 - s},
        {BATCH: row + 2 - 4 * y},
        {BATCH: row + 4 - 8 * low},
        {BATCH: row + 8 - 16 * high},
        {BATCH: row - core + s, SEQ: core},
    )
    return mine, partner


def my_core():
    return places()[0][CORE]


def call_out(ways):
    mine, partner = places()
    barrier = pltpu.get_barrier_semaphore()
    for way in ways:
        pl.semaphore_signal(barrier, inc=1, device_id=partner[way], device_id_type=MESH)

    @pl.when(mine[CORE] != mine[X])
    def _():
        pl.semaphore_signal(barrier, inc=1, device_id=partner[SWAP], device_id_type=MESH)


def hear(ways):
    mine, _ = places()
    away = mine[CORE] + mine[X] - 2 * mine[CORE] * mine[X]
    pl.semaphore_wait(pltpu.get_barrier_semaphore(), len(ways) + away)


def sending(source, target, sems, slot, way):
    return pltpu.make_async_remote_copy(
        src_ref=source,
        dst_ref=target,
        send_sem=sems.at[0, slot],
        recv_sem=sems.at[1, slot],
        device_id=places()[1][way],
        device_id_type=MESH,
    )


def start_swap(source, target, sems, slot):
    mine, _ = places()

    @pl.when(mine[CORE] != mine[X])
    def _():
        sending(source, target, sems, slot, SWAP).start()

    @pl.when(mine[CORE] == mine[X])
    def _():
        pltpu.make_async_copy(source, target, sems.at[0, slot]).start()


def wait_swap(source, target, sems, slot):
    mine, _ = places()

    @pl.when(mine[CORE] != mine[X])
    def _():
        sending(source, target, sems, slot, SWAP).wait()

    @pl.when(mine[CORE] == mine[X])
    def _():
        pltpu.make_async_copy(source, target, sems.at[0, slot]).wait()


class RowSwap:
    def __init__(self, source, target, pieces, sems, slot, near_sem):
        mine, _ = places()
        self.here = mine[CORE] == mine[X]
        self.pieces = range(len(pieces))
        whole = target(mine[X], None)
        self.near = lambda: pltpu.make_async_copy(source, whole, near_sem)
        self.early = lambda: sending(source, whole, sems, slot, CORE)
        self.across = lambda k: sending(source.at[pieces[k]], target(mine[X], pieces[k]), sems, slot + 1 + k, SWAP)

        def onward(k):
            ref = target(mine[CORE], pieces[k])
            return sending(ref, ref, sems, slot + 1 + len(pieces) + k, CORE)

        self.onward = onward

    def start(self):
        @pl.when(self.here)
        def _():
            self.near().start()
            self.early().start()

        @pl.when(jnp.logical_not(self.here))
        def _():
            for k in self.pieces:
                self.across(k).start()

    def pass_on(self):
        @pl.when(jnp.logical_not(self.here))
        def _():
            for k in self.pieces:
                self.across(k).wait()
                self.onward(k).start()

    def finish(self):
        @pl.when(self.here)
        def _():
            self.near().wait()
            self.early().wait_send()
            for k in self.pieces:
                self.onward(k).wait_recv()

        @pl.when(jnp.logical_not(self.here))
        def _():
            self.early().wait_recv()
            for k in self.pieces:
                self.onward(k).wait_send()


def part_of(ref, axis, index):
    return ref.at[(slice(None),) * axis + (index,)]


class Halving:
    def __init__(self, source, axis, way, got, total, sems, slot, far=False):
        mine, _ = places()
        kept = part_of(source, axis, mine[way])
        self.kept, self.got, self.total = (total if far else kept), got, total
        self.sent = lambda: sending(part_of(source, axis, 1 - mine[way]), got, sems, slot, way)
        self.near = (lambda: pltpu.make_async_copy(kept, total, sems.at[2, slot])) if far else None

    def start(self):
        self.sent().start()
        if self.near is not None:
            self.near().start()

    def finish(self):
        if self.near is not None:
            self.near().wait()
        self.sent().wait()
        if self.total.dtype == F32:
            self.total[...] = self.kept[...].astype(F32) + self.got[...].astype(F32)
        else:
            self.total[...] = self.kept[...] + self.got[...]


class Across:
    def __init__(self, sums, got, sems, slot):
        self.sums, self.got = sums, got
        self.sent = lambda: sending(sums.at[1], got, sems, slot, CORE)

    def start(self):
        self.sent().start()

    def finish(self):
        self.sent().wait()
        self.sums[0] = self.sums[0] + self.got[...]


class Copies:
    def __init__(self, pairs, sems, first=0):
        self.copies = [
            (lambda source=source, target=target, place=place: pltpu.make_async_copy(source, target, sems.at[first + place]))
            for place, (source, target) in enumerate(pairs)
        ]

    def start(self):
        for copy in self.copies:
            copy().start()

    def wait(self):
        for copy in self.copies:
            copy().wait()


def attend_begin(r, att):
    heads = r.queries.shape[1]
    width = heads * HEAD_DIM
    columns = block(my_core(), width)
    q_from, k_from = att, att + att // 2
    q_side, k_side = jnp.minimum(att, 1), att * (2 - att)
    which = lax.rem(att, 2)
    place = lax.broadcasted_iota(jnp.int32, (HEAD_DIM, TILE), 0)
    ones = jnp.ones((TILE, HEAD_DIM), BF)
    half_tiles = r.ids.shape[3] // TILE

    @pl.loop(0, r.x_all.shape[1] // TILE)
    def _(tile):
        here = block(tile, TILE)
        lanes = block(lax.rem(tile, half_tiles), TILE)
        q_ids = r.ids[q_side, tile // half_tiles, :, lanes]
        k_ids = r.ids[k_side, tile // half_tiles, :, lanes]
        asks = jnp.where(place == q_ids, 1.0, 0.0).T.astype(BF)
        bars = jnp.where((place != k_ids) & (place < 3), NEGATIVE, 0.0).T.astype(BF)
        left_q, left_k = r.x_all[q_from, here, :], r.x_all[k_from, here, :]
        q_tile = dot(left_q, r.weights[att, 0, :, columns]).astype(BF) * BF(0.125)
        k_tile = dot(left_k, r.weights[att, 1, :, columns]).astype(BF)
        v_tile = dot(left_k, r.weights[att, 2, :, columns]).astype(BF)
        for head in range(heads):
            part = slice(head * HEAD_DIM, (head + 1) * HEAD_DIM)
            r.queries[which, head, here, :] = jnp.concatenate([q_tile[:, part], asks], axis=1)
            r.keys[which, head, here, :] = jnp.concatenate([k_tile[:, part], bars], axis=1)
            r.values[which, head, here, :] = jnp.concatenate([v_tile[:, part], ones], axis=1)


def attend_head(r, which, head, causal):
    length = r.queries.shape[2]
    count = length // TILE
    lower = lax.broadcasted_iota(jnp.int32, (TILE, TILE), 0) >= lax.broadcasted_iota(jnp.int32, (TILE, TILE), 1)

    def seen(tile):
        return (tile + 1) * TILE if causal else length

    def scores_of(tile):
        here = slice(tile * TILE, (tile + 1) * TILE)
        scores = dot(r.queries[which, head, here, :], r.keys[which, head, : seen(tile), :], 1, 1)
        if not causal:
            return scores
        last = jnp.where(lower, scores[:, seen(tile) - TILE :], NEGATIVE)
        return last if tile == 0 else jnp.concatenate([scores[:, : seen(tile) - TILE], last], axis=1)

    scores = scores_of(0)
    for tile in range(count):
        here = slice(tile * TILE, (tile + 1) * TILE)
        later = scores_of(tile + 1) if tile + 1 < count else None
        low = jnp.exp(scores - jnp.max(scores, axis=-1, keepdims=True)).astype(BF)
        r.chances[0, here, : seen(tile)] = low
        r.outs[which, head, here, :] = dot(low, r.values[which, head, : seen(tile), :])
        scores = later


def forward_body(r):
    step = pl.program_id(0)
    core = my_core()
    att = jnp.minimum(step // 4, 2)
    rows = r.source.shape[0]
    heads = r.outs.shape[1]
    width = heads * HEAD_DIM
    sems = r.sems

    def rows_of(side):
        def target(half, piece):
            first = half * rows if piece is None else half * rows + piece.start
            count = rows if piece is None else piece.size
            return r.x_all.at[side, pl.ds(pl.multiple_of(first, count), count)]

        return target

    def ids_of(side):
        return lambda half, piece: r.ids.at[side, half]

    quarters = [pl.ds(k * rows // 4, rows // 4) for k in range(4)]
    source = RowSwap(r.source, rows_of(0), quarters, sems, 0, r.near_sems.at[0])
    target = RowSwap(r.target, rows_of(1), quarters, sems, 9, r.near_sems.at[1])
    one = [pl.ds(0, 1)]
    ids = (
        RowSwap(r.source_ids, ids_of(0), one, sems, 18, r.near_sems.at[2]),
        RowSwap(r.target_ids, ids_of(1), one, sems, 21, r.near_sems.at[3]),
    )
    first_across = sending(r.x_all.at[2, block(core, rows)], r.x_all.at[2, block(core, rows)], sems, 24, CORE)

    def att_across(index):
        return sending(r.att_send.at[index], r.att_all.at[index, :, block(core, width)], sems, 25 + index, CORE)

    def memory_across(tile):
        ref = r.x_all.at[3, pl.ds(pl.multiple_of(core * rows + tile * TILE, TILE), TILE)]
        return sending(ref, ref, sems, 28 + tile, CORE)

    loads = Copies(
        [
            (r.enc_qkv, r.weights.at[0]), (r.dec_qkv, r.weights.at[1]), (r.cross_qkv, r.weights.at[2]),
            (r.enc_out_far, r.enc_out), (r.dec_out_far, r.dec_out), (r.up_far, r.up), (r.down_far, r.down),
        ],
        r.load_sems,
    )

    def saved(index):
        which = index % 2
        return Copies(
            [
                (r.queries.at[which], r.queries_far.at[index]), (r.keys.at[which], r.keys_far.at[index]),
                (r.values.at[which], r.values_far.at[index]), (r.outs.at[which], r.outs_far.at[index]),
            ],
            r.save_sems,
            index * 4,
        )

    kept = Copies(
        [
            (r.unit0, r.unit0_far), (r.scale0, r.scale0_far), (r.unit1, r.unit1_far), (r.scale1, r.scale1_far),
            (r.hidden_low, r.hidden_far), (r.act, r.act_far), (r.slope, r.slope_far), (r.first, r.first_far),
            (r.first_unit, r.first_unit_far), (r.first_scale, r.first_scale_far), (r.x_all, r.x_far),
        ],
        r.save_sems,
        12,
    )
    att_kept = Copies([(r.att_all, r.att_far)], r.save_sems, 23)

    @pl.when(step == 0)
    def _():
        call_out((CORE,))
        loads.start()
        hear((CORE,))
        for one_side in ids:
            one_side.start()
        source.start()
        target.start()
        start_swap(r.upstream, r.upstream_there, sems, 30)
        for one_side in ids:
            one_side.pass_on()
        source.pass_on()
        for one_side in ids:
            one_side.finish()
        source.finish()
        loads.wait()

    @pl.when(step == 4)
    def _():
        target.pass_on()
        target.finish()

    @pl.when(step == 9)
    def _():
        saved(0).wait()
        first_across.wait()

        @pl.loop(0, rows // TILE)
        def _(tile):
            memory_across(tile).wait()

        kept.start()

    @pl.when((step == 0) | (step == 4) | (step == 9))
    def _():
        attend_begin(r, att)

    @pl.when((step < 4) | (step > 8))
    def _():
        attend_head(r, 0, lax.rem(step - att // 2, 4), False)

    @pl.when((step >= 4) & (step < 8))
    def _():
        attend_head(r, 1, step - 4, True)

    @pl.when((step == 3) | (step == 7) | (step == 12))
    def _():
        for half in (1 - core, core):
            there = block(half, rows)
            parts = [r.outs[lax.rem(att, 2), head, there, :] for head in range(heads)]
            joined = jnp.concatenate([part[:, :HEAD_DIM] / part[:, HEAD_DIM:] for part in parts], axis=1).astype(BF)
            if half is core:
                r.att_all[att, :, block(core, width)] = joined
            else:
                r.att_send[att] = joined
                att_across(att).start()

    for index, last in enumerate((3, 7, 12)):

        @pl.when(step == last)
        def _(index=index):
            saved(index).start()

    @pl.when(step == 8)
    def _():
        att_across(0).wait()
        att_across(1).wait()

        @over_tiles(rows)
        def _(here):
            own = pl.ds(pl.multiple_of(core * rows + here.start, TILE), TILE)
            unit, scale = normed(r.x_all[1, own, :].astype(F32) + dot(r.att_all[1, here, :], r.dec_out[...]))
            r.first_unit[here, :] = unit
            r.first_scale[here, :] = scale
            value = unit * r.dec_gain[0:1, :] + r.dec_shift[0:1, :]
            r.first[here, :] = value
            r.x_all[2, own, :] = value.astype(BF)

        first_across.start()

        @pl.loop(0, rows // TILE)
        def _(tile):
            here = block(tile, TILE)
            own = pl.ds(pl.multiple_of(core * rows + tile * TILE, TILE), TILE)
            unit, scale = normed(r.x_all[0, own, :].astype(F32) + dot(r.att_all[0, here, :], r.enc_out[...]))
            r.unit0[here, :] = unit
            r.scale0[here, :] = scale
            hidden = unit * r.enc_gain[0:1, :] + r.enc_shift[0:1, :]
            low = hidden.astype(BF)
            r.hidden_low[here, :] = low
            for part in parts_of(r.up):
                value, bend = gelu_and_slope(dot(low, r.up[:, part]) + r.up_bias[:, part])
                r.slope[here, part] = bend.astype(BF)
                r.act[here, part] = value.astype(BF)
            unit, scale = normed(hidden + dot(r.act[here, :], r.down[...]) + r.down_bias[...])
            r.unit1[here, :] = unit
            r.scale1[here, :] = scale
            r.x_all[3, own, :] = (unit * r.enc_gain[1:2, :] + r.enc_shift[1:2, :]).astype(BF)
            memory_across(tile).start()

    @pl.when(step == 12)
    def _():
        kept.wait()
        saved(1).wait()
        wait_swap(r.upstream, r.upstream_there, sems, 30)
        att_across(2).wait()
        att_kept.start()
        saved(2).wait()
        att_kept.wait()


def back_begin(r, which):
    heads = r.queries.shape[1]
    width = heads * HEAD_DIM
    lane = lax.rem(lax.broadcasted_iota(jnp.int32, (TILE, width), 1), HEAD_DIM)
    same_head = (
        lax.broadcasted_iota(jnp.int32, (width, width), 0) // HEAD_DIM
        == lax.broadcasted_iota(jnp.int32, (width, width), 1) // HEAD_DIM
    ).astype(BF)

    @over_tiles(r.queries.shape[2])
    def _(here):
        grad = r.grad_all[which, here, :].astype(F32)
        lows, boths = [], []
        for head in range(heads):
            out = r.outs[which, head, here, :]
            over = 1.0 / out[:, HEAD_DIM:]
            low = (grad[:, head * HEAD_DIM : (head + 1) * HEAD_DIM] * over).astype(BF)
            lows.append(low)
            boths.append(low.astype(F32) * (out[:, :HEAD_DIM] * over))
        both = jnp.concatenate(boths, axis=1)
        high = both.astype(BF)
        rest = (both - high.astype(F32)).astype(BF)
        settle = -dot(high, same_head) - dot(rest, same_head)
        first = settle.astype(BF).astype(F32)
        second = (settle - first).astype(BF).astype(F32)
        extra = jnp.where(lane == 0, first, jnp.where(lane == 1, second, jnp.where(lane == 2, settle - first - second, 0.0)))
        extra = extra.astype(BF)
        for head in range(heads):
            r.grads[head, here, :] = jnp.concatenate(
                [lows[head], extra[:, head * HEAD_DIM : (head + 1) * HEAD_DIM]], axis=1
            )


def back_head(r, which, head, causal):
    length = r.queries.shape[2]
    count = length // TILE

    def seen(tile):
        return (tile + 1) * TILE if causal else length

    def change_of(tile):
        here = slice(tile * TILE, (tile + 1) * TILE)
        return dot(r.grads[head, here, :], r.values[which, head, : seen(tile), :], 1, 1)

    change = change_of(0)
    for tile in range(count):
        here = slice(tile * TILE, (tile + 1) * TILE)
        later = change_of(tile + 1) if tile + 1 < count else None
        low = (r.chances[0, here, : seen(tile)].astype(F32) * change).astype(BF)
        r.score_grads[here, : seen(tile)] = low
        r.dq[head, here, :] = (dot(low, r.keys[which, head, : seen(tile), :])[:, :HEAD_DIM] * 0.125).astype(BF)
        change = later
    for tile in range(count if causal else 1):
        here = slice(tile * TILE, (tile + 1) * TILE) if causal else slice(0, length)
        below = slice(tile * TILE, length)
        r.dv[block(head, HEAD_DIM), here] = dot(
            r.grads[head, below, :HEAD_DIM], r.chances[0, below, here], 0, 0
        )
        r.dk[block(head, HEAD_DIM), here] = dot(
            r.queries[which, head, below, :HEAD_DIM], r.score_grads[below, here], 0, 0
        )


class BackEnd:
    def __init__(self, r, which, unit, q_from, k_from, sems):
        self.r, self.q_from, self.k_from = r, q_from, k_from
        core = my_core()
        rows = r.d_full.shape[2]
        width = r.d_all.shape[2]
        lanes = block(core, width)
        self.other = lambda: sending(
            r.d_all.at[:, block(1 - core, rows)], r.d_full.at[which, :, :, lanes], sems, 2 * which, CORE
        )
        self.own = lambda: pltpu.make_async_copy(
            r.d_all.at[:, block(core, rows)], r.d_full.at[which, :, :, lanes], sems.at[2, 2 * which]
        )
        below = pl.ds(32, 96)
        self.across = lambda: sending(r.shares.at[1], unit.at[:, :, :, 1, below], sems, 2 * which + 1, CORE)
        self.along = lambda: pltpu.make_async_copy(r.shares.at[0], unit.at[:, :, :, 0, below], sems.at[2, 2 * which + 1])

    def start(self):
        r = self.r
        core = my_core()
        rows, heads = r.d_full.shape[2], r.dq.shape[0]

        @pl.loop(0, 2)
        def _(half):
            there = block(half, rows)
            r.d_all[0, there, :] = jnp.concatenate([r.dq[head, there, :] for head in range(heads)], axis=1)
            r.d_all[1, there, :] = r.dk[:, there].T.astype(BF)
            r.d_all[2, there, :] = r.dv[:, there].T.astype(BF)

        self.other().start()
        self.own().start()

        @pl.loop(0, 3)
        def _(kind):
            x_from = jnp.where(kind == 0, self.q_from, self.k_from)
            low = dot(r.d_all[kind], r.x_all[x_from], 0, 0).astype(BF)
            for part in range(low.shape[0] // 32):
                z_low, y, kept = part >> 2, (part >> 1) & 1, part & 1
                for s in range(2):
                    r.shares[core if kept == 0 else 1 - core, s, y, z_low, block(kind, 32), :] = low[
                        part * 32 : (part + 1) * 32, s * 256 : (s + 1) * 256
                    ]

        self.across().start()
        self.along().start()

    def wait_grads(self):
        self.own().wait()
        self.other().wait()

    def wait_sums(self):
        self.along().wait()
        self.across().wait()


BIG = (2, 2, 2, 2, 128, 256)
MID = BIG[1:]
LESS = BIG[2:]
LEAST = BIG[3:]
OUT = (2, 2, 2, 2, 32, 256)
HALF = (2, 2, 2, 2, 64, 256)


def sum_up(sums, inner_low, entering):
    core = my_core()

    @pl.loop(0, 4)
    def _(z):
        for y in range(2):
            low = dot(inner_low[:, block(z * 2 + y, 256)], entering[...], 0, 0).astype(BF)
            high = z // 2
            for kept in range(2):
                for s in range(2):
                    sums[
                        core if kept == 0 else 1 - core, s, y, lax.rem(z, 2), 1 - high if kept else high, :, :
                    ] = low[kept * 128 : (kept + 1) * 128, s * 256 : (s + 1) * 256]


def sum_down(sums, branch_low, act):
    core = my_core()

    @pl.loop(0, act.shape[1] // 512)
    def _(column):
        for index in range(2):
            low = dot(branch_low[:, index * 256 : (index + 1) * 256], act[:, block(column, 512)], 0, 0).astype(BF)
            for part in range(8):
                place = index * 8 + part
                z, y, kept = place >> 2, (place >> 1) & 1, place & 1
                for piece in range(2):
                    slot = lax.rem(column, 2) * 2 + piece
                    sums[
                        core if kept == 0 else 1 - core, column // 2, y, z & 1, (z >> 1) ^ kept, block(slot, 32), :
                    ] = low[part * 32 : (part + 1) * 32, piece * 256 : (piece + 1) * 256]


def sum_out(sums, mixed_low, att):
    core = my_core()

    @pl.loop(0, 2)
    def _(s):
        low = dot(mixed_low[...], att[:, block(s, 256)], 0, 0).astype(BF)
        for place in range(16):
            z, y, kept = place >> 2, (place >> 1) & 1, place & 1
            sums[core if kept == 0 else 1 - core, s, y, z & 1, (z >> 1) ^ kept, :, :] = low[
                place * 32 : (place + 1) * 32, :
            ]


def split_halvings(unit, bufs, totals, sems, slot):
    upper, lower = unit.at[:, :, :, :, pl.ds(0, 64)], unit.at[:, :, :, :, pl.ds(64, 64)]
    return (
        Halving(upper, 0, X, bufs.at[0], totals.at[0], sems, slot),
        Halving(lower, 1, Y, bufs.at[1], totals.at[1], sems, slot + 1),
    )


def join_halvings(source, less, both, last, final, total, sems, slot):
    return (
        Halving(source.at[0], 0, Y, less.at[0], both.at[0], sems, slot),
        Halving(source.at[1], 0, X, less.at[1], both.at[1], sems, slot + 1),
        Halving(both, 1, LOW, last.at[0], last.at[1], sems, slot + 2),
        Halving(last.at[1], 1, HIGH, final, total, sems, slot + 3),
    )


def decode_last_layers(r):
    @over_tiles(r.first.shape[0])
    def _(here):
        unit, scale = normed(r.first[here, :] + dot(r.att[here, :], r.out_w[...]))
        r.unit0[here, :] = unit
        r.scale0[here, :] = scale
        second = unit * r.dec_gain[1:2, :] + r.dec_shift[1:2, :]
        low = second.astype(BF)
        r.entering[here, :] = low
        for part in parts_of(r.up):
            value, slope = gelu_and_slope(dot(low, r.up[:, part]) + r.up_bias[:, part])
            r.act[here, part] = value.astype(BF)
            r.inner_low[here, part] = slope.astype(BF)
        unit, scale = normed(second + dot(r.act[here, :], r.down[...]) + r.down_bias[...])
        r.unit1[here, :] = unit
        r.scale1[here, :] = scale
        r.decoded[here, :] = (unit * r.dec_gain[2:3, :] + r.dec_shift[2:3, :]).astype(BF)
        r.grad[here, :] = r.upstream[here, :].astype(F32)


def layers_back(r, which):
    vectors = r.vectors

    def add(place, value):
        vectors[which, place : place + 1, :] += value

    @over_tiles(r.grad.shape[0])
    def _(here):
        grad, unit = r.grad[here, :], r.unit1[here, :]
        add(7, column_sum(grad * unit))
        add(8, column_sum(grad))
        grad = normed_back(grad, unit, r.scale1[here, :], r.gains[which, 1:2, :])
        branch = grad.astype(BF)
        r.branch_low[here, :] = branch
        add(4, column_sum(branch.astype(F32)))
        for place, part in enumerate(parts_of(r.up)):
            inner = (dot(branch, r.down[part, :], 1, 1) * r.inner_low[here, part].astype(F32)).astype(BF)
            r.inner_low[here, part] = inner
            add(place, column_sum(inner.astype(F32)))
        grad = grad + dot(r.inner_low[here, :], r.up[...], 1, 1)
        unit = r.unit0[here, :]
        add(5, column_sum(grad * unit))
        add(6, column_sum(grad))
        grad = normed_back(grad, unit, r.scale0[here, :], r.gains[which, 0:1, :])
        r.pre[which, here, :] = grad
        mixed = grad.astype(BF)
        r.mixed_low[here, :] = mixed
        r.att_grad[here, :] = dot(mixed, r.out_w[...], 1, 1).astype(BF)


def middle_body(r):
    step = pl.program_id(0)
    mine, _ = places()
    core = mine[CORE]
    sems = r.sems
    rows, width = r.first.shape[0], r.d_all.shape[2]
    cross = 2
    before = Copies(
        [(r.first_far, r.first), (r.att_far.at[2], r.att), (r.upstream_far, r.upstream), (r.cross_out, r.out_w)], r.load_sems
    )
    dec_layer = Copies([(r.dec_up, r.up), (r.dec_down, r.down)], r.load_sems, 4)
    around = Copies(
        [
            (r.queries_far.at[pl.ds(2, 1)], r.queries), (r.keys_far.at[pl.ds(2, 1)], r.keys),
            (r.values_far.at[pl.ds(2, 1)], r.values), (r.outs_far.at[pl.ds(2, 1)], r.outs), (r.x_far.at[pl.ds(2, 2)], r.x_all),
        ],
        r.load_sems,
        6,
    )
    first_layer = Copies(
        [
            (r.cross_qkv, r.cross_w), (r.dec_out, r.dec_w), (r.first_unit_far, r.first_unit),
            (r.first_scale_far, r.first_scale), (r.att_far.at[1], r.dec_att),
        ],
        r.load_sems,
        11,
    )
    enc_layer = Copies(
        [
            (r.enc_up, r.up), (r.enc_down, r.down), (r.enc_out, r.out_w), (r.unit0_far, r.unit0), (r.scale0_far, r.scale0),
            (r.unit1_far, r.unit1), (r.scale1_far, r.scale1), (r.hidden_far, r.entering), (r.act_far, r.act),
            (r.slope_far, r.inner_low), (r.att_far.at[0], r.att),
        ],
        r.load_sems,
        16,
    )
    down_x = Halving(r.down_sums.at[0], 0, X, r.got_a, r.mid_a, sems, 0)
    up_y = Halving(r.up_sums.at[0], 1, Y, r.got_b, r.mid_b, sems, 1)
    down_y = Halving(r.mid_a, 0, Y, r.got_c, r.pair.at[0], sems, 2)
    up_x = Halving(r.mid_b, 0, X, r.got_d, r.pair.at[1], sems, 3)
    down_low = Halving(r.pair.at[0], 0, LOW, r.got_e.at[0], r.mid_e, sems, 4)
    up_low = Halving(r.pair.at[1], 0, LOW, r.got_e.at[1], r.up_rest, sems, 17)
    down_high = Halving(r.mid_e, 0, HIGH, r.got_f, r.dec_down_sum, sems, 5)
    cross_x, cross_y = split_halvings(r.unit, r.got_g, r.cross_half, sems, 6)
    end = BackEnd(r, 0, r.unit, 0, 1, r.end_sems)
    shared = [
        Across(r.down_sums, r.down_got, sems, 8),
        Across(r.up_sums, r.up_got, sems, 9),
        Across(r.out_sums, r.out_got, sems, 10),
    ]
    dec_shared = Across(r.dec_out_sums, r.dec_out_got, sems, 11)
    lanes, other_lanes = block(core, width), block(1 - core, width)
    there = block(core, rows)

    def grads_of(source, target, slot):
        across = sending(source.at[:, other_lanes], target.at[there], sems, slot, CORE)
        stay = pltpu.make_async_copy(source.at[:, lanes], target.at[there], sems.at[2, slot])
        return across, stay

    cross_grads = grads_of(r.att_grad, r.grad_all.at[0], 12)
    dec_grads = grads_of(r.dec_att_grad, r.grads_far.at[1], 13)
    enc_grads = grads_of(r.att_grad, r.grads_far.at[0], 14)
    beside = pltpu.make_async_copy(r.out_sums.at[0], r.unit.at[:, :, :, :, pl.ds(0, 32)], sems.at[2, 15])
    results = Copies(
        [
            (r.down_sums.at[0], r.down_unit), (r.up_sums.at[0], r.up_unit), (r.out_sums.at[0], r.out_units.at[0]),
            (r.dec_out_sums.at[0], r.out_units.at[1]), (r.pre, r.pre_far),
        ],
        r.load_sems,
        27,
    )

    @pl.when(step == 0)
    def _():
        call_out(ALL)
        before.start()
        dec_layer.start()
        around.start()
        r.vectors[...] = jnp.zeros_like(r.vectors)
        for place, (ref, row) in enumerate(((r.dec_gain, 1), (r.dec_gain, 2), (r.enc_gain, 0), (r.enc_gain, 1))):
            r.gains[place // 2, place % 2 : place % 2 + 1, :] = ref[row : row + 1, :]
        before.wait()
        dec_layer.wait()
        decode_last_layers(r)
        hear(ALL)
        start_swap(r.decoded, r.decoded_there, sems, 16)

    @pl.when(step == 6)
    def _():
        beside.wait()
        end.wait_sums()
        cross_y.start()
        cross_x.start()
        end.wait_grads()

        @over_tiles(rows)
        def _(here):
            r.grad[here, :] = dot(r.d_full[0, 1, here, :], r.cross_w[1], 1, 1) + dot(
                r.d_full[0, 2, here, :], r.cross_w[2], 1, 1
            )
            grad = r.pre[0, here, :] + dot(r.d_full[0, 0, here, :], r.cross_w[0], 1, 1)
            unit = r.first_unit[here, :]
            r.vectors[2, 0:1, :] += column_sum(grad * unit)
            r.vectors[2, 1:2, :] += column_sum(grad)
            grad = normed_back(grad, unit, r.first_scale[here, :], r.dec_gain[0:1, :])
            r.pre[0, here, :] = grad
            mixed = grad.astype(BF)
            r.dec_mixed[here, :] = mixed
            r.dec_att_grad[here, :] = dot(mixed, r.dec_w[...], 1, 1).astype(BF)

        for copy in dec_grads:
            copy.start()
        sum_out(r.dec_out_sums, r.dec_mixed, r.dec_att)
        dec_shared.start()

    @pl.when(step == 7)
    def _():
        down_y.finish()
        down_low.start()
        enc_layer.wait()

    @pl.when((step == 1) | (step == 7))
    def _():
        layers_back(r, step // 7)

    @pl.when(step == 1)
    def _():
        for copy in cross_grads:
            copy.start()

    @pl.when(step == 7)
    def _():
        for copy in enc_grads:
            copy.start()
        down_low.finish()
        down_high.start()
        up_x.finish()
        up_low.start()

    @pl.when((step == 1) | (step == 7))
    def _():
        sum_down(r.down_sums, r.branch_low, r.act)
        shared[0].start()
        sum_up(r.up_sums, r.inner_low, r.entering)
        shared[1].start()
        shared[0].finish()

        @pl.when(step == 1)
        def _():
            down_x.start()

        sum_out(r.out_sums, r.mixed_low, r.att)
        shared[2].start()
        shared[1].finish()

        @pl.when(step == 1)
        def _():
            up_y.start()

        shared[2].finish()

    @pl.when(step == 1)
    def _():
        beside.start()
        for copy in cross_grads:
            copy.wait()
        around.wait()
        enc_layer.start()
        first_layer.start()
        back_begin(r, 0)

    @pl.when(step == 5)
    def _():
        down_x.finish()
        down_y.start()

    @pl.when((step >= 2) & (step < 6))
    def _():
        back_head(r, 0, step - 2, False)

    @pl.when(step == 5)
    def _():
        first_layer.wait()
        end.start()
        up_y.finish()
        up_x.start()

    @pl.when(step == 7)
    def _():
        dec_shared.finish()
        results.start()
        for copy in (*dec_grads, *enc_grads):
            copy.wait()
        down_high.finish()
        up_low.finish()
        cross_y.finish()
        cross_x.finish()
        results.wait()
        wait_swap(r.decoded, r.decoded_there, sems, 16)


def last_body(r):
    step = pl.program_id(0)
    which = step // 4
    mine, _ = places()
    sems = r.sems
    rows = r.pre.shape[1]

    def side(att):
        return Copies(
            [
                (r.queries_far.at[att], r.queries.at[att]), (r.keys_far.at[att], r.keys.at[att]),
                (r.values_far.at[att], r.values.at[att]), (r.outs_far.at[att], r.outs.at[att]),
                (r.grads_far.at[att], r.grad_all.at[att]), (r.x_far.at[att], r.x_all.at[att]),
                ((r.enc_qkv, r.dec_qkv)[att], r.weights.at[att]), (r.pre_far.at[1 - att], r.pre.at[att]),
                (r.out_units.at[att], r.units.at[att, :, :, :, :, pl.ds(0, 32)]),
            ],
            r.load_sems,
            att * 9,
        )

    def layer_steps(unit, bufs, total, slot, ways):
        left, steps, source = [X, Y, LOW, HIGH], [], unit
        for place, way in enumerate(ways):
            got, kept = (bufs[2 * place], bufs[2 * place + 1]) if place < 3 else (bufs[6], total)
            steps.append(Halving(source, left.index(way), way, got, kept, sems, slot + place, far=place == 0))
            left.remove(way)
            source = kept
        return steps

    down = layer_steps(r.down_unit, r.down_bufs, r.enc_sums.at[0], 0, (X, Y, LOW, HIGH))
    up = layer_steps(r.up_unit, r.up_bufs, r.enc_sums.at[1], 4, (Y, LOW, HIGH, X))
    cross = join_halvings(r.cross_half, *r.cross_bufs, r.cross_sum, sems, 8)
    dec_up_high = Halving(r.up_rest, 0, HIGH, r.rest_got, r.dec_up_sum, sems, 17)
    enc_got, enc_mid, *enc_bufs = r.enc_bufs
    enc_x, enc_y = split_halvings(r.units.at[0], enc_got, enc_mid, sems, 18)
    enc_att = join_halvings(enc_mid, *enc_bufs, r.enc_att_sum, sems, 20)
    dec_got, dec_mid, *dec_bufs = r.dec_bufs
    dec_x, dec_y = split_halvings(r.units.at[1], dec_got, dec_mid, sems, 24)
    dec_att = join_halvings(dec_mid, *dec_bufs, r.dec_att_sum, sems, 26)
    vector_ways = (CORE, LOW, HIGH, X, Y)

    def vector_parts(place):
        source = r.vectors if place == 0 else r.vector_mid.at[place - 1]
        total = r.vector_sum if place == 4 else r.vector_mid.at[place]
        copy = sending(source, r.vector_got.at[place], sems, 12 + place, vector_ways[place])
        return source, r.vector_got.at[place], total, copy

    def vector_start(place):
        vector_parts(place)[3].start()

    def vector_finish(place):
        source, got, total, copy = vector_parts(place)
        copy.wait()
        total[...] = source[...] + got[...]

    end = BackEnd(r, which, r.units.at[which], which, which, r.end_sems)

    def row_grads(index):
        @over_tiles(rows)
        def _(here):
            total = r.pre[index, here, :]
            for kind in range(3):
                total = total + dot(r.d_full[index, kind, here, :], r.weights[index, kind], 1, 1)
            r.row_grad[index, here, :] = total.astype(BF)

    src_swap = (r.row_grad.at[0], r.src_there, sems, 30)
    tgt_swap = (r.row_grad.at[1], r.tgt_there, sems, 31)

    @pl.when(step == 0)
    def _():
        call_out(ALL)
        side(0).start()
        side(1).start()
        side(0).wait()
        hear(ALL)
        dec_up_high.start()
        cross[0].start()
        cross[1].start()
        down[0].start()
        up[0].start()
        vector_start(0)

    @pl.when(step == 4)
    def _():
        side(1).wait()
        BackEnd(r, 0, r.units.at[0], 0, 0, r.end_sems).wait_sums()
        enc_x.start()
        enc_y.start()

    @pl.when((step == 0) | (step == 4))
    def _():
        back_begin(r, which)

    @pl.when(step == 1)
    def _():
        vector_finish(0)
        vector_start(1)

    @pl.when(step == 2)
    def _():
        vector_finish(1)
        vector_start(2)
        dec_up_high.finish()
        cross[0].finish()
        cross[1].finish()
        cross[2].start()

    @pl.when(step == 3)
    def _():
        vector_finish(2)
        vector_start(3)

    @pl.when(step == 4)
    def _():
        BackEnd(r, 0, r.units.at[0], 0, 0, r.end_sems).wait_grads()
        row_grads(0)
        start_swap(*src_swap)
        down[0].finish()
        down[1].start()
        up[0].finish()
        up[1].start()

    @pl.when(step == 5)
    def _():
        vector_finish(3)
        vector_start(4)
        cross[3].finish()

    @pl.when(step == 7)
    def _():
        enc_x.finish()
        enc_att[0].start()
        enc_y.finish()
        enc_att[1].start()

    @pl.when(step < 4)
    def _():
        back_head(r, 0, step, False)

    @pl.when(step >= 4)
    def _():
        back_head(r, 1, step - 4, True)

    @pl.when((step == 3) | (step == 7))
    def _():
        end.start()

    @pl.when(step == 3)
    def _():
        cross[2].finish()
        cross[3].start()

    @pl.when(step == 7)
    def _():
        up[1].finish()
        up[2].start()
        end_of_dec = BackEnd(r, 1, r.units.at[1], 1, 1, r.end_sems)
        end_of_dec.wait_sums()
        dec_x.start()
        dec_y.start()
        end_of_dec.wait_grads()
        row_grads(1)
        down[1].finish()
        down[2].start()
        vector_finish(4)
        enc_att[0].finish()
        enc_att[1].finish()
        enc_att[2].start()
        up[2].finish()
        up[3].start()
        down[2].finish()
        down[3].start()
        dec_x.finish()
        dec_att[0].start()
        dec_y.finish()
        dec_att[1].start()
        start_swap(*tgt_swap)
        enc_att[2].finish()
        enc_att[3].start()
        down[3].finish()
        up[3].finish()
        dec_att[0].finish()
        dec_att[1].finish()
        dec_att[2].start()
        enc_att[3].finish()
        dec_att[2].finish()
        dec_att[3].start()
        dec_att[3].finish()
        wait_swap(*src_swap)
        wait_swap(*tgt_swap)


def finish_body(r):
    r.decoded_out[...] = r.decoded[...]
    r.src_out[...] = r.src[...]
    r.tgt_out[...] = r.tgt[...]
    for sums, down in ((r.dec_down_sum[...], r.dec_down), (r.enc_sums[0], r.enc_down)):
        for slot in range(4):
            down[:, slot * 256 : (slot + 1) * 256] = sums[slot * 32 : (slot + 1) * 32, :]
    r.dec_up[...] = r.dec_up_sum[...].T
    r.enc_up[...] = r.enc_sums[1].T
    cross, enc_att, dec_att = [
        jnp.concatenate([one[0], one[1]], axis=0) for one in (r.cross_sum, r.enc_att_sum, r.dec_att_sum)
    ]
    for sums, out, qkv in (
        (cross, r.cross_out, r.cross_qkv),
        (enc_att, r.enc_out, r.enc_qkv),
        (dec_att, r.dec_out, r.dec_qkv),
    ):
        out[...] = sums[:32]
        for kind in range(3):
            qkv[kind] = sums[32 + kind * 32 : 64 + kind * 32]
    vectors = r.vectors
    for which, up_bias, down_bias in ((0, r.dec_up_bias, r.dec_down_bias), (1, r.enc_up_bias, r.enc_down_bias)):
        for part in range(4):
            up_bias[:, part * 512 : (part + 1) * 512] = vectors[which, part : part + 1, :]
        down_bias[...] = vectors[which, 4:5, :]
    for ref, found in (
        (r.dec_gain, ((2, 0), (0, 5), (0, 7))),
        (r.dec_shift, ((2, 1), (0, 6), (0, 8))),
        (r.enc_gain, ((1, 5), (1, 7))),
        (r.enc_shift, ((1, 6), (1, 8))),
    ):
        for index, (which, place) in enumerate(found):
            ref[index : index + 1, :] = vectors[which, place : place + 1, :]


def launch(body, micros, grid, meeting, ins, far, blocks, outs, far_outs, scratch):
    def once(shape):
        rank = len(shape)
        return pl.BlockSpec(shape, lambda step: (0,) * rank, pipeline_mode=pl.Buffered(1))

    names, arrays, in_specs, out_names, shapes, out_specs = [], [], [], [], [], []
    for name, array in {**ins, **far}.items():
        names.append(name)
        arrays.append(array)
        in_specs.append(once(array.shape) if name in ins else ANY)
    for name, (shape, kind) in {**outs, **far_outs}.items():
        out_names.append(name)
        shapes.append(jax.ShapeDtypeStruct(shape, kind))
        out_specs.append(once(shape) if name in outs else ANY)
    for name, (array, part, index, is_out) in blocks.items():
        spec = pl.BlockSpec(part, index)
        if is_out:
            out_names.append(name)
            shapes.append(jax.ShapeDtypeStruct(*array))
            out_specs.append(spec)
        else:
            names.append(name)
            arrays.append(array)
            in_specs.append(spec)
    every = (*names, *out_names, *scratch)

    def kernel(*refs):
        body(types.SimpleNamespace(**dict(zip(every, refs))))

    results = pl.pallas_call(
        kernel,
        grid=(grid,),
        out_shape=shapes,
        in_specs=in_specs,
        out_specs=out_specs,
        scratch_shapes=list(scratch.values()),
        compiler_params=pltpu.CompilerParams(
            vmem_limit_bytes=60 * 2**20, collective_id=meeting, has_side_effects=meeting is not None
        ),
        cost_estimate=pl.CostEstimate(flops=int(micros * 1e9), bytes_accessed=0, transcendentals=0),
        name=body.__name__,
    )(*arrays)
    return types.SimpleNamespace(**dict(zip(out_names, results)))


def low(*shape):
    return pltpu.VMEM(shape, BF)


def wide(*shape):
    return pltpu.VMEM(shape, F32)


def fast_shards(source, target, source_ids, target_ids, out_grad, *params):
    (
        enc_qkv, enc_out, enc_up, enc_up_bias, enc_down, enc_down_bias, enc_gain, enc_shift, dec_qkv, dec_out,
        cross_qkv, cross_out, dec_up, dec_up_bias, dec_down, dec_down_bias, dec_gain, dec_shift,
    ) = params
    source, target, upstream = source[0], target[0], out_grad[0]
    rows, size = source.shape
    length, inner, width = 2 * rows, enc_up.shape[1], size // 2
    heads = width // HEAD_DIM
    sem = pltpu.SemaphoreType.DMA
    full, thin, low_full, low_inner = ((rows, size), F32), ((rows, 1), F32), ((rows, size), BF), ((rows, inner), BF)
    biases = [one[None, :] for one in (enc_up_bias, enc_down_bias, dec_up_bias, dec_down_bias)]
    enc_up_b, enc_down_b, dec_up_b, dec_down_b = biases
    head_block = (1, length, length)
    per_head = (heads, length, 2 * HEAD_DIM)

    f = launch(
        forward_body,
        60,
        13,
        0,
        dict(up_bias=enc_up_b, down_bias=enc_down_b, enc_gain=enc_gain, enc_shift=enc_shift, dec_gain=dec_gain, dec_shift=dec_shift),
        dict(
            source=source, target=target, source_ids=source_ids, target_ids=target_ids, upstream=upstream,
            enc_qkv=enc_qkv, dec_qkv=dec_qkv, cross_qkv=cross_qkv, enc_out_far=enc_out, dec_out_far=dec_out,
            up_far=enc_up, down_far=enc_down,
        ),
        dict(
            chances=(
                ((3 * heads, length, length), BF),
                head_block,
                lambda step: (jnp.where(step < 8, step, jnp.maximum(step - 1, 8)), 0, 0),
                True,
            )
        ),
        {},
        dict(
            x_far=((4, length, size), BF), upstream_there=low_full, queries_far=((3, *per_head), BF),
            keys_far=((3, *per_head), BF), values_far=((3, *per_head), BF), outs_far=((3, *per_head), F32),
            att_far=((3, rows, size), BF), unit0_far=full, scale0_far=thin, unit1_far=full, scale1_far=thin,
            hidden_far=low_full, act_far=low_inner, slope_far=low_inner, first_far=full, first_unit_far=full,
            first_scale_far=thin,
        ),
        dict(
            sems=sem((2, 31)), near_sems=sem((4,)), load_sems=sem((7,)), save_sems=sem((24,)),
            x_all=low(4, length, size), ids=pltpu.VMEM((2, 2, 1, rows), jnp.int32), weights=low(3, 3, size, size),
            queries=low(2, *per_head), keys=low(2, *per_head), values=low(2, *per_head),
            outs=wide(2, *per_head), att_all=low(3, rows, size),
            att_send=low(3, rows, width), enc_out=low(size, size), dec_out=low(size, size), up=low(size, inner),
            down=low(inner, size), unit0=wide(rows, size), scale0=wide(rows, 1), unit1=wide(rows, size),
            scale1=wide(rows, 1), hidden_low=low(rows, size), act=low(rows, inner), slope=low(rows, inner),
            first=wide(rows, size), first_unit=wide(rows, size), first_scale=wide(rows, 1),
        ),
    )
    work = dict(
        grads=low(*per_head), score_grads=low(length, length), dq=low(heads, length, HEAD_DIM), dk=wide(width, length),
        dv=wide(width, length), d_all=low(3, length, width), shares=low(2, 2, 2, 2, 96, 256), end_sems=sem((3, 4)),
    )
    one_sum = ((128, 256), F32)
    sums_out = ((2, 128, 256), F32)
    halves = ((2, 64, 256), F32)
    m = launch(
        middle_body,
        50,
        8,
        1,
        dict(dec_gain=dec_gain, dec_shift=dec_shift, enc_gain=enc_gain, up_bias=dec_up_b, down_bias=dec_down_b),
        dict(
            first_far=f.first_far, att_far=f.att_far, upstream_far=f.upstream_there, cross_out=cross_out, dec_up=dec_up,
            dec_down=dec_down, queries_far=f.queries_far, keys_far=f.keys_far, values_far=f.values_far,
            outs_far=f.outs_far, x_far=f.x_far, cross_qkv=cross_qkv, dec_out=dec_out, first_unit_far=f.first_unit_far,
            first_scale_far=f.first_scale_far, enc_up=enc_up, enc_down=enc_down, enc_out=enc_out,
            unit0_far=f.unit0_far, scale0_far=f.scale0_far, unit1_far=f.unit1_far, scale1_far=f.scale1_far,
            hidden_far=f.hidden_far, act_far=f.act_far, slope_far=f.slope_far,
        ),
        dict(chances=(f.chances, head_block, lambda step: (8 + jnp.clip(step - 2, 0, 3), 0, 0), False)),
        dict(dec_down_sum=one_sum, up_rest=(LEAST, BF), cross_half=(HALF, BF), vectors=((3, 16, size), F32)),
        dict(
            decoded_there=low_full, grads_far=((2, length, width), BF), down_unit=(BIG, BF), up_unit=(BIG, BF),
            out_units=((2, *OUT), BF), pre_far=((2, rows, size), F32),
        ),
        dict(
            sems=sem((3, 18)), load_sems=sem((32,)), **work,
            first=wide(rows, size), att=low(rows, size), upstream=low(rows, size), out_w=low(size, size),
            up=low(size, inner), down=low(inner, size), queries=low(1, *per_head), keys=low(1, *per_head),
            values=low(1, *per_head), outs=wide(1, *per_head), x_all=low(2, length, size), cross_w=low(3, size, size),
            dec_w=low(size, size), first_unit=wide(rows, size), first_scale=wide(rows, 1), dec_att=low(rows, size),
            unit0=wide(rows, size), scale0=wide(rows, 1), unit1=wide(rows, size), scale1=wide(rows, 1),
            entering=low(rows, size), act=low(rows, inner), inner_low=low(rows, inner), branch_low=low(rows, size),
            mixed_low=low(rows, size), att_grad=low(rows, size), dec_att_grad=low(rows, size), dec_mixed=low(rows, size),
            grad=wide(rows, size), pre=wide(2, rows, size), gains=wide(2, 2, size), decoded=low(rows, size),
            grad_all=low(1, length, width), d_full=low(1, 3, rows, size), unit=low(*BIG),
            down_sums=low(2, *BIG), up_sums=low(2, *BIG), out_sums=low(2, *OUT), dec_out_sums=low(2, *OUT),
            down_got=low(*BIG), up_got=low(*BIG), out_got=low(*OUT), dec_out_got=low(*OUT),
            got_a=low(*MID), mid_a=low(*MID), got_b=low(*MID), mid_b=low(*MID), got_c=low(*LESS), got_d=low(*LESS),
            pair=low(2, *LESS), got_e=low(2, *LEAST), mid_e=low(*LEAST), got_f=low(128, 256), got_g=low(*HALF),
        ),
    )
    less, least = (2, 2, 2, 64, 256), (2, 64, 256)
    down_bufs = [low(*MID), low(*MID), low(*LESS), low(*LESS), low(*LEAST), low(*LEAST), low(128, 256)]
    up_bufs = [low(*MID), low(*MID), low(*LESS), low(*LESS), low(*LEAST), low(*LEAST), low(128, 256)]
    join_bufs = [low(*less), low(*less), low(*less), low(*least)]
    split_bufs = [low(*HALF), low(*HALF), *join_bufs]
    b = launch(
        last_body,
        60,
        8,
        2,
        dict(cross_half=m.cross_half, up_rest=m.up_rest, vectors=m.vectors),
        dict(
            queries_far=f.queries_far, keys_far=f.keys_far, values_far=f.values_far, outs_far=f.outs_far, x_far=f.x_far,
            grads_far=m.grads_far, enc_qkv=enc_qkv, dec_qkv=dec_qkv, pre_far=m.pre_far, out_units=m.out_units,
            down_unit=m.down_unit, up_unit=m.up_unit,
        ),
        dict(chances=(f.chances, head_block, lambda step: (step, 0, 0), False)),
        dict(
            enc_sums=sums_out, dec_up_sum=one_sum, cross_sum=halves, enc_att_sum=halves, dec_att_sum=halves,
            vector_sum=((3, 16, size), F32),
        ),
        dict(src_there=low_full, tgt_there=low_full),
        dict(
            sems=sem((3, 32)), load_sems=sem((18,)), **work,
            queries=low(2, *per_head), keys=low(2, *per_head), values=low(2, *per_head), outs=wide(2, *per_head),
            grad_all=low(2, length, width), x_all=low(2, length, size), weights=low(2, 3, size, size),
            pre=wide(2, rows, size), d_full=low(2, 3, rows, size), units=low(2, *BIG), row_grad=low(2, rows, size),
            vector_got=wide(5, 3, 16, size), vector_mid=wide(4, 3, 16, size), down_bufs=down_bufs, up_bufs=up_bufs,
            enc_bufs=split_bufs, cross_bufs=join_bufs, dec_bufs=split_bufs, rest_got=low(128, 256),
        ),
    )
    cut3, cut, pair, triple = ((3, 32, 256), F32), ((32, 256), F32), ((2, size), F32), ((3, size), F32)
    up_cut, down_cut, up_b, down_b = ((256, 128), F32), ((32, 1024), F32), ((1, inner), F32), ((1, size), F32)
    o = launch(
        finish_body,
        2,
        1,
        None,
        dict(
            decoded=m.decoded_there, src=b.src_there, tgt=b.tgt_there, dec_down_sum=m.dec_down_sum, dec_up_sum=b.dec_up_sum,
            enc_sums=b.enc_sums,
            cross_sum=b.cross_sum, enc_att_sum=b.enc_att_sum, dec_att_sum=b.dec_att_sum, vectors=b.vector_sum,
        ),
        {},
        {},
        dict(
            decoded_out=low_full, src_out=low_full, tgt_out=low_full, enc_qkv=cut3, enc_out=cut, enc_up=up_cut,
            enc_up_bias=up_b, enc_down=down_cut, enc_down_bias=down_b, enc_gain=pair, enc_shift=pair, dec_qkv=cut3,
            dec_out=cut, cross_qkv=cut3, cross_out=cut, dec_up=up_cut, dec_up_bias=up_b, dec_down=down_cut,
            dec_down_bias=down_b, dec_gain=triple, dec_shift=triple,
        ),
        {},
        {},
    )

    def turned(value):
        return jnp.swapaxes(value, -1, -2)

    return (
        o.decoded_out[None], o.src_out[None], o.tgt_out[None], turned(o.enc_qkv), turned(o.enc_out), o.enc_up,
        o.enc_up_bias[0], turned(o.enc_down), o.enc_down_bias[0], o.enc_gain, o.enc_shift, turned(o.dec_qkv),
        turned(o.dec_out), turned(o.cross_qkv), turned(o.cross_out), o.dec_up, o.dec_up_bias[0], turned(o.dec_down),
        o.dec_down_bias[0], o.dec_gain, o.dec_shift,
    )


def solution(mesh):
    if mesh.shape[SEQ] != 2 or mesh.shape[BATCH] != 16:
        return general(mesh)
    tokens = P(BATCH, SEQ, None)
    ids = P(BATCH, SEQ)
    cut, cut3 = P(SEQ, BATCH), P(None, SEQ, BATCH)
    return jax.shard_map(
        fast_shards,
        mesh=mesh,
        in_specs=(tokens, tokens, ids, ids, tokens) + (P(),) * 18,
        out_specs=(
            tokens, tokens, tokens, cut3, cut, cut, P(), cut, P(), P(), P(), cut3, cut, cut3, cut, cut, P(), cut,
            P(), P(), P(),
        ),
        check_vma=False,
    )
```

```python
import types

import jax
import jax.numpy as jnp
from jax import lax
from jax.experimental import pallas as pl
from jax.experimental.pallas import tpu as pltpu
from jax.sharding import PartitionSpec as P

HEAD_DIM = 64
NEGATIVE = -1e30
BF = jnp.bfloat16
F32 = jnp.float32


def layer_norm(value, gain, shift):
    mean = jnp.mean(value, axis=-1, keepdims=True)
    centred = value - mean
    spread = jnp.mean(centred * centred, axis=-1, keepdims=True)
    return centred * lax.rsqrt(spread + 1e-06) * gain + shift


def norm_back(value, gain, shift, grad):
    _, pull = jax.vjp(layer_norm, value, gain, shift)
    return pull(grad)


def gelu_back(inner, grad):
    _, pull = jax.vjp(jax.nn.gelu, inner)
    return pull(grad)[0]


def matmul(left, right):
    return jnp.dot(left, right, preferred_element_type=jnp.float32)


def weight_grad(inputs, grad):
    return lax.dot_general(
        inputs, grad, (((0,), (0,)), ((), ())), preferred_element_type=jnp.float32
    )


def input_grad(grad, weight):
    return lax.dot_general(
        grad, weight, (((1,), (1,)), ((), ())), preferred_element_type=jnp.float32
    )


def to_low(value):
    return value.astype(jnp.bfloat16)


def split_heads(value):
    return value.reshape(value.shape[0], -1, HEAD_DIM)


def block_live(query_ids, key_ids, offset, block, rows, causal):
    first_key = lax.dynamic_index_in_dim(key_ids, block * rows, 0, keepdims=False)
    last_key = lax.dynamic_index_in_dim(key_ids, block * rows + rows - 1, 0, keepdims=False)
    live = (first_key <= query_ids[rows - 1]) & (query_ids[0] <= last_key)
    if causal:
        live = live & (block * rows <= offset + rows - 1)
    return live


def block_scores(queries, keys_all, query_ids, key_ids, offset, block, causal):
    rows = queries.shape[0]
    key_block = lax.dynamic_slice_in_dim(keys_all, block * rows, rows, 0)
    id_block = lax.dynamic_slice_in_dim(key_ids, block * rows, rows, 0)
    scores = (
        jnp.einsum("qhe,khe->hqk", queries, key_block, preferred_element_type=jnp.float32) * 0.125
    )
    allowed = query_ids[:, None] == id_block[None, :]
    if causal:
        positions = jnp.arange(rows, dtype=jnp.int32)
        allowed = allowed & ((offset + positions)[:, None] >= (block * rows + positions)[None, :])
    allowed = allowed[None]
    return (jnp.where(allowed, scores, NEGATIVE), allowed, key_block)


def attend_forward(queries, keys_all, values_all, query_ids, key_ids, offset, causal):
    rows = queries.shape[0]
    heads_count = queries.shape[1]
    count = keys_all.shape[0] // rows

    def first_pass(block, carry):

        def first_compute(state):
            largest, total = state
            scores, allowed, _ = block_scores(
                queries, keys_all, query_ids, key_ids, offset, block, causal
            )
            newest = jnp.maximum(largest, jnp.max(scores, axis=-1))
            terms = jnp.where(allowed, jnp.exp(scores - newest[..., None]), 0.0)
            return (newest, total * jnp.exp(largest - newest) + jnp.sum(terms, axis=-1))

        live = block_live(query_ids, key_ids, offset, block, rows, causal)
        return lax.cond(live, first_compute, lambda state: state, carry)

    initial = (
        jnp.full((heads_count, rows), NEGATIVE, jnp.float32),
        jnp.zeros((heads_count, rows), jnp.float32),
    )
    largest, total = lax.fori_loop(0, count, first_pass, initial)
    log_total = largest + jnp.log(total)

    def second_pass(block, carry):

        def second_compute(output):
            scores, allowed, _ = block_scores(
                queries, keys_all, query_ids, key_ids, offset, block, causal
            )
            value_block = lax.dynamic_slice_in_dim(values_all, block * rows, rows, 0)
            chances = jnp.where(allowed, jnp.exp(scores - log_total[..., None]), 0.0)
            return output + jnp.einsum(
                "hqk,khe->qhe", to_low(chances), value_block, preferred_element_type=jnp.float32
            )

        live = block_live(query_ids, key_ids, offset, block, rows, causal)
        return lax.cond(live, second_compute, lambda output: output, carry)

    output = lax.fori_loop(0, count, second_pass, jnp.zeros(queries.shape, jnp.float32))
    return (output, log_total)


def attend_backward(
    queries, keys_all, values_all, query_ids, key_ids, offset, causal, grad_out, settle, log_total
):
    rows = queries.shape[0]
    count = keys_all.shape[0] // rows

    def step_block(block, carry):

        def step_compute(state):
            query_grad, key_grads, value_grads = state
            scores, allowed, key_block = block_scores(
                queries, keys_all, query_ids, key_ids, offset, block, causal
            )
            value_block = lax.dynamic_slice_in_dim(values_all, block * rows, rows, 0)
            chances = jnp.where(allowed, jnp.exp(scores - log_total[..., None]), 0.0)
            chance_grad = jnp.einsum(
                "qhe,khe->hqk", grad_out, value_block, preferred_element_type=jnp.float32
            )
            score_grad = to_low(chances * (chance_grad - settle[..., None]))
            query_grad = (
                query_grad
                + jnp.einsum(
                    "hqk,khe->qhe", score_grad, key_block, preferred_element_type=jnp.float32
                )
                * 0.125
            )
            key_part = (
                jnp.einsum("hqk,qhe->khe", score_grad, queries, preferred_element_type=jnp.float32)
                * 0.125
            )
            value_part = jnp.einsum(
                "hqk,qhe->khe", to_low(chances), grad_out, preferred_element_type=jnp.float32
            )
            key_grads = lax.dynamic_update_slice_in_dim(key_grads, key_part, block * rows, 0)
            value_grads = lax.dynamic_update_slice_in_dim(value_grads, value_part, block * rows, 0)
            return (query_grad, key_grads, value_grads)

        live = block_live(query_ids, key_ids, offset, block, rows, causal)
        return lax.cond(live, step_compute, lambda state: state, carry)

    initial = (
        jnp.zeros(queries.shape, jnp.float32),
        jnp.zeros(keys_all.shape, jnp.float32),
        jnp.zeros(values_all.shape, jnp.float32),
    )
    return lax.fori_loop(0, count, step_block, initial)


def attention_back(
    queries, keys_all, values_all, query_ids, key_ids_all, causal, grad_out, output, log_total
):
    rows = queries.shape[0]
    offset = lax.axis_index("seq") * rows
    settle = jnp.einsum("qhe,qhe->hq", grad_out.astype(jnp.float32), output)
    query_grad, key_terms, value_terms = attend_backward(
        queries,
        keys_all,
        values_all,
        query_ids,
        key_ids_all,
        offset,
        causal,
        grad_out,
        settle,
        log_total,
    )
    key_sum, value_sum = (
        lax.psum_scatter(
            key_terms.reshape(key_terms.shape[0], -1).astype(jnp.bfloat16),
            "seq",
            scatter_dimension=0,
            tiled=True,
        ).astype(jnp.float32),
        lax.psum_scatter(
            value_terms.reshape(value_terms.shape[0], -1).astype(jnp.bfloat16),
            "seq",
            scatter_dimension=0,
            tiled=True,
        ).astype(jnp.float32),
    )
    return (query_grad, key_sum, value_sum)


def general_shards(
    source,
    target,
    source_ids,
    target_ids,
    out_grad,
    enc_qkv,
    enc_out,
    enc_up,
    enc_up_bias,
    enc_down,
    enc_down_bias,
    enc_gain,
    enc_shift,
    dec_qkv,
    dec_out,
    cross_qkv,
    cross_out,
    dec_up,
    dec_up_bias,
    dec_down,
    dec_down_bias,
    dec_gain,
    dec_shift,
):
    src_rows = source[0]
    tgt_rows = target[0]
    src_ids = source_ids[0]
    tgt_ids = target_ids[0]
    rows = src_rows.shape[0]
    offset = lax.axis_index("seq") * rows
    enc_queries = to_low(matmul(src_rows, enc_qkv[0]))
    enc_keys = to_low(matmul(src_rows, enc_qkv[1]))
    enc_values = to_low(matmul(src_rows, enc_qkv[2]))
    enc_keys_all, enc_values_all, src_ids_all = (
        lax.all_gather(enc_keys, "seq", axis=0, tiled=True),
        lax.all_gather(enc_values, "seq", axis=0, tiled=True),
        lax.all_gather(src_ids, "seq", axis=0, tiled=True),
    )
    enc_att, enc_lse = attend_forward(
        split_heads(enc_queries),
        split_heads(enc_keys_all),
        split_heads(enc_values_all),
        src_ids,
        src_ids_all,
        offset,
        False,
    )
    enc_att_low = to_low(enc_att.reshape(rows, -1))
    enc_pre = src_rows.astype(jnp.float32) + matmul(enc_att_low, enc_out)
    hidden = layer_norm(enc_pre, enc_gain[0], enc_shift[0])
    hidden_low = to_low(hidden)
    enc_inner = matmul(hidden_low, enc_up) + enc_up_bias
    enc_act = to_low(jax.nn.gelu(enc_inner))
    enc_last = hidden + matmul(enc_act, enc_down) + enc_down_bias
    memory = layer_norm(enc_last, enc_gain[1], enc_shift[1])
    memory_low = to_low(memory)
    mem_keys = to_low(matmul(memory_low, cross_qkv[1]))
    mem_values = to_low(matmul(memory_low, cross_qkv[2]))
    mem_keys_all, mem_values_all = (
        lax.all_gather(mem_keys, "seq", axis=0, tiled=True),
        lax.all_gather(mem_values, "seq", axis=0, tiled=True),
    )
    dec_queries = to_low(matmul(tgt_rows, dec_qkv[0]))
    dec_keys = to_low(matmul(tgt_rows, dec_qkv[1]))
    dec_values = to_low(matmul(tgt_rows, dec_qkv[2]))
    dec_keys_all, dec_values_all, tgt_ids_all = (
        lax.all_gather(dec_keys, "seq", axis=0, tiled=True),
        lax.all_gather(dec_values, "seq", axis=0, tiled=True),
        lax.all_gather(tgt_ids, "seq", axis=0, tiled=True),
    )
    dec_att, dec_lse = attend_forward(
        split_heads(dec_queries),
        split_heads(dec_keys_all),
        split_heads(dec_values_all),
        tgt_ids,
        tgt_ids_all,
        offset,
        True,
    )
    dec_att_low = to_low(dec_att.reshape(rows, -1))
    dec_pre = tgt_rows.astype(jnp.float32) + matmul(dec_att_low, dec_out)
    first = layer_norm(dec_pre, dec_gain[0], dec_shift[0])
    first_low = to_low(first)
    cross_queries = to_low(matmul(first_low, cross_qkv[0]))
    cross_att, cross_lse = attend_forward(
        split_heads(cross_queries),
        split_heads(mem_keys_all),
        split_heads(mem_values_all),
        tgt_ids,
        src_ids_all,
        offset,
        False,
    )
    cross_att_low = to_low(cross_att.reshape(rows, -1))
    cross_pre = first + matmul(cross_att_low, cross_out)
    second = layer_norm(cross_pre, dec_gain[1], dec_shift[1])
    second_low = to_low(second)
    dec_inner = matmul(second_low, dec_up) + dec_up_bias
    dec_act = to_low(jax.nn.gelu(dec_inner))
    dec_last = second + matmul(dec_act, dec_down) + dec_down_bias
    decoded = layer_norm(dec_last, dec_gain[2], dec_shift[2])
    upstream = out_grad[0].astype(jnp.float32)
    grad_last, gain_two, shift_two = norm_back(dec_last, dec_gain[2], dec_shift[2], upstream)
    branch_low = to_low(grad_last)
    dec_down_g = weight_grad(dec_act, branch_low)
    dec_down_bias_g = jnp.sum(branch_low.astype(jnp.float32), axis=0)
    inner_low = to_low(gelu_back(dec_inner, input_grad(branch_low, dec_down)))
    dec_up_g = weight_grad(second_low, inner_low)
    dec_up_bias_g = jnp.sum(inner_low.astype(jnp.float32), axis=0)
    grad_second = grad_last + input_grad(inner_low, dec_up)
    grad_cross_pre, gain_one, shift_one = norm_back(
        cross_pre, dec_gain[1], dec_shift[1], grad_second
    )
    mixed_low = to_low(grad_cross_pre)
    cross_out_g = weight_grad(cross_att_low, mixed_low)
    cross_att_grad = to_low(input_grad(mixed_low, cross_out))
    cross_query_grad, mem_key_sum, mem_value_sum = attention_back(
        split_heads(cross_queries),
        split_heads(mem_keys_all),
        split_heads(mem_values_all),
        tgt_ids,
        src_ids_all,
        False,
        split_heads(cross_att_grad),
        cross_att,
        cross_lse,
    )
    mem_key_low = to_low(mem_key_sum)
    mem_value_low = to_low(mem_value_sum)
    cross_query_low = to_low(cross_query_grad.reshape(rows, -1))
    cross_qkv_g = jnp.stack(
        [
            weight_grad(first_low, cross_query_low),
            weight_grad(memory_low, mem_key_low),
            weight_grad(memory_low, mem_value_low),
        ]
    )
    grad_first = grad_cross_pre + input_grad(cross_query_low, cross_qkv[0])
    grad_dec_pre, gain_zero, shift_zero = norm_back(dec_pre, dec_gain[0], dec_shift[0], grad_first)
    self_low = to_low(grad_dec_pre)
    dec_out_g = weight_grad(dec_att_low, self_low)
    dec_att_grad = to_low(input_grad(self_low, dec_out))
    dec_query_grad, dec_key_sum, dec_value_sum = attention_back(
        split_heads(dec_queries),
        split_heads(dec_keys_all),
        split_heads(dec_values_all),
        tgt_ids,
        tgt_ids_all,
        True,
        split_heads(dec_att_grad),
        dec_att,
        dec_lse,
    )
    dec_query_low = to_low(dec_query_grad.reshape(rows, -1))
    dec_key_low = to_low(dec_key_sum)
    dec_value_low = to_low(dec_value_sum)
    dec_qkv_g = jnp.stack(
        [
            weight_grad(tgt_rows, dec_query_low),
            weight_grad(tgt_rows, dec_key_low),
            weight_grad(tgt_rows, dec_value_low),
        ]
    )
    tgt_grad = (
        grad_dec_pre
        + input_grad(dec_query_low, dec_qkv[0])
        + input_grad(dec_key_low, dec_qkv[1])
        + input_grad(dec_value_low, dec_qkv[2])
    )
    dec_gain_g = jnp.stack([gain_zero, gain_one, gain_two])
    dec_shift_g = jnp.stack([shift_zero, shift_one, shift_two])
    grad_memory = input_grad(mem_key_low, cross_qkv[1]) + input_grad(mem_value_low, cross_qkv[2])
    grad_enc_last, enc_gain_one, enc_shift_one = norm_back(
        enc_last, enc_gain[1], enc_shift[1], grad_memory
    )
    enc_branch_low = to_low(grad_enc_last)
    enc_down_g = weight_grad(enc_act, enc_branch_low)
    enc_down_bias_g = jnp.sum(enc_branch_low.astype(jnp.float32), axis=0)
    enc_inner_low = to_low(gelu_back(enc_inner, input_grad(enc_branch_low, enc_down)))
    enc_up_g = weight_grad(hidden_low, enc_inner_low)
    enc_up_bias_g = jnp.sum(enc_inner_low.astype(jnp.float32), axis=0)
    grad_hidden = grad_enc_last + input_grad(enc_inner_low, enc_up)
    grad_enc_pre, enc_gain_zero, enc_shift_zero = norm_back(
        enc_pre, enc_gain[0], enc_shift[0], grad_hidden
    )
    enc_mixed_low = to_low(grad_enc_pre)
    enc_out_g = weight_grad(enc_att_low, enc_mixed_low)
    enc_att_grad = to_low(input_grad(enc_mixed_low, enc_out))
    enc_query_grad, enc_key_sum, enc_value_sum = attention_back(
        split_heads(enc_queries),
        split_heads(enc_keys_all),
        split_heads(enc_values_all),
        src_ids,
        src_ids_all,
        False,
        split_heads(enc_att_grad),
        enc_att,
        enc_lse,
    )
    enc_query_low = to_low(enc_query_grad.reshape(rows, -1))
    enc_key_low = to_low(enc_key_sum)
    enc_value_low = to_low(enc_value_sum)
    enc_qkv_g = jnp.stack(
        [
            weight_grad(src_rows, enc_query_low),
            weight_grad(src_rows, enc_key_low),
            weight_grad(src_rows, enc_value_low),
        ]
    )
    src_grad = (
        grad_enc_pre
        + input_grad(enc_query_low, enc_qkv[0])
        + input_grad(enc_key_low, enc_qkv[1])
        + input_grad(enc_value_low, enc_qkv[2])
    )
    enc_gain_g = jnp.stack([enc_gain_zero, enc_gain_one])
    enc_shift_g = jnp.stack([enc_shift_zero, enc_shift_one])
    all_rows = (
        lax.psum_scatter(
            enc_qkv_g.astype(jnp.bfloat16), "seq", scatter_dimension=1, tiled=True
        ).astype(jnp.float32),
        lax.psum_scatter(
            enc_out_g.astype(jnp.bfloat16), "seq", scatter_dimension=0, tiled=True
        ).astype(jnp.float32),
        lax.psum_scatter(
            enc_up_g.astype(jnp.bfloat16), "seq", scatter_dimension=0, tiled=True
        ).astype(jnp.float32),
        lax.psum_scatter(
            enc_down_g.astype(jnp.bfloat16), "seq", scatter_dimension=0, tiled=True
        ).astype(jnp.float32),
        lax.psum_scatter(
            dec_qkv_g.astype(jnp.bfloat16), "seq", scatter_dimension=1, tiled=True
        ).astype(jnp.float32),
        lax.psum_scatter(
            dec_out_g.astype(jnp.bfloat16), "seq", scatter_dimension=0, tiled=True
        ).astype(jnp.float32),
        lax.psum_scatter(
            cross_qkv_g.astype(jnp.bfloat16), "seq", scatter_dimension=1, tiled=True
        ).astype(jnp.float32),
        lax.psum_scatter(
            cross_out_g.astype(jnp.bfloat16), "seq", scatter_dimension=0, tiled=True
        ).astype(jnp.float32),
        lax.psum_scatter(
            dec_up_g.astype(jnp.bfloat16), "seq", scatter_dimension=0, tiled=True
        ).astype(jnp.float32),
        lax.psum_scatter(
            dec_down_g.astype(jnp.bfloat16), "seq", scatter_dimension=0, tiled=True
        ).astype(jnp.float32),
    )
    reduced = (
        lax.psum_scatter(
            all_rows[0].astype(jnp.bfloat16), "batch", scatter_dimension=2, tiled=True
        ).astype(jnp.float32),
        lax.psum_scatter(
            all_rows[1].astype(jnp.bfloat16), "batch", scatter_dimension=1, tiled=True
        ).astype(jnp.float32),
        lax.psum_scatter(
            all_rows[2].astype(jnp.bfloat16), "batch", scatter_dimension=1, tiled=True
        ).astype(jnp.float32),
        lax.psum_scatter(
            all_rows[3].astype(jnp.bfloat16), "batch", scatter_dimension=1, tiled=True
        ).astype(jnp.float32),
        lax.psum_scatter(
            all_rows[4].astype(jnp.bfloat16), "batch", scatter_dimension=2, tiled=True
        ).astype(jnp.float32),
        lax.psum_scatter(
            all_rows[5].astype(jnp.bfloat16), "batch", scatter_dimension=1, tiled=True
        ).astype(jnp.float32),
        lax.psum_scatter(
            all_rows[6].astype(jnp.bfloat16), "batch", scatter_dimension=2, tiled=True
        ).astype(jnp.float32),
        lax.psum_scatter(
            all_rows[7].astype(jnp.bfloat16), "batch", scatter_dimension=1, tiled=True
        ).astype(jnp.float32),
        lax.psum_scatter(
            all_rows[8].astype(jnp.bfloat16), "batch", scatter_dimension=1, tiled=True
        ).astype(jnp.float32),
        lax.psum_scatter(
            all_rows[9].astype(jnp.bfloat16), "batch", scatter_dimension=1, tiled=True
        ).astype(jnp.float32),
    )
    vectors = lax.psum(
        (
            enc_up_bias_g,
            enc_down_bias_g,
            enc_gain_g,
            enc_shift_g,
            dec_up_bias_g,
            dec_down_bias_g,
            dec_gain_g,
            dec_shift_g,
        ),
        ("batch", "seq"),
    )
    return (
        to_low(decoded)[None],
        to_low(src_grad)[None],
        to_low(tgt_grad)[None],
        reduced[0],
        reduced[1],
        reduced[2],
        vectors[0],
        reduced[3],
        vectors[1],
        vectors[2],
        vectors[3],
        reduced[4],
        reduced[5],
        reduced[6],
        reduced[7],
        reduced[8],
        vectors[4],
        reduced[9],
        vectors[5],
        vectors[6],
        vectors[7],
    )


def general(mesh):
    placed = (
        P("batch", "seq", None),
        P("batch", "seq", None),
        P("batch", "seq"),
        P("batch", "seq"),
        P("batch", "seq", None),
        P(),
        P(),
        P(),
        P(),
        P(),
        P(),
        P(),
        P(),
        P(),
        P(),
        P(),
        P(),
        P(),
        P(),
        P(),
        P(),
        P(),
        P(),
    )
    return jax.shard_map(
        general_shards,
        mesh=mesh,
        in_specs=placed,
        out_specs=(
            P("batch", "seq", None),
            P("batch", "seq", None),
            P("batch", "seq", None),
            P(None, "seq", "batch"),
            P("seq", "batch"),
            P("seq", "batch"),
            P(),
            P("seq", "batch"),
            P(),
            P(),
            P(),
            P(None, "seq", "batch"),
            P("seq", "batch"),
            P(None, "seq", "batch"),
            P("seq", "batch"),
            P("seq", "batch"),
            P(),
            P("seq", "batch"),
            P(),
            P(),
            P(),
        ),
        check_vma=False,
    )


BATCH, SEQ = "batch", "seq"
CORE, X, Y, LOW, HIGH, SWAP = range(6)
ALL = (CORE, X, Y, LOW, HIGH)
TILE = 256
MESH = pl.DeviceIdType.MESH
VMEM = pl.BlockSpec(memory_space=pltpu.VMEM)
ANY = pl.BlockSpec(memory_space=pl.ANY)


def dot(left, right, left_dim=1, right_dim=0):
    return lax.dot_general(
        left, right, (((left_dim,), (right_dim,)), ((), ())), preferred_element_type=F32
    )


def block(index, size):
    return pl.ds(pl.multiple_of(index * size, size), size)


def normed(value):
    centred = value - jnp.mean(value, axis=-1, keepdims=True)
    scale = lax.rsqrt(jnp.mean(centred * centred, axis=-1, keepdims=True) + 1e-06)
    return centred * scale, scale


def normed_back(grad, unit, scale, gain):
    scaled = grad * gain
    first = jnp.mean(scaled, axis=-1, keepdims=True)
    second = jnp.mean(scaled * unit, axis=-1, keepdims=True)
    return scale * (scaled - first - unit * second)


def gelu_and_slope(inner):
    square = inner * inner
    bent = jnp.tanh(0.7978845608028654 * inner * (1.0 + 0.044715 * square))
    half = 0.5 * (1.0 + bent)
    slope = half + 0.5 * inner * (1.0 - bent * bent) * (
        0.7978845608028654 * (1.0 + 0.134145 * square)
    )
    return inner * half, slope


def column_sum(value):
    return jnp.sum(value, axis=0, keepdims=True)


def parts_of(up):
    return [slice(p * 512, (p + 1) * 512) for p in range(up.shape[1] // 512)]


def over_tiles(rows):
    def run(body):
        @pl.loop(0, rows // TILE, unroll=2)
        def _(tile):
            body(block(tile, TILE))

    return run


def places():
    row, s = lax.axis_index(BATCH), lax.axis_index(SEQ)
    core = lax.rem(row, 2)
    y = lax.rem(row // 2, 2)
    low = lax.rem(row // 4, 2)
    high = row // 8
    mine = (core, s, y, low, high + core - 2 * high * core)
    partner = (
        {BATCH: row + 1 - 2 * core},
        {SEQ: 1 - s},
        {BATCH: row + 2 - 4 * y},
        {BATCH: row + 4 - 8 * low},
        {BATCH: row + 8 - 16 * high},
        {BATCH: row - core + s, SEQ: core},
    )
    return mine, partner


def my_core():
    return places()[0][CORE]


def call_out(ways):
    mine, partner = places()
    barrier = pltpu.get_barrier_semaphore()
    for way in ways:
        pl.semaphore_signal(barrier, inc=1, device_id=partner[way], device_id_type=MESH)

    @pl.when(mine[CORE] != mine[X])
    def _():
        pl.semaphore_signal(barrier, inc=1, device_id=partner[SWAP], device_id_type=MESH)


def hear(ways):
    mine, _ = places()
    away = mine[CORE] + mine[X] - 2 * mine[CORE] * mine[X]
    pl.semaphore_wait(pltpu.get_barrier_semaphore(), len(ways) + away)


def sending(source, target, sems, slot, way):
    return pltpu.make_async_remote_copy(
        src_ref=source,
        dst_ref=target,
        send_sem=sems.at[0, slot],
        recv_sem=sems.at[1, slot],
        device_id=places()[1][way],
        device_id_type=MESH,
    )


def start_swap(source, target, sems, slot):
    mine, _ = places()

    @pl.when(mine[CORE] != mine[X])
    def _():
        sending(source, target, sems, slot, SWAP).start()

    @pl.when(mine[CORE] == mine[X])
    def _():
        pltpu.make_async_copy(source, target, sems.at[0, slot]).start()


def wait_swap(source, target, sems, slot):
    mine, _ = places()

    @pl.when(mine[CORE] != mine[X])
    def _():
        sending(source, target, sems, slot, SWAP).wait()

    @pl.when(mine[CORE] == mine[X])
    def _():
        pltpu.make_async_copy(source, target, sems.at[0, slot]).wait()


class RowSwap:
    def __init__(self, source, target, pieces, sems, slot, near_sem):
        mine, _ = places()
        self.here = mine[CORE] == mine[X]
        self.pieces = range(len(pieces))
        whole = target(mine[X], None)
        self.near = lambda: pltpu.make_async_copy(source, whole, near_sem)
        self.early = lambda: sending(source, whole, sems, slot, CORE)
        self.across = lambda k: sending(source.at[pieces[k]], target(mine[X], pieces[k]), sems, slot + 1 + k, SWAP)

        def onward(k):
            ref = target(mine[CORE], pieces[k])
            return sending(ref, ref, sems, slot + 1 + len(pieces) + k, CORE)

        self.onward = onward

    def start(self):
        @pl.when(self.here)
        def _():
            self.near().start()
            self.early().start()

        @pl.when(jnp.logical_not(self.here))
        def _():
            for k in self.pieces:
                self.across(k).start()

    def pass_on(self):
        @pl.when(jnp.logical_not(self.here))
        def _():
            for k in self.pieces:
                self.across(k).wait()
                self.onward(k).start()

    def finish(self):
        @pl.when(self.here)
        def _():
            self.near().wait()
            self.early().wait_send()
            for k in self.pieces:
                self.onward(k).wait_recv()

        @pl.when(jnp.logical_not(self.here))
        def _():
            self.early().wait_recv()
            for k in self.pieces:
                self.onward(k).wait_send()


def part_of(ref, axis, index):
    return ref.at[(slice(None),) * axis + (index,)]


class Halving:
    def __init__(self, source, axis, way, got, total, sems, slot, far=False):
        mine, _ = places()
        kept = part_of(source, axis, mine[way])
        self.kept, self.got, self.total = (total if far else kept), got, total
        self.sent = lambda: sending(part_of(source, axis, 1 - mine[way]), got, sems, slot, way)
        self.near = (lambda: pltpu.make_async_copy(kept, total, sems.at[2, slot])) if far else None

    def start(self):
        self.sent().start()
        if self.near is not None:
            self.near().start()

    def finish(self):
        if self.near is not None:
            self.near().wait()
        self.sent().wait()
        if self.total.dtype == F32:
            self.total[...] = self.kept[...].astype(F32) + self.got[...].astype(F32)
        else:
            self.total[...] = self.kept[...] + self.got[...]


class Across:
    def __init__(self, sums, got, sems, slot):
        self.sums, self.got = sums, got
        self.sent = lambda: sending(sums.at[1], got, sems, slot, CORE)

    def start(self):
        self.sent().start()

    def finish(self):
        self.sent().wait()
        self.sums[0] = self.sums[0] + self.got[...]


class Copies:
    def __init__(self, pairs, sems, first=0):
        self.copies = [
            (lambda source=source, target=target, place=place: pltpu.make_async_copy(source, target, sems.at[first + place]))
            for place, (source, target) in enumerate(pairs)
        ]

    def start(self):
        for copy in self.copies:
            copy().start()

    def wait(self):
        for copy in self.copies:
            copy().wait()


def attend_begin(r, att):
    heads = r.queries.shape[1]
    width = heads * HEAD_DIM
    columns = block(my_core(), width)
    q_from, k_from = att, att + att // 2
    q_side, k_side = jnp.minimum(att, 1), att * (2 - att)
    which = lax.rem(att, 2)
    place = lax.broadcasted_iota(jnp.int32, (HEAD_DIM, TILE), 0)
    ones = jnp.ones((TILE, HEAD_DIM), BF)
    half_tiles = r.ids.shape[3] // TILE

    @pl.loop(0, r.x_all.shape[1] // TILE, unroll=4)
    def _(tile):
        here = block(tile, TILE)
        lanes = block(lax.rem(tile, half_tiles), TILE)
        q_ids = r.ids[q_side, tile // half_tiles, :, lanes]
        k_ids = r.ids[k_side, tile // half_tiles, :, lanes]
        asks = jnp.where(place == q_ids, 1.0, 0.0).T.astype(BF)
        bars = jnp.where((place != k_ids) & (place < 3), NEGATIVE, 0.0).T.astype(BF)
        left_q, left_k = r.x_all[q_from, here, :], r.x_all[k_from, here, :]
        q_tile = dot(left_q, r.weights[att, 0, :, columns]).astype(BF) * BF(0.125)
        k_tile = dot(left_k, r.weights[att, 1, :, columns]).astype(BF)
        v_tile = dot(left_k, r.weights[att, 2, :, columns]).astype(BF)
        for head in range(heads):
            part = slice(head * HEAD_DIM, (head + 1) * HEAD_DIM)
            r.queries[which, head, here, :] = jnp.concatenate([q_tile[:, part], asks], axis=1)
            r.keys[which, head, here, :] = jnp.concatenate([k_tile[:, part], bars], axis=1)
            r.values[which, head, here, :] = jnp.concatenate([v_tile[:, part], ones], axis=1)


def attend_heads(r, which, first, causal):
    length = r.queries.shape[2]
    lower = lax.broadcasted_iota(jnp.int32, (TILE, TILE), 0) >= lax.broadcasted_iota(jnp.int32, (TILE, TILE), 1)
    work = [(head, tile) for head in range(2) for tile in range(length // TILE)]

    def seen(tile):
        return (tile + 1) * TILE if causal else length

    def scores_of(head, tile):
        here = slice(tile * TILE, (tile + 1) * TILE)
        scores = dot(r.queries[which, first + head, here, :], r.keys[which, first + head, : seen(tile), :], 1, 1)
        if not causal:
            return scores
        last = jnp.where(lower, scores[:, seen(tile) - TILE :], NEGATIVE)
        return last if tile == 0 else jnp.concatenate([scores[:, : seen(tile) - TILE], last], axis=1)

    scores = scores_of(*work[0])
    for place, (head, tile) in enumerate(work):
        here = slice(tile * TILE, (tile + 1) * TILE)
        later = scores_of(*work[place + 1]) if place + 1 < len(work) else None
        low = jnp.exp(scores - jnp.max(scores, axis=-1, keepdims=True)).astype(BF)
        r.chances[head, here, : seen(tile)] = low
        r.outs[which, first + head, here, :] = dot(low, r.values[which, first + head, : seen(tile), :])
        scores = later


def forward_body(r):
    step = pl.program_id(0)
    core = my_core()
    att = jnp.minimum(step // 2, 2)
    rows = r.source.shape[0]
    heads = r.outs.shape[1]
    width = heads * HEAD_DIM
    sems = r.sems

    def rows_of(side):
        def target(half, piece):
            first = half * rows if piece is None else half * rows + piece.start
            count = rows if piece is None else piece.size
            return r.x_all.at[side, pl.ds(pl.multiple_of(first, count), count)]

        return target

    def ids_of(side):
        return lambda half, piece: r.ids.at[side, half]

    quarters = [pl.ds(k * rows // 4, rows // 4) for k in range(4)]
    source = RowSwap(r.source, rows_of(0), quarters, sems, 0, r.near_sems.at[0])
    target = RowSwap(r.target, rows_of(1), quarters, sems, 9, r.near_sems.at[1])
    one = [pl.ds(0, 1)]
    ids = (
        RowSwap(r.source_ids, ids_of(0), one, sems, 18, r.near_sems.at[2]),
        RowSwap(r.target_ids, ids_of(1), one, sems, 21, r.near_sems.at[3]),
    )
    first_across = sending(r.x_all.at[2, block(core, rows)], r.x_all.at[2, block(core, rows)], sems, 24, CORE)

    def att_across(index):
        return sending(r.att_send.at[index], r.att_all.at[index, :, block(core, width)], sems, 25 + index, CORE)

    def memory_across(tile):
        ref = r.x_all.at[3, pl.ds(pl.multiple_of(core * rows + tile * TILE, TILE), TILE)]
        return sending(ref, ref, sems, 28 + tile, CORE)

    loads = Copies(
        [
            (r.enc_qkv, r.weights.at[0]), (r.dec_qkv, r.weights.at[1]), (r.cross_qkv, r.weights.at[2]),
            (r.enc_out_far, r.enc_out), (r.dec_out_far, r.dec_out), (r.up_far, r.up), (r.down_far, r.down),
        ],
        r.load_sems,
    )

    def saved(index):
        which = index % 2
        return Copies(
            [
                (r.queries.at[which], r.queries_far.at[index]), (r.keys.at[which], r.keys_far.at[index]),
                (r.values.at[which], r.values_far.at[index]), (r.outs.at[which], r.outs_far.at[index]),
            ],
            r.save_sems,
            index * 4,
        )

    kept = Copies(
        [
            (r.unit0, r.unit0_far), (r.scale0, r.scale0_far), (r.unit1, r.unit1_far), (r.scale1, r.scale1_far),
            (r.hidden_low, r.hidden_far), (r.act, r.act_far), (r.slope, r.slope_far), (r.first, r.first_far),
            (r.first_unit, r.first_unit_far), (r.first_scale, r.first_scale_far), (r.x_all, r.x_far),
        ],
        r.save_sems,
        12,
    )
    att_kept = Copies([(r.att_all, r.att_far)], r.save_sems, 23)

    @pl.when(step == 0)
    def _():
        call_out((CORE,))
        loads.start()
        hear((CORE,))
        for one_side in ids:
            one_side.start()
        source.start()
        target.start()
        start_swap(r.upstream, r.upstream_there, sems, 30)
        for one_side in ids:
            one_side.pass_on()
        source.pass_on()
        for one_side in ids:
            one_side.finish()
        source.finish()
        loads.wait()

    @pl.when(step == 2)
    def _():
        target.pass_on()
        target.finish()

    @pl.when(step == 5)
    def _():
        saved(0).wait()
        first_across.wait()

        @pl.loop(0, rows // TILE)
        def _(tile):
            memory_across(tile).wait()

        kept.start()

    @pl.when((step == 0) | (step == 2) | (step == 5))
    def _():
        attend_begin(r, att)

    @pl.when((step < 2) | (step > 4))
    def _():
        attend_heads(r, 0, 2 * lax.rem(step - att // 2, 2), False)

    @pl.when((step == 2) | (step == 3))
    def _():
        attend_heads(r, 1, 2 * (step - 2), True)

    @pl.when((step == 1) | (step == 3) | (step == 6))
    def _():
        for half in (1 - core, core):
            there = block(half, rows)
            parts = [r.outs[lax.rem(att, 2), head, there, :] for head in range(heads)]
            joined = jnp.concatenate([part[:, :HEAD_DIM] / part[:, HEAD_DIM:] for part in parts], axis=1).astype(BF)
            if half is core:
                r.att_all[att, :, block(core, width)] = joined
            else:
                r.att_send[att] = joined
                att_across(att).start()

    for index, last in enumerate((1, 3, 6)):

        @pl.when(step == last)
        def _(index=index):
            saved(index).start()

    @pl.when(step == 4)
    def _():
        att_across(0).wait()
        att_across(1).wait()

        @over_tiles(rows)
        def _(here):
            own = pl.ds(pl.multiple_of(core * rows + here.start, TILE), TILE)
            unit, scale = normed(r.x_all[1, own, :].astype(F32) + dot(r.att_all[1, here, :], r.dec_out[...]))
            r.first_unit[here, :] = unit
            r.first_scale[here, :] = scale
            value = unit * r.dec_gain[0:1, :] + r.dec_shift[0:1, :]
            r.first[here, :] = value
            r.x_all[2, own, :] = value.astype(BF)

        first_across.start()

        @pl.loop(0, rows // TILE)
        def _(tile):
            here = block(tile, TILE)
            own = pl.ds(pl.multiple_of(core * rows + tile * TILE, TILE), TILE)
            unit, scale = normed(r.x_all[0, own, :].astype(F32) + dot(r.att_all[0, here, :], r.enc_out[...]))
            r.unit0[here, :] = unit
            r.scale0[here, :] = scale
            hidden = unit * r.enc_gain[0:1, :] + r.enc_shift[0:1, :]
            low = hidden.astype(BF)
            r.hidden_low[here, :] = low
            for part in parts_of(r.up):
                value, bend = gelu_and_slope(dot(low, r.up[:, part]) + r.up_bias[:, part])
                r.slope[here, part] = bend.astype(BF)
                r.act[here, part] = value.astype(BF)
            unit, scale = normed(hidden + dot(r.act[here, :], r.down[...]) + r.down_bias[...])
            r.unit1[here, :] = unit
            r.scale1[here, :] = scale
            r.x_all[3, own, :] = (unit * r.enc_gain[1:2, :] + r.enc_shift[1:2, :]).astype(BF)
            memory_across(tile).start()

    @pl.when(step == 6)
    def _():
        kept.wait()
        saved(1).wait()
        wait_swap(r.upstream, r.upstream_there, sems, 30)
        att_across(2).wait()
        att_kept.start()
        saved(2).wait()
        att_kept.wait()


def back_begin(r, which):
    heads = r.queries.shape[1]
    width = heads * HEAD_DIM
    lane = lax.rem(lax.broadcasted_iota(jnp.int32, (TILE, width), 1), HEAD_DIM)
    same_head = (
        lax.broadcasted_iota(jnp.int32, (width, width), 0) // HEAD_DIM
        == lax.broadcasted_iota(jnp.int32, (width, width), 1) // HEAD_DIM
    ).astype(BF)

    @over_tiles(r.queries.shape[2])
    def _(here):
        grad = r.grad_all[which, here, :].astype(F32)
        lows, boths = [], []
        for head in range(heads):
            out = r.outs[which, head, here, :]
            over = 1.0 / out[:, HEAD_DIM:]
            low = (grad[:, head * HEAD_DIM : (head + 1) * HEAD_DIM] * over).astype(BF)
            lows.append(low)
            boths.append(low.astype(F32) * (out[:, :HEAD_DIM] * over))
        both = jnp.concatenate(boths, axis=1)
        high = both.astype(BF)
        rest = (both - high.astype(F32)).astype(BF)
        settle = -dot(high, same_head) - dot(rest, same_head)
        first = settle.astype(BF).astype(F32)
        second = (settle - first).astype(BF).astype(F32)
        extra = jnp.where(lane == 0, first, jnp.where(lane == 1, second, jnp.where(lane == 2, settle - first - second, 0.0)))
        extra = extra.astype(BF)
        for head in range(heads):
            r.grads[head, here, :] = jnp.concatenate(
                [lows[head], extra[:, head * HEAD_DIM : (head + 1) * HEAD_DIM]], axis=1
            )


def back_head(r, which, head, causal):
    length = r.queries.shape[2]
    count = length // TILE

    def seen(tile):
        return (tile + 1) * TILE if causal else length

    def change_of(tile):
        here = slice(tile * TILE, (tile + 1) * TILE)
        return dot(r.grads[head, here, :], r.values[which, head, : seen(tile), :], 1, 1)

    change = change_of(0)
    for tile in range(count):
        here = slice(tile * TILE, (tile + 1) * TILE)
        later = change_of(tile + 1) if tile + 1 < count else None
        low = (r.chances[0, here, : seen(tile)].astype(F32) * change).astype(BF)
        r.score_grads[here, : seen(tile)] = low
        r.dq[head, here, :] = (dot(low, r.keys[which, head, : seen(tile), :])[:, :HEAD_DIM] * 0.125).astype(BF)
        change = later
    for tile in range(count if causal else 1):
        here = slice(tile * TILE, (tile + 1) * TILE) if causal else slice(0, length)
        below = slice(tile * TILE, length)
        r.dv[block(head, HEAD_DIM), here] = dot(
            r.grads[head, below, :HEAD_DIM], r.chances[0, below, here], 0, 0
        )
        r.dk[block(head, HEAD_DIM), here] = dot(
            r.queries[which, head, below, :HEAD_DIM], r.score_grads[below, here], 0, 0
        )


class BackEnd:
    def __init__(self, r, which, unit, q_from, k_from, sems):
        self.r, self.q_from, self.k_from = r, q_from, k_from
        core = my_core()
        rows = r.d_full.shape[2]
        width = r.d_all.shape[2]
        lanes = block(core, width)
        self.other = lambda: sending(
            r.d_all.at[:, block(1 - core, rows)], r.d_full.at[which, :, :, lanes], sems, 2 * which, CORE
        )
        self.own = lambda: pltpu.make_async_copy(
            r.d_all.at[:, block(core, rows)], r.d_full.at[which, :, :, lanes], sems.at[2, 2 * which]
        )
        below = pl.ds(32, 96)
        self.across = lambda: sending(r.shares.at[1], unit.at[:, :, :, 1, below], sems, 2 * which + 1, CORE)
        self.along = lambda: pltpu.make_async_copy(r.shares.at[0], unit.at[:, :, :, 0, below], sems.at[2, 2 * which + 1])

    def start(self):
        r = self.r
        core = my_core()
        rows, heads = r.d_full.shape[2], r.dq.shape[0]

        @pl.loop(0, 2, unroll=2)
        def _(half):
            there = block(half, rows)
            r.d_all[0, there, :] = jnp.concatenate([r.dq[head, there, :] for head in range(heads)], axis=1)
            r.d_all[1, there, :] = r.dk[:, there].T.astype(BF)
            r.d_all[2, there, :] = r.dv[:, there].T.astype(BF)

        self.other().start()
        self.own().start()

        @pl.loop(0, 3, unroll=3)
        def _(kind):
            x_from = jnp.where(kind == 0, self.q_from, self.k_from)
            low = dot(r.d_all[kind], r.x_all[x_from], 0, 0).astype(BF)
            for part in range(low.shape[0] // 32):
                z_low, y, kept = part >> 2, (part >> 1) & 1, part & 1
                for s in range(2):
                    r.shares[core if kept == 0 else 1 - core, s, y, z_low, block(kind, 32), :] = low[
                        part * 32 : (part + 1) * 32, s * 256 : (s + 1) * 256
                    ]

        self.across().start()
        self.along().start()

    def wait_grads(self):
        self.own().wait()
        self.other().wait()

    def wait_sums(self):
        self.along().wait()
        self.across().wait()


BIG = (2, 2, 2, 2, 128, 256)
MID = BIG[1:]
LESS = BIG[2:]
LEAST = BIG[3:]
OUT = (2, 2, 2, 2, 32, 256)
HALF = (2, 2, 2, 2, 64, 256)


def sum_up(sums, inner_low, entering):
    core = my_core()

    @pl.loop(0, 4, unroll=4)
    def _(z):
        for y in range(2):
            low = dot(inner_low[:, block(z * 2 + y, 256)], entering[...], 0, 0).astype(BF)
            high = z // 2
            for kept in range(2):
                for s in range(2):
                    sums[
                        core if kept == 0 else 1 - core, s, y, lax.rem(z, 2), 1 - high if kept else high, :, :
                    ] = low[kept * 128 : (kept + 1) * 128, s * 256 : (s + 1) * 256]


def sum_down(sums, branch_low, act):
    core = my_core()

    @pl.loop(0, act.shape[1] // 512, unroll=4)
    def _(column):
        for index in range(2):
            low = dot(branch_low[:, index * 256 : (index + 1) * 256], act[:, block(column, 512)], 0, 0).astype(BF)
            for part in range(8):
                place = index * 8 + part
                z, y, kept = place >> 2, (place >> 1) & 1, place & 1
                for piece in range(2):
                    slot = lax.rem(column, 2) * 2 + piece
                    sums[
                        core if kept == 0 else 1 - core, column // 2, y, z & 1, (z >> 1) ^ kept, block(slot, 32), :
                    ] = low[part * 32 : (part + 1) * 32, piece * 256 : (piece + 1) * 256]


def sum_out(sums, mixed_low, att):
    core = my_core()

    @pl.loop(0, 2, unroll=2)
    def _(s):
        low = dot(mixed_low[...], att[:, block(s, 256)], 0, 0).astype(BF)
        for place in range(16):
            z, y, kept = place >> 2, (place >> 1) & 1, place & 1
            sums[core if kept == 0 else 1 - core, s, y, z & 1, (z >> 1) ^ kept, :, :] = low[
                place * 32 : (place + 1) * 32, :
            ]


def split_halvings(unit, bufs, totals, sems, slot):
    upper, lower = unit.at[:, :, :, :, pl.ds(0, 64)], unit.at[:, :, :, :, pl.ds(64, 64)]
    return (
        Halving(upper, 0, X, bufs.at[0], totals.at[0], sems, slot),
        Halving(lower, 1, Y, bufs.at[1], totals.at[1], sems, slot + 1),
    )


def join_halvings(source, less, both, last, final, total, sems, slot):
    return (
        Halving(source.at[0], 0, Y, less.at[0], both.at[0], sems, slot),
        Halving(source.at[1], 0, X, less.at[1], both.at[1], sems, slot + 1),
        Halving(both, 1, LOW, last.at[0], last.at[1], sems, slot + 2),
        Halving(last.at[1], 1, HIGH, final, total, sems, slot + 3),
    )


def decode_last_layers(r):
    @over_tiles(r.first.shape[0])
    def _(here):
        unit, scale = normed(r.first[here, :] + dot(r.att[here, :], r.out_w[...]))
        r.unit0[here, :] = unit
        r.scale0[here, :] = scale
        second = unit * r.dec_gain[1:2, :] + r.dec_shift[1:2, :]
        low = second.astype(BF)
        r.entering[here, :] = low
        for part in parts_of(r.up):
            value, slope = gelu_and_slope(dot(low, r.up[:, part]) + r.up_bias[:, part])
            r.act[here, part] = value.astype(BF)
            r.inner_low[here, part] = slope.astype(BF)
        unit, scale = normed(second + dot(r.act[here, :], r.down[...]) + r.down_bias[...])
        r.unit1[here, :] = unit
        r.scale1[here, :] = scale
        r.decoded[here, :] = (unit * r.dec_gain[2:3, :] + r.dec_shift[2:3, :]).astype(BF)
        r.grad[here, :] = r.upstream[here, :].astype(F32)


def layers_back(r, which):
    vectors = r.vectors

    def add(place, value):
        vectors[which, place : place + 1, :] += value

    @over_tiles(r.grad.shape[0])
    def _(here):
        grad, unit = r.grad[here, :], r.unit1[here, :]
        add(7, column_sum(grad * unit))
        add(8, column_sum(grad))
        grad = normed_back(grad, unit, r.scale1[here, :], r.gains[which, 1:2, :])
        branch = grad.astype(BF)
        r.branch_low[here, :] = branch
        add(4, column_sum(branch.astype(F32)))
        for place, part in enumerate(parts_of(r.up)):
            inner = (dot(branch, r.down[part, :], 1, 1) * r.inner_low[here, part].astype(F32)).astype(BF)
            r.inner_low[here, part] = inner
            add(place, column_sum(inner.astype(F32)))
        grad = grad + dot(r.inner_low[here, :], r.up[...], 1, 1)
        unit = r.unit0[here, :]
        add(5, column_sum(grad * unit))
        add(6, column_sum(grad))
        grad = normed_back(grad, unit, r.scale0[here, :], r.gains[which, 0:1, :])
        r.pre[which, here, :] = grad
        mixed = grad.astype(BF)
        r.mixed_low[here, :] = mixed
        r.att_grad[here, :] = dot(mixed, r.out_w[...], 1, 1).astype(BF)


def middle_body(r):
    step = pl.program_id(0)
    mine, _ = places()
    core = mine[CORE]
    sems = r.sems
    rows, width = r.first.shape[0], r.d_all.shape[2]
    cross = 2
    before = Copies(
        [(r.first_far, r.first), (r.att_far.at[2], r.att), (r.upstream_far, r.upstream), (r.cross_out, r.out_w)], r.load_sems
    )
    dec_layer = Copies([(r.dec_up, r.up), (r.dec_down, r.down)], r.load_sems, 4)
    around = Copies(
        [
            (r.queries_far.at[pl.ds(2, 1)], r.queries), (r.keys_far.at[pl.ds(2, 1)], r.keys),
            (r.values_far.at[pl.ds(2, 1)], r.values), (r.outs_far.at[pl.ds(2, 1)], r.outs), (r.x_far.at[pl.ds(2, 2)], r.x_all),
        ],
        r.load_sems,
        6,
    )
    first_layer = Copies(
        [
            (r.cross_qkv, r.cross_w), (r.dec_out, r.dec_w), (r.first_unit_far, r.first_unit),
            (r.first_scale_far, r.first_scale), (r.att_far.at[1], r.dec_att),
        ],
        r.load_sems,
        11,
    )
    enc_layer = Copies(
        [
            (r.enc_up, r.up), (r.enc_down, r.down), (r.enc_out, r.out_w), (r.unit0_far, r.unit0), (r.scale0_far, r.scale0),
            (r.unit1_far, r.unit1), (r.scale1_far, r.scale1), (r.hidden_far, r.entering), (r.act_far, r.act),
            (r.slope_far, r.inner_low), (r.att_far.at[0], r.att),
        ],
        r.load_sems,
        16,
    )
    down_x = Halving(r.down_sums.at[0], 0, X, r.got_a, r.mid_a, sems, 0)
    up_y = Halving(r.up_sums.at[0], 1, Y, r.got_b, r.mid_b, sems, 1)
    down_y = Halving(r.mid_a, 0, Y, r.got_c, r.pair.at[0], sems, 2)
    up_x = Halving(r.mid_b, 0, X, r.got_d, r.pair.at[1], sems, 3)
    down_low = Halving(r.pair.at[0], 0, LOW, r.got_e.at[0], r.mid_e, sems, 4)
    up_low = Halving(r.pair.at[1], 0, LOW, r.got_e.at[1], r.up_rest, sems, 17)
    down_high = Halving(r.mid_e, 0, HIGH, r.got_f, r.dec_down_sum, sems, 5)
    cross_x, cross_y = split_halvings(r.unit, r.got_g, r.cross_half, sems, 6)
    end = BackEnd(r, 0, r.unit, 0, 1, r.end_sems)
    shared = [
        Across(r.down_sums, r.down_got, sems, 8),
        Across(r.up_sums, r.up_got, sems, 9),
        Across(r.out_sums, r.out_got, sems, 10),
    ]
    dec_shared = Across(r.dec_out_sums, r.dec_out_got, sems, 11)
    lanes, other_lanes = block(core, width), block(1 - core, width)
    there = block(core, rows)

    def grads_of(source, target, slot):
        across = sending(source.at[:, other_lanes], target.at[there], sems, slot, CORE)
        stay = pltpu.make_async_copy(source.at[:, lanes], target.at[there], sems.at[2, slot])
        return across, stay

    cross_grads = grads_of(r.att_grad, r.grad_all.at[0], 12)
    dec_grads = grads_of(r.dec_att_grad, r.grads_far.at[1], 13)
    enc_grads = grads_of(r.att_grad, r.grads_far.at[0], 14)
    beside = pltpu.make_async_copy(r.out_sums.at[0], r.unit.at[:, :, :, :, pl.ds(0, 32)], sems.at[2, 15])
    results = Copies(
        [
            (r.down_sums.at[0], r.down_unit), (r.up_sums.at[0], r.up_unit), (r.out_sums.at[0], r.out_units.at[0]),
            (r.dec_out_sums.at[0], r.out_units.at[1]), (r.pre, r.pre_far),
        ],
        r.load_sems,
        27,
    )

    @pl.when(step == 0)
    def _():
        call_out(ALL)
        before.start()
        dec_layer.start()
        around.start()
        r.vectors[...] = jnp.zeros_like(r.vectors)
        for place, (ref, row) in enumerate(((r.dec_gain, 1), (r.dec_gain, 2), (r.enc_gain, 0), (r.enc_gain, 1))):
            r.gains[place // 2, place % 2 : place % 2 + 1, :] = ref[row : row + 1, :]
        before.wait()
        dec_layer.wait()
        decode_last_layers(r)
        hear(ALL)
        start_swap(r.decoded, r.decoded_there, sems, 16)

    @pl.when(step == 6)
    def _():
        beside.wait()
        end.wait_sums()
        cross_y.start()
        cross_x.start()
        end.wait_grads()

        @over_tiles(rows)
        def _(here):
            r.grad[here, :] = dot(r.d_full[0, 1, here, :], r.cross_w[1], 1, 1) + dot(
                r.d_full[0, 2, here, :], r.cross_w[2], 1, 1
            )
            grad = r.pre[0, here, :] + dot(r.d_full[0, 0, here, :], r.cross_w[0], 1, 1)
            unit = r.first_unit[here, :]
            r.vectors[2, 0:1, :] += column_sum(grad * unit)
            r.vectors[2, 1:2, :] += column_sum(grad)
            grad = normed_back(grad, unit, r.first_scale[here, :], r.dec_gain[0:1, :])
            r.pre[0, here, :] = grad
            mixed = grad.astype(BF)
            r.dec_mixed[here, :] = mixed
            r.dec_att_grad[here, :] = dot(mixed, r.dec_w[...], 1, 1).astype(BF)

        for copy in dec_grads:
            copy.start()
        sum_out(r.dec_out_sums, r.dec_mixed, r.dec_att)
        dec_shared.start()

    @pl.when(step == 7)
    def _():
        down_y.finish()
        down_low.start()
        enc_layer.wait()

    @pl.when((step == 1) | (step == 7))
    def _():
        layers_back(r, step // 7)

    @pl.when(step == 1)
    def _():
        for copy in cross_grads:
            copy.start()

    @pl.when(step == 7)
    def _():
        for copy in enc_grads:
            copy.start()
        down_low.finish()
        down_high.start()
        up_x.finish()
        up_low.start()

    @pl.when((step == 1) | (step == 7))
    def _():
        sum_down(r.down_sums, r.branch_low, r.act)
        shared[0].start()
        sum_up(r.up_sums, r.inner_low, r.entering)
        shared[1].start()
        shared[0].finish()

        @pl.when(step == 1)
        def _():
            down_x.start()

        sum_out(r.out_sums, r.mixed_low, r.att)
        shared[2].start()
        shared[1].finish()

        @pl.when(step == 1)
        def _():
            up_y.start()

        shared[2].finish()

    @pl.when(step == 1)
    def _():
        beside.start()
        for copy in cross_grads:
            copy.wait()
        around.wait()
        enc_layer.start()
        first_layer.start()
        back_begin(r, 0)

    @pl.when(step == 5)
    def _():
        down_x.finish()
        down_y.start()

    @pl.when((step >= 2) & (step < 6))
    def _():
        back_head(r, 0, step - 2, False)

    @pl.when(step == 5)
    def _():
        first_layer.wait()
        end.start()
        up_y.finish()
        up_x.start()

    @pl.when(step == 7)
    def _():
        dec_shared.finish()
        results.start()
        for copy in (*dec_grads, *enc_grads):
            copy.wait()
        down_high.finish()
        up_low.finish()
        cross_y.finish()
        cross_x.finish()
        results.wait()
        wait_swap(r.decoded, r.decoded_there, sems, 16)


def last_body(r):
    step = pl.program_id(0)
    which = step // 4
    mine, _ = places()
    sems = r.sems
    rows = r.pre.shape[1]

    def side(att):
        return Copies(
            [
                (r.queries_far.at[att], r.queries.at[att]), (r.keys_far.at[att], r.keys.at[att]),
                (r.values_far.at[att], r.values.at[att]), (r.outs_far.at[att], r.outs.at[att]),
                (r.grads_far.at[att], r.grad_all.at[att]), (r.x_far.at[att], r.x_all.at[att]),
                ((r.enc_qkv, r.dec_qkv)[att], r.weights.at[att]), (r.pre_far.at[1 - att], r.pre.at[att]),
                (r.out_units.at[att], r.units.at[att, :, :, :, :, pl.ds(0, 32)]),
            ],
            r.load_sems,
            att * 9,
        )

    def layer_steps(unit, bufs, total, slot, ways):
        left, steps, source = [X, Y, LOW, HIGH], [], unit
        for place, way in enumerate(ways):
            got, kept = (bufs[2 * place], bufs[2 * place + 1]) if place < 3 else (bufs[6], total)
            steps.append(Halving(source, left.index(way), way, got, kept, sems, slot + place, far=place == 0))
            left.remove(way)
            source = kept
        return steps

    down = layer_steps(r.down_unit, r.down_bufs, r.enc_sums.at[0], 0, (X, Y, LOW, HIGH))
    up = layer_steps(r.up_unit, r.up_bufs, r.enc_sums.at[1], 4, (Y, LOW, HIGH, X))
    cross = join_halvings(r.cross_half, *r.cross_bufs, r.cross_sum, sems, 8)
    dec_up_high = Halving(r.up_rest, 0, HIGH, r.rest_got, r.dec_up_sum, sems, 17)
    enc_got, enc_mid, *enc_bufs = r.enc_bufs
    enc_x, enc_y = split_halvings(r.units.at[0], enc_got, enc_mid, sems, 18)
    enc_att = join_halvings(enc_mid, *enc_bufs, r.enc_att_sum, sems, 20)
    dec_got, dec_mid, *dec_bufs = r.dec_bufs
    dec_x, dec_y = split_halvings(r.units.at[1], dec_got, dec_mid, sems, 24)
    dec_att = join_halvings(dec_mid, *dec_bufs, r.dec_att_sum, sems, 26)
    vector_ways = (X, Y, CORE, LOW, HIGH)

    def vector_parts(place):
        source = r.vectors if place == 0 else r.vector_mid.at[place - 1]
        total = r.vector_sum if place == 4 else r.vector_mid.at[place]
        copy = sending(source, r.vector_got.at[place], sems, 12 + place, vector_ways[place])
        return source, r.vector_got.at[place], total, copy

    def vector_start(place):
        vector_parts(place)[3].start()

    def vector_finish(place):
        source, got, total, copy = vector_parts(place)
        copy.wait()
        total[...] = source[...] + got[...]

    end = BackEnd(r, which, r.units.at[which], which, which, r.end_sems)

    def row_grads(index):
        @over_tiles(rows)
        def _(here):
            total = r.pre[index, here, :]
            for kind in range(3):
                total = total + dot(r.d_full[index, kind, here, :], r.weights[index, kind], 1, 1)
            r.row_grad[index, here, :] = total.astype(BF)

    src_swap = (r.row_grad.at[0], r.src_there, sems, 30)
    tgt_swap = (r.row_grad.at[1], r.tgt_there, sems, 31)

    @pl.when(step == 0)
    def _():
        call_out(ALL)
        side(0).start()
        side(1).start()
        side(0).wait()
        hear(ALL)
        vector_start(0)
        dec_up_high.start()
        cross[0].start()
        cross[1].start()
        down[0].start()
        up[0].start()

    @pl.when(step == 4)
    def _():
        side(1).wait()
        BackEnd(r, 0, r.units.at[0], 0, 0, r.end_sems).wait_sums()
        enc_x.start()
        enc_y.start()

    @pl.when((step == 0) | (step == 4))
    def _():
        back_begin(r, which)

    @pl.when(step == 1)
    def _():
        vector_finish(0)
        vector_start(1)

    @pl.when(step == 2)
    def _():
        dec_up_high.finish()
        cross[0].finish()
        cross[1].finish()
        cross[2].start()

    @pl.when(step == 4)
    def _():
        BackEnd(r, 0, r.units.at[0], 0, 0, r.end_sems).wait_grads()
        row_grads(0)
        start_swap(*src_swap)
        down[0].finish()
        down[1].start()
        up[0].finish()
        up[1].start()

    @pl.when(step == 6)
    def _():
        vector_finish(2)
        vector_start(3)

    @pl.when(step == 5)
    def _():
        vector_finish(1)
        vector_start(2)
        cross[3].finish()

    @pl.when(step == 7)
    def _():
        enc_x.finish()
        enc_att[0].start()
        enc_y.finish()
        enc_att[1].start()

    @pl.when(step < 4)
    def _():
        back_head(r, 0, step, False)

    @pl.when(step >= 4)
    def _():
        back_head(r, 1, step - 4, True)

    @pl.when((step == 3) | (step == 7))
    def _():
        end.start()

    @pl.when(step == 3)
    def _():
        cross[2].finish()
        cross[3].start()

    @pl.when(step == 7)
    def _():
        up[1].finish()
        up[2].start()
        end_of_dec = BackEnd(r, 1, r.units.at[1], 1, 1, r.end_sems)
        end_of_dec.wait_sums()
        dec_x.start()
        dec_y.start()
        end_of_dec.wait_grads()
        row_grads(1)
        down[1].finish()
        down[2].start()
        enc_att[0].finish()
        enc_att[1].finish()
        enc_att[2].start()
        vector_finish(3)
        vector_start(4)
        down[2].finish()
        down[3].start()
        dec_x.finish()
        dec_att[0].start()
        dec_y.finish()
        dec_att[1].start()
        start_swap(*tgt_swap)
        up[2].finish()
        up[3].start()
        enc_att[2].finish()
        enc_att[3].start()
        dec_att[0].finish()
        dec_att[1].finish()
        dec_att[2].start()
        vector_finish(4)
        down[3].finish()
        up[3].finish()
        enc_att[3].finish()
        dec_att[2].finish()
        dec_att[3].start()
        dec_att[3].finish()
        wait_swap(*src_swap)
        wait_swap(*tgt_swap)


def finish_body(r):
    r.decoded_out[...] = r.decoded[...]
    r.src_out[...] = r.src[...]
    r.tgt_out[...] = r.tgt[...]
    for sums, down in ((r.dec_down_sum[...], r.dec_down), (r.enc_sums[0], r.enc_down)):
        for slot in range(4):
            down[:, slot * 256 : (slot + 1) * 256] = sums[slot * 32 : (slot + 1) * 32, :]
    r.dec_up[...] = r.dec_up_sum[...].T
    r.enc_up[...] = r.enc_sums[1].T
    cross, enc_att, dec_att = [
        jnp.concatenate([one[0], one[1]], axis=0) for one in (r.cross_sum, r.enc_att_sum, r.dec_att_sum)
    ]
    for sums, out, qkv in (
        (cross, r.cross_out, r.cross_qkv),
        (enc_att, r.enc_out, r.enc_qkv),
        (dec_att, r.dec_out, r.dec_qkv),
    ):
        out[...] = sums[:32]
        for kind in range(3):
            qkv[kind] = sums[32 + kind * 32 : 64 + kind * 32]
    vectors = r.vectors
    for which, up_bias, down_bias in ((0, r.dec_up_bias, r.dec_down_bias), (1, r.enc_up_bias, r.enc_down_bias)):
        for part in range(4):
            up_bias[:, part * 512 : (part + 1) * 512] = vectors[which, part : part + 1, :]
        down_bias[...] = vectors[which, 4:5, :]
    for ref, found in (
        (r.dec_gain, ((2, 0), (0, 5), (0, 7))),
        (r.dec_shift, ((2, 1), (0, 6), (0, 8))),
        (r.enc_gain, ((1, 5), (1, 7))),
        (r.enc_shift, ((1, 6), (1, 8))),
    ):
        for index, (which, place) in enumerate(found):
            ref[index : index + 1, :] = vectors[which, place : place + 1, :]


def launch(body, micros, grid, meeting, ins, far, blocks, outs, far_outs, scratch):
    def once(shape):
        rank = len(shape)
        return pl.BlockSpec(shape, lambda step: (0,) * rank, pipeline_mode=pl.Buffered(1))

    names, arrays, in_specs, out_names, shapes, out_specs = [], [], [], [], [], []
    for name, array in {**ins, **far}.items():
        names.append(name)
        arrays.append(array)
        in_specs.append(once(array.shape) if name in ins else ANY)
    for name, (shape, kind) in {**outs, **far_outs}.items():
        out_names.append(name)
        shapes.append(jax.ShapeDtypeStruct(shape, kind))
        out_specs.append(once(shape) if name in outs else ANY)
    for name, (array, part, index, is_out) in blocks.items():
        spec = pl.BlockSpec(part, index)
        if is_out:
            out_names.append(name)
            shapes.append(jax.ShapeDtypeStruct(*array))
            out_specs.append(spec)
        else:
            names.append(name)
            arrays.append(array)
            in_specs.append(spec)
    every = (*names, *out_names, *scratch)

    def kernel(*refs):
        body(types.SimpleNamespace(**dict(zip(every, refs))))

    results = pl.pallas_call(
        kernel,
        grid=(grid,),
        out_shape=shapes,
        in_specs=in_specs,
        out_specs=out_specs,
        scratch_shapes=list(scratch.values()),
        compiler_params=pltpu.CompilerParams(
            vmem_limit_bytes=60 * 2**20, collective_id=meeting, has_side_effects=meeting is not None
        ),
        cost_estimate=pl.CostEstimate(flops=int(micros * 1e9), bytes_accessed=0, transcendentals=0),
        name=body.__name__,
    )(*arrays)
    return types.SimpleNamespace(**dict(zip(out_names, results)))


def low(*shape):
    return pltpu.VMEM(shape, BF)


def wide(*shape):
    return pltpu.VMEM(shape, F32)


def fast_shards(source, target, source_ids, target_ids, out_grad, *params):
    (
        enc_qkv, enc_out, enc_up, enc_up_bias, enc_down, enc_down_bias, enc_gain, enc_shift, dec_qkv, dec_out,
        cross_qkv, cross_out, dec_up, dec_up_bias, dec_down, dec_down_bias, dec_gain, dec_shift,
    ) = params
    source, target, upstream = source[0], target[0], out_grad[0]
    rows, size = source.shape
    length, inner, width = 2 * rows, enc_up.shape[1], size // 2
    heads = width // HEAD_DIM
    sem = pltpu.SemaphoreType.DMA
    full, thin, low_full, low_inner = ((rows, size), F32), ((rows, 1), F32), ((rows, size), BF), ((rows, inner), BF)
    biases = [one[None, :] for one in (enc_up_bias, enc_down_bias, dec_up_bias, dec_down_bias)]
    enc_up_b, enc_down_b, dec_up_b, dec_down_b = biases
    head_block = (1, length, length)
    per_head = (heads, length, 2 * HEAD_DIM)

    f = launch(
        forward_body,
        60,
        7,
        0,
        dict(up_bias=enc_up_b, down_bias=enc_down_b, enc_gain=enc_gain, enc_shift=enc_shift, dec_gain=dec_gain, dec_shift=dec_shift),
        dict(
            source=source, target=target, source_ids=source_ids, target_ids=target_ids, upstream=upstream,
            enc_qkv=enc_qkv, dec_qkv=dec_qkv, cross_qkv=cross_qkv, enc_out_far=enc_out, dec_out_far=dec_out,
            up_far=enc_up, down_far=enc_down,
        ),
        dict(
            chances=(
                ((3 * heads, length, length), BF),
                (2, length, length),
                lambda step: (jnp.where(step < 4, step, jnp.maximum(step - 1, 4)), 0, 0),
                True,
            )
        ),
        {},
        dict(
            x_far=((4, length, size), BF), upstream_there=low_full, queries_far=((3, *per_head), BF),
            keys_far=((3, *per_head), BF), values_far=((3, *per_head), BF), outs_far=((3, *per_head), F32),
            att_far=((3, rows, size), BF), unit0_far=full, scale0_far=thin, unit1_far=full, scale1_far=thin,
            hidden_far=low_full, act_far=low_inner, slope_far=low_inner, first_far=full, first_unit_far=full,
            first_scale_far=thin,
        ),
        dict(
            sems=sem((2, 31)), near_sems=sem((4,)), load_sems=sem((7,)), save_sems=sem((24,)),
            x_all=low(4, length, size), ids=pltpu.VMEM((2, 2, 1, rows), jnp.int32), weights=low(3, 3, size, size),
            queries=low(2, *per_head), keys=low(2, *per_head), values=low(2, *per_head),
            outs=wide(2, *per_head), att_all=low(3, rows, size),
            att_send=low(3, rows, width), enc_out=low(size, size), dec_out=low(size, size), up=low(size, inner),
            down=low(inner, size), unit0=wide(rows, size), scale0=wide(rows, 1), unit1=wide(rows, size),
            scale1=wide(rows, 1), hidden_low=low(rows, size), act=low(rows, inner), slope=low(rows, inner),
            first=wide(rows, size), first_unit=wide(rows, size), first_scale=wide(rows, 1),
        ),
    )
    work = dict(
        grads=low(*per_head), score_grads=low(length, length), dq=low(heads, length, HEAD_DIM), dk=wide(width, length),
        dv=wide(width, length), d_all=low(3, length, width), shares=low(2, 2, 2, 2, 96, 256), end_sems=sem((3, 4)),
    )
    one_sum = ((128, 256), F32)
    sums_out = ((2, 128, 256), F32)
    halves = ((2, 64, 256), F32)
    m = launch(
        middle_body,
        50,
        8,
        1,
        dict(dec_gain=dec_gain, dec_shift=dec_shift, enc_gain=enc_gain, up_bias=dec_up_b, down_bias=dec_down_b),
        dict(
            first_far=f.first_far, att_far=f.att_far, upstream_far=f.upstream_there, cross_out=cross_out, dec_up=dec_up,
            dec_down=dec_down, queries_far=f.queries_far, keys_far=f.keys_far, values_far=f.values_far,
            outs_far=f.outs_far, x_far=f.x_far, cross_qkv=cross_qkv, dec_out=dec_out, first_unit_far=f.first_unit_far,
            first_scale_far=f.first_scale_far, enc_up=enc_up, enc_down=enc_down, enc_out=enc_out,
            unit0_far=f.unit0_far, scale0_far=f.scale0_far, unit1_far=f.unit1_far, scale1_far=f.scale1_far,
            hidden_far=f.hidden_far, act_far=f.act_far, slope_far=f.slope_far,
        ),
        dict(chances=(f.chances, head_block, lambda step: (8 + jnp.clip(step - 2, 0, 3), 0, 0), False)),
        dict(dec_down_sum=one_sum, up_rest=(LEAST, BF), cross_half=(HALF, BF), vectors=((3, 16, size), F32)),
        dict(
            decoded_there=low_full, grads_far=((2, length, width), BF), down_unit=(BIG, BF), up_unit=(BIG, BF),
            out_units=((2, *OUT), BF), pre_far=((2, rows, size), F32),
        ),
        dict(
            sems=sem((3, 18)), load_sems=sem((32,)), **work,
            first=wide(rows, size), att=low(rows, size), upstream=low(rows, size), out_w=low(size, size),
            up=low(size, inner), down=low(inner, size), queries=low(1, *per_head), keys=low(1, *per_head),
            values=low(1, *per_head), outs=wide(1, *per_head), x_all=low(2, length, size), cross_w=low(3, size, size),
            dec_w=low(size, size), first_unit=wide(rows, size), first_scale=wide(rows, 1), dec_att=low(rows, size),
            unit0=wide(rows, size), scale0=wide(rows, 1), unit1=wide(rows, size), scale1=wide(rows, 1),
            entering=low(rows, size), act=low(rows, inner), inner_low=low(rows, inner), branch_low=low(rows, size),
            mixed_low=low(rows, size), att_grad=low(rows, size), dec_att_grad=low(rows, size), dec_mixed=low(rows, size),
            grad=wide(rows, size), pre=wide(2, rows, size), gains=wide(2, 2, size), decoded=low(rows, size),
            grad_all=low(1, length, width), d_full=low(1, 3, rows, size), unit=low(*BIG),
            down_sums=low(2, *BIG), up_sums=low(2, *BIG), out_sums=low(2, *OUT), dec_out_sums=low(2, *OUT),
            down_got=low(*BIG), up_got=low(*BIG), out_got=low(*OUT), dec_out_got=low(*OUT),
            got_a=low(*MID), mid_a=low(*MID), got_b=low(*MID), mid_b=low(*MID), got_c=low(*LESS), got_d=low(*LESS),
            pair=low(2, *LESS), got_e=low(2, *LEAST), mid_e=low(*LEAST), got_f=low(128, 256), got_g=low(*HALF),
        ),
    )
    less, least = (2, 2, 2, 64, 256), (2, 64, 256)
    down_bufs = [low(*MID), low(*MID), low(*LESS), low(*LESS), low(*LEAST), low(*LEAST), low(128, 256)]
    up_bufs = [low(*MID), low(*MID), low(*LESS), low(*LESS), low(*LEAST), low(*LEAST), low(128, 256)]
    join_bufs = [low(*less), low(*less), low(*less), low(*least)]
    split_bufs = [low(*HALF), low(*HALF), *join_bufs]
    b = launch(
        last_body,
        60,
        8,
        2,
        dict(cross_half=m.cross_half, up_rest=m.up_rest, vectors=m.vectors),
        dict(
            queries_far=f.queries_far, keys_far=f.keys_far, values_far=f.values_far, outs_far=f.outs_far, x_far=f.x_far,
            grads_far=m.grads_far, enc_qkv=enc_qkv, dec_qkv=dec_qkv, pre_far=m.pre_far, out_units=m.out_units,
            down_unit=m.down_unit, up_unit=m.up_unit,
        ),
        dict(chances=(f.chances, head_block, lambda step: (step, 0, 0), False)),
        dict(
            enc_sums=sums_out, dec_up_sum=one_sum, cross_sum=halves, enc_att_sum=halves, dec_att_sum=halves,
            vector_sum=((3, 16, size), F32),
        ),
        dict(src_there=low_full, tgt_there=low_full),
        dict(
            sems=sem((3, 32)), load_sems=sem((18,)), **work,
            queries=low(2, *per_head), keys=low(2, *per_head), values=low(2, *per_head), outs=wide(2, *per_head),
            grad_all=low(2, length, width), x_all=low(2, length, size), weights=low(2, 3, size, size),
            pre=wide(2, rows, size), d_full=low(2, 3, rows, size), units=low(2, *BIG), row_grad=low(2, rows, size),
            vector_got=wide(5, 3, 16, size), vector_mid=wide(4, 3, 16, size), down_bufs=down_bufs, up_bufs=up_bufs,
            enc_bufs=split_bufs, cross_bufs=join_bufs, dec_bufs=split_bufs, rest_got=low(128, 256),
        ),
    )
    cut3, cut, pair, triple = ((3, 32, 256), F32), ((32, 256), F32), ((2, size), F32), ((3, size), F32)
    up_cut, down_cut, up_b, down_b = ((256, 128), F32), ((32, 1024), F32), ((1, inner), F32), ((1, size), F32)
    o = launch(
        finish_body,
        2,
        1,
        None,
        dict(
            decoded=m.decoded_there, src=b.src_there, tgt=b.tgt_there, dec_down_sum=m.dec_down_sum, dec_up_sum=b.dec_up_sum,
            enc_sums=b.enc_sums,
            cross_sum=b.cross_sum, enc_att_sum=b.enc_att_sum, dec_att_sum=b.dec_att_sum, vectors=b.vector_sum,
        ),
        {},
        {},
        dict(
            decoded_out=low_full, src_out=low_full, tgt_out=low_full, enc_qkv=cut3, enc_out=cut, enc_up=up_cut,
            enc_up_bias=up_b, enc_down=down_cut, enc_down_bias=down_b, enc_gain=pair, enc_shift=pair, dec_qkv=cut3,
            dec_out=cut, cross_qkv=cut3, cross_out=cut, dec_up=up_cut, dec_up_bias=up_b, dec_down=down_cut,
            dec_down_bias=down_b, dec_gain=triple, dec_shift=triple,
        ),
        {},
        {},
    )

    def turned(value):
        return jnp.swapaxes(value, -1, -2)

    return (
        o.decoded_out[None], o.src_out[None], o.tgt_out[None], turned(o.enc_qkv), turned(o.enc_out), o.enc_up,
        o.enc_up_bias[0], turned(o.enc_down), o.enc_down_bias[0], o.enc_gain, o.enc_shift, turned(o.dec_qkv),
        turned(o.dec_out), turned(o.cross_qkv), turned(o.cross_out), o.dec_up, o.dec_up_bias[0], turned(o.dec_down),
        o.dec_down_bias[0], o.dec_gain, o.dec_shift,
    )


def solution(mesh):
    if mesh.shape[SEQ] != 2 or mesh.shape[BATCH] != 16:
        return general(mesh)
    tokens = P(BATCH, SEQ, None)
    ids = P(BATCH, SEQ)
    cut, cut3 = P(SEQ, BATCH), P(None, SEQ, BATCH)
    return jax.shard_map(
        fast_shards,
        mesh=mesh,
        in_specs=(tokens, tokens, ids, ids, tokens) + (P(),) * 18,
        out_specs=(
            tokens, tokens, tokens, cut3, cut, cut, P(), cut, P(), P(), P(), cut3, cut, cut3, cut, cut, P(), cut,
            P(), P(), P(),
        ),
        check_vma=False,
    )
```

```python
import types

import jax
import jax.numpy as jnp
from jax import lax
from jax.experimental import pallas as pl
from jax.experimental.pallas import tpu as pltpu
from jax.sharding import PartitionSpec as P

HEAD_DIM = 64
NEGATIVE = -1e30
BF = jnp.bfloat16
F32 = jnp.float32


def layer_norm(value, gain, shift):
    mean = jnp.mean(value, axis=-1, keepdims=True)
    centred = value - mean
    spread = jnp.mean(centred * centred, axis=-1, keepdims=True)
    return centred * lax.rsqrt(spread + 1e-06) * gain + shift


def norm_back(value, gain, shift, grad):
    _, pull = jax.vjp(layer_norm, value, gain, shift)
    return pull(grad)


def gelu_back(inner, grad):
    _, pull = jax.vjp(jax.nn.gelu, inner)
    return pull(grad)[0]


def matmul(left, right):
    return jnp.dot(left, right, preferred_element_type=jnp.float32)


def weight_grad(inputs, grad):
    return lax.dot_general(
        inputs, grad, (((0,), (0,)), ((), ())), preferred_element_type=jnp.float32
    )


def input_grad(grad, weight):
    return lax.dot_general(
        grad, weight, (((1,), (1,)), ((), ())), preferred_element_type=jnp.float32
    )


def to_low(value):
    return value.astype(jnp.bfloat16)


def split_heads(value):
    return value.reshape(value.shape[0], -1, HEAD_DIM)


def block_live(query_ids, key_ids, offset, block, rows, causal):
    first_key = lax.dynamic_index_in_dim(key_ids, block * rows, 0, keepdims=False)
    last_key = lax.dynamic_index_in_dim(key_ids, block * rows + rows - 1, 0, keepdims=False)
    live = (first_key <= query_ids[rows - 1]) & (query_ids[0] <= last_key)
    if causal:
        live = live & (block * rows <= offset + rows - 1)
    return live


def block_scores(queries, keys_all, query_ids, key_ids, offset, block, causal):
    rows = queries.shape[0]
    key_block = lax.dynamic_slice_in_dim(keys_all, block * rows, rows, 0)
    id_block = lax.dynamic_slice_in_dim(key_ids, block * rows, rows, 0)
    scores = (
        jnp.einsum("qhe,khe->hqk", queries, key_block, preferred_element_type=jnp.float32) * 0.125
    )
    allowed = query_ids[:, None] == id_block[None, :]
    if causal:
        positions = jnp.arange(rows, dtype=jnp.int32)
        allowed = allowed & ((offset + positions)[:, None] >= (block * rows + positions)[None, :])
    allowed = allowed[None]
    return (jnp.where(allowed, scores, NEGATIVE), allowed, key_block)


def attend_forward(queries, keys_all, values_all, query_ids, key_ids, offset, causal):
    rows = queries.shape[0]
    heads_count = queries.shape[1]
    count = keys_all.shape[0] // rows

    def first_pass(block, carry):

        def first_compute(state):
            largest, total = state
            scores, allowed, _ = block_scores(
                queries, keys_all, query_ids, key_ids, offset, block, causal
            )
            newest = jnp.maximum(largest, jnp.max(scores, axis=-1))
            terms = jnp.where(allowed, jnp.exp(scores - newest[..., None]), 0.0)
            return (newest, total * jnp.exp(largest - newest) + jnp.sum(terms, axis=-1))

        live = block_live(query_ids, key_ids, offset, block, rows, causal)
        return lax.cond(live, first_compute, lambda state: state, carry)

    initial = (
        jnp.full((heads_count, rows), NEGATIVE, jnp.float32),
        jnp.zeros((heads_count, rows), jnp.float32),
    )
    largest, total = lax.fori_loop(0, count, first_pass, initial)
    log_total = largest + jnp.log(total)

    def second_pass(block, carry):

        def second_compute(output):
            scores, allowed, _ = block_scores(
                queries, keys_all, query_ids, key_ids, offset, block, causal
            )
            value_block = lax.dynamic_slice_in_dim(values_all, block * rows, rows, 0)
            chances = jnp.where(allowed, jnp.exp(scores - log_total[..., None]), 0.0)
            return output + jnp.einsum(
                "hqk,khe->qhe", to_low(chances), value_block, preferred_element_type=jnp.float32
            )

        live = block_live(query_ids, key_ids, offset, block, rows, causal)
        return lax.cond(live, second_compute, lambda output: output, carry)

    output = lax.fori_loop(0, count, second_pass, jnp.zeros(queries.shape, jnp.float32))
    return (output, log_total)


def attend_backward(
    queries, keys_all, values_all, query_ids, key_ids, offset, causal, grad_out, settle, log_total
):
    rows = queries.shape[0]
    count = keys_all.shape[0] // rows

    def step_block(block, carry):

        def step_compute(state):
            query_grad, key_grads, value_grads = state
            scores, allowed, key_block = block_scores(
                queries, keys_all, query_ids, key_ids, offset, block, causal
            )
            value_block = lax.dynamic_slice_in_dim(values_all, block * rows, rows, 0)
            chances = jnp.where(allowed, jnp.exp(scores - log_total[..., None]), 0.0)
            chance_grad = jnp.einsum(
                "qhe,khe->hqk", grad_out, value_block, preferred_element_type=jnp.float32
            )
            score_grad = to_low(chances * (chance_grad - settle[..., None]))
            query_grad = (
                query_grad
                + jnp.einsum(
                    "hqk,khe->qhe", score_grad, key_block, preferred_element_type=jnp.float32
                )
                * 0.125
            )
            key_part = (
                jnp.einsum("hqk,qhe->khe", score_grad, queries, preferred_element_type=jnp.float32)
                * 0.125
            )
            value_part = jnp.einsum(
                "hqk,qhe->khe", to_low(chances), grad_out, preferred_element_type=jnp.float32
            )
            key_grads = lax.dynamic_update_slice_in_dim(key_grads, key_part, block * rows, 0)
            value_grads = lax.dynamic_update_slice_in_dim(value_grads, value_part, block * rows, 0)
            return (query_grad, key_grads, value_grads)

        live = block_live(query_ids, key_ids, offset, block, rows, causal)
        return lax.cond(live, step_compute, lambda state: state, carry)

    initial = (
        jnp.zeros(queries.shape, jnp.float32),
        jnp.zeros(keys_all.shape, jnp.float32),
        jnp.zeros(values_all.shape, jnp.float32),
    )
    return lax.fori_loop(0, count, step_block, initial)


def attention_back(
    queries, keys_all, values_all, query_ids, key_ids_all, causal, grad_out, output, log_total
):
    rows = queries.shape[0]
    offset = lax.axis_index("seq") * rows
    settle = jnp.einsum("qhe,qhe->hq", grad_out.astype(jnp.float32), output)
    query_grad, key_terms, value_terms = attend_backward(
        queries,
        keys_all,
        values_all,
        query_ids,
        key_ids_all,
        offset,
        causal,
        grad_out,
        settle,
        log_total,
    )
    key_sum, value_sum = (
        lax.psum_scatter(
            key_terms.reshape(key_terms.shape[0], -1).astype(jnp.bfloat16),
            "seq",
            scatter_dimension=0,
            tiled=True,
        ).astype(jnp.float32),
        lax.psum_scatter(
            value_terms.reshape(value_terms.shape[0], -1).astype(jnp.bfloat16),
            "seq",
            scatter_dimension=0,
            tiled=True,
        ).astype(jnp.float32),
    )
    return (query_grad, key_sum, value_sum)


def general_shards(
    source,
    target,
    source_ids,
    target_ids,
    out_grad,
    enc_qkv,
    enc_out,
    enc_up,
    enc_up_bias,
    enc_down,
    enc_down_bias,
    enc_gain,
    enc_shift,
    dec_qkv,
    dec_out,
    cross_qkv,
    cross_out,
    dec_up,
    dec_up_bias,
    dec_down,
    dec_down_bias,
    dec_gain,
    dec_shift,
):
    src_rows = source[0]
    tgt_rows = target[0]
    src_ids = source_ids[0]
    tgt_ids = target_ids[0]
    rows = src_rows.shape[0]
    offset = lax.axis_index("seq") * rows
    enc_queries = to_low(matmul(src_rows, enc_qkv[0]))
    enc_keys = to_low(matmul(src_rows, enc_qkv[1]))
    enc_values = to_low(matmul(src_rows, enc_qkv[2]))
    enc_keys_all, enc_values_all, src_ids_all = (
        lax.all_gather(enc_keys, "seq", axis=0, tiled=True),
        lax.all_gather(enc_values, "seq", axis=0, tiled=True),
        lax.all_gather(src_ids, "seq", axis=0, tiled=True),
    )
    enc_att, enc_lse = attend_forward(
        split_heads(enc_queries),
        split_heads(enc_keys_all),
        split_heads(enc_values_all),
        src_ids,
        src_ids_all,
        offset,
        False,
    )
    enc_att_low = to_low(enc_att.reshape(rows, -1))
    enc_pre = src_rows.astype(jnp.float32) + matmul(enc_att_low, enc_out)
    hidden = layer_norm(enc_pre, enc_gain[0], enc_shift[0])
    hidden_low = to_low(hidden)
    enc_inner = matmul(hidden_low, enc_up) + enc_up_bias
    enc_act = to_low(jax.nn.gelu(enc_inner))
    enc_last = hidden + matmul(enc_act, enc_down) + enc_down_bias
    memory = layer_norm(enc_last, enc_gain[1], enc_shift[1])
    memory_low = to_low(memory)
    mem_keys = to_low(matmul(memory_low, cross_qkv[1]))
    mem_values = to_low(matmul(memory_low, cross_qkv[2]))
    mem_keys_all, mem_values_all = (
        lax.all_gather(mem_keys, "seq", axis=0, tiled=True),
        lax.all_gather(mem_values, "seq", axis=0, tiled=True),
    )
    dec_queries = to_low(matmul(tgt_rows, dec_qkv[0]))
    dec_keys = to_low(matmul(tgt_rows, dec_qkv[1]))
    dec_values = to_low(matmul(tgt_rows, dec_qkv[2]))
    dec_keys_all, dec_values_all, tgt_ids_all = (
        lax.all_gather(dec_keys, "seq", axis=0, tiled=True),
        lax.all_gather(dec_values, "seq", axis=0, tiled=True),
        lax.all_gather(tgt_ids, "seq", axis=0, tiled=True),
    )
    dec_att, dec_lse = attend_forward(
        split_heads(dec_queries),
        split_heads(dec_keys_all),
        split_heads(dec_values_all),
        tgt_ids,
        tgt_ids_all,
        offset,
        True,
    )
    dec_att_low = to_low(dec_att.reshape(rows, -1))
    dec_pre = tgt_rows.astype(jnp.float32) + matmul(dec_att_low, dec_out)
    first = layer_norm(dec_pre, dec_gain[0], dec_shift[0])
    first_low = to_low(first)
    cross_queries = to_low(matmul(first_low, cross_qkv[0]))
    cross_att, cross_lse = attend_forward(
        split_heads(cross_queries),
        split_heads(mem_keys_all),
        split_heads(mem_values_all),
        tgt_ids,
        src_ids_all,
        offset,
        False,
    )
    cross_att_low = to_low(cross_att.reshape(rows, -1))
    cross_pre = first + matmul(cross_att_low, cross_out)
    second = layer_norm(cross_pre, dec_gain[1], dec_shift[1])
    second_low = to_low(second)
    dec_inner = matmul(second_low, dec_up) + dec_up_bias
    dec_act = to_low(jax.nn.gelu(dec_inner))
    dec_last = second + matmul(dec_act, dec_down) + dec_down_bias
    decoded = layer_norm(dec_last, dec_gain[2], dec_shift[2])
    upstream = out_grad[0].astype(jnp.float32)
    grad_last, gain_two, shift_two = norm_back(dec_last, dec_gain[2], dec_shift[2], upstream)
    branch_low = to_low(grad_last)
    dec_down_g = weight_grad(dec_act, branch_low)
    dec_down_bias_g = jnp.sum(branch_low.astype(jnp.float32), axis=0)
    inner_low = to_low(gelu_back(dec_inner, input_grad(branch_low, dec_down)))
    dec_up_g = weight_grad(second_low, inner_low)
    dec_up_bias_g = jnp.sum(inner_low.astype(jnp.float32), axis=0)
    grad_second = grad_last + input_grad(inner_low, dec_up)
    grad_cross_pre, gain_one, shift_one = norm_back(
        cross_pre, dec_gain[1], dec_shift[1], grad_second
    )
    mixed_low = to_low(grad_cross_pre)
    cross_out_g = weight_grad(cross_att_low, mixed_low)
    cross_att_grad = to_low(input_grad(mixed_low, cross_out))
    cross_query_grad, mem_key_sum, mem_value_sum = attention_back(
        split_heads(cross_queries),
        split_heads(mem_keys_all),
        split_heads(mem_values_all),
        tgt_ids,
        src_ids_all,
        False,
        split_heads(cross_att_grad),
        cross_att,
        cross_lse,
    )
    mem_key_low = to_low(mem_key_sum)
    mem_value_low = to_low(mem_value_sum)
    cross_query_low = to_low(cross_query_grad.reshape(rows, -1))
    cross_qkv_g = jnp.stack(
        [
            weight_grad(first_low, cross_query_low),
            weight_grad(memory_low, mem_key_low),
            weight_grad(memory_low, mem_value_low),
        ]
    )
    grad_first = grad_cross_pre + input_grad(cross_query_low, cross_qkv[0])
    grad_dec_pre, gain_zero, shift_zero = norm_back(dec_pre, dec_gain[0], dec_shift[0], grad_first)
    self_low = to_low(grad_dec_pre)
    dec_out_g = weight_grad(dec_att_low, self_low)
    dec_att_grad = to_low(input_grad(self_low, dec_out))
    dec_query_grad, dec_key_sum, dec_value_sum = attention_back(
        split_heads(dec_queries),
        split_heads(dec_keys_all),
        split_heads(dec_values_all),
        tgt_ids,
        tgt_ids_all,
        True,
        split_heads(dec_att_grad),
        dec_att,
        dec_lse,
    )
    dec_query_low = to_low(dec_query_grad.reshape(rows, -1))
    dec_key_low = to_low(dec_key_sum)
    dec_value_low = to_low(dec_value_sum)
    dec_qkv_g = jnp.stack(
        [
            weight_grad(tgt_rows, dec_query_low),
            weight_grad(tgt_rows, dec_key_low),
            weight_grad(tgt_rows, dec_value_low),
        ]
    )
    tgt_grad = (
        grad_dec_pre
        + input_grad(dec_query_low, dec_qkv[0])
        + input_grad(dec_key_low, dec_qkv[1])
        + input_grad(dec_value_low, dec_qkv[2])
    )
    dec_gain_g = jnp.stack([gain_zero, gain_one, gain_two])
    dec_shift_g = jnp.stack([shift_zero, shift_one, shift_two])
    grad_memory = input_grad(mem_key_low, cross_qkv[1]) + input_grad(mem_value_low, cross_qkv[2])
    grad_enc_last, enc_gain_one, enc_shift_one = norm_back(
        enc_last, enc_gain[1], enc_shift[1], grad_memory
    )
    enc_branch_low = to_low(grad_enc_last)
    enc_down_g = weight_grad(enc_act, enc_branch_low)
    enc_down_bias_g = jnp.sum(enc_branch_low.astype(jnp.float32), axis=0)
    enc_inner_low = to_low(gelu_back(enc_inner, input_grad(enc_branch_low, enc_down)))
    enc_up_g = weight_grad(hidden_low, enc_inner_low)
    enc_up_bias_g = jnp.sum(enc_inner_low.astype(jnp.float32), axis=0)
    grad_hidden = grad_enc_last + input_grad(enc_inner_low, enc_up)
    grad_enc_pre, enc_gain_zero, enc_shift_zero = norm_back(
        enc_pre, enc_gain[0], enc_shift[0], grad_hidden
    )
    enc_mixed_low = to_low(grad_enc_pre)
    enc_out_g = weight_grad(enc_att_low, enc_mixed_low)
    enc_att_grad = to_low(input_grad(enc_mixed_low, enc_out))
    enc_query_grad, enc_key_sum, enc_value_sum = attention_back(
        split_heads(enc_queries),
        split_heads(enc_keys_all),
        split_heads(enc_values_all),
        src_ids,
        src_ids_all,
        False,
        split_heads(enc_att_grad),
        enc_att,
        enc_lse,
    )
    enc_query_low = to_low(enc_query_grad.reshape(rows, -1))
    enc_key_low = to_low(enc_key_sum)
    enc_value_low = to_low(enc_value_sum)
    enc_qkv_g = jnp.stack(
        [
            weight_grad(src_rows, enc_query_low),
            weight_grad(src_rows, enc_key_low),
            weight_grad(src_rows, enc_value_low),
        ]
    )
    src_grad = (
        grad_enc_pre
        + input_grad(enc_query_low, enc_qkv[0])
        + input_grad(enc_key_low, enc_qkv[1])
        + input_grad(enc_value_low, enc_qkv[2])
    )
    enc_gain_g = jnp.stack([enc_gain_zero, enc_gain_one])
    enc_shift_g = jnp.stack([enc_shift_zero, enc_shift_one])
    all_rows = (
        lax.psum_scatter(
            enc_qkv_g.astype(jnp.bfloat16), "seq", scatter_dimension=1, tiled=True
        ).astype(jnp.float32),
        lax.psum_scatter(
            enc_out_g.astype(jnp.bfloat16), "seq", scatter_dimension=0, tiled=True
        ).astype(jnp.float32),
        lax.psum_scatter(
            enc_up_g.astype(jnp.bfloat16), "seq", scatter_dimension=0, tiled=True
        ).astype(jnp.float32),
        lax.psum_scatter(
            enc_down_g.astype(jnp.bfloat16), "seq", scatter_dimension=0, tiled=True
        ).astype(jnp.float32),
        lax.psum_scatter(
            dec_qkv_g.astype(jnp.bfloat16), "seq", scatter_dimension=1, tiled=True
        ).astype(jnp.float32),
        lax.psum_scatter(
            dec_out_g.astype(jnp.bfloat16), "seq", scatter_dimension=0, tiled=True
        ).astype(jnp.float32),
        lax.psum_scatter(
            cross_qkv_g.astype(jnp.bfloat16), "seq", scatter_dimension=1, tiled=True
        ).astype(jnp.float32),
        lax.psum_scatter(
            cross_out_g.astype(jnp.bfloat16), "seq", scatter_dimension=0, tiled=True
        ).astype(jnp.float32),
        lax.psum_scatter(
            dec_up_g.astype(jnp.bfloat16), "seq", scatter_dimension=0, tiled=True
        ).astype(jnp.float32),
        lax.psum_scatter(
            dec_down_g.astype(jnp.bfloat16), "seq", scatter_dimension=0, tiled=True
        ).astype(jnp.float32),
    )
    reduced = (
        lax.psum_scatter(
            all_rows[0].astype(jnp.bfloat16), "batch", scatter_dimension=2, tiled=True
        ).astype(jnp.float32),
        lax.psum_scatter(
            all_rows[1].astype(jnp.bfloat16), "batch", scatter_dimension=1, tiled=True
        ).astype(jnp.float32),
        lax.psum_scatter(
            all_rows[2].astype(jnp.bfloat16), "batch", scatter_dimension=1, tiled=True
        ).astype(jnp.float32),
        lax.psum_scatter(
            all_rows[3].astype(jnp.bfloat16), "batch", scatter_dimension=1, tiled=True
        ).astype(jnp.float32),
        lax.psum_scatter(
            all_rows[4].astype(jnp.bfloat16), "batch", scatter_dimension=2, tiled=True
        ).astype(jnp.float32),
        lax.psum_scatter(
            all_rows[5].astype(jnp.bfloat16), "batch", scatter_dimension=1, tiled=True
        ).astype(jnp.float32),
        lax.psum_scatter(
            all_rows[6].astype(jnp.bfloat16), "batch", scatter_dimension=2, tiled=True
        ).astype(jnp.float32),
        lax.psum_scatter(
            all_rows[7].astype(jnp.bfloat16), "batch", scatter_dimension=1, tiled=True
        ).astype(jnp.float32),
        lax.psum_scatter(
            all_rows[8].astype(jnp.bfloat16), "batch", scatter_dimension=1, tiled=True
        ).astype(jnp.float32),
        lax.psum_scatter(
            all_rows[9].astype(jnp.bfloat16), "batch", scatter_dimension=1, tiled=True
        ).astype(jnp.float32),
    )
    vectors = lax.psum(
        (
            enc_up_bias_g,
            enc_down_bias_g,
            enc_gain_g,
            enc_shift_g,
            dec_up_bias_g,
            dec_down_bias_g,
            dec_gain_g,
            dec_shift_g,
        ),
        ("batch", "seq"),
    )
    return (
        to_low(decoded)[None],
        to_low(src_grad)[None],
        to_low(tgt_grad)[None],
        reduced[0],
        reduced[1],
        reduced[2],
        vectors[0],
        reduced[3],
        vectors[1],
        vectors[2],
        vectors[3],
        reduced[4],
        reduced[5],
        reduced[6],
        reduced[7],
        reduced[8],
        vectors[4],
        reduced[9],
        vectors[5],
        vectors[6],
        vectors[7],
    )


def general(mesh):
    placed = (
        P("batch", "seq", None),
        P("batch", "seq", None),
        P("batch", "seq"),
        P("batch", "seq"),
        P("batch", "seq", None),
        P(),
        P(),
        P(),
        P(),
        P(),
        P(),
        P(),
        P(),
        P(),
        P(),
        P(),
        P(),
        P(),
        P(),
        P(),
        P(),
        P(),
        P(),
    )
    return jax.shard_map(
        general_shards,
        mesh=mesh,
        in_specs=placed,
        out_specs=(
            P("batch", "seq", None),
            P("batch", "seq", None),
            P("batch", "seq", None),
            P(None, "seq", "batch"),
            P("seq", "batch"),
            P("seq", "batch"),
            P(),
            P("seq", "batch"),
            P(),
            P(),
            P(),
            P(None, "seq", "batch"),
            P("seq", "batch"),
            P(None, "seq", "batch"),
            P("seq", "batch"),
            P("seq", "batch"),
            P(),
            P("seq", "batch"),
            P(),
            P(),
            P(),
        ),
        check_vma=False,
    )


BATCH, SEQ = "batch", "seq"
CORE, X, Y, LOW, HIGH, SWAP = range(6)
ALL = (CORE, X, Y, LOW, HIGH)
TILE = 256
MESH = pl.DeviceIdType.MESH
VMEM = pl.BlockSpec(memory_space=pltpu.VMEM)
ANY = pl.BlockSpec(memory_space=pl.ANY)


def dot(left, right, left_dim=1, right_dim=0):
    return lax.dot_general(
        left, right, (((left_dim,), (right_dim,)), ((), ())), preferred_element_type=F32
    )


def block(index, size):
    return pl.ds(pl.multiple_of(index * size, size), size)


def normed(value):
    centred = value - jnp.mean(value, axis=-1, keepdims=True)
    scale = lax.rsqrt(jnp.mean(centred * centred, axis=-1, keepdims=True) + 1e-06)
    return centred * scale, scale


def normed_back(grad, unit, scale, gain):
    scaled = grad * gain
    first = jnp.mean(scaled, axis=-1, keepdims=True)
    second = jnp.mean(scaled * unit, axis=-1, keepdims=True)
    return scale * (scaled - first - unit * second)


def gelu_and_slope(inner):
    square = inner * inner
    bent = jnp.tanh(0.7978845608028654 * inner * (1.0 + 0.044715 * square))
    half = 0.5 * (1.0 + bent)
    slope = half + 0.5 * inner * (1.0 - bent * bent) * (
        0.7978845608028654 * (1.0 + 0.134145 * square)
    )
    return inner * half, slope


def column_sum(value):
    return jnp.sum(value, axis=0, keepdims=True)


def parts_of(up):
    return [slice(p * 512, (p + 1) * 512) for p in range(up.shape[1] // 512)]


def over_tiles(rows):
    def run(body):
        @pl.loop(0, rows // TILE, unroll=2)
        def _(tile):
            body(block(tile, TILE))

    return run


def places():
    row, s = lax.axis_index(BATCH), lax.axis_index(SEQ)
    core = lax.rem(row, 2)
    y = lax.rem(row // 2, 2)
    low = lax.rem(row // 4, 2)
    high = row // 8
    mine = (core, s, y, low, high + core - 2 * high * core)
    partner = (
        {BATCH: row + 1 - 2 * core},
        {SEQ: 1 - s},
        {BATCH: row + 2 - 4 * y},
        {BATCH: row + 4 - 8 * low},
        {BATCH: row + 8 - 16 * high},
        {BATCH: row - core + s, SEQ: core},
    )
    return mine, partner


def my_core():
    return places()[0][CORE]


def call_out(ways):
    mine, partner = places()
    barrier = pltpu.get_barrier_semaphore()
    for way in ways:
        pl.semaphore_signal(barrier, inc=1, device_id=partner[way], device_id_type=MESH)

    @pl.when(mine[CORE] != mine[X])
    def _():
        pl.semaphore_signal(barrier, inc=1, device_id=partner[SWAP], device_id_type=MESH)


def hear(ways):
    mine, _ = places()
    away = mine[CORE] + mine[X] - 2 * mine[CORE] * mine[X]
    pl.semaphore_wait(pltpu.get_barrier_semaphore(), len(ways) + away)


def sending(source, target, sems, slot, way):
    return pltpu.make_async_remote_copy(
        src_ref=source,
        dst_ref=target,
        send_sem=sems.at[0, slot],
        recv_sem=sems.at[1, slot],
        device_id=places()[1][way],
        device_id_type=MESH,
    )


def start_swap(source, target, sems, slot):
    mine, _ = places()

    @pl.when(mine[CORE] != mine[X])
    def _():
        sending(source, target, sems, slot, SWAP).start()

    @pl.when(mine[CORE] == mine[X])
    def _():
        pltpu.make_async_copy(source, target, sems.at[0, slot]).start()


def wait_swap(source, target, sems, slot):
    mine, _ = places()

    @pl.when(mine[CORE] != mine[X])
    def _():
        sending(source, target, sems, slot, SWAP).wait()

    @pl.when(mine[CORE] == mine[X])
    def _():
        pltpu.make_async_copy(source, target, sems.at[0, slot]).wait()


class RowSwap:
    def __init__(self, source, target, pieces, sems, slot, near_sem):
        mine, _ = places()
        self.here = mine[CORE] == mine[X]
        self.pieces = range(len(pieces))
        whole = target(mine[X], None)
        self.near = lambda: pltpu.make_async_copy(source, whole, near_sem)
        self.early = lambda: sending(source, whole, sems, slot, CORE)
        self.across = lambda k: sending(source.at[pieces[k]], target(mine[X], pieces[k]), sems, slot + 1 + k, SWAP)

        def onward(k):
            ref = target(mine[CORE], pieces[k])
            return sending(ref, ref, sems, slot + 1 + len(pieces) + k, CORE)

        self.onward = onward

    def finish_early(self):
        @pl.when(self.here)
        def _():
            self.near().wait()

        @pl.when(jnp.logical_not(self.here))
        def _():
            self.early().wait_recv()

    def start(self):
        @pl.when(self.here)
        def _():
            self.near().start()
            self.early().start()

        @pl.when(jnp.logical_not(self.here))
        def _():
            for k in self.pieces:
                self.across(k).start()

    def pass_on(self):
        @pl.when(jnp.logical_not(self.here))
        def _():
            for k in self.pieces:
                self.across(k).wait()
                self.onward(k).start()

    def finish(self):
        @pl.when(self.here)
        def _():
            self.early().wait_send()
            for k in self.pieces:
                self.onward(k).wait_recv()

        @pl.when(jnp.logical_not(self.here))
        def _():
            for k in self.pieces:
                self.onward(k).wait_send()


def part_of(ref, axis, index):
    return ref.at[(slice(None),) * axis + (index,)]


class Halving:
    def __init__(self, source, axis, way, got, total, sems, slot, far=False):
        mine, _ = places()
        kept = part_of(source, axis, mine[way])
        self.kept, self.got, self.total = (total if far else kept), got, total
        self.sent = lambda: sending(part_of(source, axis, 1 - mine[way]), got, sems, slot, way)
        self.near = (lambda: pltpu.make_async_copy(kept, total, sems.at[2, slot])) if far else None

    def start(self):
        self.sent().start()
        if self.near is not None:
            self.near().start()

    def finish(self):
        if self.near is not None:
            self.near().wait()
        self.sent().wait()
        if self.total.dtype == F32:
            self.total[...] = self.kept[...].astype(F32) + self.got[...].astype(F32)
        else:
            self.total[...] = self.kept[...] + self.got[...]


class Across:
    def __init__(self, sums, got, sems, slot):
        self.sums, self.got = sums, got
        self.sent = lambda: sending(sums.at[1], got, sems, slot, CORE)

    def start(self):
        self.sent().start()

    def finish(self):
        self.sent().wait()
        self.sums[0] = self.sums[0] + self.got[...]


class Copies:
    def __init__(self, pairs, sems, first=0):
        self.copies = [
            (lambda source=source, target=target, place=place: pltpu.make_async_copy(source, target, sems.at[first + place]))
            for place, (source, target) in enumerate(pairs)
        ]

    def start(self):
        for copy in self.copies:
            copy().start()

    def wait(self):
        for copy in self.copies:
            copy().wait()


def attend_begin(r, att, half):
    heads = r.queries.shape[1]
    width = heads * HEAD_DIM
    columns = block(my_core(), width)
    q_from, k_from = att, att + att // 2
    q_side, k_side = jnp.minimum(att, 1), att * (2 - att)
    which = lax.rem(att, 2)
    place = lax.broadcasted_iota(jnp.int32, (HEAD_DIM, TILE), 0)
    ones = jnp.ones((TILE, HEAD_DIM), BF)
    half_tiles = r.ids.shape[3] // TILE

    @pl.loop(0, half_tiles, unroll=2)
    def _(tile):
        here = pl.ds(pl.multiple_of(half * r.ids.shape[3] + tile * TILE, TILE), TILE)
        lanes = block(tile, TILE)
        q_ids = r.ids[q_side, half, :, lanes]
        k_ids = r.ids[k_side, half, :, lanes]
        asks = jnp.where(place == q_ids, 1.0, 0.0).T.astype(BF)
        bars = jnp.where((place != k_ids) & (place < 3), NEGATIVE, 0.0).T.astype(BF)
        left_q, left_k = r.x_all[q_from, here, :], r.x_all[k_from, here, :]
        q_tile = dot(left_q, r.weights[att, 0, :, columns]).astype(BF) * BF(0.125)
        k_tile = dot(left_k, r.weights[att, 1, :, columns]).astype(BF)
        v_tile = dot(left_k, r.weights[att, 2, :, columns]).astype(BF)
        for head in range(heads):
            part = slice(head * HEAD_DIM, (head + 1) * HEAD_DIM)
            r.queries[which, head, here, :] = jnp.concatenate([q_tile[:, part], asks], axis=1)
            r.keys[which, head, here, :] = jnp.concatenate([k_tile[:, part], bars], axis=1)
            r.values[which, head, here, :] = jnp.concatenate([v_tile[:, part], ones], axis=1)


def attend_heads(r, which, first, causal):
    length = r.queries.shape[2]
    lower = lax.broadcasted_iota(jnp.int32, (TILE, TILE), 0) >= lax.broadcasted_iota(jnp.int32, (TILE, TILE), 1)
    work = [(head, tile) for head in range(2) for tile in range(length // TILE)]

    def seen(tile):
        return (tile + 1) * TILE if causal else length

    def scores_of(head, tile):
        here = slice(tile * TILE, (tile + 1) * TILE)
        scores = dot(r.queries[which, first + head, here, :], r.keys[which, first + head, : seen(tile), :], 1, 1)
        if not causal:
            return scores
        last = jnp.where(lower, scores[:, seen(tile) - TILE :], NEGATIVE)
        return last if tile == 0 else jnp.concatenate([scores[:, : seen(tile) - TILE], last], axis=1)

    scores = scores_of(*work[0])
    for place, (head, tile) in enumerate(work):
        here = slice(tile * TILE, (tile + 1) * TILE)
        later = scores_of(*work[place + 1]) if place + 1 < len(work) else None
        low = jnp.exp(scores - jnp.max(scores, axis=-1, keepdims=True)).astype(BF)
        r.chances[head, here, : seen(tile)] = low
        r.outs[which, first + head, here, :] = dot(low, r.values[which, first + head, : seen(tile), :])
        scores = later


def forward_body(r):
    step = pl.program_id(0)
    mine, _ = places()
    core = mine[CORE]
    att = jnp.minimum(step // 2, 2)
    rows = r.source.shape[0]
    heads = r.outs.shape[1]
    width = heads * HEAD_DIM
    sems = r.sems

    def rows_of(side):
        def target(half, piece):
            first = half * rows if piece is None else half * rows + piece.start
            count = rows if piece is None else piece.size
            return r.x_all.at[side, pl.ds(pl.multiple_of(first, count), count)]

        return target

    def ids_of(side):
        return lambda half, piece: r.ids.at[side, half]

    quarters = [pl.ds(k * rows // 4, rows // 4) for k in range(4)]
    source = RowSwap(r.source, rows_of(0), quarters, sems, 0, r.near_sems.at[0])
    target = RowSwap(r.target, rows_of(1), quarters, sems, 9, r.near_sems.at[1])
    one = [pl.ds(0, 1)]
    ids = (
        RowSwap(r.source_ids, ids_of(0), one, sems, 18, r.near_sems.at[2]),
        RowSwap(r.target_ids, ids_of(1), one, sems, 21, r.near_sems.at[3]),
    )
    first_across = sending(r.x_all.at[2, block(core, rows)], r.x_all.at[2, block(core, rows)], sems, 24, CORE)

    def att_across(index):
        return sending(r.att_send.at[index], r.att_all.at[index, :, block(core, width)], sems, 25 + index, CORE)

    def memory_across(tile):
        ref = r.x_all.at[3, pl.ds(pl.multiple_of(core * rows + tile * TILE, TILE), TILE)]
        return sending(ref, ref, sems, 28 + tile, CORE)

    loads = Copies(
        [
            (r.enc_qkv, r.weights.at[0]), (r.dec_qkv, r.weights.at[1]), (r.cross_qkv, r.weights.at[2]),
            (r.enc_out_far, r.enc_out), (r.dec_out_far, r.dec_out), (r.up_far, r.up), (r.down_far, r.down),
        ],
        r.load_sems,
    )

    def saved(index):
        which = index % 2
        return Copies(
            [
                (r.queries.at[which], r.queries_far.at[index]), (r.keys.at[which], r.keys_far.at[index]),
                (r.values.at[which], r.values_far.at[index]),
            ],
            r.save_sems,
            index * 4,
        )

    def saved_outs(index):
        return Copies([(r.outs.at[index % 2], r.outs_far.at[index])], r.save_sems, index * 4 + 3)

    kept = Copies(
        [
            (r.unit0, r.unit0_far), (r.scale0, r.scale0_far), (r.unit1, r.unit1_far), (r.scale1, r.scale1_far),
            (r.hidden_low, r.hidden_far), (r.act, r.act_far), (r.slope, r.slope_far), (r.first, r.first_far),
            (r.first_unit, r.first_unit_far), (r.first_scale, r.first_scale_far), (r.x_all, r.x_far),
        ],
        r.save_sems,
        12,
    )
    att_kept = Copies([(r.att_all, r.att_far)], r.save_sems, 23)

    @pl.when(step == 0)
    def _():
        call_out((CORE,))
        loads.start()
        hear((CORE,))
        for one_side in ids:
            one_side.start()
        source.start()
        target.start()
        start_swap(r.upstream, r.upstream_there, sems, 30)
        loads.wait()
        for one_side in ids:
            one_side.finish_early()
        source.finish_early()

    @pl.when(step == 2)
    def _():
        target.pass_on()
        target.finish_early()

    @pl.when(step == 5)
    def _():
        saved(0).wait()
        saved_outs(0).wait()
        first_across.wait()

        @pl.loop(0, rows // TILE)
        def _(tile):
            memory_across(tile).wait()

        kept.start()

    begins = (step == 0) | (step == 2) | (step == 5)

    @pl.when(begins)
    def _():
        attend_begin(r, att, mine[X])

    @pl.when(step == 0)
    def _():
        for one_side in ids:
            one_side.pass_on()
        source.pass_on()
        for one_side in ids:
            one_side.finish()
        source.finish()

    @pl.when(step == 2)
    def _():
        target.finish()

    @pl.when(begins)
    def _():
        attend_begin(r, att, 1 - mine[X])

    for index, begun in enumerate((0, 2, 5)):

        @pl.when(step == begun)
        def _(index=index):
            saved(index).start()

    @pl.when((step < 2) | (step > 4))
    def _():
        attend_heads(r, 0, 2 * lax.rem(step - att // 2, 2), False)

    @pl.when((step == 2) | (step == 3))
    def _():
        attend_heads(r, 1, 2 * (step - 2), True)

    @pl.when((step == 1) | (step == 3) | (step == 6))
    def _():
        for half in (1 - core, core):
            there = block(half, rows)
            parts = [r.outs[lax.rem(att, 2), head, there, :] for head in range(heads)]
            joined = jnp.concatenate([part[:, :HEAD_DIM] / part[:, HEAD_DIM:] for part in parts], axis=1).astype(BF)
            if half is core:
                r.att_all[att, :, block(core, width)] = joined
            else:
                r.att_send[att] = joined
                att_across(att).start()

    for index, last in enumerate((1, 3, 6)):

        @pl.when(step == last)
        def _(index=index):
            saved_outs(index).start()

    @pl.when(step == 4)
    def _():
        att_across(0).wait()
        att_across(1).wait()

        @over_tiles(rows)
        def _(here):
            own = pl.ds(pl.multiple_of(core * rows + here.start, TILE), TILE)
            unit, scale = normed(r.x_all[1, own, :].astype(F32) + dot(r.att_all[1, here, :], r.dec_out[...]))
            r.first_unit[here, :] = unit
            r.first_scale[here, :] = scale
            value = unit * r.dec_gain[0:1, :] + r.dec_shift[0:1, :]
            r.first[here, :] = value
            r.x_all[2, own, :] = value.astype(BF)

        first_across.start()

        @pl.loop(0, rows // TILE)
        def _(tile):
            here = block(tile, TILE)
            own = pl.ds(pl.multiple_of(core * rows + tile * TILE, TILE), TILE)
            unit, scale = normed(r.x_all[0, own, :].astype(F32) + dot(r.att_all[0, here, :], r.enc_out[...]))
            r.unit0[here, :] = unit
            r.scale0[here, :] = scale
            hidden = unit * r.enc_gain[0:1, :] + r.enc_shift[0:1, :]
            low = hidden.astype(BF)
            r.hidden_low[here, :] = low
            for part in parts_of(r.up):
                value, bend = gelu_and_slope(dot(low, r.up[:, part]) + r.up_bias[:, part])
                r.slope[here, part] = bend.astype(BF)
                r.act[here, part] = value.astype(BF)
            unit, scale = normed(hidden + dot(r.act[here, :], r.down[...]) + r.down_bias[...])
            r.unit1[here, :] = unit
            r.scale1[here, :] = scale
            r.x_all[3, own, :] = (unit * r.enc_gain[1:2, :] + r.enc_shift[1:2, :]).astype(BF)
            memory_across(tile).start()

    @pl.when(step == 6)
    def _():
        kept.wait()
        saved(1).wait()
        saved_outs(1).wait()
        wait_swap(r.upstream, r.upstream_there, sems, 30)
        att_across(2).wait()
        att_kept.start()
        saved(2).wait()
        saved_outs(2).wait()
        att_kept.wait()


def back_begin(r, which):
    heads = r.queries.shape[1]
    width = heads * HEAD_DIM
    lane = lax.rem(lax.broadcasted_iota(jnp.int32, (TILE, width), 1), HEAD_DIM)
    same_head = (
        lax.broadcasted_iota(jnp.int32, (width, width), 0) // HEAD_DIM
        == lax.broadcasted_iota(jnp.int32, (width, width), 1) // HEAD_DIM
    ).astype(BF)

    @over_tiles(r.queries.shape[2])
    def _(here):
        grad = r.grad_all[which, here, :].astype(F32)
        lows, boths = [], []
        for head in range(heads):
            out = r.outs[which, head, here, :]
            over = 1.0 / out[:, HEAD_DIM:]
            low = (grad[:, head * HEAD_DIM : (head + 1) * HEAD_DIM] * over).astype(BF)
            lows.append(low)
            boths.append(low.astype(F32) * (out[:, :HEAD_DIM] * over))
        both = jnp.concatenate(boths, axis=1)
        high = both.astype(BF)
        rest = (both - high.astype(F32)).astype(BF)
        settle = -dot(high, same_head) - dot(rest, same_head)
        first = settle.astype(BF).astype(F32)
        second = (settle - first).astype(BF).astype(F32)
        extra = jnp.where(lane == 0, first, jnp.where(lane == 1, second, jnp.where(lane == 2, settle - first - second, 0.0)))
        extra = extra.astype(BF)
        for head in range(heads):
            r.grads[head, here, :] = jnp.concatenate(
                [lows[head], extra[:, head * HEAD_DIM : (head + 1) * HEAD_DIM]], axis=1
            )


def back_head(r, which, head, causal):
    length = r.queries.shape[2]
    count = length // TILE

    def seen(tile):
        return (tile + 1) * TILE if causal else length

    def change_of(tile):
        here = slice(tile * TILE, (tile + 1) * TILE)
        return dot(r.grads[head, here, :], r.values[which, head, : seen(tile), :], 1, 1)

    change = change_of(0)
    for tile in range(count):
        here = slice(tile * TILE, (tile + 1) * TILE)
        later = change_of(tile + 1) if tile + 1 < count else None
        low = (r.chances[0, here, : seen(tile)].astype(F32) * change).astype(BF)
        r.score_grads[here, : seen(tile)] = low
        r.dq[head, here, :] = (dot(low, r.keys[which, head, : seen(tile), :])[:, :HEAD_DIM] * 0.125).astype(BF)
        change = later
    for tile in range(count if causal else 1):
        here = slice(tile * TILE, (tile + 1) * TILE) if causal else slice(0, length)
        below = slice(tile * TILE, length)
        r.dv[block(head, HEAD_DIM), here] = dot(
            r.grads[head, below, :HEAD_DIM], r.chances[0, below, here], 0, 0
        )
        r.dk[block(head, HEAD_DIM), here] = dot(
            r.queries[which, head, below, :HEAD_DIM], r.score_grads[below, here], 0, 0
        )


class BackEnd:
    def __init__(self, r, which, unit, q_from, k_from, sems):
        self.r, self.q_from, self.k_from = r, q_from, k_from
        core = my_core()
        rows = r.d_full.shape[2]
        width = r.d_all.shape[2]
        lanes = block(core, width)
        self.other = lambda: sending(
            r.d_all.at[:, block(1 - core, rows)], r.d_full.at[which, :, :, lanes], sems, 2 * which, CORE
        )
        self.own = lambda: pltpu.make_async_copy(
            r.d_all.at[:, block(core, rows)], r.d_full.at[which, :, :, lanes], sems.at[2, 2 * which]
        )
        below = pl.ds(32, 96)
        self.across = lambda: sending(r.shares.at[1], unit.at[:, :, :, 1, below], sems, 2 * which + 1, CORE)
        self.along = lambda: pltpu.make_async_copy(r.shares.at[0], unit.at[:, :, :, 0, below], sems.at[2, 2 * which + 1])

    def start(self):
        r = self.r
        core = my_core()
        rows, heads = r.d_full.shape[2], r.dq.shape[0]

        @pl.loop(0, 2, unroll=2)
        def _(half):
            there = block(half, rows)
            r.d_all[0, there, :] = jnp.concatenate([r.dq[head, there, :] for head in range(heads)], axis=1)
            r.d_all[1, there, :] = r.dk[:, there].T.astype(BF)
            r.d_all[2, there, :] = r.dv[:, there].T.astype(BF)

        self.other().start()
        self.own().start()

        @pl.loop(0, 3, unroll=3)
        def _(kind):
            x_from = jnp.where(kind == 0, self.q_from, self.k_from)
            low = dot(r.d_all[kind], r.x_all[x_from], 0, 0).astype(BF)
            for part in range(low.shape[0] // 32):
                z_low, y, kept = part >> 2, (part >> 1) & 1, part & 1
                for s in range(2):
                    r.shares[core if kept == 0 else 1 - core, s, y, z_low, block(kind, 32), :] = low[
                        part * 32 : (part + 1) * 32, s * 256 : (s + 1) * 256
                    ]

        self.across().start()
        self.along().start()

    def wait_grads(self):
        self.own().wait()
        self.other().wait()

    def wait_sums(self):
        self.along().wait()
        self.across().wait()


BIG = (2, 2, 2, 2, 128, 256)
MID = BIG[1:]
LESS = BIG[2:]
LEAST = BIG[3:]
OUT = (2, 2, 2, 2, 32, 256)
HALF = (2, 2, 2, 2, 64, 256)


def sum_up(sums, inner_low, entering):
    core = my_core()

    @pl.loop(0, 4, unroll=4)
    def _(z):
        for y in range(2):
            low = dot(inner_low[:, block(z * 2 + y, 256)], entering[...], 0, 0).astype(BF)
            high = z // 2
            for kept in range(2):
                for s in range(2):
                    sums[
                        core if kept == 0 else 1 - core, s, y, lax.rem(z, 2), 1 - high if kept else high, :, :
                    ] = low[kept * 128 : (kept + 1) * 128, s * 256 : (s + 1) * 256]


def sum_down(sums, branch_low, act):
    core = my_core()

    @pl.loop(0, act.shape[1] // 512, unroll=4)
    def _(column):
        for index in range(2):
            low = dot(branch_low[:, index * 256 : (index + 1) * 256], act[:, block(column, 512)], 0, 0).astype(BF)
            for part in range(8):
                place = index * 8 + part
                z, y, kept = place >> 2, (place >> 1) & 1, place & 1
                for piece in range(2):
                    slot = lax.rem(column, 2) * 2 + piece
                    sums[
                        core if kept == 0 else 1 - core, column // 2, y, z & 1, (z >> 1) ^ kept, block(slot, 32), :
                    ] = low[part * 32 : (part + 1) * 32, piece * 256 : (piece + 1) * 256]


def sum_out(sums, mixed_low, att):
    core = my_core()

    @pl.loop(0, 2, unroll=2)
    def _(s):
        low = dot(mixed_low[...], att[:, block(s, 256)], 0, 0).astype(BF)
        for place in range(16):
            z, y, kept = place >> 2, (place >> 1) & 1, place & 1
            sums[core if kept == 0 else 1 - core, s, y, z & 1, (z >> 1) ^ kept, :, :] = low[
                place * 32 : (place + 1) * 32, :
            ]


def split_halvings(unit, bufs, totals, sems, slot):
    upper, lower = unit.at[:, :, :, :, pl.ds(0, 64)], unit.at[:, :, :, :, pl.ds(64, 64)]
    return (
        Halving(upper, 0, X, bufs.at[0], totals.at[0], sems, slot),
        Halving(lower, 1, Y, bufs.at[1], totals.at[1], sems, slot + 1),
    )


def join_halvings(source, less, both, last, final, total, sems, slot):
    return (
        Halving(source.at[0], 0, Y, less.at[0], both.at[0], sems, slot),
        Halving(source.at[1], 0, X, less.at[1], both.at[1], sems, slot + 1),
        Halving(both, 1, LOW, last.at[0], last.at[1], sems, slot + 2),
        Halving(last.at[1], 1, HIGH, final, total, sems, slot + 3),
    )


def decode_last_layers(r):
    @over_tiles(r.first.shape[0])
    def _(here):
        unit, scale = normed(r.first[here, :] + dot(r.att[here, :], r.out_w[...]))
        r.unit0[here, :] = unit
        r.scale0[here, :] = scale
        second = unit * r.dec_gain[1:2, :] + r.dec_shift[1:2, :]
        low = second.astype(BF)
        r.entering[here, :] = low
        for part in parts_of(r.up):
            value, slope = gelu_and_slope(dot(low, r.up[:, part]) + r.up_bias[:, part])
            r.act[here, part] = value.astype(BF)
            r.inner_low[here, part] = slope.astype(BF)
        unit, scale = normed(second + dot(r.act[here, :], r.down[...]) + r.down_bias[...])
        r.unit1[here, :] = unit
        r.scale1[here, :] = scale
        r.decoded[here, :] = (unit * r.dec_gain[2:3, :] + r.dec_shift[2:3, :]).astype(BF)
        r.grad[here, :] = r.upstream[here, :].astype(F32)


def layers_back(r, which):
    vectors = r.vectors

    def add(place, value):
        vectors[which, place : place + 1, :] += value

    @over_tiles(r.grad.shape[0])
    def _(here):
        grad, unit = r.grad[here, :], r.unit1[here, :]
        add(7, column_sum(grad * unit))
        add(8, column_sum(grad))
        grad = normed_back(grad, unit, r.scale1[here, :], r.gains[which, 1:2, :])
        branch = grad.astype(BF)
        r.branch_low[here, :] = branch
        add(4, column_sum(branch.astype(F32)))
        for place, part in enumerate(parts_of(r.up)):
            inner = (dot(branch, r.down[part, :], 1, 1) * r.inner_low[here, part].astype(F32)).astype(BF)
            r.inner_low[here, part] = inner
            add(place, column_sum(inner.astype(F32)))
        grad = grad + dot(r.inner_low[here, :], r.up[...], 1, 1)
        unit = r.unit0[here, :]
        add(5, column_sum(grad * unit))
        add(6, column_sum(grad))
        grad = normed_back(grad, unit, r.scale0[here, :], r.gains[which, 0:1, :])
        r.pre[which, here, :] = grad
        mixed = grad.astype(BF)
        r.mixed_low[here, :] = mixed
        r.att_grad[here, :] = dot(mixed, r.out_w[...], 1, 1).astype(BF)


def middle_body(r):
    step = pl.program_id(0)
    mine, _ = places()
    core = mine[CORE]
    sems = r.sems
    rows, width = r.first.shape[0], r.d_all.shape[2]
    cross = 2
    before = Copies(
        [(r.first_far, r.first), (r.att_far.at[2], r.att), (r.upstream_far, r.upstream), (r.cross_out, r.out_w)], r.load_sems
    )
    dec_layer = Copies([(r.dec_up, r.up), (r.dec_down, r.down)], r.load_sems, 4)
    around = Copies(
        [
            (r.queries_far.at[pl.ds(2, 1)], r.queries), (r.keys_far.at[pl.ds(2, 1)], r.keys),
            (r.values_far.at[pl.ds(2, 1)], r.values), (r.outs_far.at[pl.ds(2, 1)], r.outs), (r.x_far.at[pl.ds(2, 2)], r.x_all),
        ],
        r.load_sems,
        6,
    )
    first_layer = Copies(
        [
            (r.cross_qkv, r.cross_w), (r.dec_out, r.dec_w), (r.first_unit_far, r.first_unit),
            (r.first_scale_far, r.first_scale), (r.att_far.at[1], r.dec_att),
        ],
        r.load_sems,
        11,
    )
    enc_layer = Copies(
        [
            (r.enc_up, r.up), (r.enc_down, r.down), (r.enc_out, r.out_w), (r.unit0_far, r.unit0), (r.scale0_far, r.scale0),
            (r.unit1_far, r.unit1), (r.scale1_far, r.scale1), (r.hidden_far, r.entering), (r.act_far, r.act),
            (r.slope_far, r.inner_low), (r.att_far.at[0], r.att),
        ],
        r.load_sems,
        16,
    )
    down_x = Halving(r.down_sums.at[0], 0, X, r.got_a, r.mid_a, sems, 0)
    up_y = Halving(r.up_sums.at[0], 1, Y, r.got_b, r.mid_b, sems, 1)
    down_y = Halving(r.mid_a, 0, Y, r.got_c, r.pair.at[0], sems, 2)
    up_x = Halving(r.mid_b, 0, X, r.got_d, r.pair.at[1], sems, 3)
    down_low = Halving(r.pair.at[0], 0, LOW, r.got_e.at[0], r.mid_e, sems, 4)
    up_low = Halving(r.pair.at[1], 0, LOW, r.got_e.at[1], r.up_rest, sems, 17)
    down_high = Halving(r.mid_e, 0, HIGH, r.got_f, r.dec_down_sum, sems, 5)
    cross_x, cross_y = split_halvings(r.unit, r.got_g, r.cross_half, sems, 6)
    end = BackEnd(r, 0, r.unit, 0, 1, r.end_sems)
    shared = [
        Across(r.down_sums, r.down_got, sems, 8),
        Across(r.up_sums, r.up_got, sems, 9),
        Across(r.out_sums, r.out_got, sems, 10),
    ]
    dec_shared = Across(r.dec_out_sums, r.dec_out_got, sems, 11)
    lanes, other_lanes = block(core, width), block(1 - core, width)
    there = block(core, rows)

    def grads_of(source, target, slot):
        across = sending(source.at[:, other_lanes], target.at[there], sems, slot, CORE)
        stay = pltpu.make_async_copy(source.at[:, lanes], target.at[there], sems.at[2, slot])
        return across, stay

    cross_grads = grads_of(r.att_grad, r.grad_all.at[0], 12)
    dec_grads = grads_of(r.dec_att_grad, r.grads_far.at[1], 13)
    enc_grads = grads_of(r.att_grad, r.grads_far.at[0], 14)
    beside = pltpu.make_async_copy(r.out_sums.at[0], r.unit.at[:, :, :, :, pl.ds(0, 32)], sems.at[2, 15])
    results = Copies(
        [
            (r.down_sums.at[0], r.down_unit), (r.up_sums.at[0], r.up_unit), (r.out_sums.at[0], r.out_units.at[0]),
            (r.dec_out_sums.at[0], r.out_units.at[1]), (r.pre, r.pre_far),
        ],
        r.load_sems,
        27,
    )

    @pl.when(step == 0)
    def _():
        call_out(ALL)
        before.start()
        dec_layer.start()
        around.start()
        r.vectors[...] = jnp.zeros_like(r.vectors)
        for place, (ref, row) in enumerate(((r.dec_gain, 1), (r.dec_gain, 2), (r.enc_gain, 0), (r.enc_gain, 1))):
            r.gains[place // 2, place % 2 : place % 2 + 1, :] = ref[row : row + 1, :]
        before.wait()
        dec_layer.wait()
        decode_last_layers(r)
        hear(ALL)
        start_swap(r.decoded, r.decoded_there, sems, 16)

    @pl.when(step == 6)
    def _():
        beside.wait()
        end.wait_sums()
        cross_y.start()
        cross_x.start()
        end.wait_grads()

        @over_tiles(rows)
        def _(here):
            r.grad[here, :] = dot(r.d_full[0, 1, here, :], r.cross_w[1], 1, 1) + dot(
                r.d_full[0, 2, here, :], r.cross_w[2], 1, 1
            )
            grad = r.pre[0, here, :] + dot(r.d_full[0, 0, here, :], r.cross_w[0], 1, 1)
            unit = r.first_unit[here, :]
            r.vectors[2, 0:1, :] += column_sum(grad * unit)
            r.vectors[2, 1:2, :] += column_sum(grad)
            grad = normed_back(grad, unit, r.first_scale[here, :], r.dec_gain[0:1, :])
            r.pre[0, here, :] = grad
            mixed = grad.astype(BF)
            r.dec_mixed[here, :] = mixed
            r.dec_att_grad[here, :] = dot(mixed, r.dec_w[...], 1, 1).astype(BF)

        for copy in dec_grads:
            copy.start()
        sum_out(r.dec_out_sums, r.dec_mixed, r.dec_att)
        dec_shared.start()

    @pl.when(step == 7)
    def _():
        down_y.finish()
        down_low.start()
        enc_layer.wait()

    @pl.when((step == 1) | (step == 7))
    def _():
        layers_back(r, step // 7)

    @pl.when(step == 1)
    def _():
        for copy in cross_grads:
            copy.start()

    @pl.when(step == 7)
    def _():
        for copy in enc_grads:
            copy.start()
        down_low.finish()
        down_high.start()
        up_x.finish()
        up_low.start()

    @pl.when((step == 1) | (step == 7))
    def _():
        sum_down(r.down_sums, r.branch_low, r.act)
        shared[0].start()
        sum_up(r.up_sums, r.inner_low, r.entering)
        shared[1].start()
        shared[0].finish()

        @pl.when(step == 1)
        def _():
            down_x.start()

        sum_out(r.out_sums, r.mixed_low, r.att)
        shared[2].start()

        @pl.when(step == 1)
        def _():
            for copy in cross_grads:
                copy.wait()
            around.wait()
            back_begin(r, 0)

        shared[1].finish()

        @pl.when(step == 1)
        def _():
            up_y.start()

        shared[2].finish()

    @pl.when(step == 1)
    def _():
        beside.start()
        enc_layer.start()
        first_layer.start()

    @pl.when(step == 5)
    def _():
        down_x.finish()
        down_y.start()

    @pl.when((step >= 2) & (step < 6))
    def _():
        back_head(r, 0, step - 2, False)

    @pl.when(step == 5)
    def _():
        first_layer.wait()
        end.start()
        up_y.finish()
        up_x.start()

    @pl.when(step == 7)
    def _():
        dec_shared.finish()
        results.start()
        for copy in (*dec_grads, *enc_grads):
            copy.wait()
        down_high.finish()
        up_low.finish()
        cross_y.finish()
        cross_x.finish()
        results.wait()
        wait_swap(r.decoded, r.decoded_there, sems, 16)


def last_body(r):
    step = pl.program_id(0)
    which = step // 4
    mine, _ = places()
    sems = r.sems
    rows = r.pre.shape[1]

    def side(att):
        return Copies(
            [
                (r.queries_far.at[att], r.queries.at[att]), (r.keys_far.at[att], r.keys.at[att]),
                (r.values_far.at[att], r.values.at[att]), (r.outs_far.at[att], r.outs.at[att]),
                (r.grads_far.at[att], r.grad_all.at[att]), (r.x_far.at[att], r.x_all.at[att]),
                ((r.enc_qkv, r.dec_qkv)[att], r.weights.at[att]), (r.pre_far.at[1 - att], r.pre.at[att]),
                (r.out_units.at[att], r.units.at[att, :, :, :, :, pl.ds(0, 32)]),
            ],
            r.load_sems,
            att * 9,
        )

    def layer_steps(unit, bufs, total, slot, ways):
        left, steps, source = [X, Y, LOW, HIGH], [], unit
        for place, way in enumerate(ways):
            got, kept = (bufs[2 * place], bufs[2 * place + 1]) if place < 3 else (bufs[6], total)
            steps.append(Halving(source, left.index(way), way, got, kept, sems, slot + place, far=place == 0))
            left.remove(way)
            source = kept
        return steps

    down = layer_steps(r.down_unit, r.down_bufs, r.enc_sums.at[0], 0, (X, Y, LOW, HIGH))
    up = layer_steps(r.up_unit, r.up_bufs, r.enc_sums.at[1], 4, (Y, LOW, HIGH, X))
    cross = join_halvings(r.cross_half, *r.cross_bufs, r.cross_sum, sems, 8)
    dec_up_high = Halving(r.up_rest, 0, HIGH, r.rest_got, r.dec_up_sum, sems, 17)
    enc_got, enc_mid, *enc_bufs = r.enc_bufs
    enc_x, enc_y = split_halvings(r.units.at[0], enc_got, enc_mid, sems, 18)
    enc_att = join_halvings(enc_mid, *enc_bufs, r.enc_att_sum, sems, 20)
    dec_got, dec_mid, *dec_bufs = r.dec_bufs
    dec_x, dec_y = split_halvings(r.units.at[1], dec_got, dec_mid, sems, 24)
    dec_att = join_halvings(dec_mid, *dec_bufs, r.dec_att_sum, sems, 26)
    vector_ways = (X, Y, CORE, LOW, HIGH)

    def vector_parts(place):
        source = r.vectors if place == 0 else r.vector_mid.at[place - 1]
        total = r.vector_sum if place == 4 else r.vector_mid.at[place]
        copy = sending(source, r.vector_got.at[place], sems, 12 + place, vector_ways[place])
        return source, r.vector_got.at[place], total, copy

    def vector_start(place):
        vector_parts(place)[3].start()

    def vector_finish(place):
        source, got, total, copy = vector_parts(place)
        copy.wait()
        total[...] = source[...] + got[...]

    end = BackEnd(r, which, r.units.at[which], which, which, r.end_sems)

    def row_grads(index):
        @over_tiles(rows)
        def _(here):
            total = r.pre[index, here, :]
            for kind in range(3):
                total = total + dot(r.d_full[index, kind, here, :], r.weights[index, kind], 1, 1)
            r.row_grad[index, here, :] = total.astype(BF)

    src_swap = (r.row_grad.at[0], r.src_there, sems, 30)
    tgt_swap = (r.row_grad.at[1], r.tgt_there, sems, 31)

    @pl.when(step == 0)
    def _():
        call_out(ALL)
        side(0).start()
        side(1).start()
        side(0).wait()
        hear(ALL)
        vector_start(0)
        dec_up_high.start()
        cross[0].start()
        cross[1].start()
        down[0].start()
        up[0].start()

    @pl.when(step == 4)
    def _():
        side(1).wait()
        BackEnd(r, 0, r.units.at[0], 0, 0, r.end_sems).wait_sums()
        enc_x.start()
        enc_y.start()

    @pl.when((step == 0) | (step == 4))
    def _():
        back_begin(r, which)

    @pl.when(step == 1)
    def _():
        vector_finish(0)
        vector_start(1)

    @pl.when(step == 2)
    def _():
        dec_up_high.finish()
        cross[0].finish()
        cross[1].finish()
        cross[2].start()

    @pl.when(step == 4)
    def _():
        BackEnd(r, 0, r.units.at[0], 0, 0, r.end_sems).wait_grads()
        row_grads(0)
        start_swap(*src_swap)
        down[0].finish()
        down[1].start()
        up[0].finish()
        up[1].start()

    @pl.when(step == 6)
    def _():
        vector_finish(2)
        vector_start(3)

    @pl.when(step == 5)
    def _():
        vector_finish(1)
        vector_start(2)
        cross[3].finish()

    @pl.when(step == 7)
    def _():
        enc_x.finish()
        enc_att[0].start()
        enc_y.finish()
        enc_att[1].start()

    @pl.when(step < 4)
    def _():
        back_head(r, 0, step, False)

    @pl.when(step >= 4)
    def _():
        back_head(r, 1, step - 4, True)

    @pl.when((step == 3) | (step == 7))
    def _():
        end.start()

    @pl.when(step == 3)
    def _():
        cross[2].finish()
        cross[3].start()

    @pl.when(step == 7)
    def _():
        up[1].finish()
        up[2].start()
        end_of_dec = BackEnd(r, 1, r.units.at[1], 1, 1, r.end_sems)
        end_of_dec.wait_sums()
        dec_x.start()
        dec_y.start()
        end_of_dec.wait_grads()
        row_grads(1)
        down[1].finish()
        down[2].start()
        enc_att[0].finish()
        enc_att[1].finish()
        enc_att[2].start()
        vector_finish(3)
        vector_start(4)
        down[2].finish()
        down[3].start()
        dec_x.finish()
        dec_att[0].start()
        dec_y.finish()
        dec_att[1].start()
        start_swap(*tgt_swap)
        up[2].finish()
        up[3].start()
        enc_att[2].finish()
        enc_att[3].start()
        dec_att[0].finish()
        dec_att[1].finish()
        dec_att[2].start()
        vector_finish(4)
        down[3].finish()
        up[3].finish()
        enc_att[3].finish()
        dec_att[2].finish()
        dec_att[3].start()
        dec_att[3].finish()
        wait_swap(*src_swap)
        wait_swap(*tgt_swap)


def finish_body(r):
    r.decoded_out[...] = r.decoded[...]
    r.src_out[...] = r.src[...]
    r.tgt_out[...] = r.tgt[...]
    for sums, down in ((r.dec_down_sum[...], r.dec_down), (r.enc_sums[0], r.enc_down)):
        for slot in range(4):
            down[:, slot * 256 : (slot + 1) * 256] = sums[slot * 32 : (slot + 1) * 32, :]
    r.dec_up[...] = r.dec_up_sum[...].T
    r.enc_up[...] = r.enc_sums[1].T
    cross, enc_att, dec_att = [
        jnp.concatenate([one[0], one[1]], axis=0) for one in (r.cross_sum, r.enc_att_sum, r.dec_att_sum)
    ]
    for sums, out, qkv in (
        (cross, r.cross_out, r.cross_qkv),
        (enc_att, r.enc_out, r.enc_qkv),
        (dec_att, r.dec_out, r.dec_qkv),
    ):
        out[...] = sums[:32]
        for kind in range(3):
            qkv[kind] = sums[32 + kind * 32 : 64 + kind * 32]
    vectors = r.vectors
    for which, up_bias, down_bias in ((0, r.dec_up_bias, r.dec_down_bias), (1, r.enc_up_bias, r.enc_down_bias)):
        for part in range(4):
            up_bias[:, part * 512 : (part + 1) * 512] = vectors[which, part : part + 1, :]
        down_bias[...] = vectors[which, 4:5, :]
    for ref, found in (
        (r.dec_gain, ((2, 0), (0, 5), (0, 7))),
        (r.dec_shift, ((2, 1), (0, 6), (0, 8))),
        (r.enc_gain, ((1, 5), (1, 7))),
        (r.enc_shift, ((1, 6), (1, 8))),
    ):
        for index, (which, place) in enumerate(found):
            ref[index : index + 1, :] = vectors[which, place : place + 1, :]


def launch(body, micros, grid, meeting, ins, far, blocks, outs, far_outs, scratch):
    def once(shape):
        rank = len(shape)
        return pl.BlockSpec(shape, lambda step: (0,) * rank, pipeline_mode=pl.Buffered(1))

    names, arrays, in_specs, out_names, shapes, out_specs = [], [], [], [], [], []
    for name, array in {**ins, **far}.items():
        names.append(name)
        arrays.append(array)
        in_specs.append(once(array.shape) if name in ins else ANY)
    for name, (shape, kind) in {**outs, **far_outs}.items():
        out_names.append(name)
        shapes.append(jax.ShapeDtypeStruct(shape, kind))
        out_specs.append(once(shape) if name in outs else ANY)
    for name, (array, part, index, is_out) in blocks.items():
        spec = pl.BlockSpec(part, index)
        if is_out:
            out_names.append(name)
            shapes.append(jax.ShapeDtypeStruct(*array))
            out_specs.append(spec)
        else:
            names.append(name)
            arrays.append(array)
            in_specs.append(spec)
    every = (*names, *out_names, *scratch)

    def kernel(*refs):
        body(types.SimpleNamespace(**dict(zip(every, refs))))

    results = pl.pallas_call(
        kernel,
        grid=(grid,),
        out_shape=shapes,
        in_specs=in_specs,
        out_specs=out_specs,
        scratch_shapes=list(scratch.values()),
        compiler_params=pltpu.CompilerParams(
            vmem_limit_bytes=60 * 2**20, collective_id=meeting, has_side_effects=meeting is not None
        ),
        cost_estimate=pl.CostEstimate(flops=int(micros * 1e9), bytes_accessed=0, transcendentals=0),
        name=body.__name__,
    )(*arrays)
    return types.SimpleNamespace(**dict(zip(out_names, results)))


def low(*shape):
    return pltpu.VMEM(shape, BF)


def wide(*shape):
    return pltpu.VMEM(shape, F32)


def fast_shards(source, target, source_ids, target_ids, out_grad, *params):
    (
        enc_qkv, enc_out, enc_up, enc_up_bias, enc_down, enc_down_bias, enc_gain, enc_shift, dec_qkv, dec_out,
        cross_qkv, cross_out, dec_up, dec_up_bias, dec_down, dec_down_bias, dec_gain, dec_shift,
    ) = params
    source, target, upstream = source[0], target[0], out_grad[0]
    rows, size = source.shape
    length, inner, width = 2 * rows, enc_up.shape[1], size // 2
    heads = width // HEAD_DIM
    sem = pltpu.SemaphoreType.DMA
    full, thin, low_full, low_inner = ((rows, size), F32), ((rows, 1), F32), ((rows, size), BF), ((rows, inner), BF)
    biases = [one[None, :] for one in (enc_up_bias, enc_down_bias, dec_up_bias, dec_down_bias)]
    enc_up_b, enc_down_b, dec_up_b, dec_down_b = biases
    head_block = (1, length, length)
    per_head = (heads, length, 2 * HEAD_DIM)

    f = launch(
        forward_body,
        60,
        7,
        0,
        dict(up_bias=enc_up_b, down_bias=enc_down_b, enc_gain=enc_gain, enc_shift=enc_shift, dec_gain=dec_gain, dec_shift=dec_shift),
        dict(
            source=source, target=target, source_ids=source_ids, target_ids=target_ids, upstream=upstream,
            enc_qkv=enc_qkv, dec_qkv=dec_qkv, cross_qkv=cross_qkv, enc_out_far=enc_out, dec_out_far=dec_out,
            up_far=enc_up, down_far=enc_down,
        ),
        dict(
            chances=(
                ((3 * heads, length, length), BF),
                (2, length, length),
                lambda step: (jnp.where(step < 4, step, jnp.maximum(step - 1, 4)), 0, 0),
                True,
            )
        ),
        {},
        dict(
            x_far=((4, length, size), BF), upstream_there=low_full, queries_far=((3, *per_head), BF),
            keys_far=((3, *per_head), BF), values_far=((3, *per_head), BF), outs_far=((3, *per_head), F32),
            att_far=((3, rows, size), BF), unit0_far=full, scale0_far=thin, unit1_far=full, scale1_far=thin,
            hidden_far=low_full, act_far=low_inner, slope_far=low_inner, first_far=full, first_unit_far=full,
            first_scale_far=thin,
        ),
        dict(
            sems=sem((2, 31)), near_sems=sem((4,)), load_sems=sem((7,)), save_sems=sem((24,)),
            x_all=low(4, length, size), ids=pltpu.VMEM((2, 2, 1, rows), jnp.int32), weights=low(3, 3, size, size),
            queries=low(2, *per_head), keys=low(2, *per_head), values=low(2, *per_head),
            outs=wide(2, *per_head), att_all=low(3, rows, size),
            att_send=low(3, rows, width), enc_out=low(size, size), dec_out=low(size, size), up=low(size, inner),
            down=low(inner, size), unit0=wide(rows, size), scale0=wide(rows, 1), unit1=wide(rows, size),
            scale1=wide(rows, 1), hidden_low=low(rows, size), act=low(rows, inner), slope=low(rows, inner),
            first=wide(rows, size), first_unit=wide(rows, size), first_scale=wide(rows, 1),
        ),
    )
    work = dict(
        grads=low(*per_head), score_grads=low(length, length), dq=low(heads, length, HEAD_DIM), dk=wide(width, length),
        dv=wide(width, length), d_all=low(3, length, width), shares=low(2, 2, 2, 2, 96, 256), end_sems=sem((3, 4)),
    )
    one_sum = ((128, 256), F32)
    sums_out = ((2, 128, 256), F32)
    halves = ((2, 64, 256), F32)
    m = launch(
        middle_body,
        50,
        8,
        1,
        dict(dec_gain=dec_gain, dec_shift=dec_shift, enc_gain=enc_gain, up_bias=dec_up_b, down_bias=dec_down_b),
        dict(
            first_far=f.first_far, att_far=f.att_far, upstream_far=f.upstream_there, cross_out=cross_out, dec_up=dec_up,
            dec_down=dec_down, queries_far=f.queries_far, keys_far=f.keys_far, values_far=f.values_far,
            outs_far=f.outs_far, x_far=f.x_far, cross_qkv=cross_qkv, dec_out=dec_out, first_unit_far=f.first_unit_far,
            first_scale_far=f.first_scale_far, enc_up=enc_up, enc_down=enc_down, enc_out=enc_out,
            unit0_far=f.unit0_far, scale0_far=f.scale0_far, unit1_far=f.unit1_far, scale1_far=f.scale1_far,
            hidden_far=f.hidden_far, act_far=f.act_far, slope_far=f.slope_far,
        ),
        dict(chances=(f.chances, head_block, lambda step: (8 + jnp.clip(step - 2, 0, 3), 0, 0), False)),
        dict(dec_down_sum=one_sum, up_rest=(LEAST, BF), cross_half=(HALF, BF), vectors=((3, 16, size), F32)),
        dict(
            decoded_there=low_full, grads_far=((2, length, width), BF), down_unit=(BIG, BF), up_unit=(BIG, BF),
            out_units=((2, *OUT), BF), pre_far=((2, rows, size), F32),
        ),
        dict(
            sems=sem((3, 18)), load_sems=sem((32,)), **work,
            first=wide(rows, size), att=low(rows, size), upstream=low(rows, size), out_w=low(size, size),
            up=low(size, inner), down=low(inner, size), queries=low(1, *per_head), keys=low(1, *per_head),
            values=low(1, *per_head), outs=wide(1, *per_head), x_all=low(2, length, size), cross_w=low(3, size, size),
            dec_w=low(size, size), first_unit=wide(rows, size), first_scale=wide(rows, 1), dec_att=low(rows, size),
            unit0=wide(rows, size), scale0=wide(rows, 1), unit1=wide(rows, size), scale1=wide(rows, 1),
            entering=low(rows, size), act=low(rows, inner), inner_low=low(rows, inner), branch_low=low(rows, size),
            mixed_low=low(rows, size), att_grad=low(rows, size), dec_att_grad=low(rows, size), dec_mixed=low(rows, size),
            grad=wide(rows, size), pre=wide(2, rows, size), gains=wide(2, 2, size), decoded=low(rows, size),
            grad_all=low(1, length, width), d_full=low(1, 3, rows, size), unit=low(*BIG),
            down_sums=low(2, *BIG), up_sums=low(2, *BIG), out_sums=low(2, *OUT), dec_out_sums=low(2, *OUT),
            down_got=low(*BIG), up_got=low(*BIG), out_got=low(*OUT), dec_out_got=low(*OUT),
            got_a=low(*MID), mid_a=low(*MID), got_b=low(*MID), mid_b=low(*MID), got_c=low(*LESS), got_d=low(*LESS),
            pair=low(2, *LESS), got_e=low(2, *LEAST), mid_e=low(*LEAST), got_f=low(128, 256), got_g=low(*HALF),
        ),
    )
    less, least = (2, 2, 2, 64, 256), (2, 64, 256)
    down_bufs = [low(*MID), low(*MID), low(*LESS), low(*LESS), low(*LEAST), low(*LEAST), low(128, 256)]
    up_bufs = [low(*MID), low(*MID), low(*LESS), low(*LESS), low(*LEAST), low(*LEAST), low(128, 256)]
    join_bufs = [low(*less), low(*less), low(*less), low(*least)]
    split_bufs = [low(*HALF), low(*HALF), *join_bufs]
    b = launch(
        last_body,
        60,
        8,
        2,
        dict(cross_half=m.cross_half, up_rest=m.up_rest, vectors=m.vectors),
        dict(
            queries_far=f.queries_far, keys_far=f.keys_far, values_far=f.values_far, outs_far=f.outs_far, x_far=f.x_far,
            grads_far=m.grads_far, enc_qkv=enc_qkv, dec_qkv=dec_qkv, pre_far=m.pre_far, out_units=m.out_units,
            down_unit=m.down_unit, up_unit=m.up_unit,
        ),
        dict(chances=(f.chances, head_block, lambda step: (step, 0, 0), False)),
        dict(
            enc_sums=sums_out, dec_up_sum=one_sum, cross_sum=halves, enc_att_sum=halves, dec_att_sum=halves,
            vector_sum=((3, 16, size), F32),
        ),
        dict(src_there=low_full, tgt_there=low_full),
        dict(
            sems=sem((3, 32)), load_sems=sem((18,)), **work,
            queries=low(2, *per_head), keys=low(2, *per_head), values=low(2, *per_head), outs=wide(2, *per_head),
            grad_all=low(2, length, width), x_all=low(2, length, size), weights=low(2, 3, size, size),
            pre=wide(2, rows, size), d_full=low(2, 3, rows, size), units=low(2, *BIG), row_grad=low(2, rows, size),
            vector_got=wide(5, 3, 16, size), vector_mid=wide(4, 3, 16, size), down_bufs=down_bufs, up_bufs=up_bufs,
            enc_bufs=split_bufs, cross_bufs=join_bufs, dec_bufs=split_bufs, rest_got=low(128, 256),
        ),
    )
    cut3, cut, pair, triple = ((3, 32, 256), F32), ((32, 256), F32), ((2, size), F32), ((3, size), F32)
    up_cut, down_cut, up_b, down_b = ((256, 128), F32), ((32, 1024), F32), ((1, inner), F32), ((1, size), F32)
    o = launch(
        finish_body,
        2,
        1,
        None,
        dict(
            decoded=m.decoded_there, src=b.src_there, tgt=b.tgt_there, dec_down_sum=m.dec_down_sum, dec_up_sum=b.dec_up_sum,
            enc_sums=b.enc_sums,
            cross_sum=b.cross_sum, enc_att_sum=b.enc_att_sum, dec_att_sum=b.dec_att_sum, vectors=b.vector_sum,
        ),
        {},
        {},
        dict(
            decoded_out=low_full, src_out=low_full, tgt_out=low_full, enc_qkv=cut3, enc_out=cut, enc_up=up_cut,
            enc_up_bias=up_b, enc_down=down_cut, enc_down_bias=down_b, enc_gain=pair, enc_shift=pair, dec_qkv=cut3,
            dec_out=cut, cross_qkv=cut3, cross_out=cut, dec_up=up_cut, dec_up_bias=up_b, dec_down=down_cut,
            dec_down_bias=down_b, dec_gain=triple, dec_shift=triple,
        ),
        {},
        {},
    )

    def turned(value):
        return jnp.swapaxes(value, -1, -2)

    return (
        o.decoded_out[None], o.src_out[None], o.tgt_out[None], turned(o.enc_qkv), turned(o.enc_out), o.enc_up,
        o.enc_up_bias[0], turned(o.enc_down), o.enc_down_bias[0], o.enc_gain, o.enc_shift, turned(o.dec_qkv),
        turned(o.dec_out), turned(o.cross_qkv), turned(o.cross_out), o.dec_up, o.dec_up_bias[0], turned(o.dec_down),
        o.dec_down_bias[0], o.dec_gain, o.dec_shift,
    )


def solution(mesh):
    if mesh.shape[SEQ] != 2 or mesh.shape[BATCH] != 16:
        return general(mesh)
    tokens = P(BATCH, SEQ, None)
    ids = P(BATCH, SEQ)
    cut, cut3 = P(SEQ, BATCH), P(None, SEQ, BATCH)
    return jax.shard_map(
        fast_shards,
        mesh=mesh,
        in_specs=(tokens, tokens, ids, ids, tokens) + (P(),) * 18,
        out_specs=(
            tokens, tokens, tokens, cut3, cut, cut, P(), cut, P(), P(), P(), cut3, cut, cut3, cut, cut, P(), cut,
            P(), P(), P(),
        ),
        check_vma=False,
    )
```

```python
import types

import jax
import jax.numpy as jnp
from jax import lax
from jax.experimental import pallas as pl
from jax.experimental.pallas import tpu as pltpu
from jax.sharding import PartitionSpec as P

HEAD_DIM = 64
NEGATIVE = -1e30
BF = jnp.bfloat16
F32 = jnp.float32


def layer_norm(value, gain, shift):
    mean = jnp.mean(value, axis=-1, keepdims=True)
    centred = value - mean
    spread = jnp.mean(centred * centred, axis=-1, keepdims=True)
    return centred * lax.rsqrt(spread + 1e-06) * gain + shift


def norm_back(value, gain, shift, grad):
    _, pull = jax.vjp(layer_norm, value, gain, shift)
    return pull(grad)


def gelu_back(inner, grad):
    _, pull = jax.vjp(jax.nn.gelu, inner)
    return pull(grad)[0]


def matmul(left, right):
    return jnp.dot(left, right, preferred_element_type=jnp.float32)


def weight_grad(inputs, grad):
    return lax.dot_general(
        inputs, grad, (((0,), (0,)), ((), ())), preferred_element_type=jnp.float32
    )


def input_grad(grad, weight):
    return lax.dot_general(
        grad, weight, (((1,), (1,)), ((), ())), preferred_element_type=jnp.float32
    )


def to_low(value):
    return value.astype(jnp.bfloat16)


def split_heads(value):
    return value.reshape(value.shape[0], -1, HEAD_DIM)


def block_live(query_ids, key_ids, offset, block, rows, causal):
    first_key = lax.dynamic_index_in_dim(key_ids, block * rows, 0, keepdims=False)
    last_key = lax.dynamic_index_in_dim(key_ids, block * rows + rows - 1, 0, keepdims=False)
    live = (first_key <= query_ids[rows - 1]) & (query_ids[0] <= last_key)
    if causal:
        live = live & (block * rows <= offset + rows - 1)
    return live


def block_scores(queries, keys_all, query_ids, key_ids, offset, block, causal):
    rows = queries.shape[0]
    key_block = lax.dynamic_slice_in_dim(keys_all, block * rows, rows, 0)
    id_block = lax.dynamic_slice_in_dim(key_ids, block * rows, rows, 0)
    scores = (
        jnp.einsum("qhe,khe->hqk", queries, key_block, preferred_element_type=jnp.float32) * 0.125
    )
    allowed = query_ids[:, None] == id_block[None, :]
    if causal:
        positions = jnp.arange(rows, dtype=jnp.int32)
        allowed = allowed & ((offset + positions)[:, None] >= (block * rows + positions)[None, :])
    allowed = allowed[None]
    return (jnp.where(allowed, scores, NEGATIVE), allowed, key_block)


def attend_forward(queries, keys_all, values_all, query_ids, key_ids, offset, causal):
    rows = queries.shape[0]
    heads_count = queries.shape[1]
    count = keys_all.shape[0] // rows

    def first_pass(block, carry):

        def first_compute(state):
            largest, total = state
            scores, allowed, _ = block_scores(
                queries, keys_all, query_ids, key_ids, offset, block, causal
            )
            newest = jnp.maximum(largest, jnp.max(scores, axis=-1))
            terms = jnp.where(allowed, jnp.exp(scores - newest[..., None]), 0.0)
            return (newest, total * jnp.exp(largest - newest) + jnp.sum(terms, axis=-1))

        live = block_live(query_ids, key_ids, offset, block, rows, causal)
        return lax.cond(live, first_compute, lambda state: state, carry)

    initial = (
        jnp.full((heads_count, rows), NEGATIVE, jnp.float32),
        jnp.zeros((heads_count, rows), jnp.float32),
    )
    largest, total = lax.fori_loop(0, count, first_pass, initial)
    log_total = largest + jnp.log(total)

    def second_pass(block, carry):

        def second_compute(output):
            scores, allowed, _ = block_scores(
                queries, keys_all, query_ids, key_ids, offset, block, causal
            )
            value_block = lax.dynamic_slice_in_dim(values_all, block * rows, rows, 0)
            chances = jnp.where(allowed, jnp.exp(scores - log_total[..., None]), 0.0)
            return output + jnp.einsum(
                "hqk,khe->qhe", to_low(chances), value_block, preferred_element_type=jnp.float32
            )

        live = block_live(query_ids, key_ids, offset, block, rows, causal)
        return lax.cond(live, second_compute, lambda output: output, carry)

    output = lax.fori_loop(0, count, second_pass, jnp.zeros(queries.shape, jnp.float32))
    return (output, log_total)


def attend_backward(
    queries, keys_all, values_all, query_ids, key_ids, offset, causal, grad_out, settle, log_total
):
    rows = queries.shape[0]
    count = keys_all.shape[0] // rows

    def step_block(block, carry):

        def step_compute(state):
            query_grad, key_grads, value_grads = state
            scores, allowed, key_block = block_scores(
                queries, keys_all, query_ids, key_ids, offset, block, causal
            )
            value_block = lax.dynamic_slice_in_dim(values_all, block * rows, rows, 0)
            chances = jnp.where(allowed, jnp.exp(scores - log_total[..., None]), 0.0)
            chance_grad = jnp.einsum(
                "qhe,khe->hqk", grad_out, value_block, preferred_element_type=jnp.float32
            )
            score_grad = to_low(chances * (chance_grad - settle[..., None]))
            query_grad = (
                query_grad
                + jnp.einsum(
                    "hqk,khe->qhe", score_grad, key_block, preferred_element_type=jnp.float32
                )
                * 0.125
            )
            key_part = (
                jnp.einsum("hqk,qhe->khe", score_grad, queries, preferred_element_type=jnp.float32)
                * 0.125
            )
            value_part = jnp.einsum(
                "hqk,qhe->khe", to_low(chances), grad_out, preferred_element_type=jnp.float32
            )
            key_grads = lax.dynamic_update_slice_in_dim(key_grads, key_part, block * rows, 0)
            value_grads = lax.dynamic_update_slice_in_dim(value_grads, value_part, block * rows, 0)
            return (query_grad, key_grads, value_grads)

        live = block_live(query_ids, key_ids, offset, block, rows, causal)
        return lax.cond(live, step_compute, lambda state: state, carry)

    initial = (
        jnp.zeros(queries.shape, jnp.float32),
        jnp.zeros(keys_all.shape, jnp.float32),
        jnp.zeros(values_all.shape, jnp.float32),
    )
    return lax.fori_loop(0, count, step_block, initial)


def attention_back(
    queries, keys_all, values_all, query_ids, key_ids_all, causal, grad_out, output, log_total
):
    rows = queries.shape[0]
    offset = lax.axis_index("seq") * rows
    settle = jnp.einsum("qhe,qhe->hq", grad_out.astype(jnp.float32), output)
    query_grad, key_terms, value_terms = attend_backward(
        queries,
        keys_all,
        values_all,
        query_ids,
        key_ids_all,
        offset,
        causal,
        grad_out,
        settle,
        log_total,
    )
    key_sum, value_sum = (
        lax.psum_scatter(
            key_terms.reshape(key_terms.shape[0], -1).astype(jnp.bfloat16),
            "seq",
            scatter_dimension=0,
            tiled=True,
        ).astype(jnp.float32),
        lax.psum_scatter(
            value_terms.reshape(value_terms.shape[0], -1).astype(jnp.bfloat16),
            "seq",
            scatter_dimension=0,
            tiled=True,
        ).astype(jnp.float32),
    )
    return (query_grad, key_sum, value_sum)


def general_shards(
    source,
    target,
    source_ids,
    target_ids,
    out_grad,
    enc_qkv,
    enc_out,
    enc_up,
    enc_up_bias,
    enc_down,
    enc_down_bias,
    enc_gain,
    enc_shift,
    dec_qkv,
    dec_out,
    cross_qkv,
    cross_out,
    dec_up,
    dec_up_bias,
    dec_down,
    dec_down_bias,
    dec_gain,
    dec_shift,
):
    src_rows = source[0]
    tgt_rows = target[0]
    src_ids = source_ids[0]
    tgt_ids = target_ids[0]
    rows = src_rows.shape[0]
    offset = lax.axis_index("seq") * rows
    enc_queries = to_low(matmul(src_rows, enc_qkv[0]))
    enc_keys = to_low(matmul(src_rows, enc_qkv[1]))
    enc_values = to_low(matmul(src_rows, enc_qkv[2]))
    enc_keys_all, enc_values_all, src_ids_all = (
        lax.all_gather(enc_keys, "seq", axis=0, tiled=True),
        lax.all_gather(enc_values, "seq", axis=0, tiled=True),
        lax.all_gather(src_ids, "seq", axis=0, tiled=True),
    )
    enc_att, enc_lse = attend_forward(
        split_heads(enc_queries),
        split_heads(enc_keys_all),
        split_heads(enc_values_all),
        src_ids,
        src_ids_all,
        offset,
        False,
    )
    enc_att_low = to_low(enc_att.reshape(rows, -1))
    enc_pre = src_rows.astype(jnp.float32) + matmul(enc_att_low, enc_out)
    hidden = layer_norm(enc_pre, enc_gain[0], enc_shift[0])
    hidden_low = to_low(hidden)
    enc_inner = matmul(hidden_low, enc_up) + enc_up_bias
    enc_act = to_low(jax.nn.gelu(enc_inner))
    enc_last = hidden + matmul(enc_act, enc_down) + enc_down_bias
    memory = layer_norm(enc_last, enc_gain[1], enc_shift[1])
    memory_low = to_low(memory)
    mem_keys = to_low(matmul(memory_low, cross_qkv[1]))
    mem_values = to_low(matmul(memory_low, cross_qkv[2]))
    mem_keys_all, mem_values_all = (
        lax.all_gather(mem_keys, "seq", axis=0, tiled=True),
        lax.all_gather(mem_values, "seq", axis=0, tiled=True),
    )
    dec_queries = to_low(matmul(tgt_rows, dec_qkv[0]))
    dec_keys = to_low(matmul(tgt_rows, dec_qkv[1]))
    dec_values = to_low(matmul(tgt_rows, dec_qkv[2]))
    dec_keys_all, dec_values_all, tgt_ids_all = (
        lax.all_gather(dec_keys, "seq", axis=0, tiled=True),
        lax.all_gather(dec_values, "seq", axis=0, tiled=True),
        lax.all_gather(tgt_ids, "seq", axis=0, tiled=True),
    )
    dec_att, dec_lse = attend_forward(
        split_heads(dec_queries),
        split_heads(dec_keys_all),
        split_heads(dec_values_all),
        tgt_ids,
        tgt_ids_all,
        offset,
        True,
    )
    dec_att_low = to_low(dec_att.reshape(rows, -1))
    dec_pre = tgt_rows.astype(jnp.float32) + matmul(dec_att_low, dec_out)
    first = layer_norm(dec_pre, dec_gain[0], dec_shift[0])
    first_low = to_low(first)
    cross_queries = to_low(matmul(first_low, cross_qkv[0]))
    cross_att, cross_lse = attend_forward(
        split_heads(cross_queries),
        split_heads(mem_keys_all),
        split_heads(mem_values_all),
        tgt_ids,
        src_ids_all,
        offset,
        False,
    )
    cross_att_low = to_low(cross_att.reshape(rows, -1))
    cross_pre = first + matmul(cross_att_low, cross_out)
    second = layer_norm(cross_pre, dec_gain[1], dec_shift[1])
    second_low = to_low(second)
    dec_inner = matmul(second_low, dec_up) + dec_up_bias
    dec_act = to_low(jax.nn.gelu(dec_inner))
    dec_last = second + matmul(dec_act, dec_down) + dec_down_bias
    decoded = layer_norm(dec_last, dec_gain[2], dec_shift[2])
    upstream = out_grad[0].astype(jnp.float32)
    grad_last, gain_two, shift_two = norm_back(dec_last, dec_gain[2], dec_shift[2], upstream)
    branch_low = to_low(grad_last)
    dec_down_g = weight_grad(dec_act, branch_low)
    dec_down_bias_g = jnp.sum(branch_low.astype(jnp.float32), axis=0)
    inner_low = to_low(gelu_back(dec_inner, input_grad(branch_low, dec_down)))
    dec_up_g = weight_grad(second_low, inner_low)
    dec_up_bias_g = jnp.sum(inner_low.astype(jnp.float32), axis=0)
    grad_second = grad_last + input_grad(inner_low, dec_up)
    grad_cross_pre, gain_one, shift_one = norm_back(
        cross_pre, dec_gain[1], dec_shift[1], grad_second
    )
    mixed_low = to_low(grad_cross_pre)
    cross_out_g = weight_grad(cross_att_low, mixed_low)
    cross_att_grad = to_low(input_grad(mixed_low, cross_out))
    cross_query_grad, mem_key_sum, mem_value_sum = attention_back(
        split_heads(cross_queries),
        split_heads(mem_keys_all),
        split_heads(mem_values_all),
        tgt_ids,
        src_ids_all,
        False,
        split_heads(cross_att_grad),
        cross_att,
        cross_lse,
    )
    mem_key_low = to_low(mem_key_sum)
    mem_value_low = to_low(mem_value_sum)
    cross_query_low = to_low(cross_query_grad.reshape(rows, -1))
    cross_qkv_g = jnp.stack(
        [
            weight_grad(first_low, cross_query_low),
            weight_grad(memory_low, mem_key_low),
            weight_grad(memory_low, mem_value_low),
        ]
    )
    grad_first = grad_cross_pre + input_grad(cross_query_low, cross_qkv[0])
    grad_dec_pre, gain_zero, shift_zero = norm_back(dec_pre, dec_gain[0], dec_shift[0], grad_first)
    self_low = to_low(grad_dec_pre)
    dec_out_g = weight_grad(dec_att_low, self_low)
    dec_att_grad = to_low(input_grad(self_low, dec_out))
    dec_query_grad, dec_key_sum, dec_value_sum = attention_back(
        split_heads(dec_queries),
        split_heads(dec_keys_all),
        split_heads(dec_values_all),
        tgt_ids,
        tgt_ids_all,
        True,
        split_heads(dec_att_grad),
        dec_att,
        dec_lse,
    )
    dec_query_low = to_low(dec_query_grad.reshape(rows, -1))
    dec_key_low = to_low(dec_key_sum)
    dec_value_low = to_low(dec_value_sum)
    dec_qkv_g = jnp.stack(
        [
            weight_grad(tgt_rows, dec_query_low),
            weight_grad(tgt_rows, dec_key_low),
            weight_grad(tgt_rows, dec_value_low),
        ]
    )
    tgt_grad = (
        grad_dec_pre
        + input_grad(dec_query_low, dec_qkv[0])
        + input_grad(dec_key_low, dec_qkv[1])
        + input_grad(dec_value_low, dec_qkv[2])
    )
    dec_gain_g = jnp.stack([gain_zero, gain_one, gain_two])
    dec_shift_g = jnp.stack([shift_zero, shift_one, shift_two])
    grad_memory = input_grad(mem_key_low, cross_qkv[1]) + input_grad(mem_value_low, cross_qkv[2])
    grad_enc_last, enc_gain_one, enc_shift_one = norm_back(
        enc_last, enc_gain[1], enc_shift[1], grad_memory
    )
    enc_branch_low = to_low(grad_enc_last)
    enc_down_g = weight_grad(enc_act, enc_branch_low)
    enc_down_bias_g = jnp.sum(enc_branch_low.astype(jnp.float32), axis=0)
    enc_inner_low = to_low(gelu_back(enc_inner, input_grad(enc_branch_low, enc_down)))
    enc_up_g = weight_grad(hidden_low, enc_inner_low)
    enc_up_bias_g = jnp.sum(enc_inner_low.astype(jnp.float32), axis=0)
    grad_hidden = grad_enc_last + input_grad(enc_inner_low, enc_up)
    grad_enc_pre, enc_gain_zero, enc_shift_zero = norm_back(
        enc_pre, enc_gain[0], enc_shift[0], grad_hidden
    )
    enc_mixed_low = to_low(grad_enc_pre)
    enc_out_g = weight_grad(enc_att_low, enc_mixed_low)
    enc_att_grad = to_low(input_grad(enc_mixed_low, enc_out))
    enc_query_grad, enc_key_sum, enc_value_sum = attention_back(
        split_heads(enc_queries),
        split_heads(enc_keys_all),
        split_heads(enc_values_all),
        src_ids,
        src_ids_all,
        False,
        split_heads(enc_att_grad),
        enc_att,
        enc_lse,
    )
    enc_query_low = to_low(enc_query_grad.reshape(rows, -1))
    enc_key_low = to_low(enc_key_sum)
    enc_value_low = to_low(enc_value_sum)
    enc_qkv_g = jnp.stack(
        [
            weight_grad(src_rows, enc_query_low),
            weight_grad(src_rows, enc_key_low),
            weight_grad(src_rows, enc_value_low),
        ]
    )
    src_grad = (
        grad_enc_pre
        + input_grad(enc_query_low, enc_qkv[0])
        + input_grad(enc_key_low, enc_qkv[1])
        + input_grad(enc_value_low, enc_qkv[2])
    )
    enc_gain_g = jnp.stack([enc_gain_zero, enc_gain_one])
    enc_shift_g = jnp.stack([enc_shift_zero, enc_shift_one])
    all_rows = (
        lax.psum_scatter(
            enc_qkv_g.astype(jnp.bfloat16), "seq", scatter_dimension=1, tiled=True
        ).astype(jnp.float32),
        lax.psum_scatter(
            enc_out_g.astype(jnp.bfloat16), "seq", scatter_dimension=0, tiled=True
        ).astype(jnp.float32),
        lax.psum_scatter(
            enc_up_g.astype(jnp.bfloat16), "seq", scatter_dimension=0, tiled=True
        ).astype(jnp.float32),
        lax.psum_scatter(
            enc_down_g.astype(jnp.bfloat16), "seq", scatter_dimension=0, tiled=True
        ).astype(jnp.float32),
        lax.psum_scatter(
            dec_qkv_g.astype(jnp.bfloat16), "seq", scatter_dimension=1, tiled=True
        ).astype(jnp.float32),
        lax.psum_scatter(
            dec_out_g.astype(jnp.bfloat16), "seq", scatter_dimension=0, tiled=True
        ).astype(jnp.float32),
        lax.psum_scatter(
            cross_qkv_g.astype(jnp.bfloat16), "seq", scatter_dimension=1, tiled=True
        ).astype(jnp.float32),
        lax.psum_scatter(
            cross_out_g.astype(jnp.bfloat16), "seq", scatter_dimension=0, tiled=True
        ).astype(jnp.float32),
        lax.psum_scatter(
            dec_up_g.astype(jnp.bfloat16), "seq", scatter_dimension=0, tiled=True
        ).astype(jnp.float32),
        lax.psum_scatter(
            dec_down_g.astype(jnp.bfloat16), "seq", scatter_dimension=0, tiled=True
        ).astype(jnp.float32),
    )
    reduced = (
        lax.psum_scatter(
            all_rows[0].astype(jnp.bfloat16), "batch", scatter_dimension=2, tiled=True
        ).astype(jnp.float32),
        lax.psum_scatter(
            all_rows[1].astype(jnp.bfloat16), "batch", scatter_dimension=1, tiled=True
        ).astype(jnp.float32),
        lax.psum_scatter(
            all_rows[2].astype(jnp.bfloat16), "batch", scatter_dimension=1, tiled=True
        ).astype(jnp.float32),
        lax.psum_scatter(
            all_rows[3].astype(jnp.bfloat16), "batch", scatter_dimension=1, tiled=True
        ).astype(jnp.float32),
        lax.psum_scatter(
            all_rows[4].astype(jnp.bfloat16), "batch", scatter_dimension=2, tiled=True
        ).astype(jnp.float32),
        lax.psum_scatter(
            all_rows[5].astype(jnp.bfloat16), "batch", scatter_dimension=1, tiled=True
        ).astype(jnp.float32),
        lax.psum_scatter(
            all_rows[6].astype(jnp.bfloat16), "batch", scatter_dimension=2, tiled=True
        ).astype(jnp.float32),
        lax.psum_scatter(
            all_rows[7].astype(jnp.bfloat16), "batch", scatter_dimension=1, tiled=True
        ).astype(jnp.float32),
        lax.psum_scatter(
            all_rows[8].astype(jnp.bfloat16), "batch", scatter_dimension=1, tiled=True
        ).astype(jnp.float32),
        lax.psum_scatter(
            all_rows[9].astype(jnp.bfloat16), "batch", scatter_dimension=1, tiled=True
        ).astype(jnp.float32),
    )
    vectors = lax.psum(
        (
            enc_up_bias_g,
            enc_down_bias_g,
            enc_gain_g,
            enc_shift_g,
            dec_up_bias_g,
            dec_down_bias_g,
            dec_gain_g,
            dec_shift_g,
        ),
        ("batch", "seq"),
    )
    return (
        to_low(decoded)[None],
        to_low(src_grad)[None],
        to_low(tgt_grad)[None],
        reduced[0],
        reduced[1],
        reduced[2],
        vectors[0],
        reduced[3],
        vectors[1],
        vectors[2],
        vectors[3],
        reduced[4],
        reduced[5],
        reduced[6],
        reduced[7],
        reduced[8],
        vectors[4],
        reduced[9],
        vectors[5],
        vectors[6],
        vectors[7],
    )


def general(mesh):
    placed = (
        P("batch", "seq", None),
        P("batch", "seq", None),
        P("batch", "seq"),
        P("batch", "seq"),
        P("batch", "seq", None),
        P(),
        P(),
        P(),
        P(),
        P(),
        P(),
        P(),
        P(),
        P(),
        P(),
        P(),
        P(),
        P(),
        P(),
        P(),
        P(),
        P(),
        P(),
    )
    return jax.shard_map(
        general_shards,
        mesh=mesh,
        in_specs=placed,
        out_specs=(
            P("batch", "seq", None),
            P("batch", "seq", None),
            P("batch", "seq", None),
            P(None, "seq", "batch"),
            P("seq", "batch"),
            P("seq", "batch"),
            P(),
            P("seq", "batch"),
            P(),
            P(),
            P(),
            P(None, "seq", "batch"),
            P("seq", "batch"),
            P(None, "seq", "batch"),
            P("seq", "batch"),
            P("seq", "batch"),
            P(),
            P("seq", "batch"),
            P(),
            P(),
            P(),
        ),
        check_vma=False,
    )


BATCH, SEQ = "batch", "seq"
CORE, X, Y, LOW, HIGH, SWAP = range(6)
ALL = (CORE, X, Y, LOW, HIGH)
TILE = 256
MESH = pl.DeviceIdType.MESH
VMEM = pl.BlockSpec(memory_space=pltpu.VMEM)
ANY = pl.BlockSpec(memory_space=pl.ANY)


def dot(left, right, left_dim=1, right_dim=0):
    return lax.dot_general(
        left, right, (((left_dim,), (right_dim,)), ((), ())), preferred_element_type=F32
    )


def block(index, size):
    return pl.ds(pl.multiple_of(index * size, size), size)


def normed(value):
    centred = value - jnp.mean(value, axis=-1, keepdims=True)
    scale = lax.rsqrt(jnp.mean(centred * centred, axis=-1, keepdims=True) + 1e-06)
    return centred * scale, scale


def normed_back(grad, unit, scale, gain):
    scaled = grad * gain
    first = jnp.mean(scaled, axis=-1, keepdims=True)
    second = jnp.mean(scaled * unit, axis=-1, keepdims=True)
    return scale * (scaled - first - unit * second)


def gelu_and_slope(inner):
    square = inner * inner
    bent = jnp.tanh(0.7978845608028654 * inner * (1.0 + 0.044715 * square))
    half = 0.5 * (1.0 + bent)
    slope = half + 0.5 * inner * (1.0 - bent * bent) * (
        0.7978845608028654 * (1.0 + 0.134145 * square)
    )
    return inner * half, slope


def column_sum(value):
    return jnp.sum(value, axis=0, keepdims=True)


def parts_of(up):
    return [slice(p * 512, (p + 1) * 512) for p in range(up.shape[1] // 512)]


def over_tiles(rows):
    def run(body):
        @pl.loop(0, rows // TILE, unroll=2)
        def _(tile):
            body(block(tile, TILE))

    return run


def places():
    row, s = lax.axis_index(BATCH), lax.axis_index(SEQ)
    core = lax.rem(row, 2)
    y = lax.rem(row // 2, 2)
    low = lax.rem(row // 4, 2)
    high = row // 8
    mine = (core, s, y, low, high + core - 2 * high * core)
    partner = (
        {BATCH: row + 1 - 2 * core},
        {SEQ: 1 - s},
        {BATCH: row + 2 - 4 * y},
        {BATCH: row + 4 - 8 * low},
        {BATCH: row + 8 - 16 * high},
        {BATCH: row - core + s, SEQ: core},
    )
    return mine, partner


def my_core():
    return places()[0][CORE]


def call_out(ways):
    mine, partner = places()
    barrier = pltpu.get_barrier_semaphore()
    for way in ways:
        pl.semaphore_signal(barrier, inc=1, device_id=partner[way], device_id_type=MESH)

    @pl.when(mine[CORE] != mine[X])
    def _():
        pl.semaphore_signal(barrier, inc=1, device_id=partner[SWAP], device_id_type=MESH)


def hear(ways):
    mine, _ = places()
    away = mine[CORE] + mine[X] - 2 * mine[CORE] * mine[X]
    pl.semaphore_wait(pltpu.get_barrier_semaphore(), len(ways) + away)


def sending(source, target, sems, slot, way):
    return pltpu.make_async_remote_copy(
        src_ref=source,
        dst_ref=target,
        send_sem=sems.at[0, slot],
        recv_sem=sems.at[1, slot],
        device_id=places()[1][way],
        device_id_type=MESH,
    )


def start_swap(source, target, sems, slot):
    mine, _ = places()

    @pl.when(mine[CORE] != mine[X])
    def _():
        sending(source, target, sems, slot, SWAP).start()

    @pl.when(mine[CORE] == mine[X])
    def _():
        pltpu.make_async_copy(source, target, sems.at[0, slot]).start()


def wait_swap(source, target, sems, slot):
    mine, _ = places()

    @pl.when(mine[CORE] != mine[X])
    def _():
        sending(source, target, sems, slot, SWAP).wait()

    @pl.when(mine[CORE] == mine[X])
    def _():
        pltpu.make_async_copy(source, target, sems.at[0, slot]).wait()


class RowSwap:
    def __init__(self, source, target, pieces, sems, slot, near_sem):
        mine, _ = places()
        self.here = mine[CORE] == mine[X]
        self.pieces = range(len(pieces))
        whole = target(mine[X], None)
        self.near = lambda: pltpu.make_async_copy(source, whole, near_sem)
        self.early = lambda: sending(source, whole, sems, slot, CORE)
        self.across = lambda k: sending(source.at[pieces[k]], target(mine[X], pieces[k]), sems, slot + 1 + k, SWAP)

        def onward(k):
            ref = target(mine[CORE], pieces[k])
            return sending(ref, ref, sems, slot + 1 + len(pieces) + k, CORE)

        self.onward = onward

    def finish_early(self):
        @pl.when(self.here)
        def _():
            self.near().wait()

        @pl.when(jnp.logical_not(self.here))
        def _():
            self.early().wait_recv()

    def start(self):
        @pl.when(self.here)
        def _():
            self.near().start()
            self.early().start()

        @pl.when(jnp.logical_not(self.here))
        def _():
            for k in self.pieces:
                self.across(k).start()

    def pass_on(self):
        @pl.when(jnp.logical_not(self.here))
        def _():
            for k in self.pieces:
                self.across(k).wait()
                self.onward(k).start()

    def finish(self):
        @pl.when(self.here)
        def _():
            self.early().wait_send()
            for k in self.pieces:
                self.onward(k).wait_recv()

        @pl.when(jnp.logical_not(self.here))
        def _():
            for k in self.pieces:
                self.onward(k).wait_send()


def part_of(ref, axis, index):
    return ref.at[(slice(None),) * axis + (index,)]


class Halving:
    def __init__(self, source, axis, way, got, total, sems, slot, far=False):
        mine, _ = places()
        kept = part_of(source, axis, mine[way])
        self.kept, self.got, self.total = (total if far else kept), got, total
        self.sent = lambda: sending(part_of(source, axis, 1 - mine[way]), got, sems, slot, way)
        self.near = (lambda: pltpu.make_async_copy(kept, total, sems.at[2, slot])) if far else None

    def start(self):
        self.sent().start()
        if self.near is not None:
            self.near().start()

    def finish(self):
        if self.near is not None:
            self.near().wait()
        self.sent().wait()
        if self.total.dtype == F32:
            self.total[...] = self.kept[...].astype(F32) + self.got[...].astype(F32)
        else:
            self.total[...] = self.kept[...] + self.got[...]


class Across:
    def __init__(self, sums, got, sems, slot):
        self.sums, self.got = sums, got
        self.sent = lambda: sending(sums.at[1], got, sems, slot, CORE)

    def start(self):
        self.sent().start()

    def finish(self):
        self.sent().wait()
        self.sums[0] = self.sums[0] + self.got[...]


class Copies:
    def __init__(self, pairs, sems, first=0):
        self.copies = [
            (lambda source=source, target=target, place=place: pltpu.make_async_copy(source, target, sems.at[first + place]))
            for place, (source, target) in enumerate(pairs)
        ]

    def start(self):
        for copy in self.copies:
            copy().start()

    def wait(self):
        for copy in self.copies:
            copy().wait()


def attend_begin(r, att, half):
    heads = r.queries.shape[1]
    width = heads * HEAD_DIM
    columns = block(my_core(), width)
    q_from, k_from = att, att + att // 2
    q_side, k_side = jnp.minimum(att, 1), att * (2 - att)
    which = lax.rem(att, 2)
    place = lax.broadcasted_iota(jnp.int32, (HEAD_DIM, TILE), 0)
    ones = jnp.ones((TILE, HEAD_DIM), BF)
    half_tiles = r.ids.shape[3] // TILE

    @pl.loop(0, half_tiles, unroll=2)
    def _(tile):
        here = pl.ds(pl.multiple_of(half * r.ids.shape[3] + tile * TILE, TILE), TILE)
        lanes = block(tile, TILE)
        q_ids = r.ids[q_side, half, :, lanes]
        k_ids = r.ids[k_side, half, :, lanes]
        asks = jnp.where(place == q_ids, 1.0, 0.0).T.astype(BF)
        bars = jnp.where((place != k_ids) & (place < 3), NEGATIVE, 0.0).T.astype(BF)
        left_q, left_k = r.x_all[q_from, here, :], r.x_all[k_from, here, :]
        q_tile = dot(left_q, r.weights[att, 0, :, columns]).astype(BF) * BF(0.125)
        k_tile = dot(left_k, r.weights[att, 1, :, columns]).astype(BF)
        v_tile = dot(left_k, r.weights[att, 2, :, columns]).astype(BF)
        for head in range(heads):
            part = slice(head * HEAD_DIM, (head + 1) * HEAD_DIM)
            r.queries[which, head, here, :] = jnp.concatenate([q_tile[:, part], asks], axis=1)
            r.keys[which, head, here, :] = jnp.concatenate([k_tile[:, part], bars], axis=1)
            r.values[which, head, here, :] = jnp.concatenate([v_tile[:, part], ones], axis=1)


def attend_heads(r, which, first, causal):
    length = r.queries.shape[2]
    lower = lax.broadcasted_iota(jnp.int32, (TILE, TILE), 0) >= lax.broadcasted_iota(jnp.int32, (TILE, TILE), 1)
    work = [(head, tile) for head in range(2) for tile in range(length // TILE)]

    def seen(tile):
        return (tile + 1) * TILE if causal else length

    def scores_of(head, tile):
        here = slice(tile * TILE, (tile + 1) * TILE)
        scores = dot(r.queries[which, first + head, here, :], r.keys[which, first + head, : seen(tile), :], 1, 1)
        if not causal:
            return scores
        last = jnp.where(lower, scores[:, seen(tile) - TILE :], NEGATIVE)
        return last if tile == 0 else jnp.concatenate([scores[:, : seen(tile) - TILE], last], axis=1)

    scores = scores_of(*work[0])
    for place, (head, tile) in enumerate(work):
        here = slice(tile * TILE, (tile + 1) * TILE)
        later = scores_of(*work[place + 1]) if place + 1 < len(work) else None
        low = jnp.exp(scores - jnp.max(scores, axis=-1, keepdims=True)).astype(BF)
        r.chances[head, here, : seen(tile)] = low
        r.outs[which, first + head, here, :] = dot(low, r.values[which, first + head, : seen(tile), :])
        scores = later


def forward_body(r):
    step = pl.program_id(0)
    mine, _ = places()
    core = mine[CORE]
    att = jnp.minimum(step // 2, 2)
    rows = r.source.shape[0]
    heads = r.outs.shape[1]
    width = heads * HEAD_DIM
    sems = r.sems

    def rows_of(side):
        def target(half, piece):
            first = half * rows if piece is None else half * rows + piece.start
            count = rows if piece is None else piece.size
            return r.x_all.at[side, pl.ds(pl.multiple_of(first, count), count)]

        return target

    def ids_of(side):
        return lambda half, piece: r.ids.at[side, half]

    quarters = [pl.ds(k * rows // 4, rows // 4) for k in range(4)]
    source = RowSwap(r.source, rows_of(0), quarters, sems, 0, r.near_sems.at[0])
    target = RowSwap(r.target, rows_of(1), quarters, sems, 9, r.near_sems.at[1])
    one = [pl.ds(0, 1)]
    ids = (
        RowSwap(r.source_ids, ids_of(0), one, sems, 18, r.near_sems.at[2]),
        RowSwap(r.target_ids, ids_of(1), one, sems, 21, r.near_sems.at[3]),
    )
    first_across = sending(r.x_all.at[2, block(core, rows)], r.x_all.at[2, block(core, rows)], sems, 24, CORE)

    def att_across(index):
        return sending(r.att_send.at[index], r.att_all.at[index, :, block(core, width)], sems, 25 + index, CORE)

    def memory_across(tile):
        ref = r.x_all.at[3, pl.ds(pl.multiple_of(core * rows + tile * TILE, TILE), TILE)]
        return sending(ref, ref, sems, 28 + tile, CORE)

    loads = Copies(
        [
            (r.enc_qkv, r.weights.at[0]), (r.dec_qkv, r.weights.at[1]), (r.cross_qkv, r.weights.at[2]),
            (r.enc_out_far, r.enc_out), (r.dec_out_far, r.dec_out), (r.up_far, r.up), (r.down_far, r.down),
        ],
        r.load_sems,
    )

    def saved(index):
        which = index % 2
        return Copies(
            [
                (r.queries.at[which], r.queries_far.at[index]), (r.keys.at[which], r.keys_far.at[index]),
                (r.values.at[which], r.values_far.at[index]),
            ],
            r.save_sems,
            index * 4,
        )

    def saved_outs(index):
        return Copies([(r.outs.at[index % 2], r.outs_far.at[index])], r.save_sems, index * 4 + 3)

    kept = Copies(
        [
            (r.unit0, r.unit0_far), (r.scale0, r.scale0_far), (r.unit1, r.unit1_far), (r.scale1, r.scale1_far),
            (r.hidden_low, r.hidden_far), (r.act, r.act_far), (r.slope, r.slope_far), (r.first, r.first_far),
            (r.first_unit, r.first_unit_far), (r.first_scale, r.first_scale_far), (r.x_all, r.x_far),
        ],
        r.save_sems,
        12,
    )
    att_kept = Copies([(r.att_all, r.att_far)], r.save_sems, 23)

    @pl.when(step == 0)
    def _():
        call_out((CORE,))
        loads.start()
        hear((CORE,))
        for one_side in ids:
            one_side.start()
        source.start()
        target.start()
        start_swap(r.upstream, r.upstream_there, sems, 30)
        loads.wait()
        for one_side in ids:
            one_side.finish_early()
        source.finish_early()

    @pl.when(step == 2)
    def _():
        target.pass_on()
        target.finish_early()

    @pl.when(step == 5)
    def _():
        saved(0).wait()
        saved_outs(0).wait()
        first_across.wait()

        @pl.loop(0, rows // TILE)
        def _(tile):
            memory_across(tile).wait()

        kept.start()

    begins = (step == 0) | (step == 2) | (step == 5)

    @pl.when(begins)
    def _():
        attend_begin(r, att, mine[X])

    @pl.when(step == 0)
    def _():
        for one_side in ids:
            one_side.pass_on()
        source.pass_on()
        for one_side in ids:
            one_side.finish()
        source.finish()

    @pl.when(step == 2)
    def _():
        target.finish()

    @pl.when(begins)
    def _():
        attend_begin(r, att, 1 - mine[X])

    for index, begun in enumerate((0, 2, 5)):

        @pl.when(step == begun)
        def _(index=index):
            saved(index).start()

    @pl.when((step < 2) | (step > 4))
    def _():
        attend_heads(r, 0, 2 * lax.rem(step - att // 2, 2), False)

    @pl.when((step == 2) | (step == 3))
    def _():
        attend_heads(r, 1, 2 * (step - 2), True)

    @pl.when((step == 1) | (step == 3) | (step == 6))
    def _():
        for half in (1 - core, core):
            there = block(half, rows)
            parts = [r.outs[lax.rem(att, 2), head, there, :] for head in range(heads)]
            joined = jnp.concatenate([part[:, :HEAD_DIM] / part[:, HEAD_DIM:] for part in parts], axis=1).astype(BF)
            if half is core:
                r.att_all[att, :, block(core, width)] = joined
            else:
                r.att_send[att] = joined
                att_across(att).start()

    for index, last in enumerate((1, 3, 6)):

        @pl.when(step == last)
        def _(index=index):
            saved_outs(index).start()

    @pl.when(step == 4)
    def _():
        att_across(0).wait()
        att_across(1).wait()

        @over_tiles(rows)
        def _(here):
            own = pl.ds(pl.multiple_of(core * rows + here.start, TILE), TILE)
            unit, scale = normed(r.x_all[1, own, :].astype(F32) + dot(r.att_all[1, here, :], r.dec_out[...]))
            r.first_unit[here, :] = unit
            r.first_scale[here, :] = scale
            value = unit * r.dec_gain[0:1, :] + r.dec_shift[0:1, :]
            r.first[here, :] = value
            r.x_all[2, own, :] = value.astype(BF)

        first_across.start()

        @pl.loop(0, rows // TILE)
        def _(tile):
            here = block(tile, TILE)
            own = pl.ds(pl.multiple_of(core * rows + tile * TILE, TILE), TILE)
            unit, scale = normed(r.x_all[0, own, :].astype(F32) + dot(r.att_all[0, here, :], r.enc_out[...]))
            r.unit0[here, :] = unit
            r.scale0[here, :] = scale
            hidden = unit * r.enc_gain[0:1, :] + r.enc_shift[0:1, :]
            low = hidden.astype(BF)
            r.hidden_low[here, :] = low
            for part in parts_of(r.up):
                value, bend = gelu_and_slope(dot(low, r.up[:, part]) + r.up_bias[:, part])
                r.slope[here, part] = bend.astype(BF)
                r.act[here, part] = value.astype(BF)
            unit, scale = normed(hidden + dot(r.act[here, :], r.down[...]) + r.down_bias[...])
            r.unit1[here, :] = unit
            r.scale1[here, :] = scale
            r.x_all[3, own, :] = (unit * r.enc_gain[1:2, :] + r.enc_shift[1:2, :]).astype(BF)
            memory_across(tile).start()

    @pl.when(step == 6)
    def _():
        kept.wait()
        saved(1).wait()
        saved_outs(1).wait()
        wait_swap(r.upstream, r.upstream_there, sems, 30)
        att_across(2).wait()
        att_kept.start()
        saved(2).wait()
        saved_outs(2).wait()
        att_kept.wait()


def back_begin(r, which):
    heads = r.queries.shape[1]
    width = heads * HEAD_DIM
    lane = lax.rem(lax.broadcasted_iota(jnp.int32, (TILE, width), 1), HEAD_DIM)
    same_head = (
        lax.broadcasted_iota(jnp.int32, (width, width), 0) // HEAD_DIM
        == lax.broadcasted_iota(jnp.int32, (width, width), 1) // HEAD_DIM
    ).astype(BF)

    @over_tiles(r.queries.shape[2])
    def _(here):
        grad = r.grad_all[which, here, :].astype(F32)
        lows, boths = [], []
        for head in range(heads):
            out = r.outs[which, head, here, :]
            over = 1.0 / out[:, HEAD_DIM:]
            low = (grad[:, head * HEAD_DIM : (head + 1) * HEAD_DIM] * over).astype(BF)
            lows.append(low)
            boths.append(low.astype(F32) * (out[:, :HEAD_DIM] * over))
        both = jnp.concatenate(boths, axis=1)
        high = both.astype(BF)
        rest = (both - high.astype(F32)).astype(BF)
        settle = -dot(high, same_head) - dot(rest, same_head)
        first = settle.astype(BF).astype(F32)
        second = (settle - first).astype(BF).astype(F32)
        extra = jnp.where(lane == 0, first, jnp.where(lane == 1, second, jnp.where(lane == 2, settle - first - second, 0.0)))
        extra = extra.astype(BF)
        for head in range(heads):
            r.grads[head, here, :] = jnp.concatenate(
                [lows[head], extra[:, head * HEAD_DIM : (head + 1) * HEAD_DIM]], axis=1
            )


def back_head(r, which, head, causal):
    length = r.queries.shape[2]
    count = length // TILE

    def seen(tile):
        return (tile + 1) * TILE if causal else length

    def change_of(tile):
        here = slice(tile * TILE, (tile + 1) * TILE)
        return dot(r.grads[head, here, :], r.values[which, head, : seen(tile), :], 1, 1)

    change = change_of(0)
    for tile in range(count):
        here = slice(tile * TILE, (tile + 1) * TILE)
        later = change_of(tile + 1) if tile + 1 < count else None
        low = (r.chances[0, here, : seen(tile)].astype(F32) * change).astype(BF)
        r.score_grads[here, : seen(tile)] = low
        r.dq[head, here, :] = (dot(low, r.keys[which, head, : seen(tile), :])[:, :HEAD_DIM] * 0.125).astype(BF)
        change = later
    for tile in range(count if causal else 1):
        here = slice(tile * TILE, (tile + 1) * TILE) if causal else slice(0, length)
        below = slice(tile * TILE, length)
        r.dv[block(head, HEAD_DIM), here] = dot(
            r.grads[head, below, :HEAD_DIM], r.chances[0, below, here], 0, 0
        )
        r.dk[block(head, HEAD_DIM), here] = dot(
            r.queries[which, head, below, :HEAD_DIM], r.score_grads[below, here], 0, 0
        )


class BackEnd:
    def __init__(self, r, which, unit, q_from, k_from, sems):
        self.r, self.q_from, self.k_from = r, q_from, k_from
        core = my_core()
        rows = r.d_full.shape[2]
        width = r.d_all.shape[2]
        lanes = block(core, width)
        self.other = lambda: sending(
            r.d_all.at[:, block(1 - core, rows)], r.d_full.at[which, :, :, lanes], sems, 2 * which, CORE
        )
        self.own = lambda: pltpu.make_async_copy(
            r.d_all.at[:, block(core, rows)], r.d_full.at[which, :, :, lanes], sems.at[2, 2 * which]
        )
        below = pl.ds(32, 96)
        self.across = lambda: sending(r.shares.at[1], unit.at[:, :, :, 1, below], sems, 2 * which + 1, CORE)
        self.along = lambda: pltpu.make_async_copy(r.shares.at[0], unit.at[:, :, :, 0, below], sems.at[2, 2 * which + 1])

    def start(self):
        r = self.r
        core = my_core()
        rows, heads = r.d_full.shape[2], r.dq.shape[0]

        @pl.loop(0, 2, unroll=2)
        def _(half):
            there = block(half, rows)
            r.d_all[0, there, :] = jnp.concatenate([r.dq[head, there, :] for head in range(heads)], axis=1)
            r.d_all[1, there, :] = r.dk[:, there].T.astype(BF)
            r.d_all[2, there, :] = r.dv[:, there].T.astype(BF)

        self.other().start()
        self.own().start()

        @pl.loop(0, 3, unroll=3)
        def _(kind):
            x_from = jnp.where(kind == 0, self.q_from, self.k_from)
            low = dot(r.d_all[kind], r.x_all[x_from], 0, 0).astype(BF)
            for part in range(low.shape[0] // 32):
                z_low, y, kept = part >> 2, (part >> 1) & 1, part & 1
                for s in range(2):
                    r.shares[core if kept == 0 else 1 - core, s, y, z_low, block(kind, 32), :] = low[
                        part * 32 : (part + 1) * 32, s * 256 : (s + 1) * 256
                    ]

        self.across().start()
        self.along().start()

    def wait_grads(self):
        self.own().wait()
        self.other().wait()

    def wait_sums(self):
        self.along().wait()
        self.across().wait()


BIG = (2, 2, 2, 2, 128, 256)
MID = BIG[1:]
LESS = BIG[2:]
LEAST = BIG[3:]
OUT = (2, 2, 2, 2, 32, 256)
HALF = (2, 2, 2, 2, 64, 256)


def sum_up(sums, inner_low, entering):
    core = my_core()

    @pl.loop(0, 4, unroll=4)
    def _(z):
        for y in range(2):
            low = dot(inner_low[:, block(z * 2 + y, 256)], entering[...], 0, 0).astype(BF)
            high = z // 2
            for kept in range(2):
                for s in range(2):
                    sums[
                        core if kept == 0 else 1 - core, s, y, lax.rem(z, 2), 1 - high if kept else high, :, :
                    ] = low[kept * 128 : (kept + 1) * 128, s * 256 : (s + 1) * 256]


def sum_down(sums, branch_low, act):
    core = my_core()

    @pl.loop(0, act.shape[1] // 512, unroll=4)
    def _(column):
        for index in range(2):
            low = dot(branch_low[:, index * 256 : (index + 1) * 256], act[:, block(column, 512)], 0, 0).astype(BF)
            for part in range(8):
                place = index * 8 + part
                z, y, kept = place >> 2, (place >> 1) & 1, place & 1
                for piece in range(2):
                    slot = lax.rem(column, 2) * 2 + piece
                    sums[
                        core if kept == 0 else 1 - core, column // 2, y, z & 1, (z >> 1) ^ kept, block(slot, 32), :
                    ] = low[part * 32 : (part + 1) * 32, piece * 256 : (piece + 1) * 256]


def sum_out(sums, mixed_low, att):
    core = my_core()

    @pl.loop(0, 2, unroll=2)
    def _(s):
        low = dot(mixed_low[...], att[:, block(s, 256)], 0, 0).astype(BF)
        for place in range(16):
            z, y, kept = place >> 2, (place >> 1) & 1, place & 1
            sums[core if kept == 0 else 1 - core, s, y, z & 1, (z >> 1) ^ kept, :, :] = low[
                place * 32 : (place + 1) * 32, :
            ]


def split_halvings(unit, bufs, totals, sems, slot):
    upper, lower = unit.at[:, :, :, :, pl.ds(0, 64)], unit.at[:, :, :, :, pl.ds(64, 64)]
    return (
        Halving(upper, 0, X, bufs.at[0], totals.at[0], sems, slot),
        Halving(lower, 1, Y, bufs.at[1], totals.at[1], sems, slot + 1),
    )


def join_halvings(source, less, both, last, final, total, sems, slot):
    return (
        Halving(source.at[0], 0, Y, less.at[0], both.at[0], sems, slot),
        Halving(source.at[1], 0, X, less.at[1], both.at[1], sems, slot + 1),
        Halving(both, 1, LOW, last.at[0], last.at[1], sems, slot + 2),
        Halving(last.at[1], 1, HIGH, final, total, sems, slot + 3),
    )


def decode_last_layers(r):
    @over_tiles(r.first.shape[0])
    def _(here):
        unit, scale = normed(r.first[here, :] + dot(r.att[here, :], r.out_w[...]))
        r.unit0[here, :] = unit
        r.scale0[here, :] = scale
        second = unit * r.dec_gain[1:2, :] + r.dec_shift[1:2, :]
        low = second.astype(BF)
        r.entering[here, :] = low
        for part in parts_of(r.up):
            value, slope = gelu_and_slope(dot(low, r.up[:, part]) + r.up_bias[:, part])
            r.act[here, part] = value.astype(BF)
            r.inner_low[here, part] = slope.astype(BF)
        unit, scale = normed(second + dot(r.act[here, :], r.down[...]) + r.down_bias[...])
        r.unit1[here, :] = unit
        r.scale1[here, :] = scale
        r.decoded[here, :] = (unit * r.dec_gain[2:3, :] + r.dec_shift[2:3, :]).astype(BF)
        r.grad[here, :] = r.upstream[here, :].astype(F32)


def layers_back(r, which):
    vectors = r.vectors

    def add(place, value):
        vectors[which, place : place + 1, :] += value

    @over_tiles(r.grad.shape[0])
    def _(here):
        grad, unit = r.grad[here, :], r.unit1[here, :]
        add(7, column_sum(grad * unit))
        add(8, column_sum(grad))
        grad = normed_back(grad, unit, r.scale1[here, :], r.gains[which, 1:2, :])
        branch = grad.astype(BF)
        r.branch_low[here, :] = branch
        add(4, column_sum(branch.astype(F32)))
        for place, part in enumerate(parts_of(r.up)):
            inner = (dot(branch, r.down[part, :], 1, 1) * r.inner_low[here, part].astype(F32)).astype(BF)
            r.inner_low[here, part] = inner
            add(place, column_sum(inner.astype(F32)))
        grad = grad + dot(r.inner_low[here, :], r.up[...], 1, 1)
        unit = r.unit0[here, :]
        add(5, column_sum(grad * unit))
        add(6, column_sum(grad))
        grad = normed_back(grad, unit, r.scale0[here, :], r.gains[which, 0:1, :])
        r.pre[which, here, :] = grad
        mixed = grad.astype(BF)
        r.mixed_low[here, :] = mixed
        r.att_grad[here, :] = dot(mixed, r.out_w[...], 1, 1).astype(BF)


def middle_body(r):
    step = pl.program_id(0)
    mine, _ = places()
    core = mine[CORE]
    sems = r.sems
    rows, width = r.first.shape[0], r.d_all.shape[2]
    cross = 2
    before = Copies(
        [(r.first_far, r.first), (r.att_far.at[2], r.att), (r.upstream_far, r.upstream), (r.cross_out, r.out_w)], r.load_sems
    )
    dec_layer = Copies([(r.dec_up, r.up), (r.dec_down, r.down)], r.load_sems, 4)
    around = Copies(
        [
            (r.queries_far.at[pl.ds(2, 1)], r.queries), (r.keys_far.at[pl.ds(2, 1)], r.keys),
            (r.values_far.at[pl.ds(2, 1)], r.values), (r.outs_far.at[pl.ds(2, 1)], r.outs), (r.x_far.at[pl.ds(2, 2)], r.x_all),
        ],
        r.load_sems,
        6,
    )
    first_layer = Copies(
        [
            (r.cross_qkv, r.cross_w), (r.dec_out, r.dec_w), (r.first_unit_far, r.first_unit),
            (r.first_scale_far, r.first_scale), (r.att_far.at[1], r.dec_att),
        ],
        r.load_sems,
        11,
    )
    enc_layer = Copies(
        [
            (r.enc_up, r.up), (r.enc_down, r.down), (r.enc_out, r.out_w), (r.unit0_far, r.unit0), (r.scale0_far, r.scale0),
            (r.unit1_far, r.unit1), (r.scale1_far, r.scale1), (r.hidden_far, r.entering), (r.act_far, r.act),
            (r.slope_far, r.inner_low), (r.att_far.at[0], r.att),
        ],
        r.load_sems,
        16,
    )
    down_x = Halving(r.down_sums.at[0], 0, X, r.got_a, r.mid_a, sems, 0)
    up_y = Halving(r.up_sums.at[0], 1, Y, r.got_b, r.mid_b, sems, 1)
    down_y = Halving(r.mid_a, 0, Y, r.got_c, r.pair.at[0], sems, 2)
    up_x = Halving(r.mid_b, 0, X, r.got_d, r.pair.at[1], sems, 3)
    down_low = Halving(r.pair.at[0], 0, LOW, r.got_e.at[0], r.mid_e, sems, 4)
    up_low = Halving(r.pair.at[1], 0, LOW, r.got_e.at[1], r.up_rest, sems, 17)
    down_high = Halving(r.mid_e, 0, HIGH, r.got_f, r.dec_down_sum, sems, 5)
    cross_x, cross_y = split_halvings(r.unit, r.got_g, r.cross_half, sems, 6)
    end = BackEnd(r, 0, r.unit, 0, 1, r.end_sems)
    shared = [
        Across(r.down_sums, r.down_got, sems, 8),
        Across(r.up_sums, r.up_got, sems, 9),
        Across(r.out_sums, r.out_got, sems, 10),
    ]
    dec_shared = Across(r.dec_out_sums, r.dec_out_got, sems, 11)
    lanes, other_lanes = block(core, width), block(1 - core, width)
    there = block(core, rows)

    def grads_of(source, target, slot):
        across = sending(source.at[:, other_lanes], target.at[there], sems, slot, CORE)
        stay = pltpu.make_async_copy(source.at[:, lanes], target.at[there], sems.at[2, slot])
        return across, stay

    cross_grads = grads_of(r.att_grad, r.grad_all.at[0], 12)
    dec_grads = grads_of(r.dec_att_grad, r.grads_far.at[1], 13)
    enc_grads = grads_of(r.att_grad, r.grads_far.at[0], 14)
    beside = pltpu.make_async_copy(r.out_sums.at[0], r.unit.at[:, :, :, :, pl.ds(0, 32)], sems.at[2, 15])
    results = Copies(
        [
            (r.down_sums.at[0], r.down_unit), (r.up_sums.at[0], r.up_unit), (r.out_sums.at[0], r.out_units.at[0]),
            (r.dec_out_sums.at[0], r.out_units.at[1]),
        ],
        r.load_sems,
        27,
    )
    pre_result = Copies([(r.pre, r.pre_far)], r.load_sems, 31)

    @pl.when(step == 0)
    def _():
        call_out(ALL)
        before.start()
        dec_layer.start()
        around.start()
        r.vectors[...] = jnp.zeros_like(r.vectors)
        for place, (ref, row) in enumerate(((r.dec_gain, 1), (r.dec_gain, 2), (r.enc_gain, 0), (r.enc_gain, 1))):
            r.gains[place // 2, place % 2 : place % 2 + 1, :] = ref[row : row + 1, :]
        before.wait()
        dec_layer.wait()
        decode_last_layers(r)
        hear(ALL)
        start_swap(r.decoded, r.decoded_there, sems, 16)

    @pl.when(step == 6)
    def _():
        beside.wait()
        end.wait_sums()
        cross_y.start()
        cross_x.start()
        end.wait_grads()

        @over_tiles(rows)
        def _(here):
            r.grad[here, :] = dot(r.d_full[0, 1, here, :], r.cross_w[1], 1, 1) + dot(
                r.d_full[0, 2, here, :], r.cross_w[2], 1, 1
            )
            grad = r.pre[0, here, :] + dot(r.d_full[0, 0, here, :], r.cross_w[0], 1, 1)
            unit = r.first_unit[here, :]
            r.vectors[2, 0:1, :] += column_sum(grad * unit)
            r.vectors[2, 1:2, :] += column_sum(grad)
            grad = normed_back(grad, unit, r.first_scale[here, :], r.dec_gain[0:1, :])
            r.pre[0, here, :] = grad
            mixed = grad.astype(BF)
            r.dec_mixed[here, :] = mixed
            r.dec_att_grad[here, :] = dot(mixed, r.dec_w[...], 1, 1).astype(BF)

        for copy in dec_grads:
            copy.start()
        sum_out(r.dec_out_sums, r.dec_mixed, r.dec_att)
        dec_shared.start()

    @pl.when(step == 7)
    def _():
        down_y.finish()
        down_low.start()
        enc_layer.wait()

    @pl.when((step == 1) | (step == 7))
    def _():
        layers_back(r, step // 7)

    @pl.when(step == 1)
    def _():
        for copy in cross_grads:
            copy.start()

    @pl.when(step == 7)
    def _():
        for copy in enc_grads:
            copy.start()
        pre_result.start()
        down_low.finish()
        down_high.start()
        up_x.finish()
        up_low.start()

    @pl.when((step == 1) | (step == 7))
    def _():
        sum_down(r.down_sums, r.branch_low, r.act)
        shared[0].start()
        sum_up(r.up_sums, r.inner_low, r.entering)
        shared[1].start()
        shared[0].finish()

        @pl.when(step == 1)
        def _():
            down_x.start()

        sum_out(r.out_sums, r.mixed_low, r.att)
        shared[2].start()

        @pl.when(step == 1)
        def _():
            for copy in cross_grads:
                copy.wait()
            around.wait()
            back_begin(r, 0)

        shared[1].finish()

        @pl.when(step == 1)
        def _():
            up_y.start()

        shared[2].finish()

    @pl.when(step == 1)
    def _():
        beside.start()
        enc_layer.start()
        first_layer.start()

    @pl.when(step == 5)
    def _():
        down_x.finish()
        down_y.start()

    @pl.when((step >= 2) & (step < 6))
    def _():
        back_head(r, 0, step - 2, False)

    @pl.when(step == 5)
    def _():
        first_layer.wait()
        end.start()
        up_y.finish()
        up_x.start()

    @pl.when(step == 7)
    def _():
        dec_shared.finish()
        results.start()
        for copy in (*dec_grads, *enc_grads):
            copy.wait()
        down_high.finish()
        up_low.finish()
        cross_y.finish()
        cross_x.finish()
        results.wait()
        pre_result.wait()
        wait_swap(r.decoded, r.decoded_there, sems, 16)


def last_body(r):
    step = pl.program_id(0)
    which = step // 4
    mine, _ = places()
    sems = r.sems
    rows = r.pre.shape[1]

    def side(att):
        return Copies(
            [
                (r.queries_far.at[att], r.queries.at[att]), (r.keys_far.at[att], r.keys.at[att]),
                (r.values_far.at[att], r.values.at[att]), (r.outs_far.at[att], r.outs.at[att]),
                (r.grads_far.at[att], r.grad_all.at[att]), (r.x_far.at[att], r.x_all.at[att]),
                ((r.enc_qkv, r.dec_qkv)[att], r.weights.at[att]), (r.pre_far.at[1 - att], r.pre.at[att]),
                (r.out_units.at[att], r.units.at[att, :, :, :, :, pl.ds(0, 32)]),
            ],
            r.load_sems,
            att * 9,
        )

    def layer_steps(unit, bufs, total, slot, ways):
        left, steps, source = [X, Y, LOW, HIGH], [], unit
        for place, way in enumerate(ways):
            got, kept = (bufs[2 * place], bufs[2 * place + 1]) if place < 3 else (bufs[6], total)
            steps.append(Halving(source, left.index(way), way, got, kept, sems, slot + place, far=place == 0))
            left.remove(way)
            source = kept
        return steps

    down = layer_steps(r.down_unit, r.down_bufs, r.enc_sums.at[0], 0, (X, Y, LOW, HIGH))
    up = layer_steps(r.up_unit, r.up_bufs, r.enc_sums.at[1], 4, (Y, LOW, HIGH, X))
    cross = join_halvings(r.cross_half, *r.cross_bufs, r.cross_sum, sems, 8)
    dec_up_high = Halving(r.up_rest, 0, HIGH, r.rest_got, r.dec_up_sum, sems, 17)
    enc_got, enc_mid, *enc_bufs = r.enc_bufs
    enc_x, enc_y = split_halvings(r.units.at[0], enc_got, enc_mid, sems, 18)
    enc_att = join_halvings(enc_mid, *enc_bufs, r.enc_att_sum, sems, 20)
    dec_got, dec_mid, *dec_bufs = r.dec_bufs
    dec_x, dec_y = split_halvings(r.units.at[1], dec_got, dec_mid, sems, 24)
    dec_att = join_halvings(dec_mid, *dec_bufs, r.dec_att_sum, sems, 26)
    vector_ways = (X, Y, CORE, LOW, HIGH)

    def vector_parts(place):
        source = r.vectors if place == 0 else r.vector_mid.at[place - 1]
        total = r.vector_sum if place == 4 else r.vector_mid.at[place]
        copy = sending(source, r.vector_got.at[place], sems, 12 + place, vector_ways[place])
        return source, r.vector_got.at[place], total, copy

    def vector_start(place):
        vector_parts(place)[3].start()

    def vector_finish(place):
        source, got, total, copy = vector_parts(place)
        copy.wait()
        total[...] = source[...] + got[...]

    end = BackEnd(r, which, r.units.at[which], which, which, r.end_sems)

    def row_grads(index):
        @over_tiles(rows)
        def _(here):
            total = r.pre[index, here, :]
            for kind in range(3):
                total = total + dot(r.d_full[index, kind, here, :], r.weights[index, kind], 1, 1)
            r.row_grad[index, here, :] = total.astype(BF)

    src_swap = (r.row_grad.at[0], r.src_there, sems, 30)
    tgt_swap = (r.row_grad.at[1], r.tgt_there, sems, 31)

    @pl.when(step == 0)
    def _():
        call_out(ALL)
        side(0).start()
        side(1).start()
        side(0).wait()
        hear(ALL)
        vector_start(0)
        dec_up_high.start()
        cross[0].start()
        cross[1].start()
        down[0].start()
        up[0].start()

    @pl.when(step == 4)
    def _():
        side(1).wait()
        BackEnd(r, 0, r.units.at[0], 0, 0, r.end_sems).wait_sums()
        enc_x.start()
        enc_y.start()

    @pl.when((step == 0) | (step == 4))
    def _():
        back_begin(r, which)

    @pl.when(step == 1)
    def _():
        vector_finish(0)
        vector_start(1)

    @pl.when(step == 2)
    def _():
        dec_up_high.finish()
        cross[0].finish()
        cross[1].finish()
        cross[2].start()

    @pl.when(step == 4)
    def _():
        BackEnd(r, 0, r.units.at[0], 0, 0, r.end_sems).wait_grads()
        row_grads(0)
        start_swap(*src_swap)
        down[0].finish()
        down[1].start()
        up[0].finish()
        up[1].start()

    @pl.when(step == 6)
    def _():
        vector_finish(2)
        vector_start(3)

    @pl.when(step == 5)
    def _():
        vector_finish(1)
        vector_start(2)
        cross[3].finish()

    @pl.when(step == 7)
    def _():
        enc_x.finish()
        enc_att[0].start()
        enc_y.finish()
        enc_att[1].start()

    @pl.when(step < 4)
    def _():
        back_head(r, 0, step, False)

    @pl.when(step >= 4)
    def _():
        back_head(r, 1, step - 4, True)

    @pl.when((step == 3) | (step == 7))
    def _():
        end.start()

    @pl.when(step == 3)
    def _():
        cross[2].finish()
        cross[3].start()

    @pl.when(step == 7)
    def _():
        up[1].finish()
        up[2].start()
        end_of_dec = BackEnd(r, 1, r.units.at[1], 1, 1, r.end_sems)
        end_of_dec.wait_sums()
        dec_x.start()
        dec_y.start()
        end_of_dec.wait_grads()
        row_grads(1)
        down[1].finish()
        down[2].start()
        enc_att[0].finish()
        enc_att[1].finish()
        enc_att[2].start()
        vector_finish(3)
        vector_start(4)
        down[2].finish()
        down[3].start()
        dec_x.finish()
        dec_att[0].start()
        dec_y.finish()
        dec_att[1].start()
        start_swap(*tgt_swap)
        up[2].finish()
        up[3].start()
        enc_att[2].finish()
        enc_att[3].start()
        dec_att[0].finish()
        dec_att[1].finish()
        dec_att[2].start()
        vector_finish(4)
        down[3].finish()
        up[3].finish()
        enc_att[3].finish()
        dec_att[2].finish()
        dec_att[3].start()
        dec_att[3].finish()
        wait_swap(*src_swap)
        wait_swap(*tgt_swap)


def finish_body(r):
    r.decoded_out[...] = r.decoded[...]
    r.src_out[...] = r.src[...]
    r.tgt_out[...] = r.tgt[...]
    for sums, down in ((r.dec_down_sum[...], r.dec_down), (r.enc_sums[0], r.enc_down)):
        for slot in range(4):
            down[:, slot * 256 : (slot + 1) * 256] = sums[slot * 32 : (slot + 1) * 32, :]
    r.dec_up[...] = r.dec_up_sum[...].T
    r.enc_up[...] = r.enc_sums[1].T
    cross, enc_att, dec_att = [
        jnp.concatenate([one[0], one[1]], axis=0) for one in (r.cross_sum, r.enc_att_sum, r.dec_att_sum)
    ]
    for sums, out, qkv in (
        (cross, r.cross_out, r.cross_qkv),
        (enc_att, r.enc_out, r.enc_qkv),
        (dec_att, r.dec_out, r.dec_qkv),
    ):
        out[...] = sums[:32]
        for kind in range(3):
            qkv[kind] = sums[32 + kind * 32 : 64 + kind * 32]
    vectors = r.vectors
    for which, up_bias, down_bias in ((0, r.dec_up_bias, r.dec_down_bias), (1, r.enc_up_bias, r.enc_down_bias)):
        for part in range(4):
            up_bias[:, part * 512 : (part + 1) * 512] = vectors[which, part : part + 1, :]
        down_bias[...] = vectors[which, 4:5, :]
    for ref, found in (
        (r.dec_gain, ((2, 0), (0, 5), (0, 7))),
        (r.dec_shift, ((2, 1), (0, 6), (0, 8))),
        (r.enc_gain, ((1, 5), (1, 7))),
        (r.enc_shift, ((1, 6), (1, 8))),
    ):
        for index, (which, place) in enumerate(found):
            ref[index : index + 1, :] = vectors[which, place : place + 1, :]


def launch(body, micros, grid, meeting, ins, far, blocks, outs, far_outs, scratch):
    def once(shape):
        rank = len(shape)
        return pl.BlockSpec(shape, lambda step: (0,) * rank, pipeline_mode=pl.Buffered(1))

    names, arrays, in_specs, out_names, shapes, out_specs = [], [], [], [], [], []
    for name, array in {**ins, **far}.items():
        names.append(name)
        arrays.append(array)
        in_specs.append(once(array.shape) if name in ins else ANY)
    for name, (shape, kind) in {**outs, **far_outs}.items():
        out_names.append(name)
        shapes.append(jax.ShapeDtypeStruct(shape, kind))
        out_specs.append(once(shape) if name in outs else ANY)
    for name, (array, part, index, is_out) in blocks.items():
        spec = pl.BlockSpec(part, index)
        if is_out:
            out_names.append(name)
            shapes.append(jax.ShapeDtypeStruct(*array))
            out_specs.append(spec)
        else:
            names.append(name)
            arrays.append(array)
            in_specs.append(spec)
    every = (*names, *out_names, *scratch)

    def kernel(*refs):
        body(types.SimpleNamespace(**dict(zip(every, refs))))

    results = pl.pallas_call(
        kernel,
        grid=(grid,),
        out_shape=shapes,
        in_specs=in_specs,
        out_specs=out_specs,
        scratch_shapes=list(scratch.values()),
        compiler_params=pltpu.CompilerParams(
            vmem_limit_bytes=60 * 2**20, collective_id=meeting, has_side_effects=meeting is not None
        ),
        cost_estimate=pl.CostEstimate(flops=int(micros * 1e9), bytes_accessed=0, transcendentals=0),
        name=body.__name__,
    )(*arrays)
    return types.SimpleNamespace(**dict(zip(out_names, results)))


def low(*shape):
    return pltpu.VMEM(shape, BF)


def wide(*shape):
    return pltpu.VMEM(shape, F32)


def fast_shards(source, target, source_ids, target_ids, out_grad, *params):
    (
        enc_qkv, enc_out, enc_up, enc_up_bias, enc_down, enc_down_bias, enc_gain, enc_shift, dec_qkv, dec_out,
        cross_qkv, cross_out, dec_up, dec_up_bias, dec_down, dec_down_bias, dec_gain, dec_shift,
    ) = params
    source, target, upstream = source[0], target[0], out_grad[0]
    rows, size = source.shape
    length, inner, width = 2 * rows, enc_up.shape[1], size // 2
    heads = width // HEAD_DIM
    sem = pltpu.SemaphoreType.DMA
    full, thin, low_full, low_inner = ((rows, size), F32), ((rows, 1), F32), ((rows, size), BF), ((rows, inner), BF)
    biases = [one[None, :] for one in (enc_up_bias, enc_down_bias, dec_up_bias, dec_down_bias)]
    enc_up_b, enc_down_b, dec_up_b, dec_down_b = biases
    head_block = (1, length, length)
    per_head = (heads, length, 2 * HEAD_DIM)

    f = launch(
        forward_body,
        60,
        7,
        0,
        dict(up_bias=enc_up_b, down_bias=enc_down_b, enc_gain=enc_gain, enc_shift=enc_shift, dec_gain=dec_gain, dec_shift=dec_shift),
        dict(
            source=source, target=target, source_ids=source_ids, target_ids=target_ids, upstream=upstream,
            enc_qkv=enc_qkv, dec_qkv=dec_qkv, cross_qkv=cross_qkv, enc_out_far=enc_out, dec_out_far=dec_out,
            up_far=enc_up, down_far=enc_down,
        ),
        dict(
            chances=(
                ((3 * heads, length, length), BF),
                (2, length, length),
                lambda step: (jnp.where(step < 4, step, jnp.maximum(step - 1, 4)), 0, 0),
                True,
            )
        ),
        {},
        dict(
            x_far=((4, length, size), BF), upstream_there=low_full, queries_far=((3, *per_head), BF),
            keys_far=((3, *per_head), BF), values_far=((3, *per_head), BF), outs_far=((3, *per_head), F32),
            att_far=((3, rows, size), BF), unit0_far=full, scale0_far=thin, unit1_far=full, scale1_far=thin,
            hidden_far=low_full, act_far=low_inner, slope_far=low_inner, first_far=full, first_unit_far=full,
            first_scale_far=thin,
        ),
        dict(
            sems=sem((2, 31)), near_sems=sem((4,)), load_sems=sem((7,)), save_sems=sem((24,)),
            x_all=low(4, length, size), ids=pltpu.VMEM((2, 2, 1, rows), jnp.int32), weights=low(3, 3, size, size),
            queries=low(2, *per_head), keys=low(2, *per_head), values=low(2, *per_head),
            outs=wide(2, *per_head), att_all=low(3, rows, size),
            att_send=low(3, rows, width), enc_out=low(size, size), dec_out=low(size, size), up=low(size, inner),
            down=low(inner, size), unit0=wide(rows, size), scale0=wide(rows, 1), unit1=wide(rows, size),
            scale1=wide(rows, 1), hidden_low=low(rows, size), act=low(rows, inner), slope=low(rows, inner),
            first=wide(rows, size), first_unit=wide(rows, size), first_scale=wide(rows, 1),
        ),
    )
    work = dict(
        grads=low(*per_head), score_grads=low(length, length), dq=low(heads, length, HEAD_DIM), dk=wide(width, length),
        dv=wide(width, length), d_all=low(3, length, width), shares=low(2, 2, 2, 2, 96, 256), end_sems=sem((3, 4)),
    )
    one_sum = ((128, 256), F32)
    sums_out = ((2, 128, 256), F32)
    halves = ((2, 64, 256), F32)
    m = launch(
        middle_body,
        50,
        8,
        1,
        dict(dec_gain=dec_gain, dec_shift=dec_shift, enc_gain=enc_gain, up_bias=dec_up_b, down_bias=dec_down_b),
        dict(
            first_far=f.first_far, att_far=f.att_far, upstream_far=f.upstream_there, cross_out=cross_out, dec_up=dec_up,
            dec_down=dec_down, queries_far=f.queries_far, keys_far=f.keys_far, values_far=f.values_far,
            outs_far=f.outs_far, x_far=f.x_far, cross_qkv=cross_qkv, dec_out=dec_out, first_unit_far=f.first_unit_far,
            first_scale_far=f.first_scale_far, enc_up=enc_up, enc_down=enc_down, enc_out=enc_out,
            unit0_far=f.unit0_far, scale0_far=f.scale0_far, unit1_far=f.unit1_far, scale1_far=f.scale1_far,
            hidden_far=f.hidden_far, act_far=f.act_far, slope_far=f.slope_far,
        ),
        dict(chances=(f.chances, head_block, lambda step: (8 + jnp.clip(step - 2, 0, 3), 0, 0), False)),
        dict(dec_down_sum=one_sum, up_rest=(LEAST, BF), cross_half=(HALF, BF), vectors=((3, 16, size), F32)),
        dict(
            decoded_there=low_full, grads_far=((2, length, width), BF), down_unit=(BIG, BF), up_unit=(BIG, BF),
            out_units=((2, *OUT), BF), pre_far=((2, rows, size), F32),
        ),
        dict(
            sems=sem((3, 18)), load_sems=sem((32,)), **work,
            first=wide(rows, size), att=low(rows, size), upstream=low(rows, size), out_w=low(size, size),
            up=low(size, inner), down=low(inner, size), queries=low(1, *per_head), keys=low(1, *per_head),
            values=low(1, *per_head), outs=wide(1, *per_head), x_all=low(2, length, size), cross_w=low(3, size, size),
            dec_w=low(size, size), first_unit=wide(rows, size), first_scale=wide(rows, 1), dec_att=low(rows, size),
            unit0=wide(rows, size), scale0=wide(rows, 1), unit1=wide(rows, size), scale1=wide(rows, 1),
            entering=low(rows, size), act=low(rows, inner), inner_low=low(rows, inner), branch_low=low(rows, size),
            mixed_low=low(rows, size), att_grad=low(rows, size), dec_att_grad=low(rows, size), dec_mixed=low(rows, size),
            grad=wide(rows, size), pre=wide(2, rows, size), gains=wide(2, 2, size), decoded=low(rows, size),
            grad_all=low(1, length, width), d_full=low(1, 3, rows, size), unit=low(*BIG),
            down_sums=low(2, *BIG), up_sums=low(2, *BIG), out_sums=low(2, *OUT), dec_out_sums=low(2, *OUT),
            down_got=low(*BIG), up_got=low(*BIG), out_got=low(*OUT), dec_out_got=low(*OUT),
            got_a=low(*MID), mid_a=low(*MID), got_b=low(*MID), mid_b=low(*MID), got_c=low(*LESS), got_d=low(*LESS),
            pair=low(2, *LESS), got_e=low(2, *LEAST), mid_e=low(*LEAST), got_f=low(128, 256), got_g=low(*HALF),
        ),
    )
    less, least = (2, 2, 2, 64, 256), (2, 64, 256)
    down_bufs = [low(*MID), low(*MID), low(*LESS), low(*LESS), low(*LEAST), low(*LEAST), low(128, 256)]
    up_bufs = [low(*MID), low(*MID), low(*LESS), low(*LESS), low(*LEAST), low(*LEAST), low(128, 256)]
    join_bufs = [low(*less), low(*less), low(*less), low(*least)]
    split_bufs = [low(*HALF), low(*HALF), *join_bufs]
    b = launch(
        last_body,
        60,
        8,
        2,
        dict(cross_half=m.cross_half, up_rest=m.up_rest, vectors=m.vectors),
        dict(
            queries_far=f.queries_far, keys_far=f.keys_far, values_far=f.values_far, outs_far=f.outs_far, x_far=f.x_far,
            grads_far=m.grads_far, enc_qkv=enc_qkv, dec_qkv=dec_qkv, pre_far=m.pre_far, out_units=m.out_units,
            down_unit=m.down_unit, up_unit=m.up_unit,
        ),
        dict(chances=(f.chances, head_block, lambda step: (step, 0, 0), False)),
        dict(
            enc_sums=sums_out, dec_up_sum=one_sum, cross_sum=halves, enc_att_sum=halves, dec_att_sum=halves,
            vector_sum=((3, 16, size), F32),
        ),
        dict(src_there=low_full, tgt_there=low_full),
        dict(
            sems=sem((3, 32)), load_sems=sem((18,)), **work,
            queries=low(2, *per_head), keys=low(2, *per_head), values=low(2, *per_head), outs=wide(2, *per_head),
            grad_all=low(2, length, width), x_all=low(2, length, size), weights=low(2, 3, size, size),
            pre=wide(2, rows, size), d_full=low(2, 3, rows, size), units=low(2, *BIG), row_grad=low(2, rows, size),
            vector_got=wide(5, 3, 16, size), vector_mid=wide(4, 3, 16, size), down_bufs=down_bufs, up_bufs=up_bufs,
            enc_bufs=split_bufs, cross_bufs=join_bufs, dec_bufs=split_bufs, rest_got=low(128, 256),
        ),
    )
    cut3, cut, pair, triple = ((3, 32, 256), F32), ((32, 256), F32), ((2, size), F32), ((3, size), F32)
    up_cut, down_cut, up_b, down_b = ((256, 128), F32), ((32, 1024), F32), ((1, inner), F32), ((1, size), F32)
    o = launch(
        finish_body,
        2,
        1,
        None,
        dict(
            decoded=m.decoded_there, src=b.src_there, tgt=b.tgt_there, dec_down_sum=m.dec_down_sum, dec_up_sum=b.dec_up_sum,
            enc_sums=b.enc_sums,
            cross_sum=b.cross_sum, enc_att_sum=b.enc_att_sum, dec_att_sum=b.dec_att_sum, vectors=b.vector_sum,
        ),
        {},
        {},
        dict(
            decoded_out=low_full, src_out=low_full, tgt_out=low_full, enc_qkv=cut3, enc_out=cut, enc_up=up_cut,
            enc_up_bias=up_b, enc_down=down_cut, enc_down_bias=down_b, enc_gain=pair, enc_shift=pair, dec_qkv=cut3,
            dec_out=cut, cross_qkv=cut3, cross_out=cut, dec_up=up_cut, dec_up_bias=up_b, dec_down=down_cut,
            dec_down_bias=down_b, dec_gain=triple, dec_shift=triple,
        ),
        {},
        {},
    )

    def turned(value):
        return jnp.swapaxes(value, -1, -2)

    return (
        o.decoded_out[None], o.src_out[None], o.tgt_out[None], turned(o.enc_qkv), turned(o.enc_out), o.enc_up,
        o.enc_up_bias[0], turned(o.enc_down), o.enc_down_bias[0], o.enc_gain, o.enc_shift, turned(o.dec_qkv),
        turned(o.dec_out), turned(o.cross_qkv), turned(o.cross_out), o.dec_up, o.dec_up_bias[0], turned(o.dec_down),
        o.dec_down_bias[0], o.dec_gain, o.dec_shift,
    )


def solution(mesh):
    if mesh.shape[SEQ] != 2 or mesh.shape[BATCH] != 16:
        return general(mesh)
    tokens = P(BATCH, SEQ, None)
    ids = P(BATCH, SEQ)
    cut, cut3 = P(SEQ, BATCH), P(None, SEQ, BATCH)
    return jax.shard_map(
        fast_shards,
        mesh=mesh,
        in_specs=(tokens, tokens, ids, ids, tokens) + (P(),) * 18,
        out_specs=(
            tokens, tokens, tokens, cut3, cut, cut, P(), cut, P(), P(), P(), cut3, cut, cut3, cut, cut, P(), cut,
            P(), P(), P(),
        ),
        check_vma=False,
    )
```
